32 devices in a mesh: ctx: 8 (over z, x), heads: 4 (over y, core).
Axes of the slice: x: 2, y: 2, z: 4, core: 2. Of those that a mesh axis runs over, the one named last changes fastest.
Arguments:
- q_raw: bfloat16 [2048, 8192], P('ctx', 'heads'), may hold values from -60 to 60
- k_raw: bfloat16 [2048, 1024], P('ctx', 'heads'), may hold values from -60 to 60
- values: bfloat16 [2048, 1024], P('ctx', 'heads'), may hold values from -6 to 6
- saved_out: bfloat16 [2048, 8192], P('ctx', 'heads'), may hold values from -6 to 6
- out_grad: bfloat16 [2048, 8192], P('ctx', 'heads'), may hold values from -60 to 60
- q_gain: float32 [128], replicated, may hold values from 0.25 to 1.75
- k_gain: float32 [128], replicated, may hold values from 0.25 to 1.75
- ancestors: int32 [32, 32], P('ctx'), may hold values from -1 to 31, as said below
Outputs:
- dq_raw: bfloat16 [2048, 8192], P('ctx', 'heads')
- dk_raw: bfloat16 [2048, 1024], P('ctx', 'heads')
- dv: bfloat16 [2048, 1024], P('ctx', 'heads')
- q_gain_grad: float32 [128], replicated
- k_gain_grad: float32 [128], replicated
The draws below stay inside these ranges and needn't reach their ends.
Inputs may be any that keep to these rules, and one draw needn't show every extreme that they name: `ancestors`: the forest is 1 trees of 32 blocks each; in tree order, tree k holds blocks (k * 32 + 256 / 64 + b) mod 32 for b = 0 to 31. Row b lists, in tree order, every block on the path from its tree's first block to b, ending with b itself, then -1s. The first 16 blocks of a tree form its prompt, each the child of the block before it; every other block's parent is a block earlier in its tree, from the prompt's last block on.
All inputs are finite; a program needn't handle non-finite values.
Results may differ from the reference program's by a relative error of at most 0.0069.
Values may be sent and summed in bfloat16 or wider, within the bound.
No kernel may reach another device: no remote copies, remote signals or barrier semaphores. Data moves between devices by JAX's collectives and lax.ppermute only.
A program may use at most 64 MiB of HBM per device.

```python
import math
import jax
import jax.numpy as jnp
from jax import lax

Q_HEADS = 64
KV_HEADS = 8
HEAD = 128
BLOCK = 64
TOK_DEV = 256
TOKENS = 2048
NBLK = 32
TREE_BLK = 32
PROMPT_BLK = 16


def draw_q_raw(key, part):
    key_scale, key_base = jax.random.split(key, 2)
    scales = jnp.exp(jax.random.uniform(key_scale, (TOKENS, Q_HEADS, 1), jnp.float32, 0.0, math.log(10.0)))
    entries = jnp.clip(jax.random.normal(key_base, (TOKENS, Q_HEADS, HEAD), jnp.float32), -5.0, 5.0)
    return (entries * scales).reshape(TOKENS, Q_HEADS * HEAD).astype(jnp.bfloat16)


def draw_k_raw(key, part):
    key_scale, key_base = jax.random.split(key, 2)
    scales = jnp.exp(jax.random.uniform(key_scale, (TOKENS, KV_HEADS, 1), jnp.float32, 0.0, math.log(10.0)))
    entries = jnp.clip(jax.random.normal(key_base, (TOKENS, KV_HEADS, HEAD), jnp.float32), -5.0, 5.0)
    return (entries * scales).reshape(TOKENS, KV_HEADS * HEAD).astype(jnp.bfloat16)


def draw_out_grad(key, part):
    key_scale, key_base = jax.random.split(key, 2)
    rising = math.log(3.0) / TOKENS * jnp.arange(TOKENS, dtype=jnp.float32)[:, None, None]
    scales = jnp.exp(rising + jax.random.uniform(key_scale, (TOKENS, Q_HEADS, 1), jnp.float32, 0.0, math.log(4.0)))
    entries = jnp.clip(jax.random.normal(key_base, (TOKENS, Q_HEADS, HEAD), jnp.float32), -5.0, 5.0)
    return (entries * scales).reshape(TOKENS, Q_HEADS * HEAD).astype(jnp.bfloat16)


def draw_ancestors(key, part):
    tree_count = NBLK // TREE_BLK
    shift_blocks = TOK_DEV // BLOCK
    within = jnp.arange(TREE_BLK, dtype=jnp.int32)

    def one_tree(tree_index):
        tree_key = jax.random.fold_in(key, tree_index)
        key_start, key_pick = jax.random.split(tree_key)
        starts = jax.random.randint(key_start, (TREE_BLK,), 0, 3) == 0
        spread = jnp.maximum(within - (PROMPT_BLK - 1), 1)
        picked = jax.random.randint(key_pick, (TREE_BLK,), 0, 1 << 20) % spread + (PROMPT_BLK - 1)
        parent = within - 1
        parent = jnp.where((within > PROMPT_BLK) & starts, picked, parent)

        def climb_up(level, loop_state):
            member, current = loop_state
            member = member | (current[:, None] == within[None, :])
            current = jnp.where(current >= 0, parent[jnp.maximum(current, 0)], -1)
            return (member, current)
        member, _ = lax.fori_loop(0, TREE_BLK, climb_up, (jnp.zeros((TREE_BLK, TREE_BLK), jnp.bool_), within))
        ordered = jnp.sort(jnp.where(member, within[None, :], TREE_BLK + within[None, :]), axis=1)
        return jnp.where(ordered < TREE_BLK, ordered + tree_index * TREE_BLK, -1)
    block_lists = jax.vmap(one_tree)(jnp.arange(tree_count, dtype=jnp.int32))
    block_lists = block_lists.reshape(NBLK, TREE_BLK).astype(jnp.int32)
    moved = jnp.where(block_lists >= 0, (block_lists + shift_blocks) % NBLK, -1)
    return jnp.roll(moved, shift_blocks, 0).astype(jnp.int32)


def block_scale(own_key, extent, pieces, smallest, largest):
    gain, own = 1.0, jax.random.fold_in(own_key, 6)
    for position, blocks in pieces:
        steps = jnp.exp(jax.random.uniform(jax.random.fold_in(own, position), (blocks,), jnp.float32, smallest / len(pieces), largest / len(pieces)))
        gain = gain * jnp.repeat(steps, extent[position] // blocks).reshape([-1 if axis == position else 1 for axis in range(len(extent))])
    return gain


def centred(rng, shape, scale, bound, cuts=(), held_as=jnp.bfloat16):
    values = scale * jax.random.normal(rng, shape, jnp.float32)
    if cuts:
        values = values * block_scale(rng, shape, cuts, -0.22, 0.18)
    return jnp.clip(values, -bound, bound).astype(held_as)


def setup_inputs(seed: int = 0) -> dict:
    seeds = jax.random.split(jax.random.key(seed), 9)
    return {
        "q_raw": draw_q_raw(jax.random.fold_in(seeds[8], 71), 0),
        "k_raw": draw_k_raw(jax.random.fold_in(seeds[8], 71), 0),
        "values": centred(seeds[2], (TOKENS, KV_HEADS * HEAD), 1.0, 6.0, ((0, 8), (1, 4))),
        "saved_out": centred(seeds[3], (TOKENS, Q_HEADS * HEAD), 1.0, 6.0, ((0, 8), (1, 4))),
        "out_grad": draw_out_grad(jax.random.fold_in(seeds[8], 71), 0),
        "q_gain": jnp.clip(1.0 + 0.15 * jax.random.normal(seeds[5], (HEAD,), jnp.float32), 0.25, 1.75),
        "k_gain": jnp.clip(1.0 + 0.15 * jax.random.normal(seeds[6], (HEAD,), jnp.float32), 0.25, 1.75),
        "ancestors": draw_ancestors(jax.random.fold_in(seeds[8], 71), 0),
    }


ROPE_BASE = 1000000.0
EPS = 1e-06

def rope_tables(positions, head_dim):
    half_dim = head_dim // 2
    frequency = jnp.exp(jnp.arange(half_dim, dtype=jnp.float32) * (-2.0 * math.log(ROPE_BASE) / head_dim))
    angles = positions.astype(jnp.float32)[:, None] * frequency[None, :]
    return (jnp.cos(angles), jnp.sin(angles))

def norm_rope(inputs, gain_vec, cos_table, sin_table):
    recip_rms = lax.rsqrt(lax.optimization_barrier(jnp.mean(inputs * inputs, -1, keepdims=True)) + EPS)
    scaled = inputs * recip_rms * gain_vec
    half_dim = inputs.shape[-1] // 2
    cos_part = cos_table[:, None, :]
    sin_part = sin_table[:, None, :]
    front_half = scaled[..., :half_dim]
    back_half = scaled[..., half_dim:]
    return jnp.concatenate([front_half * cos_part - back_half * sin_part, back_half * cos_part + front_half * sin_part], -1)

def norm_rope_back(inputs, gain_vec, cos_table, sin_table, upstream):
    half_dim = inputs.shape[-1] // 2
    cos_part = cos_table[:, None, :]
    sin_part = sin_table[:, None, :]
    front_half = upstream[..., :half_dim]
    back_half = upstream[..., half_dim:]
    unrotated = jnp.concatenate([front_half * cos_part + back_half * sin_part, back_half * cos_part - front_half * sin_part], -1)
    recip_rms = lax.rsqrt(lax.optimization_barrier(jnp.mean(inputs * inputs, -1, keepdims=True)) + EPS)
    normed = inputs * recip_rms
    gain_term = lax.optimization_barrier(jnp.sum(unrotated * normed, axis=(0, 1)))
    gain_grad = unrotated * gain_vec
    input_grad = recip_rms * (gain_grad - normed * lax.optimization_barrier(jnp.mean(gain_grad * normed, -1, keepdims=True)))
    return (input_grad, gain_term)

def reference(q_raw, k_raw, values, saved_out, out_grad, q_gain, k_gain, ancestors):
    inv_root = 1.0 / math.sqrt(HEAD)
    group_size = Q_HEADS // KV_HEADS
    shift_blocks = TOK_DEV // BLOCK
    q_raw = jnp.roll(q_raw, -TOK_DEV, 0)
    k_raw = jnp.roll(k_raw, -TOK_DEV, 0)
    values = jnp.roll(values, -TOK_DEV, 0)
    saved_out = jnp.roll(saved_out, -TOK_DEV, 0)
    out_grad = jnp.roll(out_grad, -TOK_DEV, 0)
    ancestors = jnp.roll(ancestors, -shift_blocks, 0)
    ancestors = jnp.where(ancestors >= 0, (ancestors - shift_blocks + NBLK) % NBLK, -1).astype(jnp.int32)
    offsets = jnp.arange(BLOCK, dtype=jnp.int32)
    depth_count = lax.optimization_barrier(jnp.sum((ancestors >= 0).astype(jnp.int32), 1))
    positions = (((depth_count - 1) * BLOCK)[:, None] + offsets[None, :]).reshape(TOKENS)
    cos_table, sin_table = rope_tables(positions, HEAD)
    q_float = q_raw.astype(jnp.float32).reshape(TOKENS, Q_HEADS, HEAD)
    k_float = k_raw.astype(jnp.float32).reshape(TOKENS, KV_HEADS, HEAD)
    q_rot = norm_rope(q_float, q_gain, cos_table, sin_table).astype(jnp.bfloat16)
    q_rot = q_rot.reshape(NBLK, BLOCK, KV_HEADS, group_size, HEAD)
    k_rot = norm_rope(k_float, k_gain, cos_table, sin_table).astype(jnp.bfloat16)
    v_heads = values.reshape(TOKENS, KV_HEADS, HEAD)
    grad_heads = out_grad.reshape(NBLK, BLOCK, KV_HEADS, group_size, HEAD)
    out_heads = saved_out.reshape(NBLK, BLOCK, KV_HEADS, group_size, HEAD)
    tree_len = TREE_BLK * BLOCK

    def per_block(loop_state, block_index):
        dk_acc, dv_acc = loop_state
        tree_first = block_index // TREE_BLK * TREE_BLK
        start_tok = (tree_first * BLOCK).astype(jnp.int32)
        tree_keys = lax.dynamic_slice_in_dim(k_rot, start_tok, tree_len, 0).astype(jnp.float32)
        tree_values = lax.dynamic_slice_in_dim(v_heads, start_tok, tree_len, 0).astype(jnp.float32)
        key_blocks = tree_first + jnp.arange(TREE_BLK, dtype=jnp.int32)
        block_vis = jnp.any(ancestors[block_index][:, None] == key_blocks[None, :], 0)
        key_tok = start_tok + jnp.arange(tree_len, dtype=jnp.int32)
        query_tok = block_index * BLOCK + offsets
        allowed = jnp.repeat(block_vis, BLOCK)[None, :] & (key_tok[None, :] <= query_tok[:, None])
        queries = q_rot[block_index].astype(jnp.float32)
        grad_rows = grad_heads[block_index].astype(jnp.float32)
        out_rows = out_heads[block_index].astype(jnp.float32)
        scores = jnp.einsum('ikgd,jkd->kgij', queries, tree_keys) * inv_root
        log_mass = jnp.log(lax.optimization_barrier(jnp.sum(jnp.where(allowed[None, None], jnp.exp(scores), 0.0), -1)))
        weights = jnp.where(allowed[None, None], jnp.exp(scores - log_mass[..., None]), 0.0)
        weights_low = lax.optimization_barrier(weights.astype(jnp.bfloat16)).astype(jnp.float32)
        row_delta = jnp.transpose(lax.optimization_barrier(jnp.sum(grad_rows * out_rows, -1)), (1, 2, 0))
        grad_prob = jnp.einsum('ikgd,jkd->kgij', grad_rows, tree_values)
        dscore = (weights * (grad_prob - row_delta[..., None]) * inv_root).astype(jnp.bfloat16)
        dscore = lax.optimization_barrier(dscore).astype(jnp.float32)
        dq_part = jnp.einsum('kgij,jkd->ikgd', dscore, tree_keys)
        dk_part = jnp.einsum('kgij,ikgd->jkd', dscore, queries)
        dv_part = jnp.einsum('kgij,ikgd->jkd', weights_low, grad_rows)
        current_k = lax.dynamic_slice_in_dim(dk_acc, start_tok, tree_len, 0)
        dk_acc = lax.dynamic_update_slice_in_dim(dk_acc, current_k + dk_part, start_tok, 0)
        current_v = lax.dynamic_slice_in_dim(dv_acc, start_tok, tree_len, 0)
        dv_acc = lax.dynamic_update_slice_in_dim(dv_acc, current_v + dv_part, start_tok, 0)
        return ((dk_acc, dv_acc), dq_part)
    zero_keys = jnp.zeros((TOKENS, KV_HEADS, HEAD), jnp.float32)
    (dk_rot, dv_acc), dq_parts = lax.scan(per_block, (zero_keys, zero_keys), jnp.arange(NBLK, dtype=jnp.int32))
    dq_rot = dq_parts.reshape(TOKENS, Q_HEADS, HEAD)
    dq_input, q_gain_grad = norm_rope_back(q_float, q_gain, cos_table, sin_table, dq_rot)
    dk_input, k_gain_grad = norm_rope_back(k_float, k_gain, cos_table, sin_table, dk_rot)
    dq_raw = jnp.roll(dq_input.astype(jnp.bfloat16).reshape(TOKENS, Q_HEADS * HEAD), TOK_DEV, 0)
    dk_raw = jnp.roll(dk_input.astype(jnp.bfloat16).reshape(TOKENS, KV_HEADS * HEAD), TOK_DEV, 0)
    dv = jnp.roll(dv_acc.astype(jnp.bfloat16).reshape(TOKENS, KV_HEADS * HEAD), TOK_DEV, 0)
    return (dq_raw, dk_raw, dv, q_gain_grad, k_gain_grad)
```

```python
import math

import jax
import jax.numpy as jnp
import numpy as np
from jax import lax
from jax.experimental import pallas as pl
from jax.experimental.pallas import tpu as pltpu
from jax.sharding import PartitionSpec as P

ROPE_BASE = 1000000.0
EPS = 1e-06
LOG2_E = 1.4426950408889634
HIDDEN = -100000.0
VMEM_LIMIT = 48 * 1024 * 1024
F32 = jnp.float32
BF16 = jnp.bfloat16


def rope_rows(count, head_dim):
    half = head_dim // 2
    frequency = np.exp(
        np.arange(half, dtype=np.float32) * np.float32(-2.0 * math.log(ROPE_BASE) / head_dim)
    ).astype(np.float32)
    angles = np.arange(count, dtype=np.float32)[:, None] * frequency[None, :]
    cos = np.cos(angles.astype(np.float64)).astype(np.float32)
    sin = np.sin(angles.astype(np.float64)).astype(np.float32)
    return np.concatenate([cos, cos], 1), np.concatenate([-sin, sin], 1)


def turned(rows, cos, sin):
    return rows * cos + pltpu.roll(rows, rows.shape[-1] // 2, 1) * sin


def turned_back(rows, cos, sin):
    return rows * cos - pltpu.roll(rows, rows.shape[-1] // 2, 1) * sin


def inverse_rms(rows):
    return lax.rsqrt(jnp.mean(rows * rows, -1, keepdims=True) + EPS)


def own_tables(depth_ref, cos_ref, sin_ref, blocks, block_len):
    starts = [pl.multiple_of(depth_ref[a] * block_len, block_len) for a in range(blocks)]
    cos = jnp.concatenate([cos_ref[pl.ds(s, block_len), :] for s in starts], 0)
    sin = jnp.concatenate([sin_ref[pl.ds(s, block_len), :] for s in starts], 0)
    return cos, sin


def dot_nt(lhs, rhs):
    return lax.dot_general(lhs, rhs, (((1,), (1,)), ((), ())), preferred_element_type=F32)


def dot_nn(lhs, rhs):
    return lax.dot_general(lhs, rhs, (((1,), (0,)), ((), ())), preferred_element_type=F32)


def prep_kernel(blocks, block_len, depth_ref, cos_ref, sin_ref, gain_ref, q_ref, grad_ref, out_ref,
                q_rot_ref, grad_heads_ref, delta_ref):
    heads = q_rot_ref.shape[0]
    head_dim = q_rot_ref.shape[2]
    cos, sin = own_tables(depth_ref, cos_ref, sin_ref, blocks, block_len)
    gain = gain_ref[...]
    for head in range(heads):
        cols = pl.ds(head * head_dim, head_dim)
        rows = q_ref[:, cols].astype(F32)
        scaled = rows * inverse_rms(rows) * gain
        q_rot_ref[head] = turned(scaled, cos, sin).astype(BF16)
        grad = grad_ref[:, cols]
        grad_heads_ref[head] = grad
        product = grad.astype(F32) * out_ref[:, cols].astype(F32)
        delta_ref[head] = jnp.sum(jnp.transpose(product), 0, keepdims=True)


def main_kernel(blocks, block_len, tree_dev, first_pos, inv_root,
                anc_ref, place_ref, cos_ref, sin_ref, gain_ref, k_ref, v_ref, q_ref, grad_ref, delta_ref,
                dq_ref, dk_ref, dv_ref, gain_part_ref,
                slot_blk, slot_bits, slot_depth, keys, keys_t, vals, normed, expo, mass, w_all, ds_all):
    group = q_ref.shape[0]
    tokens = q_ref.shape[1]
    head_dim = q_ref.shape[2]
    slots = tree_dev * blocks
    place = place_ref[0]

    for i in range(slots):
        slot_blk[i] = 0
        slot_bits[i] = 0
        slot_depth[i] = 0

    def merge(b, carry):
        count, steps = carry[0], carry[1:]
        bits = jnp.int32(0)
        depth = jnp.int32(0)
        later = []
        for a in range(blocks):
            hit = anc_ref[a, jnp.minimum(steps[a], slots - 1)] == b
            bits = bits | jnp.where(hit, 1 << a, 0)
            depth = jnp.where(hit, steps[a], depth)
            later.append(steps[a] + jnp.where(hit, 1, 0))
        own = b - place * blocks
        slot = jnp.where(own >= 0, own, jnp.minimum(count, slots - 1))
        slot_blk[slot] = b
        slot_bits[slot] = bits
        slot_depth[slot] = depth
        count = count + jnp.where((own < 0) & (bits != 0), 1, 0)
        return (count, *later)

    zero = jnp.int32(0)
    count = lax.fori_loop(0, (place + 1) * blocks, merge, (jnp.int32(blocks), *([zero] * blocks)))[0]
    chunks = (count + blocks - 1) // blocks

    lane = lax.broadcasted_iota(jnp.int32, (1, head_dim), 1)
    row_block = lax.broadcasted_iota(jnp.int32, (tokens, head_dim), 0) // block_len
    row_tag = (row_block == lax.broadcasted_iota(jnp.int32, (tokens, head_dim), 1)).astype(BF16)
    gain = gain_ref[...]

    def where_of(slot):
        b = slot_blk[slot]
        position = lax.rem(b // blocks + first_pos, tree_dev)
        return position, pl.ds(pl.multiple_of(lax.rem(b, blocks) * block_len, block_len), block_len)

    def tables_of(slot):
        at = pl.ds(pl.multiple_of(slot_depth[slot] * block_len, block_len), block_len)
        return cos_ref[at, :], sin_ref[at, :]

    def load_chunk(c):
        for j in range(blocks):
            slot = c * blocks + j
            position, rows = where_of(slot)
            raw = k_ref[position, rows, :].astype(F32)
            unit = raw * inverse_rms(raw)
            cos, sin = tables_of(slot)
            rotated = turned(unit * gain, cos, sin).astype(BF16)
            here = pl.ds(j * block_len, block_len)
            normed[c, here, :] = unit
            keys[c, here, 0:head_dim] = rotated
            bits = jnp.where(slot < count, slot_bits[slot], 0)
            shown = jnp.zeros((1, head_dim), F32)
            for a in range(blocks):
                seen = lax.rem(lax.shift_right_logical(bits, a), 2)
                shown = jnp.where((lane == a) & (seen == 0), HIDDEN, shown)
            keys[c, here, head_dim:] = jnp.broadcast_to(shown, (block_len, head_dim)).astype(BF16)
            vals[c, here, :] = v_ref[position, rows, :]
        keys_t[c] = jnp.transpose(keys[c, :, 0:head_dim].astype(F32)).astype(BF16)

    def masses(c, causal):
        load_chunk(c)
        for g in range(group):
            tagged = jnp.concatenate([q_ref[g], row_tag], 1)
            e = jnp.exp2(dot_nt(keys[c], tagged) * (inv_root * LOG2_E))
            if causal is not None:
                e = jnp.where(causal, e, 0.0)
            expo[c, g] = e
            part = jnp.sum(e.reshape(tokens // 8, 8, tokens), 0)
            if causal is not None:
                mass[g] = part
            else:
                mass[g] = mass[g] + part

    key_row = lax.broadcasted_iota(jnp.int32, (tokens, tokens), 0)
    query_col = lax.broadcasted_iota(jnp.int32, (tokens, tokens), 1)
    masses(0, key_row <= query_col)

    @pl.loop(1, chunks)
    def _(c):
        masses(c, None)

    for g in range(group):
        total = jnp.sum(mass[g], 0, keepdims=True)
        mass[g] = jnp.broadcast_to(1.0 / total, (8, tokens))
        dq_ref[g] = jnp.zeros((head_dim, tokens), F32)
    dk_ref[...] = jnp.zeros(dk_ref.shape, dk_ref.dtype)
    dv_ref[...] = jnp.zeros(dv_ref.shape, dv_ref.dtype)
    gain_part_ref[...] = jnp.zeros(gain_part_ref.shape, F32)

    @pl.loop(0, chunks)
    def _(c):
        for g in range(group):
            grad_prob = dot_nt(vals[c], grad_ref[g])
            weights = expo[c, g] * mass[g, 0:1, :]
            dscore = (weights * (grad_prob - delta_ref[g])).astype(BF16)
            w_all[:, pl.ds(g * tokens, tokens)] = weights.astype(BF16)
            ds_all[:, pl.ds(g * tokens, tokens)] = dscore
            dq_ref[g] = dq_ref[g] + dot_nn(keys_t[c], dscore)
        dv = dot_nn(w_all[...], grad_ref[...].reshape(group * tokens, head_dim))
        dk = dot_nn(ds_all[...], q_ref[...].reshape(group * tokens, head_dim)) * inv_root
        gain_part = jnp.zeros((1, head_dim), F32)
        for j in range(blocks):
            slot = c * blocks + j

            @pl.when(slot < count)
            def _():
                position, rows = where_of(slot)
                here = slice(j * block_len, (j + 1) * block_len)
                dk_ref[position, rows, :] = dk[here].astype(dk_ref.dtype)
                dv_ref[position, rows, :] = dv[here].astype(dv_ref.dtype)
                cos, sin = tables_of(slot)
                term = turned_back(dk[here], cos, sin) * normed[c, here, :]
                gain_part_ref[0] = gain_part_ref[0] + jnp.sum(term.reshape(block_len // 8, 8, head_dim), 0)


def query_kernel(blocks, block_len, inv_root, depth_ref, cos_ref, sin_ref, gain_ref, q_ref, dq_ref, out_ref, part_ref):
    heads, head_dim, tokens = dq_ref.shape
    cos, sin = own_tables(depth_ref, cos_ref, sin_ref, blocks, block_len)
    gain = gain_ref[...]
    part = jnp.zeros((8, head_dim), F32)
    for head in range(heads):
        cols = pl.ds(head * head_dim, head_dim)
        rows = q_ref[:, cols].astype(F32)
        recip = inverse_rms(rows)
        normed = rows * recip
        scaled_grad = turned_back(jnp.transpose(dq_ref[head]), cos, sin) * inv_root
        term = scaled_grad * normed
        part = part + jnp.sum(term.reshape(tokens // 8, 8, head_dim), 0)
        inner = jnp.mean(term * gain, -1, keepdims=True)
        out_ref[:, cols] = (recip * (scaled_grad * gain - normed * inner)).astype(BF16)
    part_ref[...] = part


def key_kernel(blocks, block_len, depth_ref, cos_ref, sin_ref, gain_ref, k_ref, dk_ref, dv_ref, dk_out_ref, dv_out_ref):
    head_dim = gain_ref.shape[1]
    cos, sin = own_tables(depth_ref, cos_ref, sin_ref, blocks, block_len)
    gain = gain_ref[...]
    for head in range(k_ref.shape[1] // head_dim):
        cols = pl.ds(head * head_dim, head_dim)
        rows = k_ref[:, cols].astype(F32)
        recip = inverse_rms(rows)
        normed = rows * recip
        grad = turned_back(dk_ref[:, cols].astype(F32), cos, sin) * gain
        inner = jnp.mean(grad * normed, -1, keepdims=True)
        dk_out_ref[:, cols] = (recip * (grad - normed * inner)).astype(BF16)
    dv_out_ref[...] = dv_ref[...].astype(BF16)


def on_device(q_raw, k_raw, values, saved_out, out_grad, q_gain, k_gain, ancestors):
    tokens = q_raw.shape[0]
    head_dim = q_gain.shape[0]
    kv_heads = k_raw.shape[1] // head_dim
    heads = q_raw.shape[1] // head_dim
    group = heads // kv_heads
    blocks = ancestors.shape[0]
    tree_blocks = ancestors.shape[1]
    block_len = tokens // blocks
    tree_dev = tree_blocks // blocks
    cycle = lax.axis_size("ctx")
    inv_root = 1.0 / math.sqrt(head_dim)
    place = (lax.axis_index("ctx") - 1 + cycle) % cycle % tree_dev
    if cycle == tree_dev:
        groups, first_pos = None, 1
    else:
        groups = [
            [(tree * tree_dev + 1 + step) % cycle for step in range(tree_dev)]
            for tree in range(cycle // tree_dev)
        ]
        first_pos = 0

    depth = jnp.sum((ancestors >= 0).astype(jnp.int32), 1) - 1
    total_blocks = blocks * cycle
    in_tree = jnp.where(
        ancestors >= 0, (ancestors - blocks + total_blocks) % total_blocks % tree_blocks, -1
    )
    place = place.reshape(1).astype(jnp.int32)
    cos_np, sin_np = rope_rows(tree_blocks * block_len, head_dim)
    cos, sin = jnp.asarray(cos_np), jnp.asarray(sin_np)
    q_gain_row, k_gain_row = q_gain.reshape(1, head_dim), k_gain.reshape(1, head_dim)

    k_all = lax.all_gather(k_raw, "ctx", axis_index_groups=groups)
    v_all = lax.all_gather(values, "ctx", axis_index_groups=groups)

    params = pltpu.CompilerParams(vmem_limit_bytes=VMEM_LIMIT)
    smem = pl.BlockSpec(memory_space=pltpu.SMEM)
    vmem = pl.BlockSpec(memory_space=pltpu.VMEM)
    sds = jax.ShapeDtypeStruct

    q_rot, grad_heads, delta = pl.pallas_call(
        lambda *refs: prep_kernel(blocks, block_len, *refs),
        out_shape=(
            sds((heads, tokens, head_dim), BF16),
            sds((heads, tokens, head_dim), BF16),
            sds((heads, 1, tokens), F32),
        ),
        in_specs=[smem] + [vmem] * 6,
        out_specs=(vmem, vmem, vmem),
        compiler_params=params,
        name="prep",
    )(depth, cos, sin, q_gain_row, q_raw, out_grad, saved_out)

    slots = tree_blocks
    keys_here = pl.BlockSpec((tree_dev, tokens, head_dim), lambda h: (0, 0, h))
    rows_here = pl.BlockSpec((group, tokens, head_dim), lambda h: (h, 0, 0))
    whole = lambda *shape: pl.BlockSpec(shape, lambda h: (0,) * len(shape))
    dq_t, dk_part, dv_part, k_gain_part = pl.pallas_call(
        lambda *refs: main_kernel(blocks, block_len, tree_dev, first_pos, inv_root, *refs),
        grid=(kv_heads,),
        out_shape=(
            sds((heads, head_dim, tokens), F32),
            sds((tree_dev, tokens, kv_heads * head_dim), BF16),
            sds((tree_dev, tokens, kv_heads * head_dim), BF16),
            sds((kv_heads, 8, head_dim), F32),
        ),
        in_specs=[
            smem,
            smem,
            whole(tree_blocks * block_len, head_dim),
            whole(tree_blocks * block_len, head_dim),
            whole(1, head_dim),
            keys_here,
            keys_here,
            rows_here,
            rows_here,
            pl.BlockSpec((group, 1, tokens), lambda h: (h, 0, 0)),
        ],
        out_specs=(
            pl.BlockSpec((group, head_dim, tokens), lambda h: (h, 0, 0)),
            keys_here,
            keys_here,
            pl.BlockSpec((1, 8, head_dim), lambda h: (h, 0, 0)),
        ),
        scratch_shapes=[
            pltpu.SMEM((slots,), jnp.int32),
            pltpu.SMEM((slots,), jnp.int32),
            pltpu.SMEM((slots,), jnp.int32),
            pltpu.VMEM((tree_dev, tokens, 2 * head_dim), BF16),
            pltpu.VMEM((tree_dev, head_dim, tokens), BF16),
            pltpu.VMEM((tree_dev, tokens, head_dim), BF16),
            pltpu.VMEM((tree_dev, tokens, head_dim), F32),
            pltpu.VMEM((tree_dev, group, tokens, tokens), F32),
            pltpu.VMEM((group, 8, tokens), F32),
            pltpu.VMEM((tokens, group * tokens), BF16),
            pltpu.VMEM((tokens, group * tokens), BF16),
        ],
        compiler_params=params,
        name="attend",
    )(in_tree, place, cos, sin, k_gain_row, k_all, v_all, q_rot, grad_heads, delta)

    dk_sum = lax.psum_scatter(dk_part, "ctx", scatter_dimension=0, axis_index_groups=groups)
    dv_sum = lax.psum_scatter(dv_part, "ctx", scatter_dimension=0, axis_index_groups=groups)

    dq_raw, q_gain_part = pl.pallas_call(
        lambda *refs: query_kernel(blocks, block_len, inv_root, *refs),
        out_shape=(sds((tokens, heads * head_dim), BF16), sds((8, head_dim), F32)),
        in_specs=[smem] + [vmem] * 5,
        out_specs=(vmem, vmem),
        compiler_params=params,
        name="query_back",
    )(depth, cos, sin, q_gain_row, q_raw, dq_t)

    gains = jnp.stack([jnp.sum(q_gain_part, 0), jnp.sum(k_gain_part, (0, 1))])
    gains = lax.psum(gains, ("ctx", "heads"))

    dk_raw, dv = pl.pallas_call(
        lambda *refs: key_kernel(blocks, block_len, *refs),
        out_shape=(sds(k_raw.shape, BF16), sds(k_raw.shape, BF16)),
        in_specs=[smem] + [vmem] * 6,
        out_specs=(vmem, vmem),
        compiler_params=params,
        name="key_back",
    )(depth, cos, sin, k_gain_row, k_raw, dk_sum, dv_sum)
    return (dq_raw, dk_raw, dv, gains[0], gains[1])


def solution(mesh):
    split = P("ctx", "heads")
    return jax.shard_map(
        on_device,
        mesh=mesh,
        in_specs=(split, split, split, split, split, P(), P(), P("ctx", None)),
        out_specs=(split, split, split, P(), P()),
        check_vma=False,
    )
```

```python
import math

import jax
import jax.numpy as jnp
import numpy as np
from jax import lax
from jax.experimental import pallas as pl
from jax.experimental.pallas import tpu as pltpu
from jax.sharding import PartitionSpec as P

ROPE_BASE = 1000000.0
EPS = 1e-06
LOG2_E = 1.4426950408889634
HIDDEN = -100000.0
VMEM_LIMIT = 48 * 1024 * 1024
GATHER_RELAYED = (True, False)
COLLECT_RELAYED = (False, True)
F32 = jnp.float32
BF16 = jnp.bfloat16


def rope_rows(count, head_dim):
    half = head_dim // 2
    frequency = np.exp(
        np.arange(half, dtype=np.float32) * np.float32(-2.0 * math.log(ROPE_BASE) / head_dim)
    ).astype(np.float32)
    angles = np.arange(count, dtype=np.float32)[:, None] * frequency[None, :]
    cos = np.cos(angles.astype(np.float64)).astype(np.float32)
    sin = np.sin(angles.astype(np.float64)).astype(np.float32)
    return np.concatenate([cos, cos], 1), np.concatenate([-sin, sin], 1)


def turned(rows, cos, sin):
    return rows * cos + pltpu.roll(rows, rows.shape[-1] // 2, 1) * sin


def turned_back(rows, cos, sin):
    return rows * cos - pltpu.roll(rows, rows.shape[-1] // 2, 1) * sin


def inverse_rms(rows):
    return lax.rsqrt(jnp.mean(rows * rows, -1, keepdims=True) + EPS)


def own_tables(depth_ref, cos_ref, sin_ref, blocks, block_len):
    starts = [pl.multiple_of(depth_ref[a] * block_len, block_len) for a in range(blocks)]
    cos = jnp.concatenate([cos_ref[pl.ds(s, block_len), :] for s in starts], 0)
    sin = jnp.concatenate([sin_ref[pl.ds(s, block_len), :] for s in starts], 0)
    return cos, sin


def dot_nt(lhs, rhs):
    return lax.dot_general(lhs, rhs, (((1,), (1,)), ((), ())), preferred_element_type=F32)


def dot_nn(lhs, rhs):
    return lax.dot_general(lhs, rhs, (((1,), (0,)), ((), ())), preferred_element_type=F32)


def plan_kernel(blocks, tree_dev, place_ref, anc_ref, plan_ref):
    slots = tree_dev * blocks
    place = place_ref[0]
    here = lax.rem(place + 1, tree_dev)
    for row in range(4):
        for i in range(slots):
            plan_ref[row, i] = 0

    def merge(b, carry):
        count, steps = carry[0], carry[1:]
        bits = jnp.int32(0)
        depth = jnp.int32(0)
        later = []
        for a in range(blocks):
            hit = anc_ref[a, jnp.minimum(steps[a], slots - 1)] == b
            bits = bits | jnp.where(hit, 1 << a, 0)
            depth = jnp.where(hit, steps[a], depth)
            later.append(steps[a] + jnp.where(hit, 1, 0))
        own = b - place * blocks
        slot = jnp.where(own >= 0, own, jnp.minimum(count, slots - 1))
        there = lax.rem(b // blocks + 1, tree_dev)
        odd = lax.rem(here + there, 2)
        near = here + odd * (1 - 2 * lax.rem(here, 2))
        piece = odd * (tree_dev // 2) + lax.rem(near - there + tree_dev, tree_dev) // 2
        plan_ref[0, slot] = piece
        plan_ref[1, slot] = lax.rem(b, blocks)
        plan_ref[2, slot] = depth
        plan_ref[3, slot] = bits
        count = count + jnp.where((own < 0) & (bits != 0), 1, 0)
        return (count, *later)

    zero = jnp.int32(0)
    count = lax.fori_loop(0, (place + 1) * blocks, merge, (jnp.int32(blocks), *([zero] * blocks)))[0]
    for i in range(slots):
        plan_ref[4, i] = count


def prep_kernel(blocks, block_len, depth_ref, cos_ref, sin_ref, gain_ref, q_ref, grad_ref, out_ref,
                q_ref_t, q_rot_ref, grad_t_ref, grad_heads_ref, delta_ref):
    heads, tokens, head_dim = q_rot_ref.shape
    cos, sin = own_tables(depth_ref, cos_ref, sin_ref, blocks, block_len)
    gain = gain_ref[...]
    tag_row = lax.broadcasted_iota(jnp.int32, (head_dim, tokens), 0)
    tag_col = lax.broadcasted_iota(jnp.int32, (head_dim, tokens), 1) // block_len
    tag = (tag_row == tag_col).astype(BF16)
    for head in range(heads):
        cols = pl.ds(head * head_dim, head_dim)
        rows = q_ref[:, cols].astype(F32)
        rotated = turned(rows * inverse_rms(rows) * gain, cos, sin)
        q_rot_ref[head] = rotated.astype(BF16)
        q_ref_t[head, 0:head_dim, :] = jnp.transpose(rotated).astype(BF16)
        q_ref_t[head, head_dim:, :] = tag
        grad = grad_ref[:, cols]
        grad_heads_ref[head] = grad
        grad_rows = jnp.transpose(grad.astype(F32))
        grad_t_ref[head] = grad_rows.astype(BF16)
        product = grad_rows * jnp.transpose(out_ref[:, cols].astype(F32))
        delta_ref[head] = jnp.sum(product, 0, keepdims=True)


def main_kernel(blocks, block_len, tree_dev, inv_root, *refs):
    plan_ref, cos_ref, sin_ref, gain_ref = refs[:4]
    pieces = refs[4:4 + tree_dev]
    q_t_ref, q_ref, grad_t_ref, grad_ref, delta_ref = refs[4 + tree_dev:9 + tree_dev]
    dq_ref, gain_part_ref = refs[9 + tree_dev:11 + tree_dev]
    parts = refs[11 + tree_dev:11 + 2 * tree_dev]
    raw, keys, keys_t, vals, with_cos, with_sin, expo, mass, w_all, ds_all, found, spread = refs[11 + 2 * tree_dev:]
    group, tokens, head_dim = q_ref.shape
    count = plan_ref[4, 0]
    chunks = (count + blocks - 1) // blocks
    gain = gain_ref[...]
    lane = lax.broadcasted_iota(jnp.int32, (1, head_dim), 1)
    for piece in range(tree_dev):
        raw[piece] = pieces[piece][...]

    def rows_of(start):
        return pl.ds(pl.multiple_of(start * block_len, block_len), block_len)

    @pl.loop(0, chunks)
    def _(c):
        for j in range(blocks):
            slot = c * blocks + j
            piece = plan_ref[0, slot]
            rows = rows_of(plan_ref[1, slot])
            table = rows_of(plan_ref[2, slot])
            cos, sin = cos_ref[table, :], sin_ref[table, :]
            unit = raw[piece, rows, 0:head_dim].astype(F32)
            unit = unit * inverse_rms(unit)
            here = pl.ds(j * block_len, block_len)
            with_cos[c, here, :] = unit * cos
            with_sin[c, here, :] = pltpu.roll(unit * sin, head_dim // 2, 1)
            keys[c, here, 0:head_dim] = turned(unit * gain, cos, sin).astype(BF16)
            bits = jnp.where(slot < count, plan_ref[3, slot], 0)
            shown = jnp.zeros((1, head_dim), F32)
            for a in range(blocks):
                seen = lax.rem(lax.shift_right_logical(bits, a), 2)
                shown = jnp.where((lane == a) & (seen == 0), HIDDEN, shown)
            keys[c, here, head_dim:] = jnp.broadcast_to(shown, (block_len, head_dim)).astype(BF16)
            vals[c, here, :] = raw[piece, rows, head_dim:]
        keys_t[c] = jnp.transpose(keys[c, :, 0:head_dim].astype(F32)).astype(BF16)

    def exps(c, g):
        return jnp.exp2(dot_nn(keys[c], q_t_ref[g]) * (inv_root * LOG2_E))

    def summed(e):
        return jnp.sum(e.reshape(tokens // 8, 8, tokens), 0)

    key_row = lax.broadcasted_iota(jnp.int32, (tokens, tokens), 0)
    query_col = lax.broadcasted_iota(jnp.int32, (tokens, tokens), 1)
    for g in range(group):
        e = jnp.where(key_row <= query_col, exps(0, g), 0.0)
        expo[0, g] = e
        mass[g] = summed(e)

    @pl.loop(1, chunks)
    def _(c):
        for g in range(group):
            e = exps(c, g)
            expo[c, g] = e
            mass[g] = mass[g] + summed(e)

    for g in range(group):
        total = jnp.sum(mass[g], 0, keepdims=True)
        mass[g] = jnp.broadcast_to(1.0 / total, (8, tokens))
        dq_ref[g] = jnp.zeros((head_dim, tokens), F32)
    gain_part_ref[...] = jnp.zeros(gain_part_ref.shape, F32)
    spread[...] = jnp.zeros(spread.shape, BF16)

    @pl.loop(0, chunks)
    def _(c):
        for g in range(group):
            grad_prob = dot_nn(vals[c], grad_t_ref[g])
            weights = expo[c, g] * mass[g, 0:1, :]
            dscore = (weights * (grad_prob - delta_ref[g])).astype(BF16)
            w_all[:, pl.ds(g * tokens, tokens)] = weights.astype(BF16)
            ds_all[:, pl.ds(g * tokens, tokens)] = dscore
            dq_ref[g] = dq_ref[g] + dot_nn(keys_t[c], dscore)
        dv = dot_nn(w_all[...], grad_ref[...].reshape(group * tokens, head_dim))
        dk = dot_nn(ds_all[...], q_ref[...].reshape(group * tokens, head_dim)) * inv_root
        found[c, :, 0:head_dim] = dk.astype(BF16)
        found[c, :, head_dim:] = dv.astype(BF16)
        front = jnp.sum((dk * with_cos[c]).reshape(tokens // 8, 8, head_dim), 0)
        back = jnp.sum((dk * with_sin[c]).reshape(tokens // 8, 8, head_dim), 0)
        gain_part_ref[...] = gain_part_ref[...] + front - pltpu.roll(back, head_dim // 2, 1)

    @pl.loop(0, count)
    def _(slot):
        rows = rows_of(lax.rem(slot, blocks))
        spread[plan_ref[0, slot], rows_of(plan_ref[1, slot]), :] = found[slot // blocks, rows, :]

    for piece in range(tree_dev):
        parts[piece][...] = spread[piece]


def query_kernel(blocks, block_len, inv_root, depth_ref, cos_ref, sin_ref, gain_ref, q_ref, *refs):
    dq_refs, (out_ref, part_ref) = refs[:-2], refs[-2:]
    group, head_dim, tokens = dq_refs[0].shape
    cos, sin = own_tables(depth_ref, cos_ref, sin_ref, blocks, block_len)
    gain = gain_ref[...]
    part = jnp.zeros((8, head_dim), F32)
    for head in range(group * len(dq_refs)):
        cols = pl.ds(head * head_dim, head_dim)
        rows = q_ref[:, cols].astype(F32)
        recip = inverse_rms(rows)
        normed = rows * recip
        dq = jnp.transpose(dq_refs[head // group][head % group])
        scaled_grad = turned_back(dq, cos, sin) * inv_root
        term = scaled_grad * normed
        part = part + jnp.sum(term.reshape(tokens // 8, 8, head_dim), 0)
        inner = jnp.mean(term * gain, -1, keepdims=True)
        out_ref[:, cols] = (recip * (scaled_grad * gain - normed * inner)).astype(BF16)
    part_ref[...] = part


def key_kernel(blocks, block_len, counts, depth_ref, cos_ref, sin_ref, gain_ref, k_ref, *refs):
    sums, (dk_out_ref, dv_out_ref) = refs[:-2], refs[-2:]
    head_dim = gain_ref.shape[1]
    cos, sin = own_tables(depth_ref, cos_ref, sin_ref, blocks, block_len)
    gain = gain_ref[...]
    for head, each in enumerate(counts):
        cols = pl.ds(head * head_dim, head_dim)
        rows = k_ref[:, cols].astype(F32)
        recip = inverse_rms(rows)
        normed = rows * recip
        mine = sums[sum(counts[:head]):][:each]
        both = mine[0][...].astype(F32)
        for other in mine[1:]:
            both = both + other[...].astype(F32)
        grad = turned_back(both[:, 0:head_dim], cos, sin) * gain
        inner = jnp.mean(grad * normed, -1, keepdims=True)
        dk_out_ref[:, cols] = (recip * (grad - normed * inner)).astype(BF16)
        dv_out_ref[:, cols] = both[:, head_dim:].astype(BF16)


class Tree:
    def __init__(self, size, cycle):
        self.size, self.cycle = size, cycle

    def order(self, index):
        return (index - 1) % self.size

    def send(self, value, target, wanted):
        pairs = []
        for tree in range(self.cycle // self.size):
            for index in range(self.size):
                if wanted(index):
                    ends = [(tree * self.size + 1 + self.order(i)) % self.cycle for i in (index, target(index))]
                    pairs.append(tuple(ends))
        return lax.ppermute(value, "ctx", pairs)

    def after(self, *pair):
        return self.order(pair[1] % self.size) > self.order(pair[0] % self.size)

    def gather(self, own, relayed):
        size, after = self.size, self.after
        cross = self.send(own, lambda i: i ^ 1, lambda i: after(i, i ^ 1))
        straight, crossed = [], []
        for step in range(2, size, 2):
            there = lambda i: (i + step) % size
            if relayed:
                piece = self.send(own, there, lambda i: after(i, there(i)) or after(i, there(i) ^ 1))
                straight.append(piece)
            else:
                straight.append(self.send(own, there, lambda i: after(i, there(i))))
                crossed.append(self.send(own, lambda i: there(i) ^ 1, lambda i: after(i, there(i) ^ 1)))
        if relayed:
            for step, piece in zip(range(2, size, 2), straight):
                crossed.append(self.send(piece, lambda i: i ^ 1, lambda i: after(i - step, i ^ 1)))
        return [own, *straight, cross, *crossed]

    def collect(self, parts, relayed):
        size, after = self.size, self.after
        half = size // 2
        terms = [parts[0]]
        if relayed:
            halves = []
            for step in range(2, size, 2):
                part = parts[half + step // 2]
                halves.append(self.send(part, lambda i: i ^ 1, lambda i: after((i ^ 1) - step, i)))
            terms.append(self.send(parts[half], lambda i: i ^ 1, lambda i: after(i ^ 1, i)))
            for step, other in zip(range(2, size, 2), halves):
                there = lambda i: (i - step) % size
                both = (parts[step // 2].astype(F32) + other.astype(F32)).astype(BF16)
                terms.append(self.send(both, there, lambda i: after(there(i), i) or after(there(i), i ^ 1)))
            return terms
        terms.append(self.send(parts[half], lambda i: i ^ 1, lambda i: after(i ^ 1, i)))
        for step in range(2, size, 2):
            there = lambda i: (i - step) % size
            across = lambda i: ((i ^ 1) - step) % size
            terms.append(self.send(parts[step // 2], there, lambda i: after(there(i), i)))
            terms.append(self.send(parts[half + step // 2], across, lambda i: after(across(i), i)))
        return terms


def on_device(q_raw, k_raw, values, saved_out, out_grad, q_gain, k_gain, ancestors):
    tokens = q_raw.shape[0]
    head_dim = q_gain.shape[0]
    kv_heads = k_raw.shape[1] // head_dim
    heads = q_raw.shape[1] // head_dim
    group = heads // kv_heads
    blocks = ancestors.shape[0]
    tree_blocks = ancestors.shape[1]
    block_len = tokens // blocks
    tree_dev = tree_blocks // blocks
    cycle = lax.axis_size("ctx")
    inv_root = 1.0 / math.sqrt(head_dim)
    tree = Tree(tree_dev, cycle)
    place = (lax.axis_index("ctx") - 1 + cycle) % cycle % tree_dev
    place = place.reshape(1).astype(jnp.int32)

    depth = jnp.sum((ancestors >= 0).astype(jnp.int32), 1) - 1
    total_blocks = blocks * cycle
    in_tree = jnp.where(
        ancestors >= 0, (ancestors - blocks + total_blocks) % total_blocks % tree_blocks, -1
    )
    cos_np, sin_np = rope_rows(tree_blocks * block_len, head_dim)
    cos, sin = jnp.asarray(cos_np), jnp.asarray(sin_np)
    q_gain_row, k_gain_row = q_gain.reshape(1, head_dim), k_gain.reshape(1, head_dim)

    own = []
    for h in range(kv_heads):
        cols = slice(h * head_dim, (h + 1) * head_dim)
        own.append(jnp.concatenate([k_raw[:, cols], values[:, cols]], 1))
    gathered = [tree.gather(own[h], GATHER_RELAYED[h > 0]) for h in range(kv_heads)]

    params = pltpu.CompilerParams(vmem_limit_bytes=VMEM_LIMIT)
    smem = pl.BlockSpec(memory_space=pltpu.SMEM)
    vmem = pl.BlockSpec(memory_space=pltpu.VMEM)
    sds = jax.ShapeDtypeStruct

    plan = pl.pallas_call(
        lambda *refs: plan_kernel(blocks, tree_dev, *refs),
        out_shape=sds((5, tree_blocks), jnp.int32),
        in_specs=[smem, smem],
        out_specs=smem,
        name="plan",
    )(place, in_tree)

    def prep(h):
        columns = pl.BlockSpec((tokens, group * head_dim), lambda i: (0, h))
        whole = lambda *shape: pl.BlockSpec(shape, lambda i: (0,) * len(shape))
        table = whole(tree_blocks * block_len, head_dim)
        shapes = (
            (group, 2 * head_dim, tokens),
            (group, tokens, head_dim),
            (group, head_dim, tokens),
            (group, tokens, head_dim),
            (group, 1, tokens),
        )
        return pl.pallas_call(
            lambda *refs: prep_kernel(blocks, block_len, *refs),
            grid=(1,),
            out_shape=tuple(sds(shape, F32 if shape[1] == 1 else BF16) for shape in shapes),
            in_specs=[smem, table, table, whole(1, head_dim), columns, columns, columns],
            out_specs=tuple(whole(*shape) for shape in shapes),
            compiler_params=params,
            name="prep",
        )(depth, cos, sin, q_gain_row, q_raw, out_grad, saved_out)

    def attend(pieces, queries):
        return pl.pallas_call(
            lambda *refs: main_kernel(blocks, block_len, tree_dev, inv_root, *refs),
            out_shape=(
                sds((group, head_dim, tokens), F32),
                sds((8, head_dim), F32),
                *[sds((tokens, 2 * head_dim), BF16)] * tree_dev,
            ),
            in_specs=[smem] + [vmem] * (8 + tree_dev),
            out_specs=tuple([vmem] * (2 + tree_dev)),
            scratch_shapes=[
                pltpu.VMEM((tree_dev, tokens, 2 * head_dim), BF16),
                pltpu.VMEM((tree_dev, tokens, 2 * head_dim), BF16),
                pltpu.VMEM((tree_dev, head_dim, tokens), BF16),
                pltpu.VMEM((tree_dev, tokens, head_dim), BF16),
                pltpu.VMEM((tree_dev, tokens, head_dim), F32),
                pltpu.VMEM((tree_dev, tokens, head_dim), F32),
                pltpu.VMEM((tree_dev, group, tokens, tokens), F32),
                pltpu.VMEM((group, 8, tokens), F32),
                pltpu.VMEM((tokens, group * tokens), BF16),
                pltpu.VMEM((tokens, group * tokens), BF16),
                pltpu.VMEM((tree_dev, tokens, 2 * head_dim), BF16),
                pltpu.VMEM((tree_dev, tokens, 2 * head_dim), BF16),
            ],
            compiler_params=params,
            cost_estimate=pl.CostEstimate(
                flops=10 * group * tokens * tree_dev * tokens * head_dim,
                bytes_accessed=8 * 1024 * 1024,
                transcendentals=group * tokens * tree_dev * tokens,
            ),
            name="attend",
        )(plan, cos, sin, k_gain_row, *pieces, *queries)

    queries = [prep(h) for h in range(kv_heads)]
    dq, terms, counts, k_gain_parts = [], [], [], []
    for h in range(kv_heads):
        dq_here, k_gain_part, *parts = attend(gathered[h], queries[h])
        dq.append(dq_here)
        k_gain_parts.append(k_gain_part)
        mine = tree.collect(parts, COLLECT_RELAYED[h > 0])
        terms.extend(mine)
        counts.append(len(mine))

    dq_raw, q_gain_part = pl.pallas_call(
        lambda *refs: query_kernel(blocks, block_len, inv_root, *refs),
        out_shape=(sds((tokens, heads * head_dim), BF16), sds((8, head_dim), F32)),
        in_specs=[smem] + [vmem] * (4 + kv_heads),
        out_specs=(vmem, vmem),
        compiler_params=params,
        name="query_back",
    )(depth, cos, sin, q_gain_row, q_raw, *dq)

    gains = jnp.stack([jnp.sum(q_gain_part, 0), jnp.sum(sum(k_gain_parts), 0)])
    gains = lax.psum(gains, ("ctx", "heads"))

    dk_raw, dv = pl.pallas_call(
        lambda *refs: key_kernel(blocks, block_len, counts, *refs),
        out_shape=(sds(k_raw.shape, BF16), sds(k_raw.shape, BF16)),
        in_specs=[smem] + [vmem] * (4 + len(terms)),
        out_specs=(vmem, vmem),
        compiler_params=params,
        name="key_back",
    )(depth, cos, sin, k_gain_row, k_raw, *terms)
    return (dq_raw, dk_raw, dv, gains[0], gains[1])


def solution(mesh):
    split = P("ctx", "heads")
    return jax.shard_map(
        on_device,
        mesh=mesh,
        in_specs=(split, split, split, split, split, P(), P(), P("ctx", None)),
        out_specs=(split, split, split, P(), P()),
        check_vma=False,
    )
```

```python
import math

import jax
import jax.numpy as jnp
import numpy as np
from jax import lax
from jax.experimental import pallas as pl
from jax.experimental.pallas import tpu as pltpu
from jax.sharding import PartitionSpec as P

ROPE_BASE = 1000000.0
EPS = 1e-06
HIDDEN = -100000.0
VMEM_LIMIT = 56 * 1024 * 1024
F32 = jnp.float32
BF16 = jnp.bfloat16


def rope_rows(starts, head_dim):
    half = head_dim // 2
    frequency = np.exp(
        np.arange(half, dtype=np.float32) * np.float32(-2.0 * math.log(ROPE_BASE) / head_dim)
    ).astype(np.float32)
    angles = np.asarray(starts, np.float32)[:, None] * frequency[None, :]
    cos = np.cos(angles.astype(np.float64)).astype(np.float32)
    sin = np.sin(angles.astype(np.float64)).astype(np.float32)
    return np.concatenate([cos, cos], 1), np.concatenate([-sin, sin], 1)


def block_tables(depth, tables):
    start_cos, start_sin, offset_cos, offset_sin = tables
    cos, sin = start_cos[pl.ds(depth, 1), :], start_sin[pl.ds(depth, 1), :]
    both_cos = cos * offset_cos[...] - sin * offset_sin[...]
    both_sin = sin * offset_cos[...] + cos * offset_sin[...]
    return both_cos, both_sin


def turned(rows, cos, sin):
    return rows * cos + pltpu.roll(rows, rows.shape[-1] // 2, 1) * sin


def turned_back(rows, cos, sin):
    return rows * cos - pltpu.roll(rows, rows.shape[-1] // 2, 1) * sin


def inverse_rms(rows):
    return lax.rsqrt(jnp.mean(rows * rows, -1, keepdims=True) + EPS)


def own_tables(depth_ref, tables, blocks):
    parts = [block_tables(depth_ref[a], tables) for a in range(blocks)]
    return jnp.concatenate([p[0] for p in parts], 0), jnp.concatenate([p[1] for p in parts], 0)


def dot_nn(lhs, rhs):
    return lax.dot_general(lhs, rhs, (((1,), (0,)), ((), ())), preferred_element_type=F32)


def plan_kernel(blocks, tree_dev, place_ref, anc_ref, plan_ref):
    slots = tree_dev * blocks
    place = place_ref[0]
    here = lax.rem(place + 1, tree_dev)
    for row in range(4):
        for i in range(slots):
            plan_ref[row, i] = 0

    def merge(b, carry):
        count, steps = carry[0], carry[1:]
        bits = jnp.int32(0)
        depth = jnp.int32(0)
        later = []
        for a in range(blocks):
            hit = anc_ref[a, jnp.minimum(steps[a], slots - 1)] == b
            bits = bits | jnp.where(hit, 1 << a, 0)
            depth = jnp.where(hit, steps[a], depth)
            later.append(steps[a] + jnp.where(hit, 1, 0))
        own = b - place * blocks
        slot = jnp.where(own >= 0, own, jnp.minimum(count, slots - 1))
        there = lax.rem(b // blocks + 1, tree_dev)
        odd = lax.rem(here + there, 2)
        near = here + odd * (1 - 2 * lax.rem(here, 2))
        piece = odd * (tree_dev // 2) + lax.rem(near - there + tree_dev, tree_dev) // 2
        plan_ref[0, slot] = piece
        plan_ref[1, slot] = lax.rem(b, blocks)
        plan_ref[2, slot] = depth
        plan_ref[3, slot] = bits
        count = count + jnp.where((own < 0) & (bits != 0), 1, 0)
        return (count, *later)

    zero = jnp.int32(0)
    count = lax.fori_loop(0, (place + 1) * blocks, merge, (jnp.int32(blocks), *([zero] * blocks)))[0]
    for i in range(slots):
        plan_ref[4, i] = count


def prep_kernel(blocks, block_len, kv_heads, depth_ref, t0, t1, t2, t3, gain_ref, q_ref, grad_ref, out_ref, *outs):
    tokens = q_ref.shape[0]
    head_dim = gain_ref.shape[1]
    cos, sin = own_tables(depth_ref, (t0, t1, t2, t3), blocks)
    gain = gain_ref[...]
    group = q_ref.shape[1] // head_dim // kv_heads
    for head in range(group * kv_heads):
        g = head % group
        q_t_ref, q_rot_ref, grad_t_ref, grad_heads_ref, delta_ref = outs[5 * (head // group):][:5]
        cols = pl.ds(head * head_dim, head_dim)
        here = pl.ds(g * tokens, tokens)
        rows = q_ref[:, cols].astype(F32)
        rotated = turned(rows * inverse_rms(rows) * gain, cos, sin)
        q_rot_ref[here, :] = rotated.astype(BF16)
        q_t_ref[:, here] = jnp.transpose(rotated).astype(BF16)
        grad = grad_ref[:, cols]
        grad_heads_ref[here, :] = grad
        grad_rows = jnp.transpose(grad.astype(F32))
        grad_t_ref[:, here] = grad_rows.astype(BF16)
        product = grad_rows * jnp.transpose(out_ref[:, cols].astype(F32))
        delta_ref[:, here] = jnp.sum(product, 0, keepdims=True)


def main_kernel(blocks, block_len, tree_dev, inv_root, head, whole_dots, *refs):
    plan_ref, gain_ref = refs[:2]
    tables = refs[2:6]
    pieces = refs[6:6 + tree_dev]
    q_t_ref, q_ref, grad_t_ref, grad_ref, delta_ref = refs[6 + tree_dev:11 + tree_dev]
    half = tree_dev // 2
    dq_ref, gain_part_ref = refs[11 + tree_dev:13 + tree_dev]
    straight = refs[13 + tree_dev:13 + tree_dev + half]
    crossed, raw, keys, keys_t, vals, shown, with_cos, with_sin, expo, mass, w_all, ds_all, found, spread, wide = refs[
        13 + tree_dev + half:]
    head_dim = gain_ref.shape[1]
    tokens = raw.shape[1]
    group = q_ref.shape[0] // tokens
    count = plan_ref[4, 0]
    chunks = (count + blocks - 1) // blocks
    gain = gain_ref[...]
    kv_heads = pieces[0].shape[1] // (2 * head_dim)
    for piece in range(tree_dev):
        raw[piece, :, 0:head_dim] = pieces[piece][:, head * head_dim:(head + 1) * head_dim]
        raw[piece, :, head_dim:] = pieces[piece][:, (kv_heads + head) * head_dim:(kv_heads + head + 1) * head_dim]
    query_block = lax.broadcasted_iota(jnp.int32, (1, tokens), 1) // block_len

    def rows_of(start):
        return pl.ds(pl.multiple_of(start * block_len, block_len), block_len)

    @pl.loop(0, chunks)
    def _(c):
        for j in range(blocks):
            slot = c * blocks + j
            piece = plan_ref[0, slot]
            rows = rows_of(plan_ref[1, slot])
            cos, sin = block_tables(plan_ref[2, slot], tables)
            unit = raw[piece, rows, 0:head_dim].astype(F32)
            unit = unit * inverse_rms(unit)
            here = pl.ds(j * block_len, block_len)
            with_cos[c, here, :] = unit * cos
            with_sin[c, here, :] = pltpu.roll(unit * sin, head_dim // 2, 1)
            keys[c, here, :] = turned(unit * gain, cos, sin).astype(BF16)
            bits = jnp.where(slot < count, plan_ref[3, slot], 0)
            row = jnp.zeros((1, tokens), F32)
            for a in range(blocks):
                seen = lax.rem(lax.shift_right_logical(bits, a), 2)
                row = jnp.where((query_block == a) & (seen == 0), HIDDEN, row)
            shown[c, j:j + 1, :] = row
            vals[c, here, :] = raw[piece, rows, head_dim:]
        keys_t[c] = jnp.transpose(keys[c].astype(F32)).astype(BF16)

    def exps(c, g, scores):
        parts = []
        for j in range(blocks):
            here = slice(j * block_len, (j + 1) * block_len)
            parts.append(jnp.exp(scores[here] * inv_root + shown[c, j:j + 1, :]))
        return jnp.concatenate(parts, 0)

    def summed(e):
        return jnp.sum(e.reshape(tokens // 8, 8, tokens), 0)

    key_row = lax.broadcasted_iota(jnp.int32, (tokens, tokens), 0)
    query_col = lax.broadcasted_iota(jnp.int32, (tokens, tokens), 1)

    def cols_of(g):
        return pl.ds(g * tokens, tokens)

    def masses(c, first):
        if whole_dots:
            wide[...] = dot_nn(keys[c], q_t_ref[...])
        for g in range(group):
            scores = wide[:, cols_of(g)] if whole_dots else dot_nn(keys[c], q_t_ref[:, cols_of(g)])
            e = exps(c, g, scores)
            if first:
                e = jnp.where(key_row <= query_col, e, 0.0)
            expo[c, g] = e
            mass[g] = summed(e) if first else mass[g] + summed(e)

    masses(0, True)

    @pl.loop(1, chunks)
    def _(c):
        masses(c, False)

    for g in range(group):
        total = jnp.sum(mass[g], 0, keepdims=True)
        mass[g] = jnp.broadcast_to(1.0 / total, (8, tokens))
    dq_ref[...] = jnp.zeros(dq_ref.shape, F32)
    gain_part_ref[...] = jnp.zeros(gain_part_ref.shape, F32)
    spread[...] = jnp.zeros(spread.shape, BF16)

    @pl.loop(0, chunks)
    def _(c):
        dk = jnp.zeros((tokens, head_dim), F32)
        dv = jnp.zeros((tokens, head_dim), F32)
        if whole_dots:
            wide[...] = dot_nn(vals[c], grad_t_ref[...])
        for g in range(group):
            cols = cols_of(g)
            grad_prob = wide[:, cols] if whole_dots else dot_nn(vals[c], grad_t_ref[:, cols])
            weights = expo[c, g] * mass[g, 0:1, :]
            dscore = (weights * (grad_prob - delta_ref[:, cols])).astype(BF16)
            weights = weights.astype(BF16)
            if whole_dots:
                w_all[:, cols] = weights
                ds_all[:, cols] = dscore
            else:
                dv = dv + dot_nn(weights, grad_ref[cols, :])
                dk = dk + dot_nn(dscore, q_ref[cols, :])
                dq_ref[:, cols] = dq_ref[:, cols] + dot_nn(keys_t[c], dscore)
        if whole_dots:
            dv = dot_nn(w_all[...], grad_ref[...])
            dk = dot_nn(ds_all[...], q_ref[...])
            dq_ref[...] = dq_ref[...] + dot_nn(keys_t[c], ds_all[...])
        dk = dk * inv_root
        found[c, :, 0:head_dim] = dk.astype(BF16)
        found[c, :, head_dim:] = dv.astype(BF16)
        front = jnp.sum((dk * with_cos[c]).reshape(tokens // 8, 8, head_dim), 0)
        back = jnp.sum((dk * with_sin[c]).reshape(tokens // 8, 8, head_dim), 0)
        gain_part_ref[...] = gain_part_ref[...] + front - pltpu.roll(back, head_dim // 2, 1)

    @pl.loop(0, count)
    def _(slot):
        rows = rows_of(lax.rem(slot, blocks))
        spread[plan_ref[0, slot], rows_of(plan_ref[1, slot]), :] = found[slot // blocks, rows, :]

    for piece in range(half):
        straight[piece][...] = spread[piece]
        crossed[piece] = spread[half + piece]


def merge_kernel(*refs):
    parts, crossed_ref, outs = refs[:len(refs) // 2], refs[len(refs) // 2], refs[len(refs) // 2 + 1:]
    outs[0][...] = (parts[0][...].astype(F32) + crossed_ref[0].astype(F32))
    for i in range(1, len(parts)):
        outs[i][...] = (parts[i][...].astype(F32) + crossed_ref[i].astype(F32)).astype(BF16)


def query_kernel(blocks, inv_root, depth_ref, t0, t1, t2, t3, gain_ref, q_ref, *refs):
    dq_refs, (out_ref, part_ref) = refs[:-2], refs[-2:]
    tokens = q_ref.shape[0]
    head_dim = gain_ref.shape[1]
    group = dq_refs[0].shape[1] // tokens
    cos, sin = own_tables(depth_ref, (t0, t1, t2, t3), blocks)
    gain = gain_ref[...]
    part = jnp.zeros((8, head_dim), F32)
    for head in range(group * len(dq_refs)):
        cols = pl.ds(head * head_dim, head_dim)
        rows = q_ref[:, cols].astype(F32)
        recip = inverse_rms(rows)
        normed = rows * recip
        dq = jnp.transpose(dq_refs[head // group][:, pl.ds(head % group * tokens, tokens)])
        scaled_grad = turned_back(dq, cos, sin) * inv_root
        term = scaled_grad * normed
        part = part + jnp.sum(term.reshape(tokens // 8, 8, head_dim), 0)
        inner = jnp.mean(term * gain, -1, keepdims=True)
        out_ref[:, cols] = (recip * (scaled_grad * gain - normed * inner)).astype(BF16)
    part_ref[...] = part


def key_kernel(blocks, counts, depth_ref, t0, t1, t2, t3, gain_ref, k_ref, *refs):
    sums, (dk_out_ref, dv_out_ref) = refs[:-2], refs[-2:]
    head_dim = gain_ref.shape[1]
    cos, sin = own_tables(depth_ref, (t0, t1, t2, t3), blocks)
    gain = gain_ref[...]
    for head, each in enumerate(counts):
        cols = pl.ds(head * head_dim, head_dim)
        rows = k_ref[:, cols].astype(F32)
        recip = inverse_rms(rows)
        normed = rows * recip
        mine = sums[sum(counts[:head]):][:each]
        both = mine[0][...].astype(F32)
        for other in mine[1:]:
            both = both + other[...].astype(F32)
        grad = turned_back(both[:, 0:head_dim], cos, sin) * gain
        inner = jnp.mean(grad * normed, -1, keepdims=True)
        dk_out_ref[:, cols] = (recip * (grad - normed * inner)).astype(BF16)
        dv_out_ref[:, cols] = both[:, head_dim:].astype(BF16)


class Tree:
    def __init__(self, size, cycle):
        self.size, self.cycle = size, cycle

    def order(self, index):
        return (index - 1) % self.size

    def send(self, value, target, wanted):
        pairs = []
        for tree in range(self.cycle // self.size):
            for index in range(self.size):
                if wanted(index):
                    ends = [(tree * self.size + 1 + self.order(i)) % self.cycle for i in (index, target(index))]
                    pairs.append(tuple(ends))
        return lax.ppermute(value, "ctx", pairs)

    def after(self, *pair):
        return self.order(pair[1] % self.size) > self.order(pair[0] % self.size)

    def gather(self, own):
        size, after = self.size, self.after
        cross = self.send(own, lambda i: i ^ 1, lambda i: after(i, i ^ 1))
        straight, crossed = [], []
        for step in range(2, size, 2):
            there = lambda i: (i + step) % size
            straight.append(self.send(own, there, lambda i: after(i, there(i)) or after(i, there(i) ^ 1)))
        for step, piece in zip(range(2, size, 2), straight):
            crossed.append(self.send(piece, lambda i: i ^ 1, lambda i: after(i - step, i ^ 1)))
        return [own, *straight, cross, *crossed]

    def across(self, crossed):
        steps = range(0, self.size, 2)
        return self.send(crossed, lambda i: i ^ 1, lambda i: any(self.after((i ^ 1) - step, i) for step in steps))

    def back(self, merged):
        size, after = self.size, self.after
        terms = []
        for step, both in zip(range(2, size, 2), merged):
            there = lambda i: (i - step) % size
            terms.append(self.send(both, there, lambda i: after(there(i), i) or after(there(i), i ^ 1)))
        return terms


def total_over(value, axis):
    size = lax.axis_size(axis)
    if size & (size - 1):
        return lax.psum(value, axis)
    bit = 1
    while bit < size:
        value = value + lax.ppermute(value, axis, [(i, i ^ bit) for i in range(size)])
        bit *= 2
    return value


def on_device(q_raw, k_raw, values, saved_out, out_grad, q_gain, k_gain, ancestors):
    tokens = q_raw.shape[0]
    head_dim = q_gain.shape[0]
    kv_heads = k_raw.shape[1] // head_dim
    heads = q_raw.shape[1] // head_dim
    group = heads // kv_heads
    blocks = ancestors.shape[0]
    tree_blocks = ancestors.shape[1]
    block_len = tokens // blocks
    tree_dev = tree_blocks // blocks
    cycle = lax.axis_size("ctx")
    inv_root = 1.0 / math.sqrt(head_dim)
    tree = Tree(tree_dev, cycle)
    place = (lax.axis_index("ctx") - 1 + cycle) % cycle % tree_dev
    place = place.reshape(1).astype(jnp.int32)

    depth = jnp.sum((ancestors >= 0).astype(jnp.int32), 1) - 1
    total_blocks = blocks * cycle
    in_tree = jnp.where(
        ancestors >= 0, (ancestors - blocks + total_blocks) % total_blocks % tree_blocks, -1
    )
    tables = [
        jnp.asarray(table)
        for starts in (range(0, tree_blocks * block_len, block_len), range(block_len))
        for table in rope_rows(starts, head_dim)
    ]
    q_gain_row, k_gain_row = q_gain.reshape(1, head_dim), k_gain.reshape(1, head_dim)

    pieces = tree.gather(jnp.concatenate([k_raw, values], 1))

    params = pltpu.CompilerParams(vmem_limit_bytes=VMEM_LIMIT)
    smem = pl.BlockSpec(memory_space=pltpu.SMEM)
    vmem = pl.BlockSpec(memory_space=pltpu.VMEM)
    sds = jax.ShapeDtypeStruct

    plan = pl.pallas_call(
        lambda *refs: plan_kernel(blocks, tree_dev, *refs),
        out_shape=sds((5, tree_blocks), jnp.int32),
        in_specs=[smem, smem],
        out_specs=smem,
        name="plan",
    )(place, in_tree)

    rows = group * tokens
    queries = pl.pallas_call(
        lambda *refs: prep_kernel(blocks, block_len, kv_heads, *refs),
        out_shape=tuple(
            [
                sds((head_dim, rows), BF16),
                sds((rows, head_dim), BF16),
                sds((head_dim, rows), BF16),
                sds((rows, head_dim), BF16),
                sds((1, rows), F32),
            ]
            * kv_heads
        ),
        in_specs=[smem] + [vmem] * 8,
        out_specs=tuple([vmem] * (5 * kv_heads)),
        compiler_params=params,
        name="prep",
    )(depth, *tables, q_gain_row, q_raw, out_grad, saved_out)

    half = tree_dev // 2

    def attend(h):
        return pl.pallas_call(
            lambda *refs: main_kernel(blocks, block_len, tree_dev, inv_root, h, h > 0, *refs),
            out_shape=(
                sds((head_dim, rows), F32),
                sds((8, head_dim), F32),
                *[sds((tokens, 2 * head_dim), BF16)] * half,
                sds((half, tokens, 2 * head_dim), BF16),
            ),
            in_specs=[smem] + [vmem] * (10 + tree_dev),
            out_specs=tuple([vmem] * (3 + half)),
            scratch_shapes=[
                pltpu.VMEM((tree_dev, tokens, 2 * head_dim), BF16),
                pltpu.VMEM((tree_dev, tokens, head_dim), BF16),
                pltpu.VMEM((tree_dev, head_dim, tokens), BF16),
                pltpu.VMEM((tree_dev, tokens, head_dim), BF16),
                pltpu.VMEM((tree_dev, 8 * ((blocks + 7) // 8), tokens), F32),
                pltpu.VMEM((tree_dev, tokens, head_dim), F32),
                pltpu.VMEM((tree_dev, tokens, head_dim), F32),
                pltpu.VMEM((tree_dev, group, tokens, tokens), F32),
                pltpu.VMEM((group, 8, tokens), F32),
                pltpu.VMEM((tokens, rows), BF16),
                pltpu.VMEM((tokens, rows), BF16),
                pltpu.VMEM((tree_dev, tokens, 2 * head_dim), BF16),
                pltpu.VMEM((tree_dev, tokens, 2 * head_dim), BF16),
                pltpu.VMEM((tokens, rows), F32),
            ],
            compiler_params=params,
            cost_estimate=pl.CostEstimate(
                flops=10 * group * tokens * tree_dev * tokens * head_dim,
                bytes_accessed=8 * 1024 * 1024,
                transcendentals=group * tokens * tree_dev * tokens,
            ),
            name="attend",
        )(plan, k_gain_row, *tables, *pieces, *queries[5 * h:5 * h + 5])

    dq, terms, counts, k_gain_parts = [], [], [], []
    for h in range(kv_heads):
        dq_here, k_gain_part, *parts, crossed = attend(h)
        dq.append(dq_here)
        k_gain_parts.append(k_gain_part)
        own, *merged = pl.pallas_call(
            merge_kernel,
            out_shape=tuple(
                sds((tokens, 2 * head_dim), F32 if i == 0 else BF16) for i in range(half)
            ),
            in_specs=[vmem] * (half + 1),
            out_specs=tuple([vmem] * half),
            compiler_params=params,
            name="merge",
        )(*parts, tree.across(crossed))
        mine = [own, *tree.back(merged)]
        terms.extend(mine)
        counts.append(len(mine))

    dq_raw, q_gain_part = pl.pallas_call(
        lambda *refs: query_kernel(blocks, inv_root, *refs),
        out_shape=(sds((tokens, heads * head_dim), BF16), sds((8, head_dim), F32)),
        in_specs=[smem] + [vmem] * (6 + kv_heads),
        out_specs=(vmem, vmem),
        compiler_params=params,
        name="query_back",
    )(depth, *tables, q_gain_row, q_raw, *dq)

    gains = jnp.stack([jnp.sum(q_gain_part, 0), jnp.sum(sum(k_gain_parts), 0)])
    gains = total_over(total_over(gains, "heads"), "ctx")

    dk_raw, dv = pl.pallas_call(
        lambda *refs: key_kernel(blocks, counts, *refs),
        out_shape=(sds(k_raw.shape, BF16), sds(k_raw.shape, BF16)),
        in_specs=[smem] + [vmem] * (6 + len(terms)),
        out_specs=(vmem, vmem),
        compiler_params=params,
        name="key_back",
    )(depth, *tables, k_gain_row, k_raw, *terms)
    return (dq_raw, dk_raw, dv, gains[0], gains[1])


def solution(mesh):
    split = P("ctx", "heads")
    return jax.shard_map(
        on_device,
        mesh=mesh,
        in_specs=(split, split, split, split, split, P(), P(), P("ctx", None)),
        out_specs=(split, split, split, P(), P()),
        check_vma=False,
    )
```

```python
import math

import jax
import jax.numpy as jnp
import numpy as np
from jax import lax
from jax.experimental import pallas as pl
from jax.experimental.pallas import tpu as pltpu
from jax.sharding import PartitionSpec as P

ROPE_BASE = 1000000.0
EPS = 1e-06
HIDDEN = -100000.0
VMEM_LIMIT = 56 * 1024 * 1024
F32 = jnp.float32
BF16 = jnp.bfloat16


def rope_rows(starts, head_dim):
    half = head_dim // 2
    frequency = np.exp(
        np.arange(half, dtype=np.float32) * np.float32(-2.0 * math.log(ROPE_BASE) / head_dim)
    ).astype(np.float32)
    angles = np.asarray(starts, np.float32)[:, None] * frequency[None, :]
    cos = np.cos(angles.astype(np.float64)).astype(np.float32)
    sin = np.sin(angles.astype(np.float64)).astype(np.float32)
    return np.concatenate([cos, cos], 1), np.concatenate([-sin, sin], 1)


def block_tables(depth, tables):
    start_cos, start_sin, offset_cos, offset_sin = tables
    cos, sin = start_cos[pl.ds(depth, 1), :], start_sin[pl.ds(depth, 1), :]
    both_cos = cos * offset_cos[...] - sin * offset_sin[...]
    both_sin = sin * offset_cos[...] + cos * offset_sin[...]
    return both_cos, both_sin


def turned(rows, cos, sin):
    return rows * cos + pltpu.roll(rows, rows.shape[-1] // 2, 1) * sin


def turned_back(rows, cos, sin):
    return rows * cos - pltpu.roll(rows, rows.shape[-1] // 2, 1) * sin


def inverse_rms(rows):
    return lax.rsqrt(jnp.mean(rows * rows, -1, keepdims=True) + EPS)


def own_tables(depth_ref, tables, blocks):
    parts = [block_tables(depth_ref[a], tables) for a in range(blocks)]
    return jnp.concatenate([p[0] for p in parts], 0), jnp.concatenate([p[1] for p in parts], 0)


def dot_nn(lhs, rhs):
    return lax.dot_general(lhs, rhs, (((1,), (0,)), ((), ())), preferred_element_type=F32)


def plan_kernel(blocks, tree_dev, place_ref, anc_ref, plan_ref):
    slots = tree_dev * blocks
    place = place_ref[0]
    here = jnp.where(place + 1 == tree_dev, 0, place + 1)
    for row in range(4):
        for i in range(slots):
            plan_ref[row, i] = 0
    count = jnp.int32(blocks)
    steps = [jnp.int32(0)] * blocks
    for b in range(slots):
        bits = jnp.int32(0)
        depth = jnp.int32(0)
        for a in range(blocks):
            hit = anc_ref[a, jnp.minimum(steps[a], slots - 1)] == b
            bits = bits | jnp.where(hit, 1 << a, 0)
            depth = jnp.where(hit, steps[a], depth)
            steps[a] = steps[a] + jnp.where(hit, 1, 0)
        own = place == b // blocks
        slot = jnp.where(own, b % blocks, jnp.minimum(count, slots - 1))
        there = (b // blocks + 1) % tree_dev
        odd = jnp.bitwise_and(here + there, 1)
        gap = jnp.bitwise_xor(here, odd) - there
        gap = jnp.where(gap < 0, gap + tree_dev, gap)
        plan_ref[0, slot] = odd * (tree_dev // 2) + lax.shift_right_logical(gap, 1)
        plan_ref[1, slot] = b % blocks
        plan_ref[2, slot] = depth
        plan_ref[3, slot] = bits
        count = count + jnp.where(own | (bits == 0), 0, 1)
    for i in range(slots):
        plan_ref[4, i] = count


def prep_kernel(blocks, block_len, kv_heads, depth_ref, t0, t1, t2, t3, gain_ref, q_ref, grad_ref, out_ref, *outs):
    tokens = q_ref.shape[0]
    head_dim = gain_ref.shape[1]
    cos, sin = own_tables(depth_ref, (t0, t1, t2, t3), blocks)
    gain = gain_ref[...]
    group = q_ref.shape[1] // head_dim // kv_heads
    for head in range(group * kv_heads):
        g = head % group
        q_t_ref, q_rot_ref, grad_t_ref, grad_heads_ref, delta_ref = outs[5 * (head // group):][:5]
        cols = pl.ds(head * head_dim, head_dim)
        here = pl.ds(g * tokens, tokens)
        rows = q_ref[:, cols].astype(F32)
        rotated = turned(rows * inverse_rms(rows) * gain, cos, sin).astype(BF16)
        q_rot_ref[here, :] = rotated
        q_t_ref[:, here] = jnp.transpose(rotated)
        grad = grad_ref[:, cols]
        grad_heads_ref[here, :] = grad
        grad_t_ref[:, here] = jnp.transpose(grad)
        product = grad.astype(F32) * out_ref[:, cols].astype(F32)
        delta_ref[:, here] = jnp.sum(jnp.transpose(product), 0, keepdims=True)


def main_kernel(blocks, block_len, tree_dev, inv_root, staged, *refs):
    plan_ref, gain_ref = refs[:2]
    tables = refs[2:6]
    pieces = refs[6:6 + tree_dev]
    q_t_ref, q_ref, grad_t_ref, grad_ref, delta_ref = refs[6 + tree_dev:11 + tree_dev]
    half = tree_dev // 2
    dq_ref, gain_part_ref = refs[11 + tree_dev:13 + tree_dev]
    straight = refs[13 + tree_dev:13 + tree_dev + half]
    crossed, raw, keys, keys_t, vals, shown, with_cos, with_sin, expo, mass, w_all, ds_all, found, spread, wide = refs[
        13 + tree_dev + half:]
    head_dim = gain_ref.shape[1]
    tokens = raw.shape[1]
    group = q_ref.shape[0] // tokens
    count = plan_ref[4, 0]
    chunks = (count + blocks - 1) // blocks
    gain = gain_ref[...]
    for piece in range(tree_dev):
        raw[piece] = pieces[piece][...]
    query_block = lax.broadcasted_iota(jnp.int32, (1, tokens), 1) // block_len

    def rows_of(start):
        return pl.ds(pl.multiple_of(start * block_len, block_len), block_len)

    def load_chunk(c):
        for j in range(blocks):
            slot = jnp.minimum(c * blocks + j, tree_dev * blocks - 1)
            piece = plan_ref[0, slot]
            rows = rows_of(plan_ref[1, slot])
            cos, sin = block_tables(plan_ref[2, slot], tables)
            unit = raw[piece, rows, 0:head_dim].astype(F32)
            unit = unit * inverse_rms(unit)
            here = pl.ds(j * block_len, block_len)
            with_cos[c, here, :] = unit * cos
            with_sin[c, here, :] = pltpu.roll(unit * sin, head_dim // 2, 1)
            keys[c, here, :] = turned(unit * gain, cos, sin).astype(BF16)
            bits = jnp.where(c * blocks + j < count, plan_ref[3, slot], 0)
            row = jnp.zeros((1, tokens), F32)
            for a in range(blocks):
                seen = lax.rem(lax.shift_right_logical(bits, a), 2)
                row = jnp.where((query_block == a) & (seen == 0), HIDDEN, row)
            shown[c, j:j + 1, :] = row
            vals[c, here, :] = raw[piece, rows, head_dim:]
        keys_t[c] = jnp.transpose(keys[c].astype(F32)).astype(BF16)

    def exps(c, g, scores):
        parts = []
        for j in range(blocks):
            here = slice(j * block_len, (j + 1) * block_len)
            parts.append(jnp.exp(scores[here] * inv_root + shown[c, j:j + 1, :]))
        return jnp.concatenate(parts, 0)

    def summed(e):
        return jnp.sum(e.reshape(tokens // 8, 8, tokens), 0)

    key_row = lax.broadcasted_iota(jnp.int32, (tokens, tokens), 0)
    query_col = lax.broadcasted_iota(jnp.int32, (tokens, tokens), 1)

    def cols_of(g):
        return pl.ds(g * tokens, tokens)

    def masses(c, first):
        if staged:
            wide[...] = dot_nn(keys[c], q_t_ref[...])
        for g in range(group):
            scores = wide[:, cols_of(g)] if staged else dot_nn(keys[c], q_t_ref[:, cols_of(g)])
            e = exps(c, g, scores)
            if first:
                e = jnp.where(key_row <= query_col, e, 0.0)
            expo[c, g] = e
            mass[g] = summed(e) if first else mass[g] + summed(e)

    load_chunk(0)
    masses(0, True)
    load_chunk(1)

    @pl.loop(1, chunks)
    def _(c):
        masses(c, False)
        load_chunk(c + 1)

    for g in range(group):
        total = jnp.sum(mass[g], 0, keepdims=True)
        mass[g] = jnp.broadcast_to(1.0 / total, (8, tokens))
    dq_ref[...] = jnp.zeros(dq_ref.shape, F32)
    gain_part_ref[...] = jnp.zeros(gain_part_ref.shape, F32)
    spread[...] = jnp.zeros(spread.shape, BF16)

    @pl.loop(0, chunks)
    def _(c):
        if staged:
            wide[...] = dot_nn(vals[c], grad_t_ref[...])
        for g in range(group):
            cols = cols_of(g)
            grad_prob = wide[:, cols] if staged else dot_nn(vals[c], grad_t_ref[:, cols])
            weights = expo[c, g] * mass[g, 0:1, :]
            ds_all[:, cols] = (weights * (grad_prob - delta_ref[:, cols])).astype(BF16)
            w_all[:, cols] = weights.astype(BF16)
        dv = dot_nn(w_all[...], grad_ref[...])
        dk = dot_nn(ds_all[...], q_ref[...])
        dq_ref[...] = dq_ref[...] + dot_nn(keys_t[c], ds_all[...])
        dk = dk * inv_root
        found[c, :, 0:head_dim] = dk.astype(BF16)
        found[c, :, head_dim:] = dv.astype(BF16)
        front = jnp.sum((dk * with_cos[c]).reshape(tokens // 8, 8, head_dim), 0)
        back = jnp.sum((dk * with_sin[c]).reshape(tokens // 8, 8, head_dim), 0)
        gain_part_ref[...] = gain_part_ref[...] + front - pltpu.roll(back, head_dim // 2, 1)

    @pl.loop(0, count)
    def _(slot):
        rows = rows_of(lax.rem(slot, blocks))
        spread[plan_ref[0, slot], rows_of(plan_ref[1, slot]), :] = found[slot // blocks, rows, :]

    for piece in range(half):
        straight[piece][...] = spread[piece]
        crossed[piece] = spread[half + piece]


def merge_kernel(*refs):
    parts, crossed_ref, outs = refs[:len(refs) // 2], refs[len(refs) // 2], refs[len(refs) // 2 + 1:]
    outs[0][...] = (parts[0][...].astype(F32) + crossed_ref[0].astype(F32))
    for i in range(1, len(parts)):
        outs[i][...] = (parts[i][...].astype(F32) + crossed_ref[i].astype(F32)).astype(BF16)


def query_kernel(blocks, inv_root, depth_ref, t0, t1, t2, t3, gain_ref, q_ref, *refs):
    dq_refs, (out_ref, part_ref) = refs[:-2], refs[-2:]
    tokens = q_ref.shape[0]
    head_dim = gain_ref.shape[1]
    group = dq_refs[0].shape[1] // tokens
    cos, sin = own_tables(depth_ref, (t0, t1, t2, t3), blocks)
    gain = gain_ref[...]
    part = jnp.zeros((8, head_dim), F32)
    for head in range(group * len(dq_refs)):
        cols = pl.ds(head * head_dim, head_dim)
        rows = q_ref[:, cols].astype(F32)
        recip = inverse_rms(rows)
        normed = rows * recip
        dq = jnp.transpose(dq_refs[head // group][:, pl.ds(head % group * tokens, tokens)])
        scaled_grad = turned_back(dq, cos, sin) * inv_root
        term = scaled_grad * normed
        part = part + jnp.sum(term.reshape(tokens // 8, 8, head_dim), 0)
        inner = jnp.mean(term * gain, -1, keepdims=True)
        out_ref[:, cols] = (recip * (scaled_grad * gain - normed * inner)).astype(BF16)
    part_ref[...] = part


def key_kernel(blocks, counts, depth_ref, t0, t1, t2, t3, gain_ref, k_ref, *refs):
    sums, (gains_ref, dk_out_ref, dv_out_ref, total_ref) = refs[:-4], refs[-4:]
    total_ref[...] = jnp.sum(gains_ref[...], 0)
    head_dim = gain_ref.shape[1]
    cos, sin = own_tables(depth_ref, (t0, t1, t2, t3), blocks)
    gain = gain_ref[...]
    for head, each in enumerate(counts):
        cols = pl.ds(head * head_dim, head_dim)
        rows = k_ref[:, cols].astype(F32)
        recip = inverse_rms(rows)
        normed = rows * recip
        mine = sums[sum(counts[:head]):][:each]
        both = mine[0][...].astype(F32)
        for other in mine[1:]:
            both = both + other[...].astype(F32)
        grad = turned_back(both[:, 0:head_dim], cos, sin) * gain
        inner = jnp.mean(grad * normed, -1, keepdims=True)
        dk_out_ref[:, cols] = (recip * (grad - normed * inner)).astype(BF16)
        dv_out_ref[:, cols] = both[:, head_dim:].astype(BF16)


class Tree:
    def __init__(self, size, cycle):
        self.size, self.cycle = size, cycle

    def order(self, index):
        return (index - 1) % self.size

    def send(self, value, target, wanted):
        pairs = []
        for tree in range(self.cycle // self.size):
            for index in range(self.size):
                if wanted(index):
                    ends = [(tree * self.size + 1 + self.order(i)) % self.cycle for i in (index, target(index))]
                    pairs.append(tuple(ends))
        return lax.ppermute(value, "ctx", pairs)

    def after(self, *pair):
        return self.order(pair[1] % self.size) > self.order(pair[0] % self.size)

    def gather(self, own):
        size, after = self.size, self.after
        pieces = [own]
        for odd in range(2):
            for step in range(0, size, 2):
                if odd or step:
                    there = lambda i: (i + step) % size ^ odd
                    pieces.append(self.send(own, there, lambda i: after(i, there(i))))
        return pieces

    def across(self, crossed):
        steps = range(0, self.size, 2)
        return self.send(crossed, lambda i: i ^ 1, lambda i: any(self.after((i ^ 1) - step, i) for step in steps))

    def back(self, merged):
        size, after = self.size, self.after
        terms = []
        for step, both in zip(range(2, size, 2), merged):
            there = lambda i: (i - step) % size
            terms.append(self.send(both, there, lambda i: after(there(i), i) or after(there(i), i ^ 1)))
        return terms


def on_device(q_raw, k_raw, values, saved_out, out_grad, q_gain, k_gain, ancestors):
    tokens = q_raw.shape[0]
    head_dim = q_gain.shape[0]
    kv_heads = k_raw.shape[1] // head_dim
    heads = q_raw.shape[1] // head_dim
    group = heads // kv_heads
    blocks = ancestors.shape[0]
    tree_blocks = ancestors.shape[1]
    block_len = tokens // blocks
    tree_dev = tree_blocks // blocks
    cycle = lax.axis_size("ctx")
    inv_root = 1.0 / math.sqrt(head_dim)
    tree = Tree(tree_dev, cycle)
    place = (lax.axis_index("ctx") - 1 + cycle) % cycle % tree_dev
    place = place.reshape(1).astype(jnp.int32)

    depth = jnp.sum((ancestors >= 0).astype(jnp.int32), 1) - 1
    total_blocks = blocks * cycle
    in_tree = jnp.where(
        ancestors >= 0, (ancestors - blocks + total_blocks) % total_blocks % tree_blocks, -1
    )
    tables = [
        jnp.asarray(table)
        for starts in (range(0, tree_blocks * block_len, block_len), range(block_len))
        for table in rope_rows(starts, head_dim)
    ]
    q_gain_row, k_gain_row = q_gain.reshape(1, head_dim), k_gain.reshape(1, head_dim)

    pieces = []
    for h in range(kv_heads):
        cols = slice(h * head_dim, (h + 1) * head_dim)
        pieces.append(tree.gather(jnp.concatenate([k_raw[:, cols], values[:, cols]], 1)))

    params = pltpu.CompilerParams(vmem_limit_bytes=VMEM_LIMIT)
    smem = pl.BlockSpec(memory_space=pltpu.SMEM)
    vmem = pl.BlockSpec(memory_space=pltpu.VMEM)
    sds = jax.ShapeDtypeStruct

    plan = pl.pallas_call(
        lambda *refs: plan_kernel(blocks, tree_dev, *refs),
        out_shape=sds((5, tree_blocks), jnp.int32),
        in_specs=[smem, smem],
        out_specs=smem,
        name="plan",
    )(place, in_tree)

    rows = group * tokens
    queries = pl.pallas_call(
        lambda *refs: prep_kernel(blocks, block_len, kv_heads, *refs),
        out_shape=tuple(
            [
                sds((head_dim, rows), BF16),
                sds((rows, head_dim), BF16),
                sds((head_dim, rows), BF16),
                sds((rows, head_dim), BF16),
                sds((1, rows), F32),
            ]
            * kv_heads
        ),
        in_specs=[smem] + [vmem] * 8,
        out_specs=tuple([vmem] * (5 * kv_heads)),
        compiler_params=params,
        name="prep",
    )(depth, *tables, q_gain_row, q_raw, out_grad, saved_out)

    half = tree_dev // 2

    def attend(h):
        return pl.pallas_call(
            lambda *refs: main_kernel(blocks, block_len, tree_dev, inv_root, h > 0, *refs),
            out_shape=(
                sds((head_dim, rows), F32),
                sds((8, head_dim), F32),
                *[sds((tokens, 2 * head_dim), BF16)] * half,
                sds((half, tokens, 2 * head_dim), BF16),
            ),
            in_specs=[smem] + [vmem] * (10 + tree_dev),
            out_specs=tuple([vmem] * (3 + half)),
            scratch_shapes=[
                pltpu.VMEM((tree_dev, tokens, 2 * head_dim), BF16),
                pltpu.VMEM((tree_dev + 1, tokens, head_dim), BF16),
                pltpu.VMEM((tree_dev + 1, head_dim, tokens), BF16),
                pltpu.VMEM((tree_dev + 1, tokens, head_dim), BF16),
                pltpu.VMEM((tree_dev + 1, 8 * ((blocks + 7) // 8), tokens), F32),
                pltpu.VMEM((tree_dev + 1, tokens, head_dim), F32),
                pltpu.VMEM((tree_dev + 1, tokens, head_dim), F32),
                pltpu.VMEM((tree_dev, group, tokens, tokens), F32),
                pltpu.VMEM((group, 8, tokens), F32),
                pltpu.VMEM((tokens, rows), BF16),
                pltpu.VMEM((tokens, rows), BF16),
                pltpu.VMEM((tree_dev, tokens, 2 * head_dim), BF16),
                pltpu.VMEM((tree_dev, tokens, 2 * head_dim), BF16),
                pltpu.VMEM((tokens, rows), F32),
            ],
            compiler_params=params,
            cost_estimate=pl.CostEstimate(
                flops=10 * group * tokens * tree_dev * tokens * head_dim,
                bytes_accessed=8 * 1024 * 1024,
                transcendentals=group * tokens * tree_dev * tokens,
            ),
            name="attend",
        )(plan, k_gain_row, *tables, *pieces[h], *queries[5 * h:5 * h + 5])

    dq, terms, counts, k_gain_parts = [], [], [], []
    for h in range(kv_heads):
        dq_here, k_gain_part, *parts, crossed = attend(h)
        dq.append(dq_here)
        k_gain_parts.append(k_gain_part)
        own, *merged = pl.pallas_call(
            merge_kernel,
            out_shape=tuple(
                sds((tokens, 2 * head_dim), F32 if i == 0 else BF16) for i in range(half)
            ),
            in_specs=[vmem] * (half + 1),
            out_specs=tuple([vmem] * half),
            compiler_params=params,
            name="merge",
        )(*parts, tree.across(crossed))
        mine = [own, *tree.back(merged)]
        terms.extend(mine)
        counts.append(len(mine))

    dq_raw, q_gain_part = pl.pallas_call(
        lambda *refs: query_kernel(blocks, inv_root, *refs),
        out_shape=(sds((tokens, heads * head_dim), BF16), sds((8, head_dim), F32)),
        in_specs=[smem] + [vmem] * (6 + kv_heads),
        out_specs=(vmem, vmem),
        compiler_params=params,
        name="query_back",
    )(depth, *tables, q_gain_row, q_raw, *dq)

    gains = jnp.stack([jnp.sum(q_gain_part, 0), jnp.sum(sum(k_gain_parts), 0)])
    gains = lax.all_gather(gains, ("ctx", "heads"))

    dk_raw, dv, total = pl.pallas_call(
        lambda *refs: key_kernel(blocks, counts, *refs),
        out_shape=(sds(k_raw.shape, BF16), sds(k_raw.shape, BF16), sds(gains.shape[1:], F32)),
        in_specs=[smem] + [vmem] * (7 + len(terms)),
        out_specs=(vmem, vmem, vmem),
        compiler_params=params,
        name="key_back",
    )(depth, *tables, k_gain_row, k_raw, *terms, gains)
    return (dq_raw, dk_raw, dv, total[0], total[1])


def solution(mesh):
    split = P("ctx", "heads")
    return jax.shard_map(
        on_device,
        mesh=mesh,
        in_specs=(split, split, split, split, split, P(), P(), P("ctx", None)),
        out_specs=(split, split, split, P(), P()),
        check_vma=False,
    )
```

```python
import math

import jax
import jax.numpy as jnp
import numpy as np
from jax import lax
from jax.experimental import pallas as pl
from jax.experimental.pallas import tpu as pltpu
from jax.sharding import PartitionSpec as P

ROPE_BASE = 1000000.0
EPS = 1e-06
HIDDEN = -100000.0
VMEM_LIMIT = 56 * 1024 * 1024
F32 = jnp.float32
BF16 = jnp.bfloat16


def rope_rows(starts, head_dim):
    half = head_dim // 2
    frequency = np.exp(
        np.arange(half, dtype=np.float32) * np.float32(-2.0 * math.log(ROPE_BASE) / head_dim)
    ).astype(np.float32)
    angles = np.asarray(starts, np.float32)[:, None] * frequency[None, :]
    cos = np.cos(angles.astype(np.float64)).astype(np.float32)
    sin = np.sin(angles.astype(np.float64)).astype(np.float32)
    return np.concatenate([cos, cos], 1), np.concatenate([-sin, sin], 1)


def block_tables(depth, tables):
    start_cos, start_sin, offset_cos, offset_sin = tables
    cos, sin = start_cos[pl.ds(depth, 1), :], start_sin[pl.ds(depth, 1), :]
    both_cos = cos * offset_cos[...] - sin * offset_sin[...]
    both_sin = sin * offset_cos[...] + cos * offset_sin[...]
    return both_cos, both_sin


def turned(rows, cos, sin):
    return rows * cos + pltpu.roll(rows, rows.shape[-1] // 2, 1) * sin


def turned_back(rows, cos, sin):
    return rows * cos - pltpu.roll(rows, rows.shape[-1] // 2, 1) * sin


def inverse_rms(rows):
    return lax.rsqrt(jnp.mean(rows * rows, -1, keepdims=True) + EPS)


def own_tables(depth_ref, tables, blocks):
    parts = [block_tables(depth_ref[a], tables) for a in range(blocks)]
    return jnp.concatenate([p[0] for p in parts], 0), jnp.concatenate([p[1] for p in parts], 0)


def dot_nn(lhs, rhs):
    return lax.dot_general(lhs, rhs, (((1,), (0,)), ((), ())), preferred_element_type=F32)


def plan_kernel(blocks, tree_dev, place_ref, anc_ref, plan_ref):
    slots = tree_dev * blocks
    place = place_ref[0]
    here = jnp.where(place + 1 == tree_dev, 0, place + 1)
    for row in range(4):
        for i in range(slots):
            plan_ref[row, i] = 0
    count = jnp.int32(blocks)
    steps = [jnp.int32(0)] * blocks
    for b in range(slots):
        bits = jnp.int32(0)
        depth = jnp.int32(0)
        for a in range(blocks):
            hit = anc_ref[a, jnp.minimum(steps[a], slots - 1)] == b
            bits = bits | jnp.where(hit, 1 << a, 0)
            depth = jnp.where(hit, steps[a], depth)
            steps[a] = steps[a] + jnp.where(hit, 1, 0)
        own = place == b // blocks
        slot = jnp.where(own, b % blocks, jnp.minimum(count, slots - 1))
        there = (b // blocks + 1) % tree_dev
        odd = jnp.bitwise_and(here + there, 1)
        gap = jnp.bitwise_xor(here, odd) - there
        gap = jnp.where(gap < 0, gap + tree_dev, gap)
        plan_ref[0, slot] = odd * (tree_dev // 2) + lax.shift_right_logical(gap, 1)
        plan_ref[1, slot] = b % blocks
        plan_ref[2, slot] = depth
        plan_ref[3, slot] = bits
        count = count + jnp.where(own | (bits == 0), 0, 1)
    for i in range(slots):
        plan_ref[4, i] = count


def prep_kernel(blocks, depth_ref, t0, t1, t2, t3, gain_ref, q_ref, grad_ref, out_ref,
                q_t_ref, q_rot_ref, grad_t_ref, grad_heads_ref, delta_ref):
    tokens = q_ref.shape[0]
    head_dim = gain_ref.shape[1]
    cos, sin = own_tables(depth_ref, (t0, t1, t2, t3), blocks)
    gain = gain_ref[...]

    @pl.loop(0, q_ref.shape[1] // head_dim)
    def _(head):
        cols = pl.ds(pl.multiple_of(head * head_dim, head_dim), head_dim)
        here = pl.ds(pl.multiple_of(head * tokens, tokens), tokens)
        rows = q_ref[:, cols].astype(F32)
        rotated = turned(rows * inverse_rms(rows) * gain, cos, sin).astype(BF16)
        q_rot_ref[0, here, :] = rotated
        q_t_ref[0, :, here] = jnp.transpose(rotated)
        grad = grad_ref[:, cols]
        grad_heads_ref[0, here, :] = grad
        grad_t_ref[0, :, here] = jnp.transpose(grad)
        product = grad.astype(F32) * out_ref[:, cols].astype(F32)
        delta_ref[0, :, here] = jnp.sum(jnp.transpose(product), 0, keepdims=True)


def main_kernel(blocks, block_len, tree_dev, inv_root, head, *refs):
    plan_ref, gain_ref = refs[:2]
    tables = refs[2:6]
    pieces = refs[6:6 + tree_dev]
    q_t_ref, q_ref, grad_t_ref, grad_ref, delta_ref = [ref.at[head] for ref in refs[6 + tree_dev:11 + tree_dev]]
    half = tree_dev // 2
    dq_ref, gain_part_ref = refs[11 + tree_dev:13 + tree_dev]
    straight = refs[13 + tree_dev:13 + tree_dev + half]
    crossed, raw, keys, keys_t, vals, shown, with_cos, with_sin, expo, mass, w_all, ds_all, found, spread = refs[
        13 + tree_dev + half:]
    head_dim = gain_ref.shape[1]
    tokens = raw.shape[1]
    group = q_ref.shape[0] // tokens
    count = plan_ref[4, 0]
    chunks = (count + blocks - 1) // blocks
    gain = gain_ref[...]
    kv_heads = pieces[0].shape[1] // (2 * head_dim)
    for piece in range(tree_dev):
        raw[piece, :, 0:head_dim] = pieces[piece][:, head * head_dim:(head + 1) * head_dim]
        raw[piece, :, head_dim:] = pieces[piece][:, (kv_heads + head) * head_dim:(kv_heads + head + 1) * head_dim]
    query_block = lax.broadcasted_iota(jnp.int32, (1, tokens), 1) // block_len

    def rows_of(start):
        return pl.ds(pl.multiple_of(start * block_len, block_len), block_len)

    def load_chunk(c):
        for j in range(blocks):
            slot = jnp.minimum(c * blocks + j, tree_dev * blocks - 1)
            piece = plan_ref[0, slot]
            rows = rows_of(plan_ref[1, slot])
            cos, sin = block_tables(plan_ref[2, slot], tables)
            unit = raw[piece, rows, 0:head_dim].astype(F32)
            unit = unit * inverse_rms(unit)
            here = pl.ds(j * block_len, block_len)
            with_cos[c, here, :] = unit * cos
            with_sin[c, here, :] = pltpu.roll(unit * sin, head_dim // 2, 1)
            keys[c, here, :] = turned(unit * gain, cos, sin).astype(BF16)
            bits = jnp.where(c * blocks + j < count, plan_ref[3, slot], 0)
            row = jnp.zeros((1, tokens), F32)
            for a in range(blocks):
                seen = lax.rem(lax.shift_right_logical(bits, a), 2)
                row = jnp.where((query_block == a) & (seen == 0), HIDDEN, row)
            shown[c, j:j + 1, :] = row
            vals[c, here, :] = raw[piece, rows, head_dim:]
        keys_t[c] = jnp.transpose(keys[c].astype(F32)).astype(BF16)

    def exps(c, scores):
        parts = []
        for j in range(blocks):
            here = slice(j * block_len, (j + 1) * block_len)
            parts.append(jnp.exp(scores[here] * inv_root + shown[c, j:j + 1, :]))
        return jnp.concatenate(parts, 0)

    def summed(e):
        return jnp.sum(e.reshape(tokens // 8, 8, tokens), 0)

    key_row = lax.broadcasted_iota(jnp.int32, (tokens, tokens), 0)
    query_col = lax.broadcasted_iota(jnp.int32, (tokens, tokens), 1)

    def cols_of(g):
        return pl.ds(g * tokens, tokens)

    mass[...] = jnp.zeros(mass.shape, F32)
    load_chunk(0)

    def masses(c, later):
        for g in range(group):
            e = exps(c, dot_nn(keys[c], q_t_ref[:, cols_of(g)]))
            expo[c, g] = e
            mass[later, g] = mass[later, g] + summed(e)

    masses(0, 0)
    load_chunk(1)

    @pl.loop(1, chunks)
    def _(c):
        masses(c, 1)
        load_chunk(c + 1)

    @pl.loop(0, group)
    def _(g):
        e = jnp.where(key_row <= query_col, expo[0, g], 0.0)
        expo[0, g] = e
        total = jnp.sum(mass[1, g] + summed(e), 0, keepdims=True)
        mass[0, g] = jnp.broadcast_to(1.0 / total, (8, tokens))

    dq_ref[...] = jnp.zeros(dq_ref.shape, F32)
    gain_part_ref[...] = jnp.zeros(gain_part_ref.shape, F32)
    spread[...] = jnp.zeros(spread.shape, BF16)

    @pl.loop(0, chunks)
    def _(c):
        for g in range(group):
            cols = cols_of(g)
            grad_prob = dot_nn(vals[c], grad_t_ref[:, cols])
            weights = expo[c, g] * mass[0, g, 0:1, :]
            ds_all[:, cols] = (weights * (grad_prob - delta_ref[:, cols])).astype(BF16)
            w_all[:, cols] = weights.astype(BF16)
        dv = dot_nn(w_all[...], grad_ref[...])
        dk = dot_nn(ds_all[...], q_ref[...])
        dq_ref[...] = dq_ref[...] + dot_nn(keys_t[c], ds_all[...])
        dk = dk * inv_root
        found[c, :, 0:head_dim] = dk.astype(BF16)
        found[c, :, head_dim:] = dv.astype(BF16)
        front = jnp.sum((dk * with_cos[c]).reshape(tokens // 8, 8, head_dim), 0)
        back = jnp.sum((dk * with_sin[c]).reshape(tokens // 8, 8, head_dim), 0)
        gain_part_ref[...] = gain_part_ref[...] + front - pltpu.roll(back, head_dim // 2, 1)

    @pl.loop(0, count)
    def _(slot):
        rows = rows_of(lax.rem(slot, blocks))
        spread[plan_ref[0, slot], rows_of(plan_ref[1, slot]), :] = found[slot // blocks, rows, :]

    for piece in range(half):
        straight[piece][...] = spread[piece]
        crossed[piece] = spread[half + piece]


def merge_kernel(*refs):
    parts, crossed_ref, outs = refs[:len(refs) // 2], refs[len(refs) // 2], refs[len(refs) // 2 + 1:]
    outs[0][...] = (parts[0][...].astype(F32) + crossed_ref[0].astype(F32))
    for i in range(1, len(parts)):
        outs[i][...] = (parts[i][...].astype(F32) + crossed_ref[i].astype(F32)).astype(BF16)


def query_kernel(blocks, inv_root, shares, depth_ref, t0, t1, t2, t3, gain_ref, q_ref, *refs):
    dq_refs, (out_ref, part_ref) = refs[:-2], refs[-2:]
    tokens = q_ref.shape[0]
    head_dim = gain_ref.shape[1]
    cos, sin = own_tables(depth_ref, (t0, t1, t2, t3), blocks)
    gain = gain_ref[...]
    step = pl.program_id(0)

    @pl.when(step == 0)
    def _():
        part_ref[...] = jnp.zeros(part_ref.shape, F32)

    for kv, dq_ref in enumerate(dq_refs):

        @pl.when(step // shares == kv)
        def _():
            @pl.loop(0, q_ref.shape[1] // head_dim)
            def _(head):
                cols = pl.ds(pl.multiple_of(head * head_dim, head_dim), head_dim)
                rows = q_ref[:, cols].astype(F32)
                recip = inverse_rms(rows)
                normed = rows * recip
                dq = jnp.transpose(dq_ref[:, pl.ds(pl.multiple_of(head * tokens, tokens), tokens)])
                scaled_grad = turned_back(dq, cos, sin) * inv_root
                term = scaled_grad * normed
                part_ref[...] = part_ref[...] + jnp.sum(term.reshape(tokens // 8, 8, head_dim), 0)
                inner = jnp.mean(term * gain, -1, keepdims=True)
                out_ref[:, cols] = (recip * (scaled_grad * gain - normed * inner)).astype(BF16)


def key_kernel(blocks, counts, depth_ref, t0, t1, t2, t3, gain_ref, k_ref, *refs):
    sums, (gains_ref, dk_out_ref, dv_out_ref, total_ref) = refs[:-4], refs[-4:]
    total_ref[...] = jnp.sum(gains_ref[...], 0)
    head_dim = gain_ref.shape[1]
    cos, sin = own_tables(depth_ref, (t0, t1, t2, t3), blocks)
    gain = gain_ref[...]
    for head, each in enumerate(counts):
        cols = pl.ds(head * head_dim, head_dim)
        rows = k_ref[:, cols].astype(F32)
        recip = inverse_rms(rows)
        normed = rows * recip
        mine = sums[sum(counts[:head]):][:each]
        both = mine[0][...].astype(F32)
        for other in mine[1:]:
            both = both + other[...].astype(F32)
        grad = turned_back(both[:, 0:head_dim], cos, sin) * gain
        inner = jnp.mean(grad * normed, -1, keepdims=True)
        dk_out_ref[:, cols] = (recip * (grad - normed * inner)).astype(BF16)
        dv_out_ref[:, cols] = both[:, head_dim:].astype(BF16)


class Tree:
    def __init__(self, size, cycle):
        self.size, self.cycle = size, cycle

    def order(self, index):
        return (index - 1) % self.size

    def send(self, value, target, wanted):
        pairs = []
        for tree in range(self.cycle // self.size):
            for index in range(self.size):
                if wanted(index):
                    ends = [(tree * self.size + 1 + self.order(i)) % self.cycle for i in (index, target(index))]
                    pairs.append(tuple(ends))
        return lax.ppermute(value, "ctx", pairs)

    def after(self, *pair):
        return self.order(pair[1] % self.size) > self.order(pair[0] % self.size)

    def passed(self, index, step):
        size, piece = self.size, index - step
        needed = self.after(piece, index) or self.after(piece, index ^ 1)
        return needed or (step + 2 < size and self.passed((index + 2) % size, step + 2))

    def gather(self, own):
        size, after = self.size, self.after
        cross = [self.send(own, lambda i: i ^ 1, lambda i: after(i, i ^ 1))]
        straight = [own]
        for step in range(2, size, 2):
            there = lambda i: (i + 2) % size
            straight.append(self.send(straight[-1], there, lambda i: self.passed(there(i), step)))
            cross.append(self.send(straight[-1], lambda i: i ^ 1, lambda i: after(i - step, i ^ 1)))
        return straight + cross

    def across(self, crossed):
        steps = range(0, self.size, 2)
        return self.send(crossed, lambda i: i ^ 1, lambda i: any(self.after((i ^ 1) - step, i) for step in steps))

    def back(self, merged):
        size, after = self.size, self.after
        terms = []
        for step, both in zip(range(2, size, 2), merged):
            there = lambda i: (i - step) % size
            terms.append(self.send(both, there, lambda i: after(there(i), i) or after(there(i), i ^ 1)))
        return terms


def on_device(q_raw, k_raw, values, saved_out, out_grad, q_gain, k_gain, ancestors):
    tokens = q_raw.shape[0]
    head_dim = q_gain.shape[0]
    kv_heads = k_raw.shape[1] // head_dim
    heads = q_raw.shape[1] // head_dim
    group = heads // kv_heads
    blocks = ancestors.shape[0]
    tree_blocks = ancestors.shape[1]
    block_len = tokens // blocks
    tree_dev = tree_blocks // blocks
    cycle = lax.axis_size("ctx")
    inv_root = 1.0 / math.sqrt(head_dim)
    tree = Tree(tree_dev, cycle)
    place = (lax.axis_index("ctx") - 1 + cycle) % cycle % tree_dev
    place = place.reshape(1).astype(jnp.int32)

    depth = jnp.sum((ancestors >= 0).astype(jnp.int32), 1) - 1
    total_blocks = blocks * cycle
    in_tree = jnp.where(
        ancestors >= 0, (ancestors - blocks + total_blocks) % total_blocks % tree_blocks, -1
    )
    tables = [
        jnp.asarray(table)
        for starts in (range(0, tree_blocks * block_len, block_len), range(block_len))
        for table in rope_rows(starts, head_dim)
    ]
    q_gain_row, k_gain_row = q_gain.reshape(1, head_dim), k_gain.reshape(1, head_dim)

    pieces = tree.gather(jnp.concatenate([k_raw, values], 1))

    params = pltpu.CompilerParams(vmem_limit_bytes=VMEM_LIMIT)
    smem = pl.BlockSpec(memory_space=pltpu.SMEM)
    vmem = pl.BlockSpec(memory_space=pltpu.VMEM)
    sds = jax.ShapeDtypeStruct

    plan = pl.pallas_call(
        lambda *refs: plan_kernel(blocks, tree_dev, *refs),
        out_shape=sds((5, tree_blocks), jnp.int32),
        in_specs=[smem, smem],
        out_specs=smem,
        name="plan",
    )(place, in_tree)

    rows = group * tokens
    shares = 2
    part_rows = rows // shares
    whole = lambda *shape: pl.BlockSpec(shape, lambda i: (0,) * len(shape))
    table_specs = [whole(*table.shape) for table in tables]
    columns = pl.BlockSpec((tokens, part_rows // tokens * head_dim), lambda i: (0, i))
    tall = pl.BlockSpec((1, part_rows, head_dim), lambda i: (i // shares, i % shares, 0))
    flat = lambda n: pl.BlockSpec((1, n, part_rows), lambda i: (i // shares, 0, i % shares))
    queries = pl.pallas_call(
        lambda *refs: prep_kernel(blocks, *refs),
        grid=(kv_heads * shares,),
        out_shape=(
            sds((kv_heads, head_dim, rows), BF16),
            sds((kv_heads, rows, head_dim), BF16),
            sds((kv_heads, head_dim, rows), BF16),
            sds((kv_heads, rows, head_dim), BF16),
            sds((kv_heads, 1, rows), F32),
        ),
        in_specs=[smem, *table_specs, whole(1, head_dim), columns, columns, columns],
        out_specs=(flat(head_dim), tall, flat(head_dim), tall, flat(1)),
        compiler_params=params,
        name="prep",
    )(depth, *tables, q_gain_row, q_raw, out_grad, saved_out)

    half = tree_dev // 2

    def attend(h):
        return pl.pallas_call(
            lambda *refs: main_kernel(blocks, block_len, tree_dev, inv_root, h, *refs),
            out_shape=(
                sds((head_dim, rows), F32),
                sds((8, head_dim), F32),
                *[sds((tokens, 2 * head_dim), BF16)] * half,
                sds((half, tokens, 2 * head_dim), BF16),
            ),
            in_specs=[smem] + [vmem] * (10 + tree_dev),
            out_specs=tuple([vmem] * (3 + half)),
            scratch_shapes=[
                pltpu.VMEM((tree_dev, tokens, 2 * head_dim), BF16),
                pltpu.VMEM((tree_dev + 1, tokens, head_dim), BF16),
                pltpu.VMEM((tree_dev + 1, head_dim, tokens), BF16),
                pltpu.VMEM((tree_dev + 1, tokens, head_dim), BF16),
                pltpu.VMEM((tree_dev + 1, 8 * ((blocks + 7) // 8), tokens), F32),
                pltpu.VMEM((tree_dev + 1, tokens, head_dim), F32),
                pltpu.VMEM((tree_dev + 1, tokens, head_dim), F32),
                pltpu.VMEM((tree_dev, group, tokens, tokens), F32),
                pltpu.VMEM((2, group, 8, tokens), F32),
                pltpu.VMEM((tokens, rows), BF16),
                pltpu.VMEM((tokens, rows), BF16),
                pltpu.VMEM((tree_dev, tokens, 2 * head_dim), BF16),
                pltpu.VMEM((tree_dev, tokens, 2 * head_dim), BF16),
            ],
            compiler_params=params,
            cost_estimate=pl.CostEstimate(
                flops=10 * group * tokens * tree_dev * tokens * head_dim,
                bytes_accessed=8 * 1024 * 1024,
                transcendentals=group * tokens * tree_dev * tokens,
            ),
            name="attend",
        )(plan, k_gain_row, *tables, *pieces, *queries)

    dq, terms, counts, k_gain_parts = [], [], [], []
    for h in range(kv_heads):
        dq_here, k_gain_part, *parts, crossed = attend(h)
        dq.append(dq_here)
        k_gain_parts.append(k_gain_part)
        own, *merged = pl.pallas_call(
            merge_kernel,
            out_shape=tuple(
                sds((tokens, 2 * head_dim), F32 if i == 0 else BF16) for i in range(half)
            ),
            in_specs=[vmem] * (half + 1),
            out_specs=tuple([vmem] * half),
            compiler_params=params,
            name="merge",
        )(*parts, tree.across(crossed))
        mine = [own, *tree.back(merged)]
        terms.extend(mine)
        counts.append(len(mine))

    def share_of(kv):
        return lambda i: (0, jnp.clip(i - kv * shares, 0, shares - 1))

    dq_raw, q_gain_part = pl.pallas_call(
        lambda *refs: query_kernel(blocks, inv_root, shares, *refs),
        grid=(kv_heads * shares,),
        out_shape=(sds((tokens, heads * head_dim), BF16), sds((8, head_dim), F32)),
        in_specs=[
            smem,
            *table_specs,
            whole(1, head_dim),
            columns,
            *[pl.BlockSpec((head_dim, part_rows), share_of(kv)) for kv in range(kv_heads)],
        ],
        out_specs=(columns, whole(8, head_dim)),
        compiler_params=params,
        name="query_back",
    )(depth, *tables, q_gain_row, q_raw, *dq)

    gains = jnp.stack([jnp.sum(q_gain_part, 0), jnp.sum(sum(k_gain_parts), 0)])
    everyone = cycle * lax.axis_size("heads")
    gains = jnp.broadcast_to(gains[None], (everyone, *gains.shape))
    gains = lax.all_to_all(gains, ("ctx", "heads"), 0, 0)

    dk_raw, dv, total = pl.pallas_call(
        lambda *refs: key_kernel(blocks, counts, *refs),
        out_shape=(sds(k_raw.shape, BF16), sds(k_raw.shape, BF16), sds(gains.shape[1:], F32)),
        in_specs=[smem] + [vmem] * (7 + len(terms)),
        out_specs=(vmem, vmem, vmem),
        compiler_params=params,
        name="key_back",
    )(depth, *tables, k_gain_row, k_raw, *terms, gains)
    return (dq_raw, dk_raw, dv, total[0], total[1])


def solution(mesh):
    split = P("ctx", "heads")
    return jax.shard_map(
        on_device,
        mesh=mesh,
        in_specs=(split, split, split, split, split, P(), P(), P("ctx", None)),
        out_specs=(split, split, split, P(), P()),
        check_vma=False,
    )
```

```python
import math

import jax
import jax.numpy as jnp
import numpy as np
from jax import lax
from jax.experimental import pallas as pl
from jax.experimental.pallas import tpu as pltpu
from jax.sharding import PartitionSpec as P

ROPE_BASE = 1000000.0
EPS = 1e-06
HIDDEN = -100000.0
VMEM_LIMIT = 56 * 1024 * 1024
F32 = jnp.float32
BF16 = jnp.bfloat16


def rope_rows(starts, head_dim):
    half = head_dim // 2
    frequency = np.exp(
        np.arange(half, dtype=np.float32) * np.float32(-2.0 * math.log(ROPE_BASE) / head_dim)
    ).astype(np.float32)
    angles = np.asarray(starts, np.float32)[:, None] * frequency[None, :]
    cos = np.cos(angles.astype(np.float64)).astype(np.float32)
    sin = np.sin(angles.astype(np.float64)).astype(np.float32)
    return np.concatenate([cos, cos], 1), np.concatenate([-sin, sin], 1)


def block_tables(depth, tables):
    start_cos, start_sin, offset_cos, offset_sin = tables
    cos, sin = start_cos[pl.ds(depth, 1), :], start_sin[pl.ds(depth, 1), :]
    both_cos = cos * offset_cos[...] - sin * offset_sin[...]
    both_sin = sin * offset_cos[...] + cos * offset_sin[...]
    return both_cos, both_sin


def turned(rows, cos, sin):
    return rows * cos + pltpu.roll(rows, rows.shape[-1] // 2, 1) * sin


def turned_back(rows, cos, sin):
    return rows * cos - pltpu.roll(rows, rows.shape[-1] // 2, 1) * sin


def inverse_rms(rows):
    return lax.rsqrt(jnp.mean(rows * rows, -1, keepdims=True) + EPS)


def own_tables(depth_ref, tables, blocks):
    parts = [block_tables(depth_ref[a], tables) for a in range(blocks)]
    return jnp.concatenate([p[0] for p in parts], 0), jnp.concatenate([p[1] for p in parts], 0)


def two_parts(values):
    high = values.astype(BF16)
    return high, (values - high.astype(F32)).astype(BF16)


def row_means(values):
    size = values.shape[-1]
    ones = jnp.ones((size, size), BF16)
    high, low = two_parts(values)
    return (dot_nn(high, ones) + dot_nn(low, ones)) * (1.0 / size)


def sums_in_row(values):
    ones = jnp.ones((8, values.shape[-1]), BF16)
    contract = (((1,), (1,)), ((), ()))
    high, low = two_parts(values)
    sums = lax.dot_general(ones, high, contract, preferred_element_type=F32)
    sums = sums + lax.dot_general(ones, low, contract, preferred_element_type=F32)
    return sums[0:1]


def dot_nn(lhs, rhs):
    return lax.dot_general(lhs, rhs, (((1,), (0,)), ((), ())), preferred_element_type=F32)


def plan_kernel(blocks, tree_dev, place_ref, anc_ref, plan_ref):
    slots = tree_dev * blocks
    place = place_ref[0]
    here = jnp.where(place + 1 == tree_dev, 0, place + 1)
    for row in range(5):
        for i in range(slots):
            plan_ref[row, i] = 0
    count = jnp.int32(blocks)
    steps = [jnp.int32(0)] * blocks
    for b in range(slots):
        bits = jnp.int32(0)
        depth = jnp.int32(0)
        for a in range(blocks):
            hit = anc_ref[a, jnp.minimum(steps[a], slots - 1)] == b
            bits = bits | jnp.where(hit, 1 << a, 0)
            depth = jnp.where(hit, steps[a], depth)
            steps[a] = steps[a] + jnp.where(hit, 1, 0)
        own = place == b // blocks
        slot = jnp.where(own, b % blocks, jnp.minimum(count, slots - 1))
        there = (b // blocks + 1) % tree_dev
        odd = jnp.bitwise_and(here + there, 1)
        gap = jnp.bitwise_xor(here, odd) - there
        gap = jnp.where(gap < 0, gap + tree_dev, gap)
        plan_ref[0, slot] = odd * (tree_dev // 2) + lax.shift_right_logical(gap, 1)
        plan_ref[1, slot] = b % blocks
        plan_ref[2, slot] = depth
        plan_ref[3, slot] = bits
        plan_ref[4, slot] = there
        count = count + jnp.where(own | (bits == 0), 0, 1)
    for i in range(slots):
        plan_ref[5, i] = count


def prep_kernel(blocks, block_len, kv_heads, depth_ref, t0, t1, t2, t3, gain_ref, q_ref, grad_ref, out_ref, *outs):
    tokens = q_ref.shape[0]
    head_dim = gain_ref.shape[1]
    cos, sin = own_tables(depth_ref, (t0, t1, t2, t3), blocks)
    gain = gain_ref[...]
    group = q_ref.shape[1] // head_dim // kv_heads
    for kv in range(kv_heads):
        q_t_ref, q_rot_ref, grad_t_ref, grad_heads_ref, delta_ref = outs[5 * kv:][:5]

        @pl.loop(0, group)
        def _(g):
            cols = pl.ds(pl.multiple_of((kv * group + g) * head_dim, head_dim), head_dim)
            here = pl.ds(pl.multiple_of(g * tokens, tokens), tokens)
            rows = q_ref[:, cols].astype(F32)
            recip = lax.rsqrt(row_means(rows * rows) + EPS)
            rotated = turned(rows * recip * gain, cos, sin).astype(BF16)
            q_rot_ref[here, :] = rotated
            q_t_ref[:, here] = jnp.transpose(rotated)
            grad = grad_ref[:, cols]
            grad_heads_ref[here, :] = grad
            grad_t_ref[:, here] = jnp.transpose(grad)
            delta_ref[:, here] = sums_in_row(grad.astype(F32) * out_ref[:, cols].astype(F32))


def main_kernel(blocks, block_len, tree_dev, inv_root, n_in, *refs):
    plan_ref, gain_ref = refs[:2]
    tables = refs[2:6]
    pieces = refs[6:6 + n_in]
    q_t_ref, q_ref, grad_t_ref, grad_ref, delta_ref = refs[6 + n_in:11 + n_in]
    dq_ref, gain_part_ref = refs[11 + n_in:13 + n_in]
    parts = refs[13 + n_in:13 + n_in + tree_dev]
    raw, keys, keys_t, vals, shown, with_cos, with_sin, expo, mass, w_all, ds_all, found, spread = refs[
        13 + n_in + tree_dev:]
    if n_in == 1:
        raw, source_row = pieces[0], 4
    else:
        source_row = 0
        for piece in range(tree_dev):
            raw[piece] = pieces[piece][...]
    head_dim = gain_ref.shape[1]
    tokens = raw.shape[1]
    group = q_ref.shape[0] // tokens
    count = plan_ref[5, 0]
    chunks = (count + blocks - 1) // blocks
    gain = gain_ref[...]
    query_block = lax.broadcasted_iota(jnp.int32, (1, tokens), 1) // block_len

    def rows_of(start):
        return pl.ds(pl.multiple_of(start * block_len, block_len), block_len)

    def load_chunk(c):
        for j in range(blocks):
            slot = jnp.minimum(c * blocks + j, tree_dev * blocks - 1)
            piece = plan_ref[source_row, slot]
            rows = rows_of(plan_ref[1, slot])
            cos, sin = block_tables(plan_ref[2, slot], tables)
            unit = raw[piece, rows, 0:head_dim].astype(F32)
            unit = unit * inverse_rms(unit)
            here = pl.ds(j * block_len, block_len)
            with_cos[c, here, :] = unit * cos
            with_sin[c, here, :] = pltpu.roll(unit * sin, head_dim // 2, 1)
            keys[c, here, :] = turned(unit * gain, cos, sin).astype(BF16)
            bits = jnp.where(c * blocks + j < count, plan_ref[3, slot], 0)
            row = jnp.zeros((1, tokens), F32)
            for a in range(blocks):
                seen = lax.rem(lax.shift_right_logical(bits, a), 2)
                row = jnp.where((query_block == a) & (seen == 0), HIDDEN, row)
            shown[c, j:j + 1, :] = row
            vals[c, here, :] = raw[piece, rows, head_dim:]
        keys_t[c] = jnp.transpose(keys[c].astype(F32)).astype(BF16)

    def exps(c, g, scores):
        parts = []
        for j in range(blocks):
            here = slice(j * block_len, (j + 1) * block_len)
            parts.append(jnp.exp(scores[here] * inv_root + shown[c, j:j + 1, :]))
        return jnp.concatenate(parts, 0)

    def summed(e):
        return jnp.sum(e.reshape(tokens // 8, 8, tokens), 0)

    key_row = lax.broadcasted_iota(jnp.int32, (tokens, tokens), 0)
    query_col = lax.broadcasted_iota(jnp.int32, (tokens, tokens), 1)

    def cols_of(g):
        return pl.ds(g * tokens, tokens)

    def masses(c, first):
        for g in range(group):
            scores = dot_nn(keys[c], q_t_ref[:, cols_of(g)])
            e = exps(c, g, scores)
            if first:
                e = jnp.where(key_row <= query_col, e, 0.0)
            expo[c, g] = e
            mass[g] = summed(e) if first else mass[g] + summed(e)

    load_chunk(0)
    masses(0, True)
    load_chunk(1)

    @pl.loop(1, chunks)
    def _(c):
        masses(c, False)
        load_chunk(c + 1)

    for g in range(group):
        total = jnp.sum(mass[g], 0, keepdims=True)
        mass[g] = jnp.broadcast_to(1.0 / total, (8, tokens))
    dq_ref[...] = jnp.zeros(dq_ref.shape, F32)
    gain_part_ref[...] = jnp.zeros(gain_part_ref.shape, F32)
    spread[...] = jnp.zeros(spread.shape, BF16)

    @pl.loop(0, chunks)
    def _(c):
        for g in range(group):
            cols = cols_of(g)
            grad_prob = dot_nn(vals[c], grad_t_ref[:, cols])
            weights = expo[c, g] * mass[g, 0:1, :]
            ds_all[:, cols] = (weights * (grad_prob - delta_ref[:, cols])).astype(BF16)
            w_all[:, cols] = weights.astype(BF16)
        dv = dot_nn(w_all[...], grad_ref[...])
        dk = dot_nn(ds_all[...], q_ref[...])
        dq_ref[...] = dq_ref[...] + dot_nn(keys_t[c], ds_all[...])
        dk = dk * inv_root
        found[c, :, 0:head_dim] = dk.astype(BF16)
        found[c, :, head_dim:] = dv.astype(BF16)
        front = jnp.sum((dk * with_cos[c]).reshape(tokens // 8, 8, head_dim), 0)
        back = jnp.sum((dk * with_sin[c]).reshape(tokens // 8, 8, head_dim), 0)
        gain_part_ref[...] = gain_part_ref[...] + front - pltpu.roll(back, head_dim // 2, 1)

    @pl.loop(0, count)
    def _(slot):
        rows = rows_of(lax.rem(slot, blocks))
        spread[plan_ref[0, slot], rows_of(plan_ref[1, slot]), :] = found[slot // blocks, rows, :]

    for piece in range(tree_dev):
        parts[piece][...] = spread[piece]


def query_kernel(blocks, inv_root, depth_ref, t0, t1, t2, t3, gain_ref, q_ref, *refs):
    dq_refs, (out_ref, part_ref) = refs[:-2], refs[-2:]
    tokens = q_ref.shape[0]
    head_dim = gain_ref.shape[1]
    group = dq_refs[0].shape[1] // tokens
    cos, sin = own_tables(depth_ref, (t0, t1, t2, t3), blocks)
    gain = gain_ref[...]
    part_ref[...] = jnp.zeros(part_ref.shape, F32)
    for kv, dq_ref in enumerate(dq_refs):

        @pl.loop(0, group)
        def _(g):
            cols = pl.ds(pl.multiple_of((kv * group + g) * head_dim, head_dim), head_dim)
            rows = q_ref[:, cols].astype(F32)
            recip = lax.rsqrt(row_means(rows * rows) + EPS)
            normed = rows * recip
            dq = jnp.transpose(dq_ref[:, pl.ds(pl.multiple_of(g * tokens, tokens), tokens)])
            scaled_grad = turned_back(dq, cos, sin) * inv_root
            term = scaled_grad * normed
            part_ref[...] = part_ref[...] + jnp.sum(term.reshape(tokens // 8, 8, head_dim), 0)
            out_ref[:, cols] = (recip * (scaled_grad * gain - normed * row_means(term * gain))).astype(BF16)


def key_kernel(blocks, counts, depth_ref, t0, t1, t2, t3, gain_ref, k_ref, *refs):
    sums, (gains_ref, dk_out_ref, dv_out_ref, total_ref) = refs[:-4], refs[-4:]
    total_ref[...] = jnp.sum(gains_ref[...], 0)
    head_dim = gain_ref.shape[1]
    cos, sin = own_tables(depth_ref, (t0, t1, t2, t3), blocks)
    gain = gain_ref[...]
    for head, each in enumerate(counts):
        cols = pl.ds(head * head_dim, head_dim)
        rows = k_ref[:, cols].astype(F32)
        recip = inverse_rms(rows)
        normed = rows * recip
        mine = sums[sum(counts[:head]):][:each]
        both = mine[0][...].astype(F32)
        for other in mine[1:]:
            both = both + other[...].astype(F32)
        grad = turned_back(both[:, 0:head_dim], cos, sin) * gain
        inner = jnp.mean(grad * normed, -1, keepdims=True)
        dk_out_ref[:, cols] = (recip * (grad - normed * inner)).astype(BF16)
        dv_out_ref[:, cols] = both[:, head_dim:].astype(BF16)


class Tree:
    def __init__(self, size, cycle):
        self.size, self.cycle = size, cycle

    def order(self, index):
        return (index - 1) % self.size

    def send(self, value, target, wanted):
        pairs = []
        for tree in range(self.cycle // self.size):
            for index in range(self.size):
                if wanted(index):
                    ends = [(tree * self.size + 1 + self.order(i)) % self.cycle for i in (index, target(index))]
                    pairs.append(tuple(ends))
        return lax.ppermute(value, "ctx", pairs)

    def after(self, *pair):
        return self.order(pair[1] % self.size) > self.order(pair[0] % self.size)

    def gather(self, own):
        size, after = self.size, self.after
        pieces = [own]
        for odd in range(2):
            for step in range(0, size, 2):
                if odd or step:
                    there = lambda i: (i + step) % size ^ odd
                    pieces.append(self.send(own, there, lambda i: after(i, there(i))))
        return pieces

    def collect(self, parts):
        size, after = self.size, self.after
        terms = [parts[0]]
        for odd in range(2):
            for step in range(0, size, 2):
                if odd or step:
                    there = lambda i: ((i ^ odd) - step) % size
                    part = parts[odd * size // 2 + step // 2]
                    terms.append(self.send(part, there, lambda i: after(there(i), i)))
        return terms


def on_device(q_raw, k_raw, values, saved_out, out_grad, q_gain, k_gain, ancestors):
    tokens = q_raw.shape[0]
    head_dim = q_gain.shape[0]
    kv_heads = k_raw.shape[1] // head_dim
    heads = q_raw.shape[1] // head_dim
    group = heads // kv_heads
    blocks = ancestors.shape[0]
    tree_blocks = ancestors.shape[1]
    block_len = tokens // blocks
    tree_dev = tree_blocks // blocks
    cycle = lax.axis_size("ctx")
    inv_root = 1.0 / math.sqrt(head_dim)
    tree = Tree(tree_dev, cycle)
    place = (lax.axis_index("ctx") - 1 + cycle) % cycle % tree_dev
    place = place.reshape(1).astype(jnp.int32)

    depth = jnp.sum((ancestors >= 0).astype(jnp.int32), 1) - 1
    total_blocks = blocks * cycle
    in_tree = jnp.where(
        ancestors >= 0, (ancestors - blocks + total_blocks) % total_blocks % tree_blocks, -1
    )
    tables = [
        jnp.asarray(table)
        for starts in (range(0, tree_blocks * block_len, block_len), range(block_len))
        for table in rope_rows(starts, head_dim)
    ]
    q_gain_row, k_gain_row = q_gain.reshape(1, head_dim), k_gain.reshape(1, head_dim)

    groups = None
    if cycle != tree_dev:
        groups = [
            [(start + 1 + tree.order(index)) % cycle for index in range(tree_dev)]
            for start in range(0, cycle, tree_dev)
        ]
    pieces = []
    for h in range(kv_heads):
        cols = slice(h * head_dim, (h + 1) * head_dim)
        own = jnp.concatenate([k_raw[:, cols], values[:, cols]], 1)
        if h == 0:
            pieces.append(tree.gather(own))
        else:
            pieces.append([lax.all_gather(own, "ctx", axis_index_groups=groups)])

    params = pltpu.CompilerParams(vmem_limit_bytes=VMEM_LIMIT)
    smem = pl.BlockSpec(memory_space=pltpu.SMEM)
    vmem = pl.BlockSpec(memory_space=pltpu.VMEM)
    sds = jax.ShapeDtypeStruct

    plan = pl.pallas_call(
        lambda *refs: plan_kernel(blocks, tree_dev, *refs),
        out_shape=sds((6, tree_blocks), jnp.int32),
        in_specs=[smem, smem],
        out_specs=smem,
        name="plan",
    )(place, in_tree)

    rows = group * tokens
    queries = pl.pallas_call(
        lambda *refs: prep_kernel(blocks, block_len, kv_heads, *refs),
        out_shape=tuple(
            [
                sds((head_dim, rows), BF16),
                sds((rows, head_dim), BF16),
                sds((head_dim, rows), BF16),
                sds((rows, head_dim), BF16),
                sds((1, rows), F32),
            ]
            * kv_heads
        ),
        in_specs=[smem] + [vmem] * 8,
        out_specs=tuple([vmem] * (5 * kv_heads)),
        compiler_params=params,
        name="prep",
    )(depth, *tables, q_gain_row, q_raw, out_grad, saved_out)

    def attend(h):
        return pl.pallas_call(
            lambda *refs: main_kernel(blocks, block_len, tree_dev, inv_root, len(pieces[h]), *refs),
            out_shape=(
                sds((head_dim, rows), F32),
                sds((8, head_dim), F32),
                *[sds((tokens, 2 * head_dim), BF16)] * tree_dev,
            ),
            in_specs=[smem] + [vmem] * (10 + len(pieces[h])),
            out_specs=tuple([vmem] * (2 + tree_dev)),
            scratch_shapes=[
                pltpu.VMEM((tree_dev, tokens, 2 * head_dim), BF16),
                pltpu.VMEM((tree_dev + 1, tokens, head_dim), BF16),
                pltpu.VMEM((tree_dev + 1, head_dim, tokens), BF16),
                pltpu.VMEM((tree_dev + 1, tokens, head_dim), BF16),
                pltpu.VMEM((tree_dev + 1, 8 * ((blocks + 7) // 8), tokens), F32),
                pltpu.VMEM((tree_dev + 1, tokens, head_dim), F32),
                pltpu.VMEM((tree_dev + 1, tokens, head_dim), F32),
                pltpu.VMEM((tree_dev, group, tokens, tokens), F32),
                pltpu.VMEM((group, 8, tokens), F32),
                pltpu.VMEM((tokens, rows), BF16),
                pltpu.VMEM((tokens, rows), BF16),
                pltpu.VMEM((tree_dev, tokens, 2 * head_dim), BF16),
                pltpu.VMEM((tree_dev, tokens, 2 * head_dim), BF16),
            ],
            compiler_params=params,
            cost_estimate=pl.CostEstimate(
                flops=10 * group * tokens * tree_dev * tokens * head_dim,
                bytes_accessed=8 * 1024 * 1024,
                transcendentals=group * tokens * tree_dev * tokens,
            ),
            name="attend",
        )(plan, k_gain_row, *tables, *pieces[h], *queries[5 * h:5 * h + 5])

    dq, terms, counts, k_gain_parts = [], [], [], []
    for h in range(kv_heads):
        dq_here, k_gain_part, *parts = attend(h)
        dq.append(dq_here)
        k_gain_parts.append(k_gain_part)
        mine = tree.collect(parts)
        terms.extend(mine)
        counts.append(len(mine))

    dq_raw, q_gain_part = pl.pallas_call(
        lambda *refs: query_kernel(blocks, inv_root, *refs),
        out_shape=(sds((tokens, heads * head_dim), BF16), sds((8, head_dim), F32)),
        in_specs=[smem] + [vmem] * (6 + kv_heads),
        out_specs=(vmem, vmem),
        compiler_params=params,
        name="query_back",
    )(depth, *tables, q_gain_row, q_raw, *dq)

    gains = jnp.stack([jnp.sum(q_gain_part, 0), jnp.sum(sum(k_gain_parts), 0)])
    everyone = cycle * lax.axis_size("heads")
    gains = jnp.broadcast_to(gains[None], (everyone, *gains.shape))
    gains = lax.all_to_all(gains, ("ctx", "heads"), 0, 0)

    dk_raw, dv, total = pl.pallas_call(
        lambda *refs: key_kernel(blocks, counts, *refs),
        out_shape=(sds(k_raw.shape, BF16), sds(k_raw.shape, BF16), sds(gains.shape[1:], F32)),
        in_specs=[smem] + [vmem] * (7 + len(terms)),
        out_specs=(vmem, vmem, vmem),
        compiler_params=params,
        name="key_back",
    )(depth, *tables, k_gain_row, k_raw, *terms, gains)
    return (dq_raw, dk_raw, dv, total[0], total[1])


def solution(mesh):
    split = P("ctx", "heads")
    return jax.shard_map(
        on_device,
        mesh=mesh,
        in_specs=(split, split, split, split, split, P(), P(), P("ctx", None)),
        out_specs=(split, split, split, P(), P()),
        check_vma=False,
    )
```

```python
import math

import jax
import jax.numpy as jnp
import numpy as np
from jax import lax
from jax.experimental import pallas as pl
from jax.experimental.pallas import tpu as pltpu
from jax.sharding import PartitionSpec as P

ROPE_BASE = 1000000.0
EPS = 1e-06
HIDDEN = -100000.0
VMEM_LIMIT = 56 * 1024 * 1024
F32 = jnp.float32
BF16 = jnp.bfloat16


def rope_rows(starts, head_dim):
    half = head_dim // 2
    frequency = np.exp(
        np.arange(half, dtype=np.float32) * np.float32(-2.0 * math.log(ROPE_BASE) / head_dim)
    ).astype(np.float32)
    angles = np.asarray(starts, np.float32)[:, None] * frequency[None, :]
    cos = np.cos(angles.astype(np.float64)).astype(np.float32)
    sin = np.sin(angles.astype(np.float64)).astype(np.float32)
    return np.concatenate([cos, cos], 1), np.concatenate([-sin, sin], 1)


def block_tables(depth, tables):
    start_cos, start_sin, offset_cos, offset_sin = tables
    cos, sin = start_cos[pl.ds(depth, 1), :], start_sin[pl.ds(depth, 1), :]
    both_cos = cos * offset_cos[...] - sin * offset_sin[...]
    both_sin = sin * offset_cos[...] + cos * offset_sin[...]
    return both_cos, both_sin


def turned(rows, cos, sin):
    return rows * cos + pltpu.roll(rows, rows.shape[-1] // 2, 1) * sin


def turned_back(rows, cos, sin):
    return rows * cos - pltpu.roll(rows, rows.shape[-1] // 2, 1) * sin


def inverse_rms(rows):
    return lax.rsqrt(jnp.mean(rows * rows, -1, keepdims=True) + EPS)


def own_tables(depth_ref, tables, blocks):
    parts = [block_tables(depth_ref[a], tables) for a in range(blocks)]
    return jnp.concatenate([p[0] for p in parts], 0), jnp.concatenate([p[1] for p in parts], 0)


def dot_nn(lhs, rhs):
    return lax.dot_general(lhs, rhs, (((1,), (0,)), ((), ())), preferred_element_type=F32)


def plan_kernel(blocks, tree_dev, place_ref, anc_ref, plan_ref):
    slots = tree_dev * blocks
    place = place_ref[0]
    here = jnp.where(place + 1 == tree_dev, 0, place + 1)
    for row in range(4):
        for i in range(slots):
            plan_ref[row, i] = 0
    count = jnp.int32(blocks)
    steps = [jnp.int32(0)] * blocks
    for b in range(slots):
        bits = jnp.int32(0)
        depth = jnp.int32(0)
        for a in range(blocks):
            hit = anc_ref[a, jnp.minimum(steps[a], slots - 1)] == b
            bits = bits | jnp.where(hit, 1 << a, 0)
            depth = jnp.where(hit, steps[a], depth)
            steps[a] = steps[a] + jnp.where(hit, 1, 0)
        own = place == b // blocks
        slot = jnp.where(own, b % blocks, jnp.minimum(count, slots - 1))
        there = (b // blocks + 1) % tree_dev
        odd = jnp.bitwise_and(here + there, 1)
        gap = jnp.bitwise_xor(here, odd) - there
        gap = jnp.where(gap < 0, gap + tree_dev, gap)
        plan_ref[0, slot] = odd * (tree_dev // 2) + lax.shift_right_logical(gap, 1)
        plan_ref[1, slot] = b % blocks
        plan_ref[2, slot] = depth
        plan_ref[3, slot] = bits
        count = count + jnp.where(own | (bits == 0), 0, 1)
    for i in range(slots):
        plan_ref[4, i] = count


def prep_kernel(blocks, block_len, kv_heads, depth_ref, t0, t1, t2, t3, gain_ref, q_ref, grad_ref, out_ref, *outs):
    tokens = q_ref.shape[0]
    head_dim = gain_ref.shape[1]
    cos, sin = own_tables(depth_ref, (t0, t1, t2, t3), blocks)
    gain = gain_ref[...]
    group = q_ref.shape[1] // head_dim // kv_heads
    for head in range(group * kv_heads):
        g = head % group
        q_t_ref, q_rot_ref, grad_t_ref, grad_heads_ref, delta_ref = outs[5 * (head // group):][:5]
        cols = pl.ds(head * head_dim, head_dim)
        here = pl.ds(g * tokens, tokens)
        rows = q_ref[:, cols].astype(F32)
        rotated = turned(rows * inverse_rms(rows) * gain, cos, sin)
        q_rot_ref[here, :] = rotated.astype(BF16)
        q_t_ref[:, here] = jnp.transpose(rotated).astype(BF16)
        grad = grad_ref[:, cols]
        grad_heads_ref[here, :] = grad
        grad_rows = jnp.transpose(grad.astype(F32))
        grad_t_ref[:, here] = grad_rows.astype(BF16)
        product = grad_rows * jnp.transpose(out_ref[:, cols].astype(F32))
        delta_ref[:, here] = jnp.sum(product, 0, keepdims=True)


def main_kernel(blocks, block_len, tree_dev, inv_root, head, *refs):
    plan_ref, gain_ref = refs[:2]
    tables = refs[2:6]
    pieces = refs[6:6 + tree_dev]
    q_t_ref, q_ref, grad_t_ref, grad_ref, delta_ref = refs[6 + tree_dev:11 + tree_dev]
    dq_ref, gain_part_ref = refs[11 + tree_dev:13 + tree_dev]
    parts = refs[13 + tree_dev:13 + 2 * tree_dev]
    raw, keys, keys_t, vals, shown, with_cos, with_sin, expo, mass, w_all, ds_all, found, spread = refs[
        13 + 2 * tree_dev:]
    head_dim = gain_ref.shape[1]
    tokens = raw.shape[1]
    group = q_ref.shape[0] // tokens
    count = plan_ref[4, 0]
    chunks = (count + blocks - 1) // blocks
    gain = gain_ref[...]
    kv_heads = pieces[0].shape[1] // (2 * head_dim)
    for piece in range(tree_dev):
        raw[piece, :, 0:head_dim] = pieces[piece][:, head * head_dim:(head + 1) * head_dim]
        raw[piece, :, head_dim:] = pieces[piece][:, (kv_heads + head) * head_dim:(kv_heads + head + 1) * head_dim]
    query_block = lax.broadcasted_iota(jnp.int32, (1, tokens), 1) // block_len

    def rows_of(start):
        return pl.ds(pl.multiple_of(start * block_len, block_len), block_len)

    def load_chunk(c):
        for j in range(blocks):
            slot = jnp.minimum(c * blocks + j, tree_dev * blocks - 1)
            piece = plan_ref[0, slot]
            rows = rows_of(plan_ref[1, slot])
            cos, sin = block_tables(plan_ref[2, slot], tables)
            unit = raw[piece, rows, 0:head_dim].astype(F32)
            unit = unit * inverse_rms(unit)
            here = pl.ds(j * block_len, block_len)
            with_cos[c, here, :] = unit * cos
            with_sin[c, here, :] = pltpu.roll(unit * sin, head_dim // 2, 1)
            keys[c, here, :] = turned(unit * gain, cos, sin).astype(BF16)
            bits = jnp.where(c * blocks + j < count, plan_ref[3, slot], 0)
            row = jnp.zeros((1, tokens), F32)
            for a in range(blocks):
                seen = lax.rem(lax.shift_right_logical(bits, a), 2)
                row = jnp.where((query_block == a) & (seen == 0), HIDDEN, row)
            shown[c, j:j + 1, :] = row
            vals[c, here, :] = raw[piece, rows, head_dim:]
        keys_t[c] = jnp.transpose(keys[c].astype(F32)).astype(BF16)

    def exps(c, g, scores):
        parts = []
        for j in range(blocks):
            here = slice(j * block_len, (j + 1) * block_len)
            parts.append(jnp.exp(scores[here] * inv_root + shown[c, j:j + 1, :]))
        return jnp.concatenate(parts, 0)

    def summed(e):
        return jnp.sum(e.reshape(tokens // 8, 8, tokens), 0)

    key_row = lax.broadcasted_iota(jnp.int32, (tokens, tokens), 0)
    query_col = lax.broadcasted_iota(jnp.int32, (tokens, tokens), 1)

    def cols_of(g):
        return pl.ds(g * tokens, tokens)

    def masses(c, first):
        for g in range(group):
            scores = dot_nn(keys[c], q_t_ref[:, cols_of(g)])
            e = exps(c, g, scores)
            if first:
                e = jnp.where(key_row <= query_col, e, 0.0)
            expo[c, g] = e
            mass[g] = summed(e) if first else mass[g] + summed(e)

    load_chunk(0)
    masses(0, True)
    load_chunk(1)

    @pl.loop(1, chunks)
    def _(c):
        masses(c, False)
        load_chunk(c + 1)

    for g in range(group):
        total = jnp.sum(mass[g], 0, keepdims=True)
        mass[g] = jnp.broadcast_to(1.0 / total, (8, tokens))
    dq_ref[...] = jnp.zeros(dq_ref.shape, F32)
    gain_part_ref[...] = jnp.zeros(gain_part_ref.shape, F32)
    spread[...] = jnp.zeros(spread.shape, BF16)

    @pl.loop(0, chunks)
    def _(c):
        for g in range(group):
            cols = cols_of(g)
            grad_prob = dot_nn(vals[c], grad_t_ref[:, cols])
            weights = expo[c, g] * mass[g, 0:1, :]
            ds_all[:, cols] = (weights * (grad_prob - delta_ref[:, cols])).astype(BF16)
            w_all[:, cols] = weights.astype(BF16)
        dv = dot_nn(w_all[...], grad_ref[...])
        dk = dot_nn(ds_all[...], q_ref[...])
        dq_ref[...] = dq_ref[...] + dot_nn(keys_t[c], ds_all[...])
        dk = dk * inv_root
        found[c, :, 0:head_dim] = dk.astype(BF16)
        found[c, :, head_dim:] = dv.astype(BF16)
        front = jnp.sum((dk * with_cos[c]).reshape(tokens // 8, 8, head_dim), 0)
        back = jnp.sum((dk * with_sin[c]).reshape(tokens // 8, 8, head_dim), 0)
        gain_part_ref[...] = gain_part_ref[...] + front - pltpu.roll(back, head_dim // 2, 1)

    @pl.loop(0, count)
    def _(slot):
        rows = rows_of(lax.rem(slot, blocks))
        spread[plan_ref[0, slot], rows_of(plan_ref[1, slot]), :] = found[slot // blocks, rows, :]

    for piece in range(tree_dev):
        parts[piece][...] = spread[piece]


def query_kernel(blocks, inv_root, depth_ref, t0, t1, t2, t3, gain_ref, q_ref, *refs):
    dq_refs, (out_ref, part_ref) = refs[:-2], refs[-2:]
    tokens = q_ref.shape[0]
    head_dim = gain_ref.shape[1]
    group = dq_refs[0].shape[1] // tokens
    cos, sin = own_tables(depth_ref, (t0, t1, t2, t3), blocks)
    gain = gain_ref[...]
    part = jnp.zeros((8, head_dim), F32)
    for head in range(group * len(dq_refs)):
        cols = pl.ds(head * head_dim, head_dim)
        rows = q_ref[:, cols].astype(F32)
        recip = inverse_rms(rows)
        normed = rows * recip
        dq = jnp.transpose(dq_refs[head // group][:, pl.ds(head % group * tokens, tokens)])
        scaled_grad = turned_back(dq, cos, sin) * inv_root
        term = scaled_grad * normed
        part = part + jnp.sum(term.reshape(tokens // 8, 8, head_dim), 0)
        inner = jnp.mean(term * gain, -1, keepdims=True)
        out_ref[:, cols] = (recip * (scaled_grad * gain - normed * inner)).astype(BF16)
    part_ref[...] = part


def key_kernel(blocks, counts, depth_ref, t0, t1, t2, t3, gain_ref, k_ref, *refs):
    sums, (gains_ref, dk_out_ref, dv_out_ref, total_ref) = refs[:-4], refs[-4:]
    total_ref[...] = jnp.sum(gains_ref[...], 0)
    head_dim = gain_ref.shape[1]
    cos, sin = own_tables(depth_ref, (t0, t1, t2, t3), blocks)
    gain = gain_ref[...]
    for head, each in enumerate(counts):
        cols = pl.ds(head * head_dim, head_dim)
        rows = k_ref[:, cols].astype(F32)
        recip = inverse_rms(rows)
        normed = rows * recip
        mine = sums[sum(counts[:head]):][:each]
        both = mine[0][...].astype(F32)
        for other in mine[1:]:
            both = both + other[...].astype(F32)
        grad = turned_back(both[:, 0:head_dim], cos, sin) * gain
        inner = jnp.mean(grad * normed, -1, keepdims=True)
        dk_out_ref[:, cols] = (recip * (grad - normed * inner)).astype(BF16)
        dv_out_ref[:, cols] = both[:, head_dim:].astype(BF16)


class Tree:
    def __init__(self, size, cycle):
        self.size, self.cycle = size, cycle

    def order(self, index):
        return (index - 1) % self.size

    def send(self, value, target, wanted):
        pairs = []
        for tree in range(self.cycle // self.size):
            for index in range(self.size):
                if wanted(index):
                    ends = [(tree * self.size + 1 + self.order(i)) % self.cycle for i in (index, target(index))]
                    pairs.append(tuple(ends))
        return lax.ppermute(value, "ctx", pairs)

    def after(self, *pair):
        return self.order(pair[1] % self.size) > self.order(pair[0] % self.size)

    def gather(self, own):
        size, after = self.size, self.after
        pieces = [own]
        for odd in range(2):
            for step in range(0, size, 2):
                if odd or step:
                    there = lambda i: (i + step) % size ^ odd
                    pieces.append(self.send(own, there, lambda i: after(i, there(i))))
        return pieces

    def collect(self, parts):
        size, after = self.size, self.after
        terms = [parts[0]]
        for odd in range(2):
            for step in range(0, size, 2):
                if odd or step:
                    there = lambda i: ((i ^ odd) - step) % size
                    part = parts[odd * size // 2 + step // 2]
                    terms.append(self.send(part, there, lambda i: after(there(i), i)))
        return terms


def on_device(q_raw, k_raw, values, saved_out, out_grad, q_gain, k_gain, ancestors):
    tokens = q_raw.shape[0]
    head_dim = q_gain.shape[0]
    kv_heads = k_raw.shape[1] // head_dim
    heads = q_raw.shape[1] // head_dim
    group = heads // kv_heads
    blocks = ancestors.shape[0]
    tree_blocks = ancestors.shape[1]
    block_len = tokens // blocks
    tree_dev = tree_blocks // blocks
    cycle = lax.axis_size("ctx")
    inv_root = 1.0 / math.sqrt(head_dim)
    tree = Tree(tree_dev, cycle)
    place = (lax.axis_index("ctx") - 1 + cycle) % cycle % tree_dev
    place = place.reshape(1).astype(jnp.int32)

    depth = jnp.sum((ancestors >= 0).astype(jnp.int32), 1) - 1
    total_blocks = blocks * cycle
    in_tree = jnp.where(
        ancestors >= 0, (ancestors - blocks + total_blocks) % total_blocks % tree_blocks, -1
    )
    tables = [
        jnp.asarray(table)
        for starts in (range(0, tree_blocks * block_len, block_len), range(block_len))
        for table in rope_rows(starts, head_dim)
    ]
    q_gain_row, k_gain_row = q_gain.reshape(1, head_dim), k_gain.reshape(1, head_dim)

    pieces = tree.gather(jnp.concatenate([k_raw, values], 1))

    params = pltpu.CompilerParams(vmem_limit_bytes=VMEM_LIMIT)
    smem = pl.BlockSpec(memory_space=pltpu.SMEM)
    vmem = pl.BlockSpec(memory_space=pltpu.VMEM)
    sds = jax.ShapeDtypeStruct

    plan = pl.pallas_call(
        lambda *refs: plan_kernel(blocks, tree_dev, *refs),
        out_shape=sds((5, tree_blocks), jnp.int32),
        in_specs=[smem, smem],
        out_specs=smem,
        name="plan",
    )(place, in_tree)

    rows = group * tokens
    queries = pl.pallas_call(
        lambda *refs: prep_kernel(blocks, block_len, kv_heads, *refs),
        out_shape=tuple(
            [
                sds((head_dim, rows), BF16),
                sds((rows, head_dim), BF16),
                sds((head_dim, rows), BF16),
                sds((rows, head_dim), BF16),
                sds((1, rows), F32),
            ]
            * kv_heads
        ),
        in_specs=[smem] + [vmem] * 8,
        out_specs=tuple([vmem] * (5 * kv_heads)),
        compiler_params=params,
        name="prep",
    )(depth, *tables, q_gain_row, q_raw, out_grad, saved_out)

    def attend(h):
        return pl.pallas_call(
            lambda *refs: main_kernel(blocks, block_len, tree_dev, inv_root, h, *refs),
            out_shape=(
                sds((head_dim, rows), F32),
                sds((8, head_dim), F32),
                *[sds((tokens, 2 * head_dim), BF16)] * tree_dev,
            ),
            in_specs=[smem] + [vmem] * (10 + tree_dev),
            out_specs=tuple([vmem] * (2 + tree_dev)),
            scratch_shapes=[
                pltpu.VMEM((tree_dev, tokens, 2 * head_dim), BF16),
                pltpu.VMEM((tree_dev + 1, tokens, head_dim), BF16),
                pltpu.VMEM((tree_dev + 1, head_dim, tokens), BF16),
                pltpu.VMEM((tree_dev + 1, tokens, head_dim), BF16),
                pltpu.VMEM((tree_dev + 1, 8 * ((blocks + 7) // 8), tokens), F32),
                pltpu.VMEM((tree_dev + 1, tokens, head_dim), F32),
                pltpu.VMEM((tree_dev + 1, tokens, head_dim), F32),
                pltpu.VMEM((tree_dev, group, tokens, tokens), F32),
                pltpu.VMEM((group, 8, tokens), F32),
                pltpu.VMEM((tokens, rows), BF16),
                pltpu.VMEM((tokens, rows), BF16),
                pltpu.VMEM((tree_dev, tokens, 2 * head_dim), BF16),
                pltpu.VMEM((tree_dev, tokens, 2 * head_dim), BF16),
            ],
            compiler_params=params,
            cost_estimate=pl.CostEstimate(
                flops=10 * group * tokens * tree_dev * tokens * head_dim,
                bytes_accessed=8 * 1024 * 1024,
                transcendentals=group * tokens * tree_dev * tokens,
            ),
            name="attend",
        )(plan, k_gain_row, *tables, *pieces, *queries[5 * h:5 * h + 5])

    dq, terms, counts, k_gain_parts = [], [], [], []
    for h in range(kv_heads):
        dq_here, k_gain_part, *parts = attend(h)
        dq.append(dq_here)
        k_gain_parts.append(k_gain_part)
        mine = tree.collect(parts)
        terms.extend(mine)
        counts.append(len(mine))

    dq_raw, q_gain_part = pl.pallas_call(
        lambda *refs: query_kernel(blocks, inv_root, *refs),
        out_shape=(sds((tokens, heads * head_dim), BF16), sds((8, head_dim), F32)),
        in_specs=[smem] + [vmem] * (6 + kv_heads),
        out_specs=(vmem, vmem),
        compiler_params=params,
        name="query_back",
    )(depth, *tables, q_gain_row, q_raw, *dq)

    gains = jnp.stack([jnp.sum(q_gain_part, 0), jnp.sum(sum(k_gain_parts), 0)])
    everyone = cycle * lax.axis_size("heads")
    gains = jnp.broadcast_to(gains[None], (everyone, *gains.shape))
    gains = lax.all_to_all(gains, ("ctx", "heads"), 0, 0)

    dk_raw, dv, total = pl.pallas_call(
        lambda *refs: key_kernel(blocks, counts, *refs),
        out_shape=(sds(k_raw.shape, BF16), sds(k_raw.shape, BF16), sds(gains.shape[1:], F32)),
        in_specs=[smem] + [vmem] * (7 + len(terms)),
        out_specs=(vmem, vmem, vmem),
        compiler_params=params,
        name="key_back",
    )(depth, *tables, k_gain_row, k_raw, *terms, gains)
    return (dq_raw, dk_raw, dv, total[0], total[1])


def solution(mesh):
    split = P("ctx", "heads")
    return jax.shard_map(
        on_device,
        mesh=mesh,
        in_specs=(split, split, split, split, split, P(), P(), P("ctx", None)),
        out_specs=(split, split, split, P(), P()),
        check_vma=False,
    )
```

```python
import math

import jax
import jax.numpy as jnp
import numpy as np
from jax import lax
from jax.experimental import pallas as pl
from jax.experimental.pallas import tpu as pltpu
from jax.sharding import PartitionSpec as P

ROPE_BASE = 1000000.0
EPS = 1e-06
HIDDEN = -100000.0
VMEM_LIMIT = 56 * 1024 * 1024
F32 = jnp.float32
BF16 = jnp.bfloat16


def rope_rows(starts, head_dim):
    half = head_dim // 2
    frequency = np.exp(
        np.arange(half, dtype=np.float32) * np.float32(-2.0 * math.log(ROPE_BASE) / head_dim)
    ).astype(np.float32)
    angles = np.asarray(starts, np.float32)[:, None] * frequency[None, :]
    cos = np.cos(angles.astype(np.float64)).astype(np.float32)
    sin = np.sin(angles.astype(np.float64)).astype(np.float32)
    return np.concatenate([cos, cos], 1), np.concatenate([-sin, sin], 1)


def block_tables(depth, tables):
    start_cos, start_sin, offset_cos, offset_sin = tables
    cos, sin = start_cos[pl.ds(depth, 1), :], start_sin[pl.ds(depth, 1), :]
    both_cos = cos * offset_cos[...] - sin * offset_sin[...]
    both_sin = sin * offset_cos[...] + cos * offset_sin[...]
    return both_cos, both_sin


def turned(rows, cos, sin):
    return rows * cos + pltpu.roll(rows, rows.shape[-1] // 2, 1) * sin


def turned_back(rows, cos, sin):
    return rows * cos - pltpu.roll(rows, rows.shape[-1] // 2, 1) * sin


def inverse_rms(rows):
    return lax.rsqrt(jnp.mean(rows * rows, -1, keepdims=True) + EPS)


def own_tables(depth_ref, tables, blocks):
    parts = [block_tables(depth_ref[a], tables) for a in range(blocks)]
    return jnp.concatenate([p[0] for p in parts], 0), jnp.concatenate([p[1] for p in parts], 0)


def dot_nn(lhs, rhs):
    return lax.dot_general(lhs, rhs, (((1,), (0,)), ((), ())), preferred_element_type=F32)


def plan_kernel(blocks, tree_dev, place_ref, anc_ref, plan_ref):
    slots = tree_dev * blocks
    place = place_ref[0]
    here = jnp.where(place + 1 == tree_dev, 0, place + 1)
    for row in range(4):
        for i in range(slots):
            plan_ref[row, i] = 0
    count = jnp.int32(blocks)
    steps = [jnp.int32(0)] * blocks
    for b in range(slots):
        bits = jnp.int32(0)
        depth = jnp.int32(0)
        for a in range(blocks):
            hit = anc_ref[a, jnp.minimum(steps[a], slots - 1)] == b
            bits = bits | jnp.where(hit, 1 << a, 0)
            depth = jnp.where(hit, steps[a], depth)
            steps[a] = steps[a] + jnp.where(hit, 1, 0)
        own = place == b // blocks
        slot = jnp.where(own, b % blocks, jnp.minimum(count, slots - 1))
        there = (b // blocks + 1) % tree_dev
        odd = jnp.bitwise_and(here + there, 1)
        gap = jnp.bitwise_xor(here, odd) - there
        gap = jnp.where(gap < 0, gap + tree_dev, gap)
        plan_ref[0, slot] = odd * (tree_dev // 2) + lax.shift_right_logical(gap, 1)
        plan_ref[1, slot] = b % blocks
        plan_ref[2, slot] = depth
        plan_ref[3, slot] = bits
        count = count + jnp.where(own | (bits == 0), 0, 1)
    for i in range(slots):
        plan_ref[4, i] = count


def prep_kernel(blocks, block_len, kv_heads, depth_ref, t0, t1, t2, t3, gain_ref, q_ref, grad_ref, out_ref, *outs):
    tokens = q_ref.shape[0]
    head_dim = gain_ref.shape[1]
    cos, sin = own_tables(depth_ref, (t0, t1, t2, t3), blocks)
    gain = gain_ref[...]
    group = q_ref.shape[1] // head_dim // kv_heads
    for head in range(group * kv_heads):
        g = head % group
        q_t_ref, q_rot_ref, grad_t_ref, grad_heads_ref, delta_ref = outs[5 * (head // group):][:5]
        cols = pl.ds(head * head_dim, head_dim)
        here = pl.ds(g * tokens, tokens)
        rows = q_ref[:, cols].astype(F32)
        rotated = turned(rows * inverse_rms(rows) * gain, cos, sin)
        q_rot_ref[here, :] = rotated.astype(BF16)
        q_t_ref[:, here] = jnp.transpose(rotated).astype(BF16)
        grad = grad_ref[:, cols]
        grad_heads_ref[here, :] = grad
        grad_rows = jnp.transpose(grad.astype(F32))
        grad_t_ref[:, here] = grad_rows.astype(BF16)
        product = grad_rows * jnp.transpose(out_ref[:, cols].astype(F32))
        delta_ref[:, here] = jnp.sum(product, 0, keepdims=True)


def main_kernel(blocks, block_len, tree_dev, inv_root, head, last, *refs):
    plan_ref, gain_ref = refs[:2]
    tables = refs[2:6]
    half = tree_dev // 2
    pieces, crossed_ref = refs[6:7 + half], refs[7 + half]
    q_t_ref, q_ref, grad_t_ref, grad_ref, delta_ref = refs[8 + half:13 + half]
    dq_ref, gain_part_ref = refs[13 + half:15 + half]
    parts = refs[15 + half:15 + 2 * half + last]
    crossed_part, raw, keys, keys_t, vals, shown, with_cos, with_sin, expo, mass, w_all, ds_all, found, spread = refs[
        15 + 2 * half + last:]
    head_dim = gain_ref.shape[1]
    tokens = raw.shape[1]
    group = q_ref.shape[0] // tokens
    count = plan_ref[4, 0]
    chunks = (count + blocks - 1) // blocks
    gain = gain_ref[...]
    kv_heads = pieces[0].shape[1] // (2 * head_dim)
    for piece in range(half + 1):
        raw[piece, :, 0:head_dim] = pieces[piece][:, head * head_dim:(head + 1) * head_dim]
        raw[piece, :, head_dim:] = pieces[piece][:, (kv_heads + head) * head_dim:(kv_heads + head + 1) * head_dim]
    raw[half + 1:] = crossed_ref[...]
    query_block = lax.broadcasted_iota(jnp.int32, (1, tokens), 1) // block_len

    def rows_of(start):
        return pl.ds(pl.multiple_of(start * block_len, block_len), block_len)

    def load_chunk(c):
        for j in range(blocks):
            slot = jnp.minimum(c * blocks + j, tree_dev * blocks - 1)
            piece = plan_ref[0, slot]
            rows = rows_of(plan_ref[1, slot])
            cos, sin = block_tables(plan_ref[2, slot], tables)
            unit = raw[piece, rows, 0:head_dim].astype(F32)
            unit = unit * inverse_rms(unit)
            here = pl.ds(j * block_len, block_len)
            with_cos[c, here, :] = unit * cos
            with_sin[c, here, :] = pltpu.roll(unit * sin, head_dim // 2, 1)
            keys[c, here, :] = turned(unit * gain, cos, sin).astype(BF16)
            bits = jnp.where(c * blocks + j < count, plan_ref[3, slot], 0)
            row = jnp.zeros((1, tokens), F32)
            for a in range(blocks):
                seen = lax.rem(lax.shift_right_logical(bits, a), 2)
                row = jnp.where((query_block == a) & (seen == 0), HIDDEN, row)
            shown[c, j:j + 1, :] = row
            vals[c, here, :] = raw[piece, rows, head_dim:]
        keys_t[c] = jnp.transpose(keys[c].astype(F32)).astype(BF16)

    def exps(c, g, scores):
        parts = []
        for j in range(blocks):
            here = slice(j * block_len, (j + 1) * block_len)
            parts.append(jnp.exp(scores[here] * inv_root + shown[c, j:j + 1, :]))
        return jnp.concatenate(parts, 0)

    def summed(e):
        return jnp.sum(e.reshape(tokens // 8, 8, tokens), 0)

    key_row = lax.broadcasted_iota(jnp.int32, (tokens, tokens), 0)
    query_col = lax.broadcasted_iota(jnp.int32, (tokens, tokens), 1)

    def cols_of(g):
        return pl.ds(g * tokens, tokens)

    def masses(c, first):
        for g in range(group):
            scores = dot_nn(keys[c], q_t_ref[:, cols_of(g)])
            e = exps(c, g, scores)
            if first:
                e = jnp.where(key_row <= query_col, e, 0.0)
            expo[c, g] = e
            mass[g] = summed(e) if first else mass[g] + summed(e)

    load_chunk(0)
    masses(0, True)
    load_chunk(1)

    @pl.loop(1, chunks)
    def _(c):
        masses(c, False)
        load_chunk(c + 1)

    for g in range(group):
        total = jnp.sum(mass[g], 0, keepdims=True)
        mass[g] = jnp.broadcast_to(1.0 / total, (8, tokens))
    dq_ref[...] = jnp.zeros(dq_ref.shape, F32)
    gain_part_ref[...] = jnp.zeros(gain_part_ref.shape, F32)
    spread[...] = jnp.zeros(spread.shape, BF16)

    @pl.loop(0, chunks)
    def _(c):
        for g in range(group):
            cols = cols_of(g)
            grad_prob = dot_nn(vals[c], grad_t_ref[:, cols])
            weights = expo[c, g] * mass[g, 0:1, :]
            ds_all[:, cols] = (weights * (grad_prob - delta_ref[:, cols])).astype(BF16)
            w_all[:, cols] = weights.astype(BF16)
        dv = dot_nn(w_all[...], grad_ref[...])
        dk = dot_nn(ds_all[...], q_ref[...])
        dq_ref[...] = dq_ref[...] + dot_nn(keys_t[c], ds_all[...])
        dk = dk * inv_root
        found[c, :, 0:head_dim] = dk.astype(BF16)
        found[c, :, head_dim:] = dv.astype(BF16)
        front = jnp.sum((dk * with_cos[c]).reshape(tokens // 8, 8, head_dim), 0)
        back = jnp.sum((dk * with_sin[c]).reshape(tokens // 8, 8, head_dim), 0)
        gain_part_ref[...] = gain_part_ref[...] + front - pltpu.roll(back, head_dim // 2, 1)

    @pl.loop(0, count)
    def _(slot):
        rows = rows_of(lax.rem(slot, blocks))
        spread[plan_ref[0, slot], rows_of(plan_ref[1, slot]), :] = found[slot // blocks, rows, :]

    for piece in range(half + last):
        parts[piece][...] = spread[piece]
    crossed_part[...] = spread[half + last:]


def join_kernel(*refs):
    head_dim = refs[-1].shape[2] // 2
    heads = refs[0].shape[1] // (2 * head_dim)
    pieces, outs = refs[:-heads], refs[-heads:]
    for head in range(heads):
        for i, piece in enumerate(pieces):
            outs[head][i, :, 0:head_dim] = piece[:, head * head_dim:(head + 1) * head_dim]
            outs[head][i, :, head_dim:] = piece[:, (heads + head) * head_dim:(heads + head + 1) * head_dim]


def query_kernel(blocks, inv_root, kv_heads, depth_ref, t0, t1, t2, t3, gain_ref, q_ref, *refs):
    dq_refs, (k_part_refs, (out_ref, gains_ref)) = refs[:kv_heads], (refs[kv_heads:-2], refs[-2:])
    tokens = q_ref.shape[0]
    head_dim = gain_ref.shape[1]
    group = dq_refs[0].shape[1] // tokens
    cos, sin = own_tables(depth_ref, (t0, t1, t2, t3), blocks)
    gain = gain_ref[...]
    part = jnp.zeros((8, head_dim), F32)
    for head in range(group * len(dq_refs)):
        cols = pl.ds(head * head_dim, head_dim)
        rows = q_ref[:, cols].astype(F32)
        recip = inverse_rms(rows)
        normed = rows * recip
        dq = jnp.transpose(dq_refs[head // group][:, pl.ds(head % group * tokens, tokens)])
        scaled_grad = turned_back(dq, cos, sin) * inv_root
        term = scaled_grad * normed
        part = part + jnp.sum(term.reshape(tokens // 8, 8, head_dim), 0)
        inner = jnp.mean(term * gain, -1, keepdims=True)
        out_ref[:, cols] = (recip * (scaled_grad * gain - normed * inner)).astype(BF16)
    k_part = sum(ref[...] for ref in k_part_refs)
    gains = jnp.concatenate([jnp.sum(part, 0, keepdims=True), jnp.sum(k_part, 0, keepdims=True)], 0)
    gains_ref[...] = jnp.broadcast_to(gains[None], gains_ref.shape)


def key_kernel(blocks, counts, depth_ref, t0, t1, t2, t3, gain_ref, k_ref, *refs):
    sums, (gains_ref, dk_out_ref, dv_out_ref, total_ref) = refs[:-4], refs[-4:]
    total_ref[...] = jnp.sum(gains_ref[...], 0)
    head_dim = gain_ref.shape[1]
    cos, sin = own_tables(depth_ref, (t0, t1, t2, t3), blocks)
    gain = gain_ref[...]
    for head, each in enumerate(counts):
        cols = pl.ds(head * head_dim, head_dim)
        rows = k_ref[:, cols].astype(F32)
        recip = inverse_rms(rows)
        normed = rows * recip
        mine = sums[sum(counts[:head]):][:each]
        both = mine[0][...].astype(F32)
        for other in mine[1:]:
            both = both + other[...].astype(F32)
        grad = turned_back(both[:, 0:head_dim], cos, sin) * gain
        inner = jnp.mean(grad * normed, -1, keepdims=True)
        dk_out_ref[:, cols] = (recip * (grad - normed * inner)).astype(BF16)
        dv_out_ref[:, cols] = both[:, head_dim:].astype(BF16)


class Tree:
    def __init__(self, size, cycle):
        self.size, self.cycle = size, cycle

    def order(self, index):
        return (index - 1) % self.size

    def send(self, value, target, wanted):
        pairs = []
        for tree in range(self.cycle // self.size):
            for index in range(self.size):
                if wanted(index):
                    ends = [(tree * self.size + 1 + self.order(i)) % self.cycle for i in (index, target(index))]
                    pairs.append(tuple(ends))
        return lax.ppermute(value, "ctx", pairs)

    def after(self, *pair):
        return self.order(pair[1] % self.size) > self.order(pair[0] % self.size)

    def gather(self, own):
        size, after = self.size, self.after
        cross = self.send(own, lambda i: i ^ 1, lambda i: after(i, i ^ 1))
        straight = []
        for step in range(2, size, 2):
            there = lambda i: (i + step) % size
            straight.append(self.send(own, there, lambda i: after(i, there(i)) or after(i, there(i) ^ 1)))
        return own, cross, straight

    def across(self, value, steps, back=False):
        if back:
            return self.send(value, lambda i: i ^ 1, lambda i: any(self.after((i ^ 1) - step, i) for step in steps))
        return self.send(value, lambda i: i ^ 1, lambda i: any(self.after(i - step, i ^ 1) for step in steps))

    def home(self, value, step):
        there = lambda i: (i - step) % self.size
        return self.send(value, there, lambda i: self.after(there(i), i) or self.after(there(i), i ^ 1))


def on_device(q_raw, k_raw, values, saved_out, out_grad, q_gain, k_gain, ancestors):
    tokens = q_raw.shape[0]
    head_dim = q_gain.shape[0]
    kv_heads = k_raw.shape[1] // head_dim
    heads = q_raw.shape[1] // head_dim
    group = heads // kv_heads
    blocks = ancestors.shape[0]
    tree_blocks = ancestors.shape[1]
    block_len = tokens // blocks
    tree_dev = tree_blocks // blocks
    cycle = lax.axis_size("ctx")
    inv_root = 1.0 / math.sqrt(head_dim)
    tree = Tree(tree_dev, cycle)
    place = (lax.axis_index("ctx") - 1 + cycle) % cycle % tree_dev
    place = place.reshape(1).astype(jnp.int32)

    depth = jnp.sum((ancestors >= 0).astype(jnp.int32), 1) - 1
    total_blocks = blocks * cycle
    in_tree = jnp.where(
        ancestors >= 0, (ancestors - blocks + total_blocks) % total_blocks % tree_blocks, -1
    )
    tables = [
        jnp.asarray(table)
        for starts in (range(0, tree_blocks * block_len, block_len), range(block_len))
        for table in rope_rows(starts, head_dim)
    ]
    q_gain_row, k_gain_row = q_gain.reshape(1, head_dim), k_gain.reshape(1, head_dim)

    steps = range(2, tree_dev, 2)
    own, cross, straight = tree.gather(jnp.concatenate([k_raw, values], 1))
    params = pltpu.CompilerParams(vmem_limit_bytes=VMEM_LIMIT)
    smem = pl.BlockSpec(memory_space=pltpu.SMEM)
    vmem = pl.BlockSpec(memory_space=pltpu.VMEM)
    sds = jax.ShapeDtypeStruct

    plan = pl.pallas_call(
        lambda *refs: plan_kernel(blocks, tree_dev, *refs),
        out_shape=sds((5, tree_blocks), jnp.int32),
        in_specs=[smem, smem],
        out_specs=smem,
        name="plan",
    )(place, in_tree)

    joined = pl.pallas_call(
        join_kernel,
        out_shape=tuple([sds((len(steps), tokens, 2 * head_dim), BF16)] * kv_heads),
        in_specs=[vmem] * len(steps),
        out_specs=tuple([vmem] * kv_heads),
        compiler_params=params,
        name="join",
    )(*straight)
    crossed = [tree.across(one, steps) for one in joined]

    rows = group * tokens
    queries = pl.pallas_call(
        lambda *refs: prep_kernel(blocks, block_len, kv_heads, *refs),
        out_shape=tuple(
            [
                sds((head_dim, rows), BF16),
                sds((rows, head_dim), BF16),
                sds((head_dim, rows), BF16),
                sds((rows, head_dim), BF16),
                sds((1, rows), F32),
            ]
            * kv_heads
        ),
        in_specs=[smem] + [vmem] * 8,
        out_specs=tuple([vmem] * (5 * kv_heads)),
        compiler_params=params,
        name="prep",
    )(depth, *tables, q_gain_row, q_raw, out_grad, saved_out)

    half = tree_dev // 2

    def attend(h):
        last = h == kv_heads - 1
        return pl.pallas_call(
            lambda *refs: main_kernel(blocks, block_len, tree_dev, inv_root, h, last, *refs),
            out_shape=(
                sds((head_dim, rows), F32),
                sds((8, head_dim), F32),
                *[sds((tokens, 2 * head_dim), BF16)] * (half + last),
                sds((half - last, tokens, 2 * head_dim), BF16),
            ),
            in_specs=[smem] + [vmem] * (12 + half),
            out_specs=tuple([vmem] * (3 + half + last)),
            scratch_shapes=[
                pltpu.VMEM((tree_dev, tokens, 2 * head_dim), BF16),
                pltpu.VMEM((tree_dev + 1, tokens, head_dim), BF16),
                pltpu.VMEM((tree_dev + 1, head_dim, tokens), BF16),
                pltpu.VMEM((tree_dev + 1, tokens, head_dim), BF16),
                pltpu.VMEM((tree_dev + 1, 8 * ((blocks + 7) // 8), tokens), F32),
                pltpu.VMEM((tree_dev + 1, tokens, head_dim), F32),
                pltpu.VMEM((tree_dev + 1, tokens, head_dim), F32),
                pltpu.VMEM((tree_dev, group, tokens, tokens), F32),
                pltpu.VMEM((group, 8, tokens), F32),
                pltpu.VMEM((tokens, rows), BF16),
                pltpu.VMEM((tokens, rows), BF16),
                pltpu.VMEM((tree_dev, tokens, 2 * head_dim), BF16),
                pltpu.VMEM((tree_dev, tokens, 2 * head_dim), BF16),
            ],
            compiler_params=params,
            cost_estimate=pl.CostEstimate(
                flops=10 * group * tokens * tree_dev * tokens * head_dim,
                bytes_accessed=8 * 1024 * 1024,
                transcendentals=group * tokens * tree_dev * tokens,
            ),
            name="attend",
        )(plan, k_gain_row, *tables, own, *straight, cross, crossed[h], *queries[5 * h:5 * h + 5])

    dq, terms, counts, k_gain_parts = [], [], [], []
    for h in range(kv_heads):
        dq_here, k_gain_part, *parts, crossed_part = attend(h)
        dq.append(dq_here)
        k_gain_parts.append(k_gain_part)
        if len(parts) > half:
            others = tree.across(crossed_part, steps, back=True)
            mine = [parts[0], tree.across(parts[half], [0], back=True)]
        else:
            others = tree.across(crossed_part, [0, *steps], back=True)
            mine = [parts[0], others[0]]
            others = others[1:]
        for i, step in enumerate(steps):
            both = (parts[i + 1].astype(F32) + others[i].astype(F32)).astype(BF16)
            mine.append(tree.home(both, step))
        terms.extend(mine)
        counts.append(len(mine))

    everyone = cycle * lax.axis_size("heads")
    dq_raw, gains = pl.pallas_call(
        lambda *refs: query_kernel(blocks, inv_root, kv_heads, *refs),
        out_shape=(sds((tokens, heads * head_dim), BF16), sds((everyone, 2, head_dim), F32)),
        in_specs=[smem] + [vmem] * (6 + 2 * kv_heads),
        out_specs=(vmem, vmem),
        compiler_params=params,
        name="query_back",
    )(depth, *tables, q_gain_row, q_raw, *dq, *k_gain_parts)

    gains = lax.all_to_all(gains, ("ctx", "heads"), 0, 0)

    dk_raw, dv, total = pl.pallas_call(
        lambda *refs: key_kernel(blocks, counts, *refs),
        out_shape=(sds(k_raw.shape, BF16), sds(k_raw.shape, BF16), sds(gains.shape[1:], F32)),
        in_specs=[smem] + [vmem] * (7 + len(terms)),
        out_specs=(vmem, vmem, vmem),
        compiler_params=params,
        name="key_back",
    )(depth, *tables, k_gain_row, k_raw, *terms, gains)
    return (dq_raw, dk_raw, dv, total[0], total[1])


def solution(mesh):
    split = P("ctx", "heads")
    return jax.shard_map(
        on_device,
        mesh=mesh,
        in_specs=(split, split, split, split, split, P(), P(), P("ctx", None)),
        out_specs=(split, split, split, P(), P()),
        check_vma=False,
    )
```

```python
import math

import jax
import jax.numpy as jnp
import numpy as np
from jax import lax
from jax.experimental import pallas as pl
from jax.experimental.pallas import tpu as pltpu
from jax.sharding import PartitionSpec as P

ROPE_BASE = 1000000.0
EPS = 1e-06
HIDDEN = -100000.0
VMEM_LIMIT = 56 * 1024 * 1024
F32 = jnp.float32
BF16 = jnp.bfloat16


def rope_rows(starts, head_dim):
    half = head_dim // 2
    frequency = np.exp(
        np.arange(half, dtype=np.float32) * np.float32(-2.0 * math.log(ROPE_BASE) / head_dim)
    ).astype(np.float32)
    angles = np.asarray(starts, np.float32)[:, None] * frequency[None, :]
    cos = np.cos(angles.astype(np.float64)).astype(np.float32)
    sin = np.sin(angles.astype(np.float64)).astype(np.float32)
    return np.concatenate([cos, cos], 1), np.concatenate([-sin, sin], 1)


def block_tables(depth, tables):
    start_cos, start_sin, offset_cos, offset_sin = tables
    cos, sin = start_cos[pl.ds(depth, 1), :], start_sin[pl.ds(depth, 1), :]
    both_cos = cos * offset_cos[...] - sin * offset_sin[...]
    both_sin = sin * offset_cos[...] + cos * offset_sin[...]
    return both_cos, both_sin


def turned(rows, cos, sin):
    return rows * cos + pltpu.roll(rows, rows.shape[-1] // 2, 1) * sin


def turned_back(rows, cos, sin):
    return rows * cos - pltpu.roll(rows, rows.shape[-1] // 2, 1) * sin


def inverse_rms(rows):
    return lax.rsqrt(jnp.mean(rows * rows, -1, keepdims=True) + EPS)


def own_tables(depth_ref, tables, blocks):
    parts = [block_tables(depth_ref[a], tables) for a in range(blocks)]
    return jnp.concatenate([p[0] for p in parts], 0), jnp.concatenate([p[1] for p in parts], 0)


def dot_nn(lhs, rhs):
    return lax.dot_general(lhs, rhs, (((1,), (0,)), ((), ())), preferred_element_type=F32)


def plan_kernel(blocks, tree_dev, place_ref, anc_ref, plan_ref):
    slots = tree_dev * blocks
    place = place_ref[0]
    here = jnp.where(place + 1 == tree_dev, 0, place + 1)
    for row in range(4):
        for i in range(slots):
            plan_ref[row, i] = 0
    count = jnp.int32(blocks)
    steps = [jnp.int32(0)] * blocks
    for b in range(slots):
        bits = jnp.int32(0)
        depth = jnp.int32(0)
        for a in range(blocks):
            hit = anc_ref[a, jnp.minimum(steps[a], slots - 1)] == b
            bits = bits | jnp.where(hit, 1 << a, 0)
            depth = jnp.where(hit, steps[a], depth)
            steps[a] = steps[a] + jnp.where(hit, 1, 0)
        own = place == b // blocks
        slot = jnp.where(own, b % blocks, jnp.minimum(count, slots - 1))
        there = (b // blocks + 1) % tree_dev
        odd = jnp.bitwise_and(here + there, 1)
        gap = jnp.bitwise_xor(here, odd) - there
        gap = jnp.where(gap < 0, gap + tree_dev, gap)
        plan_ref[0, slot] = odd * (tree_dev // 2) + lax.shift_right_logical(gap, 1)
        plan_ref[1, slot] = b % blocks
        plan_ref[2, slot] = depth
        plan_ref[3, slot] = bits
        count = count + jnp.where(own | (bits == 0), 0, 1)
    for i in range(slots):
        plan_ref[4, i] = count


def prep_kernel(blocks, block_len, kv_heads, depth_ref, t0, t1, t2, t3, gain_ref, q_ref, grad_ref, out_ref, *outs):
    tokens = q_ref.shape[0]
    head_dim = gain_ref.shape[1]
    cos, sin = own_tables(depth_ref, (t0, t1, t2, t3), blocks)
    gain = gain_ref[...]
    group = q_ref.shape[1] // head_dim // kv_heads
    for head in range(group * kv_heads):
        g = head % group
        q_t_ref, q_rot_ref, grad_t_ref, grad_heads_ref, delta_ref = outs[5 * (head // group):][:5]
        cols = pl.ds(head * head_dim, head_dim)
        here = pl.ds(g * tokens, tokens)
        rows = q_ref[:, cols].astype(F32)
        rotated = turned(rows * inverse_rms(rows) * gain, cos, sin)
        q_rot_ref[here, :] = rotated.astype(BF16)
        q_t_ref[:, here] = jnp.transpose(rotated).astype(BF16)
        grad = grad_ref[:, cols]
        grad_heads_ref[here, :] = grad
        grad_rows = jnp.transpose(grad.astype(F32))
        grad_t_ref[:, here] = grad_rows.astype(BF16)
        product = grad_rows * jnp.transpose(out_ref[:, cols].astype(F32))
        delta_ref[:, here] = jnp.sum(product, 0, keepdims=True)


def main_kernel(blocks, block_len, tree_dev, inv_root, n_in, last, *refs):
    plan_ref, gain_ref = refs[:2]
    tables = refs[2:6]
    half = tree_dev // 2
    pieces, crossed_ref = refs[6:5 + n_in], refs[5 + n_in]
    q_t_ref, q_ref, grad_t_ref, grad_ref, delta_ref = refs[6 + n_in:11 + n_in]
    dq_ref, gain_part_ref = refs[11 + n_in:13 + n_in]
    parts = refs[13 + n_in:13 + n_in + half + last]
    crossed_part, raw, keys, keys_t, vals, shown, with_cos, with_sin, expo, mass, w_all, ds_all, found, spread = refs[
        13 + n_in + half + last:]
    head_dim = gain_ref.shape[1]
    tokens = raw.shape[1]
    group = q_ref.shape[0] // tokens
    count = plan_ref[4, 0]
    chunks = (count + blocks - 1) // blocks
    gain = gain_ref[...]
    for i, piece in enumerate(pieces):
        raw[i] = piece[...]
    raw[len(pieces):] = crossed_ref[...]
    query_block = lax.broadcasted_iota(jnp.int32, (1, tokens), 1) // block_len

    def rows_of(start):
        return pl.ds(pl.multiple_of(start * block_len, block_len), block_len)

    def load_chunk(c):
        for j in range(blocks):
            slot = jnp.minimum(c * blocks + j, tree_dev * blocks - 1)
            piece = plan_ref[0, slot]
            rows = rows_of(plan_ref[1, slot])
            cos, sin = block_tables(plan_ref[2, slot], tables)
            unit = raw[piece, rows, 0:head_dim].astype(F32)
            unit = unit * inverse_rms(unit)
            here = pl.ds(j * block_len, block_len)
            with_cos[c, here, :] = unit * cos
            with_sin[c, here, :] = pltpu.roll(unit * sin, head_dim // 2, 1)
            keys[c, here, :] = turned(unit * gain, cos, sin).astype(BF16)
            bits = jnp.where(c * blocks + j < count, plan_ref[3, slot], 0)
            row = jnp.zeros((1, tokens), F32)
            for a in range(blocks):
                seen = lax.rem(lax.shift_right_logical(bits, a), 2)
                row = jnp.where((query_block == a) & (seen == 0), HIDDEN, row)
            shown[c, j:j + 1, :] = row
            vals[c, here, :] = raw[piece, rows, head_dim:]
        keys_t[c] = jnp.transpose(keys[c].astype(F32)).astype(BF16)

    def exps(c, g, scores):
        parts = []
        for j in range(blocks):
            here = slice(j * block_len, (j + 1) * block_len)
            parts.append(jnp.exp(scores[here] * inv_root + shown[c, j:j + 1, :]))
        return jnp.concatenate(parts, 0)

    def summed(e):
        return jnp.sum(e.reshape(tokens // 8, 8, tokens), 0)

    key_row = lax.broadcasted_iota(jnp.int32, (tokens, tokens), 0)
    query_col = lax.broadcasted_iota(jnp.int32, (tokens, tokens), 1)

    def cols_of(g):
        return pl.ds(g * tokens, tokens)

    def masses(c, first):
        for g in range(group):
            scores = dot_nn(keys[c], q_t_ref[:, cols_of(g)])
            e = exps(c, g, scores)
            if first:
                e = jnp.where(key_row <= query_col, e, 0.0)
            expo[c, g] = e
            mass[g] = summed(e) if first else mass[g] + summed(e)

    load_chunk(0)
    masses(0, True)
    load_chunk(1)

    @pl.loop(1, chunks)
    def _(c):
        masses(c, False)
        load_chunk(c + 1)

    for g in range(group):
        total = jnp.sum(mass[g], 0, keepdims=True)
        mass[g] = jnp.broadcast_to(1.0 / total, (8, tokens))
    dq_ref[...] = jnp.zeros(dq_ref.shape, F32)
    gain_part_ref[...] = jnp.zeros(gain_part_ref.shape, F32)
    spread[...] = jnp.zeros(spread.shape, BF16)

    @pl.loop(0, chunks)
    def _(c):
        for g in range(group):
            cols = cols_of(g)
            grad_prob = dot_nn(vals[c], grad_t_ref[:, cols])
            weights = expo[c, g] * mass[g, 0:1, :]
            ds_all[:, cols] = (weights * (grad_prob - delta_ref[:, cols])).astype(BF16)
            w_all[:, cols] = weights.astype(BF16)
        dv = dot_nn(w_all[...], grad_ref[...])
        dk = dot_nn(ds_all[...], q_ref[...])
        dq_ref[...] = dq_ref[...] + dot_nn(keys_t[c], ds_all[...])
        dk = dk * inv_root
        found[c, :, 0:head_dim] = dk.astype(BF16)
        found[c, :, head_dim:] = dv.astype(BF16)
        front = jnp.sum((dk * with_cos[c]).reshape(tokens // 8, 8, head_dim), 0)
        back = jnp.sum((dk * with_sin[c]).reshape(tokens // 8, 8, head_dim), 0)
        gain_part_ref[...] = gain_part_ref[...] + front - pltpu.roll(back, head_dim // 2, 1)

    @pl.loop(0, count)
    def _(slot):
        rows = rows_of(lax.rem(slot, blocks))
        spread[plan_ref[0, slot], rows_of(plan_ref[1, slot]), :] = found[slot // blocks, rows, :]

    for piece in range(half + last):
        parts[piece][...] = spread[piece]
    crossed_part[...] = spread[half + last:]


def join_kernel(*refs):
    arrays, joined, sems = refs[:-2], refs[-2], refs[-1]
    copies = [pltpu.make_async_copy(ref, joined.at[i], sems.at[i]) for i, ref in enumerate(arrays)]
    for copy in copies:
        copy.start()
    for copy in copies:
        copy.wait()


def query_kernel(blocks, inv_root, kv_heads, depth_ref, t0, t1, t2, t3, gain_ref, q_ref, *refs):
    dq_refs, (k_part_refs, (out_ref, gains_ref)) = refs[:kv_heads], (refs[kv_heads:-2], refs[-2:])
    tokens = q_ref.shape[0]
    head_dim = gain_ref.shape[1]
    group = dq_refs[0].shape[1] // tokens
    cos, sin = own_tables(depth_ref, (t0, t1, t2, t3), blocks)
    gain = gain_ref[...]
    part = jnp.zeros((8, head_dim), F32)
    for head in range(group * len(dq_refs)):
        cols = pl.ds(head * head_dim, head_dim)
        rows = q_ref[:, cols].astype(F32)
        recip = inverse_rms(rows)
        normed = rows * recip
        dq = jnp.transpose(dq_refs[head // group][:, pl.ds(head % group * tokens, tokens)])
        scaled_grad = turned_back(dq, cos, sin) * inv_root
        term = scaled_grad * normed
        part = part + jnp.sum(term.reshape(tokens // 8, 8, head_dim), 0)
        inner = jnp.mean(term * gain, -1, keepdims=True)
        out_ref[:, cols] = (recip * (scaled_grad * gain - normed * inner)).astype(BF16)
    k_part = sum(ref[...] for ref in k_part_refs)
    gains = jnp.concatenate([jnp.sum(part, 0, keepdims=True), jnp.sum(k_part, 0, keepdims=True)], 0)
    gains_ref[...] = jnp.broadcast_to(gains[None], gains_ref.shape)


def key_kernel(blocks, counts, depth_ref, t0, t1, t2, t3, gain_ref, k_ref, *refs):
    sums, (gains_ref, dk_out_ref, dv_out_ref, total_ref) = refs[:-4], refs[-4:]
    total_ref[...] = jnp.sum(gains_ref[...], 0)
    head_dim = gain_ref.shape[1]
    cos, sin = own_tables(depth_ref, (t0, t1, t2, t3), blocks)
    gain = gain_ref[...]
    for head, each in enumerate(counts):
        cols = pl.ds(head * head_dim, head_dim)
        rows = k_ref[:, cols].astype(F32)
        recip = inverse_rms(rows)
        normed = rows * recip
        mine = sums[sum(counts[:head]):][:each]
        both = mine[0][...].astype(F32)
        for other in mine[1:]:
            both = both + other[...].astype(F32)
        grad = turned_back(both[:, 0:head_dim], cos, sin) * gain
        inner = jnp.mean(grad * normed, -1, keepdims=True)
        dk_out_ref[:, cols] = (recip * (grad - normed * inner)).astype(BF16)
        dv_out_ref[:, cols] = both[:, head_dim:].astype(BF16)


class Tree:
    def __init__(self, size, cycle):
        self.size, self.cycle = size, cycle

    def order(self, index):
        return (index - 1) % self.size

    def send(self, value, target, wanted):
        pairs = []
        for tree in range(self.cycle // self.size):
            for index in range(self.size):
                if wanted(index):
                    ends = [(tree * self.size + 1 + self.order(i)) % self.cycle for i in (index, target(index))]
                    pairs.append(tuple(ends))
        return lax.ppermute(value, "ctx", pairs)

    def after(self, *pair):
        return self.order(pair[1] % self.size) > self.order(pair[0] % self.size)

    def along(self, own):
        pieces = []
        for step in range(2, self.size, 2):
            there = lambda i: (i + step) % self.size
            pieces.append(self.send(own, there, lambda i: self.after(i, there(i)) or self.after(i, there(i) ^ 1)))
        return pieces

    def across(self, value, steps, back=False):
        if back:
            return self.send(value, lambda i: i ^ 1, lambda i: any(self.after((i ^ 1) - step, i) for step in steps))
        return self.send(value, lambda i: i ^ 1, lambda i: any(self.after(i - step, i ^ 1) for step in steps))

    def home(self, value, step):
        there = lambda i: (i - step) % self.size
        return self.send(value, there, lambda i: self.after(there(i), i) or self.after(there(i), i ^ 1))


def on_device(q_raw, k_raw, values, saved_out, out_grad, q_gain, k_gain, ancestors):
    tokens = q_raw.shape[0]
    head_dim = q_gain.shape[0]
    kv_heads = k_raw.shape[1] // head_dim
    heads = q_raw.shape[1] // head_dim
    group = heads // kv_heads
    blocks = ancestors.shape[0]
    tree_blocks = ancestors.shape[1]
    block_len = tokens // blocks
    tree_dev = tree_blocks // blocks
    cycle = lax.axis_size("ctx")
    inv_root = 1.0 / math.sqrt(head_dim)
    tree = Tree(tree_dev, cycle)
    place = (lax.axis_index("ctx") - 1 + cycle) % cycle % tree_dev
    place = place.reshape(1).astype(jnp.int32)

    depth = jnp.sum((ancestors >= 0).astype(jnp.int32), 1) - 1
    total_blocks = blocks * cycle
    in_tree = jnp.where(
        ancestors >= 0, (ancestors - blocks + total_blocks) % total_blocks % tree_blocks, -1
    )
    tables = [
        jnp.asarray(table)
        for starts in (range(0, tree_blocks * block_len, block_len), range(block_len))
        for table in rope_rows(starts, head_dim)
    ]
    q_gain_row, k_gain_row = q_gain.reshape(1, head_dim), k_gain.reshape(1, head_dim)

    steps = range(2, tree_dev, 2)
    own = []
    for h in range(kv_heads):
        cols = slice(h * head_dim, (h + 1) * head_dim)
        own.append(jnp.concatenate([k_raw[:, cols], values[:, cols]], 1))

    params = pltpu.CompilerParams(vmem_limit_bytes=VMEM_LIMIT)
    smem = pl.BlockSpec(memory_space=pltpu.SMEM)
    vmem = pl.BlockSpec(memory_space=pltpu.VMEM)
    sds = jax.ShapeDtypeStruct

    plan = pl.pallas_call(
        lambda *refs: plan_kernel(blocks, tree_dev, *refs),
        out_shape=sds((5, tree_blocks), jnp.int32),
        in_specs=[smem, smem],
        out_specs=smem,
        name="plan",
    )(place, in_tree)

    def join(arrays):
        count = len(arrays)
        return pl.pallas_call(
            join_kernel,
            out_shape=sds((count, tokens, 2 * head_dim), BF16),
            in_specs=[pl.BlockSpec(memory_space=pl.ANY)] * count,
            out_specs=pl.BlockSpec(memory_space=pl.ANY),
            scratch_shapes=[pltpu.SemaphoreType.DMA((count,))],
            name="join",
        )(*arrays)

    pieces = []
    for h in range(kv_heads):
        straight = tree.along(own[h])
        if h == 0:
            cross = [tree.across(own[h], [0])]
            crossed = tree.across(join(straight), steps)
        else:
            cross = []
            crossed = tree.across(join([own[h], *straight]), [0, *steps])
        pieces.append([own[h], *straight, *cross, crossed])

    rows = group * tokens
    queries = pl.pallas_call(
        lambda *refs: prep_kernel(blocks, block_len, kv_heads, *refs),
        out_shape=tuple(
            [
                sds((head_dim, rows), BF16),
                sds((rows, head_dim), BF16),
                sds((head_dim, rows), BF16),
                sds((rows, head_dim), BF16),
                sds((1, rows), F32),
            ]
            * kv_heads
        ),
        in_specs=[smem] + [vmem] * 8,
        out_specs=tuple([vmem] * (5 * kv_heads)),
        compiler_params=params,
        name="prep",
    )(depth, *tables, q_gain_row, q_raw, out_grad, saved_out)

    half = tree_dev // 2

    def attend(h):
        last = h == kv_heads - 1
        return pl.pallas_call(
            lambda *refs: main_kernel(blocks, block_len, tree_dev, inv_root, len(pieces[h]), last, *refs),
            out_shape=(
                sds((head_dim, rows), F32),
                sds((8, head_dim), F32),
                *[sds((tokens, 2 * head_dim), BF16)] * (half + last),
                sds((half - last, tokens, 2 * head_dim), BF16),
            ),
            in_specs=[smem] + [vmem] * (10 + len(pieces[h])),
            out_specs=tuple([vmem] * (3 + half + last)),
            scratch_shapes=[
                pltpu.VMEM((tree_dev, tokens, 2 * head_dim), BF16),
                pltpu.VMEM((tree_dev + 1, tokens, head_dim), BF16),
                pltpu.VMEM((tree_dev + 1, head_dim, tokens), BF16),
                pltpu.VMEM((tree_dev + 1, tokens, head_dim), BF16),
                pltpu.VMEM((tree_dev + 1, 8 * ((blocks + 7) // 8), tokens), F32),
                pltpu.VMEM((tree_dev + 1, tokens, head_dim), F32),
                pltpu.VMEM((tree_dev + 1, tokens, head_dim), F32),
                pltpu.VMEM((tree_dev, group, tokens, tokens), F32),
                pltpu.VMEM((group, 8, tokens), F32),
                pltpu.VMEM((tokens, rows), BF16),
                pltpu.VMEM((tokens, rows), BF16),
                pltpu.VMEM((tree_dev, tokens, 2 * head_dim), BF16),
                pltpu.VMEM((tree_dev, tokens, 2 * head_dim), BF16),
            ],
            compiler_params=params,
            cost_estimate=pl.CostEstimate(
                flops=10 * group * tokens * tree_dev * tokens * head_dim,
                bytes_accessed=8 * 1024 * 1024,
                transcendentals=group * tokens * tree_dev * tokens,
            ),
            name="attend",
        )(plan, k_gain_row, *tables, *pieces[h], *queries[5 * h:5 * h + 5])

    dq, attended, k_gain_parts = [], [], []
    for h in range(kv_heads):
        dq_here, k_gain_part, *parts, crossed_part = attend(h)
        dq.append(dq_here)
        k_gain_parts.append(k_gain_part)
        attended.append((parts, crossed_part))

    everyone = cycle * lax.axis_size("heads")
    dq_raw, gains = pl.pallas_call(
        lambda *refs: query_kernel(blocks, inv_root, kv_heads, *refs),
        out_shape=(sds((tokens, heads * head_dim), BF16), sds((everyone, 2, head_dim), F32)),
        in_specs=[smem] + [vmem] * (6 + 2 * kv_heads),
        out_specs=(vmem, vmem),
        compiler_params=params,
        name="query_back",
    )(depth, *tables, q_gain_row, q_raw, *dq, *k_gain_parts)

    terms, counts = [], []
    for parts, crossed_part in attended:
        if len(parts) > half:
            others = tree.across(crossed_part, steps, back=True)
            mine = [parts[0], tree.across(parts[half], [0], back=True)]
        else:
            others = tree.across(crossed_part, [0, *steps], back=True)
            mine = [parts[0], others[0]]
            others = others[1:]
        merged = [
            (parts[i + 1].astype(F32) + others[i].astype(F32)).astype(BF16) for i in range(len(steps))
        ]
        if len(parts) > half:
            gains, *merged = lax.optimization_barrier((gains, *merged))
        mine.extend(tree.home(both, step) for both, step in zip(merged, steps))
        terms.extend(mine)
        counts.append(len(mine))

    gains = lax.all_to_all(gains, ("ctx", "heads"), 0, 0)

    dk_raw, dv, total = pl.pallas_call(
        lambda *refs: key_kernel(blocks, counts, *refs),
        out_shape=(sds(k_raw.shape, BF16), sds(k_raw.shape, BF16), sds(gains.shape[1:], F32)),
        in_specs=[smem] + [vmem] * (7 + len(terms)),
        out_specs=(vmem, vmem, vmem),
        compiler_params=params,
        name="key_back",
    )(depth, *tables, k_gain_row, k_raw, *terms, gains)
    return (dq_raw, dk_raw, dv, total[0], total[1])


def solution(mesh):
    split = P("ctx", "heads")
    return jax.shard_map(
        on_device,
        mesh=mesh,
        in_specs=(split, split, split, split, split, P(), P(), P("ctx", None)),
        out_specs=(split, split, split, P(), P()),
        check_vma=False,
    )
```

```python
import math

import jax
import jax.numpy as jnp
import numpy as np
from jax import lax
from jax.experimental import pallas as pl
from jax.experimental.pallas import tpu as pltpu
from jax.sharding import PartitionSpec as P

ROPE_BASE = 1000000.0
EPS = 1e-06
HIDDEN = -100000.0
VMEM_LIMIT = 56 * 1024 * 1024
F32 = jnp.float32
BF16 = jnp.bfloat16


def rope_rows(starts, head_dim):
    half = head_dim // 2
    frequency = np.exp(
        np.arange(half, dtype=np.float32) * np.float32(-2.0 * math.log(ROPE_BASE) / head_dim)
    ).astype(np.float32)
    angles = np.asarray(starts, np.float32)[:, None] * frequency[None, :]
    cos = np.cos(angles.astype(np.float64)).astype(np.float32)
    sin = np.sin(angles.astype(np.float64)).astype(np.float32)
    return np.concatenate([cos, cos], 1), np.concatenate([-sin, sin], 1)


def block_tables(depth, tables):
    start_cos, start_sin, offset_cos, offset_sin = tables
    cos, sin = start_cos[pl.ds(depth, 1), :], start_sin[pl.ds(depth, 1), :]
    both_cos = cos * offset_cos[...] - sin * offset_sin[...]
    both_sin = sin * offset_cos[...] + cos * offset_sin[...]
    return both_cos, both_sin


def turned(rows, cos, sin):
    return rows * cos + pltpu.roll(rows, rows.shape[-1] // 2, 1) * sin


def turned_back(rows, cos, sin):
    return rows * cos - pltpu.roll(rows, rows.shape[-1] // 2, 1) * sin


def inverse_rms(rows):
    return lax.rsqrt(jnp.mean(rows * rows, -1, keepdims=True) + EPS)


def own_tables(depth_ref, tables, blocks):
    parts = [block_tables(depth_ref[a], tables) for a in range(blocks)]
    return jnp.concatenate([p[0] for p in parts], 0), jnp.concatenate([p[1] for p in parts], 0)


def dot_nn(lhs, rhs):
    return lax.dot_general(lhs, rhs, (((1,), (0,)), ((), ())), preferred_element_type=F32)


def plan_kernel(blocks, tree_dev, place_ref, anc_ref, plan_ref):
    slots = tree_dev * blocks
    place = place_ref[0]
    here = jnp.where(place + 1 == tree_dev, 0, place + 1)
    for row in range(4):
        for i in range(slots):
            plan_ref[row, i] = 0
    count = jnp.int32(blocks)
    steps = [jnp.int32(0)] * blocks
    for b in range(slots):
        bits = jnp.int32(0)
        depth = jnp.int32(0)
        for a in range(blocks):
            hit = anc_ref[a, jnp.minimum(steps[a], slots - 1)] == b
            bits = bits | jnp.where(hit, 1 << a, 0)
            depth = jnp.where(hit, steps[a], depth)
            steps[a] = steps[a] + jnp.where(hit, 1, 0)
        own = place == b // blocks
        slot = jnp.where(own, b % blocks, jnp.minimum(count, slots - 1))
        there = (b // blocks + 1) % tree_dev
        odd = jnp.bitwise_and(here + there, 1)
        gap = jnp.bitwise_xor(here, odd) - there
        gap = jnp.where(gap < 0, gap + tree_dev, gap)
        plan_ref[0, slot] = odd * (tree_dev // 2) + lax.shift_right_logical(gap, 1)
        plan_ref[1, slot] = b % blocks
        plan_ref[2, slot] = depth
        plan_ref[3, slot] = bits
        count = count + jnp.where(own | (bits == 0), 0, 1)
    for i in range(slots):
        plan_ref[4, i] = count


def prep_kernel(blocks, block_len, kv_heads, depth_ref, t0, t1, t2, t3, gain_ref, q_ref, grad_ref, out_ref, *outs):
    tokens = q_ref.shape[0]
    head_dim = gain_ref.shape[1]
    cos, sin = own_tables(depth_ref, (t0, t1, t2, t3), blocks)
    gain = gain_ref[...]
    group = q_ref.shape[1] // head_dim // kv_heads
    for head in range(group * kv_heads):
        g = head % group
        q_t_ref, q_rot_ref, grad_t_ref, grad_heads_ref, delta_ref = outs[5 * (head // group):][:5]
        cols = pl.ds(head * head_dim, head_dim)
        here = pl.ds(g * tokens, tokens)
        rows = q_ref[:, cols].astype(F32)
        rotated = turned(rows * inverse_rms(rows) * gain, cos, sin)
        q_rot_ref[here, :] = rotated.astype(BF16)
        q_t_ref[:, here] = jnp.transpose(rotated).astype(BF16)
        grad = grad_ref[:, cols]
        grad_heads_ref[here, :] = grad
        grad_rows = jnp.transpose(grad.astype(F32))
        grad_t_ref[:, here] = grad_rows.astype(BF16)
        product = grad_rows * jnp.transpose(out_ref[:, cols].astype(F32))
        delta_ref[:, here] = jnp.sum(product, 0, keepdims=True)


def main_kernel(blocks, block_len, tree_dev, inv_root, n_in, last, *refs):
    plan_ref, gain_ref = refs[:2]
    tables = refs[2:6]
    half = tree_dev // 2
    pieces, crossed_ref = refs[6:5 + n_in], refs[5 + n_in]
    q_t_ref, q_ref, grad_t_ref, grad_ref, delta_ref = refs[6 + n_in:11 + n_in]
    dq_ref, gain_part_ref = refs[11 + n_in:13 + n_in]
    parts = refs[13 + n_in:13 + n_in + half + last]
    crossed_part, raw, keys, keys_t, vals, shown, with_cos, with_sin, expo, mass, w_all, ds_all, found, spread = refs[
        13 + n_in + half + last:]
    head_dim = gain_ref.shape[1]
    tokens = raw.shape[1]
    group = q_ref.shape[0] // tokens
    count = plan_ref[4, 0]
    chunks = (count + blocks - 1) // blocks
    gain = gain_ref[...]
    for i, piece in enumerate(pieces):
        raw[i] = piece[...]
    raw[len(pieces):] = crossed_ref[...]
    query_block = lax.broadcasted_iota(jnp.int32, (1, tokens), 1) // block_len

    def rows_of(start):
        return pl.ds(pl.multiple_of(start * block_len, block_len), block_len)

    def load_chunk(c):
        for j in range(blocks):
            slot = jnp.minimum(c * blocks + j, tree_dev * blocks - 1)
            piece = plan_ref[0, slot]
            rows = rows_of(plan_ref[1, slot])
            cos, sin = block_tables(plan_ref[2, slot], tables)
            unit = raw[piece, rows, 0:head_dim].astype(F32)
            unit = unit * inverse_rms(unit)
            here = pl.ds(j * block_len, block_len)
            with_cos[c, here, :] = unit * cos
            with_sin[c, here, :] = pltpu.roll(unit * sin, head_dim // 2, 1)
            keys[c, here, :] = turned(unit * gain, cos, sin).astype(BF16)
            bits = jnp.where(c * blocks + j < count, plan_ref[3, slot], 0)
            row = jnp.zeros((1, tokens), F32)
            for a in range(blocks):
                seen = lax.rem(lax.shift_right_logical(bits, a), 2)
                row = jnp.where((query_block == a) & (seen == 0), HIDDEN, row)
            shown[c, j:j + 1, :] = row
            vals[c, here, :] = raw[piece, rows, head_dim:]
        keys_t[c] = jnp.transpose(keys[c].astype(F32)).astype(BF16)

    def exps(c, g, scores):
        parts = []
        for j in range(blocks):
            here = slice(j * block_len, (j + 1) * block_len)
            parts.append(jnp.exp(scores[here] * inv_root + shown[c, j:j + 1, :]))
        return jnp.concatenate(parts, 0)

    def summed(e):
        return jnp.sum(e.reshape(tokens // 8, 8, tokens), 0)

    key_row = lax.broadcasted_iota(jnp.int32, (tokens, tokens), 0)
    query_col = lax.broadcasted_iota(jnp.int32, (tokens, tokens), 1)

    def cols_of(g):
        return pl.ds(g * tokens, tokens)

    def masses(c, first):
        for g in range(group):
            scores = dot_nn(keys[c], q_t_ref[:, cols_of(g)])
            e = exps(c, g, scores)
            if first:
                e = jnp.where(key_row <= query_col, e, 0.0)
            expo[c, g] = e
            mass[g] = summed(e) if first else mass[g] + summed(e)

    load_chunk(0)
    masses(0, True)
    load_chunk(1)

    @pl.loop(1, chunks)
    def _(c):
        masses(c, False)
        load_chunk(c + 1)

    for g in range(group):
        total = jnp.sum(mass[g], 0, keepdims=True)
        mass[g] = jnp.broadcast_to(1.0 / total, (8, tokens))
    dq_ref[...] = jnp.zeros(dq_ref.shape, F32)
    gain_part_ref[...] = jnp.zeros(gain_part_ref.shape, F32)
    spread[...] = jnp.zeros(spread.shape, BF16)

    @pl.loop(0, chunks)
    def _(c):
        for g in range(group):
            cols = cols_of(g)
            grad_prob = dot_nn(vals[c], grad_t_ref[:, cols])
            weights = expo[c, g] * mass[g, 0:1, :]
            ds_all[:, cols] = (weights * (grad_prob - delta_ref[:, cols])).astype(BF16)
            w_all[:, cols] = weights.astype(BF16)
        dv = dot_nn(w_all[...], grad_ref[...])
        dk = dot_nn(ds_all[...], q_ref[...])
        dq_ref[...] = dq_ref[...] + dot_nn(keys_t[c], ds_all[...])
        dk = dk * inv_root
        found[c, :, 0:head_dim] = dk.astype(BF16)
        found[c, :, head_dim:] = dv.astype(BF16)
        front = jnp.sum((dk * with_cos[c]).reshape(tokens // 8, 8, head_dim), 0)
        back = jnp.sum((dk * with_sin[c]).reshape(tokens // 8, 8, head_dim), 0)
        gain_part_ref[...] = gain_part_ref[...] + front - pltpu.roll(back, head_dim // 2, 1)

    @pl.loop(0, count)
    def _(slot):
        rows = rows_of(lax.rem(slot, blocks))
        spread[plan_ref[0, slot], rows_of(plan_ref[1, slot]), :] = found[slot // blocks, rows, :]

    for piece in range(half + last):
        parts[piece][...] = spread[piece]
    crossed_part[...] = spread[half + last:]


def join_kernel(*refs):
    for i in range(refs[-1].shape[0]):
        refs[-1][i] = refs[i][...]


def merge_kernel(*refs):
    count = (len(refs) - 4) // 2
    others_ref, gains_ref = refs[count:count + 2]
    for i in range(count):
        refs[-1 - count + i][...] = (refs[i][...].astype(F32) + others_ref[i].astype(F32)).astype(BF16)
    refs[-1][...] = gains_ref[...]


def query_kernel(blocks, inv_root, kv_heads, depth_ref, t0, t1, t2, t3, gain_ref, q_ref, *refs):
    dq_refs, (k_part_refs, (out_ref, gains_ref)) = refs[:kv_heads], (refs[kv_heads:-2], refs[-2:])
    tokens = q_ref.shape[0]
    head_dim = gain_ref.shape[1]
    group = dq_refs[0].shape[1] // tokens
    cos, sin = own_tables(depth_ref, (t0, t1, t2, t3), blocks)
    gain = gain_ref[...]
    part = jnp.zeros((8, head_dim), F32)
    for head in range(group * len(dq_refs)):
        cols = pl.ds(head * head_dim, head_dim)
        rows = q_ref[:, cols].astype(F32)
        recip = inverse_rms(rows)
        normed = rows * recip
        dq = jnp.transpose(dq_refs[head // group][:, pl.ds(head % group * tokens, tokens)])
        scaled_grad = turned_back(dq, cos, sin) * inv_root
        term = scaled_grad * normed
        part = part + jnp.sum(term.reshape(tokens // 8, 8, head_dim), 0)
        inner = jnp.mean(term * gain, -1, keepdims=True)
        out_ref[:, cols] = (recip * (scaled_grad * gain - normed * inner)).astype(BF16)
    k_part = sum(ref[...] for ref in k_part_refs)
    gains = jnp.concatenate([jnp.sum(part, 0, keepdims=True), jnp.sum(k_part, 0, keepdims=True)], 0)
    gains_ref[...] = jnp.broadcast_to(gains[None], gains_ref.shape)


def key_kernel(blocks, counts, depth_ref, t0, t1, t2, t3, gain_ref, k_ref, *refs):
    sums, (gains_ref, dk_out_ref, dv_out_ref, total_ref) = refs[:-4], refs[-4:]
    total_ref[...] = jnp.sum(gains_ref[...], 0)
    head_dim = gain_ref.shape[1]
    cos, sin = own_tables(depth_ref, (t0, t1, t2, t3), blocks)
    gain = gain_ref[...]
    for head, each in enumerate(counts):
        cols = pl.ds(head * head_dim, head_dim)
        rows = k_ref[:, cols].astype(F32)
        recip = inverse_rms(rows)
        normed = rows * recip
        mine = sums[sum(counts[:head]):][:each]
        both = mine[0][...].astype(F32)
        for other in mine[1:]:
            both = both + other[...].astype(F32)
        grad = turned_back(both[:, 0:head_dim], cos, sin) * gain
        inner = jnp.mean(grad * normed, -1, keepdims=True)
        dk_out_ref[:, cols] = (recip * (grad - normed * inner)).astype(BF16)
        dv_out_ref[:, cols] = both[:, head_dim:].astype(BF16)


class Tree:
    def __init__(self, size, cycle):
        self.size, self.cycle = size, cycle

    def order(self, index):
        return (index - 1) % self.size

    def send(self, value, target, wanted):
        pairs = []
        for tree in range(self.cycle // self.size):
            for index in range(self.size):
                if wanted(index):
                    ends = [(tree * self.size + 1 + self.order(i)) % self.cycle for i in (index, target(index))]
                    pairs.append(tuple(ends))
        return lax.ppermute(value, "ctx", pairs)

    def after(self, *pair):
        return self.order(pair[1] % self.size) > self.order(pair[0] % self.size)

    def along(self, own):
        pieces = []
        for step in range(2, self.size, 2):
            there = lambda i: (i + step) % self.size
            pieces.append(self.send(own, there, lambda i: self.after(i, there(i)) or self.after(i, there(i) ^ 1)))
        return pieces

    def across(self, value, steps, back=False):
        if back:
            return self.send(value, lambda i: i ^ 1, lambda i: any(self.after((i ^ 1) - step, i) for step in steps))
        return self.send(value, lambda i: i ^ 1, lambda i: any(self.after(i - step, i ^ 1) for step in steps))

    def home(self, value, step):
        there = lambda i: (i - step) % self.size
        return self.send(value, there, lambda i: self.after(there(i), i) or self.after(there(i), i ^ 1))


def on_device(q_raw, k_raw, values, saved_out, out_grad, q_gain, k_gain, ancestors):
    tokens = q_raw.shape[0]
    head_dim = q_gain.shape[0]
    kv_heads = k_raw.shape[1] // head_dim
    heads = q_raw.shape[1] // head_dim
    group = heads // kv_heads
    blocks = ancestors.shape[0]
    tree_blocks = ancestors.shape[1]
    block_len = tokens // blocks
    tree_dev = tree_blocks // blocks
    cycle = lax.axis_size("ctx")
    inv_root = 1.0 / math.sqrt(head_dim)
    tree = Tree(tree_dev, cycle)
    place = (lax.axis_index("ctx") - 1 + cycle) % cycle % tree_dev
    place = place.reshape(1).astype(jnp.int32)

    depth = jnp.sum((ancestors >= 0).astype(jnp.int32), 1) - 1
    total_blocks = blocks * cycle
    in_tree = jnp.where(
        ancestors >= 0, (ancestors - blocks + total_blocks) % total_blocks % tree_blocks, -1
    )
    tables = [
        jnp.asarray(table)
        for starts in (range(0, tree_blocks * block_len, block_len), range(block_len))
        for table in rope_rows(starts, head_dim)
    ]
    q_gain_row, k_gain_row = q_gain.reshape(1, head_dim), k_gain.reshape(1, head_dim)

    steps = range(2, tree_dev, 2)
    own = []
    for h in range(kv_heads):
        cols = slice(h * head_dim, (h + 1) * head_dim)
        own.append(jnp.concatenate([k_raw[:, cols], values[:, cols]], 1))

    params = pltpu.CompilerParams(vmem_limit_bytes=VMEM_LIMIT)
    smem = pl.BlockSpec(memory_space=pltpu.SMEM)
    vmem = pl.BlockSpec(memory_space=pltpu.VMEM)
    sds = jax.ShapeDtypeStruct
    quick = pl.CostEstimate(flops=1024, bytes_accessed=1024, transcendentals=0)

    plan = pl.pallas_call(
        lambda *refs: plan_kernel(blocks, tree_dev, *refs),
        out_shape=sds((5, tree_blocks), jnp.int32),
        in_specs=[smem, smem],
        out_specs=smem,
        cost_estimate=pl.CostEstimate(flops=4 * 10**9, bytes_accessed=16 * 1024 * 1024, transcendentals=0),
        name="plan",
    )(place, in_tree)

    def join(arrays, *after):
        count = len(arrays)
        return pl.pallas_call(
            join_kernel,
            out_shape=sds((count, tokens, 2 * head_dim), BF16),
            in_specs=[vmem] * count + [pl.BlockSpec(memory_space=pl.ANY)] * len(after),
            out_specs=vmem,
            compiler_params=params,
            cost_estimate=quick,
            name="join",
        )(*arrays, *after)

    rows = group * tokens
    queries = pl.pallas_call(
        lambda *refs: prep_kernel(blocks, block_len, kv_heads, *refs),
        out_shape=tuple(
            [
                sds((head_dim, rows), BF16),
                sds((rows, head_dim), BF16),
                sds((head_dim, rows), BF16),
                sds((rows, head_dim), BF16),
                sds((1, rows), F32),
            ]
            * kv_heads
        ),
        in_specs=[smem] + [vmem] * 8,
        out_specs=tuple([vmem] * (5 * kv_heads)),
        compiler_params=params,
        cost_estimate=quick,
        name="prep",
    )(depth, *tables, q_gain_row, q_raw, out_grad, saved_out)

    pieces = []
    for h in range(kv_heads):
        straight = tree.along(own[h])
        if h == 0:
            cross = [tree.across(own[h], [0])]
            crossed = tree.across(join(straight, queries[4], queries[-1]), steps)
        else:
            cross = []
            crossed = tree.across(join([own[h], *straight]), [0, *steps])
        pieces.append([own[h], *straight, *cross, crossed])

    half = tree_dev // 2

    def attend(h):
        last = h == kv_heads - 1
        return pl.pallas_call(
            lambda *refs: main_kernel(blocks, block_len, tree_dev, inv_root, len(pieces[h]), last, *refs),
            out_shape=(
                sds((head_dim, rows), F32),
                sds((8, head_dim), F32),
                *[sds((tokens, 2 * head_dim), BF16)] * (half + last),
                sds((half - last, tokens, 2 * head_dim), BF16),
            ),
            in_specs=[smem] + [vmem] * (10 + len(pieces[h])),
            out_specs=tuple([vmem] * (3 + half + last)),
            scratch_shapes=[
                pltpu.VMEM((tree_dev, tokens, 2 * head_dim), BF16),
                pltpu.VMEM((tree_dev + 1, tokens, head_dim), BF16),
                pltpu.VMEM((tree_dev + 1, head_dim, tokens), BF16),
                pltpu.VMEM((tree_dev + 1, tokens, head_dim), BF16),
                pltpu.VMEM((tree_dev + 1, 8 * ((blocks + 7) // 8), tokens), F32),
                pltpu.VMEM((tree_dev + 1, tokens, head_dim), F32),
                pltpu.VMEM((tree_dev + 1, tokens, head_dim), F32),
                pltpu.VMEM((tree_dev, group, tokens, tokens), F32),
                pltpu.VMEM((group, 8, tokens), F32),
                pltpu.VMEM((tokens, rows), BF16),
                pltpu.VMEM((tokens, rows), BF16),
                pltpu.VMEM((tree_dev, tokens, 2 * head_dim), BF16),
                pltpu.VMEM((tree_dev, tokens, 2 * head_dim), BF16),
            ],
            compiler_params=params,
            cost_estimate=pl.CostEstimate(
                flops=10 * group * tokens * tree_dev * tokens * head_dim,
                bytes_accessed=8 * 1024 * 1024,
                transcendentals=group * tokens * tree_dev * tokens,
            ),
            name="attend",
        )(plan, k_gain_row, *tables, *pieces[h], *queries[5 * h:5 * h + 5])

    dq, attended, k_gain_parts = [], [], []
    for h in range(kv_heads):
        dq_here, k_gain_part, *parts, crossed_part = attend(h)
        dq.append(dq_here)
        k_gain_parts.append(k_gain_part)
        attended.append((parts, crossed_part))

    everyone = cycle * lax.axis_size("heads")
    dq_raw, gains = pl.pallas_call(
        lambda *refs: query_kernel(blocks, inv_root, kv_heads, *refs),
        out_shape=(sds((tokens, heads * head_dim), BF16), sds((everyone, 2, head_dim), F32)),
        in_specs=[smem] + [vmem] * (6 + 2 * kv_heads),
        out_specs=(vmem, vmem),
        compiler_params=params,
        name="query_back",
    )(depth, *tables, q_gain_row, q_raw, *dq, *k_gain_parts)

    terms, counts = [], []
    for parts, crossed_part in attended:
        if len(parts) > half:
            others = tree.across(crossed_part, steps, back=True)
            mine = [parts[0], tree.across(parts[half], [0], back=True)]
        else:
            others = tree.across(crossed_part, [0, *steps], back=True)
            mine = [parts[0], others[0]]
            others = others[1:]
        if len(parts) > half:
            *merged, gains = pl.pallas_call(
                merge_kernel,
                out_shape=(*[sds((tokens, 2 * head_dim), BF16)] * len(steps), sds(gains.shape, F32)),
                in_specs=[vmem] * (len(steps) + 2) + [pl.BlockSpec(memory_space=pl.ANY)],
                out_specs=tuple([vmem] * (len(steps) + 1)),
                compiler_params=params,
                name="merge",
            )(*parts[1:half], others, gains, merged[-1])
        else:
            merged = [
                (parts[i + 1].astype(F32) + others[i].astype(F32)).astype(BF16) for i in range(len(steps))
            ]
        mine.extend(tree.home(both, step) for both, step in zip(merged, steps))
        terms.extend(mine)
        counts.append(len(mine))

    gains = lax.all_to_all(gains, ("ctx", "heads"), 0, 0)

    dk_raw, dv, total = pl.pallas_call(
        lambda *refs: key_kernel(blocks, counts, *refs),
        out_shape=(sds(k_raw.shape, BF16), sds(k_raw.shape, BF16), sds(gains.shape[1:], F32)),
        in_specs=[smem] + [vmem] * (7 + len(terms)),
        out_specs=(vmem, vmem, vmem),
        compiler_params=params,
        name="key_back",
    )(depth, *tables, k_gain_row, k_raw, *terms, gains)
    return (dq_raw, dk_raw, dv, total[0], total[1])


def solution(mesh):
    split = P("ctx", "heads")
    return jax.shard_map(
        on_device,
        mesh=mesh,
        in_specs=(split, split, split, split, split, P(), P(), P("ctx", None)),
        out_specs=(split, split, split, P(), P()),
        check_vma=False,
    )
```

```python
import math

import jax
import jax.numpy as jnp
import numpy as np
from jax import lax
from jax.experimental import pallas as pl
from jax.experimental.pallas import tpu as pltpu
from jax.sharding import PartitionSpec as P

ROPE_BASE = 1000000.0
EPS = 1e-06
HIDDEN = -100000.0
VMEM_LIMIT = 56 * 1024 * 1024
F32 = jnp.float32
BF16 = jnp.bfloat16


def rope_rows(starts, head_dim):
    half = head_dim // 2
    frequency = np.exp(
        np.arange(half, dtype=np.float32) * np.float32(-2.0 * math.log(ROPE_BASE) / head_dim)
    ).astype(np.float32)
    angles = np.asarray(starts, np.float32)[:, None] * frequency[None, :]
    cos = np.cos(angles.astype(np.float64)).astype(np.float32)
    sin = np.sin(angles.astype(np.float64)).astype(np.float32)
    return np.concatenate([cos, cos], 1), np.concatenate([-sin, sin], 1)


def block_tables(depth, tables):
    start_cos, start_sin, offset_cos, offset_sin = tables
    cos, sin = start_cos[pl.ds(depth, 1), :], start_sin[pl.ds(depth, 1), :]
    both_cos = cos * offset_cos[...] - sin * offset_sin[...]
    both_sin = sin * offset_cos[...] + cos * offset_sin[...]
    return both_cos, both_sin


def turned(rows, cos, sin):
    return rows * cos + pltpu.roll(rows, rows.shape[-1] // 2, 1) * sin


def turned_back(rows, cos, sin):
    return rows * cos - pltpu.roll(rows, rows.shape[-1] // 2, 1) * sin


def inverse_rms(rows):
    return lax.rsqrt(jnp.mean(rows * rows, -1, keepdims=True) + EPS)


def own_tables(depth_ref, tables, blocks):
    parts = [block_tables(depth_ref[a], tables) for a in range(blocks)]
    return jnp.concatenate([p[0] for p in parts], 0), jnp.concatenate([p[1] for p in parts], 0)


def dot_nn(lhs, rhs):
    return lax.dot_general(lhs, rhs, (((1,), (0,)), ((), ())), preferred_element_type=F32)


def plan_kernel(blocks, tree_dev, place_ref, anc_ref, plan_ref):
    slots = tree_dev * blocks
    place = place_ref[0]
    here = jnp.where(place + 1 == tree_dev, 0, place + 1)
    for row in range(4):
        for i in range(slots):
            plan_ref[row, i] = 0
    count = jnp.int32(blocks)
    steps = [jnp.int32(0)] * blocks
    for b in range(slots):
        bits = jnp.int32(0)
        depth = jnp.int32(0)
        for a in range(blocks):
            hit = anc_ref[a, jnp.minimum(steps[a], slots - 1)] == b
            bits = bits | jnp.where(hit, 1 << a, 0)
            depth = jnp.where(hit, steps[a], depth)
            steps[a] = steps[a] + jnp.where(hit, 1, 0)
        own = place == b // blocks
        slot = jnp.where(own, b % blocks, jnp.minimum(count, slots - 1))
        there = (b // blocks + 1) % tree_dev
        odd = jnp.bitwise_and(here + there, 1)
        gap = jnp.bitwise_xor(here, odd) - there
        gap = jnp.where(gap < 0, gap + tree_dev, gap)
        plan_ref[0, slot] = odd * (tree_dev // 2) + lax.shift_right_logical(gap, 1)
        plan_ref[1, slot] = b % blocks
        plan_ref[2, slot] = depth
        plan_ref[3, slot] = bits
        count = count + jnp.where(own | (bits == 0), 0, 1)
    for i in range(slots):
        plan_ref[4, i] = count


def prep_kernel(blocks, block_len, kv_heads, depth_ref, t0, t1, t2, t3, gain_ref, q_ref, grad_ref, out_ref, *outs):
    tokens = q_ref.shape[0]
    head_dim = gain_ref.shape[1]
    cos, sin = own_tables(depth_ref, (t0, t1, t2, t3), blocks)
    gain = gain_ref[...]
    group = q_ref.shape[1] // head_dim // kv_heads
    for head in range(group * kv_heads):
        g = head % group
        q_t_ref, q_rot_ref, grad_t_ref, grad_heads_ref, delta_ref = outs[5 * (head // group):][:5]
        cols = pl.ds(head * head_dim, head_dim)
        here = pl.ds(g * tokens, tokens)
        rows = q_ref[:, cols].astype(F32)
        rotated = turned(rows * inverse_rms(rows) * gain, cos, sin)
        q_rot_ref[here, :] = rotated.astype(BF16)
        q_t_ref[:, here] = jnp.transpose(rotated).astype(BF16)
        grad = grad_ref[:, cols]
        grad_heads_ref[here, :] = grad
        grad_rows = jnp.transpose(grad.astype(F32))
        grad_t_ref[:, here] = grad_rows.astype(BF16)
        product = grad_rows * jnp.transpose(out_ref[:, cols].astype(F32))
        delta_ref[:, here] = jnp.sum(product, 0, keepdims=True)


def main_kernel(blocks, block_len, tree_dev, inv_root, n_in, *refs):
    plan_ref, gain_ref = refs[:2]
    tables = refs[2:6]
    half = tree_dev // 2
    pieces, crossed_ref = refs[6:5 + n_in], refs[5 + n_in]
    q_t_ref, q_ref, grad_t_ref, grad_ref, delta_ref = refs[6 + n_in:11 + n_in]
    dq_ref, gain_part_ref = refs[11 + n_in:13 + n_in]
    parts = refs[13 + n_in:13 + n_in + half]
    crossed_part, raw, keys, keys_t, vals, shown, with_cos, with_sin, expo, mass, w_all, ds_all, found, spread = refs[
        13 + n_in + half:]
    head_dim = gain_ref.shape[1]
    tokens = raw.shape[1]
    group = q_ref.shape[0] // tokens
    count = plan_ref[4, 0]
    chunks = (count + blocks - 1) // blocks
    gain = gain_ref[...]
    for i, piece in enumerate(pieces):
        raw[i] = piece[...]
    raw[len(pieces):] = crossed_ref[...]
    query_block = lax.broadcasted_iota(jnp.int32, (1, tokens), 1) // block_len

    def rows_of(start):
        return pl.ds(pl.multiple_of(start * block_len, block_len), block_len)

    def load_chunk(c):
        for j in range(blocks):
            slot = jnp.minimum(c * blocks + j, tree_dev * blocks - 1)
            piece = plan_ref[0, slot]
            rows = rows_of(plan_ref[1, slot])
            cos, sin = block_tables(plan_ref[2, slot], tables)
            unit = raw[piece, rows, 0:head_dim].astype(F32)
            unit = unit * inverse_rms(unit)
            here = pl.ds(j * block_len, block_len)
            with_cos[c, here, :] = unit * cos
            with_sin[c, here, :] = pltpu.roll(unit * sin, head_dim // 2, 1)
            keys[c, here, :] = turned(unit * gain, cos, sin).astype(BF16)
            bits = jnp.where(c * blocks + j < count, plan_ref[3, slot], 0)
            row = jnp.zeros((1, tokens), F32)
            for a in range(blocks):
                seen = lax.rem(lax.shift_right_logical(bits, a), 2)
                row = jnp.where((query_block == a) & (seen == 0), HIDDEN, row)
            shown[c, j:j + 1, :] = row
            vals[c, here, :] = raw[piece, rows, head_dim:]
        keys_t[c] = jnp.transpose(keys[c].astype(F32)).astype(BF16)

    def exps(c, g, scores):
        parts = []
        for j in range(blocks):
            here = slice(j * block_len, (j + 1) * block_len)
            parts.append(jnp.exp(scores[here] * inv_root + shown[c, j:j + 1, :]))
        return jnp.concatenate(parts, 0)

    def summed(e):
        return jnp.sum(e.reshape(tokens // 8, 8, tokens), 0)

    key_row = lax.broadcasted_iota(jnp.int32, (tokens, tokens), 0)
    query_col = lax.broadcasted_iota(jnp.int32, (tokens, tokens), 1)

    def cols_of(g):
        return pl.ds(g * tokens, tokens)

    def masses(c, first):
        for g in range(group):
            scores = dot_nn(keys[c], q_t_ref[:, cols_of(g)])
            e = exps(c, g, scores)
            if first:
                e = jnp.where(key_row <= query_col, e, 0.0)
            expo[c, g] = e
            mass[g] = summed(e) if first else mass[g] + summed(e)

    load_chunk(0)
    masses(0, True)
    load_chunk(1)

    @pl.loop(1, chunks)
    def _(c):
        masses(c, False)
        load_chunk(c + 1)

    for g in range(group):
        total = jnp.sum(mass[g], 0, keepdims=True)
        mass[g] = jnp.broadcast_to(1.0 / total, (8, tokens))
    dq_ref[...] = jnp.zeros(dq_ref.shape, F32)
    gain_part_ref[...] = jnp.zeros(gain_part_ref.shape, F32)
    spread[...] = jnp.zeros(spread.shape, BF16)

    @pl.loop(0, chunks)
    def _(c):
        for g in range(group):
            cols = cols_of(g)
            grad_prob = dot_nn(vals[c], grad_t_ref[:, cols])
            weights = expo[c, g] * mass[g, 0:1, :]
            ds_all[:, cols] = (weights * (grad_prob - delta_ref[:, cols])).astype(BF16)
            w_all[:, cols] = weights.astype(BF16)
        dv = dot_nn(w_all[...], grad_ref[...])
        dk = dot_nn(ds_all[...], q_ref[...])
        dq_ref[...] = dq_ref[...] + dot_nn(keys_t[c], ds_all[...])
        dk = dk * inv_root
        found[c, :, 0:head_dim] = dk.astype(BF16)
        found[c, :, head_dim:] = dv.astype(BF16)
        front = jnp.sum((dk * with_cos[c]).reshape(tokens // 8, 8, head_dim), 0)
        back = jnp.sum((dk * with_sin[c]).reshape(tokens // 8, 8, head_dim), 0)
        gain_part_ref[...] = gain_part_ref[...] + front - pltpu.roll(back, head_dim // 2, 1)

    @pl.loop(0, count)
    def _(slot):
        rows = rows_of(lax.rem(slot, blocks))
        spread[plan_ref[0, slot], rows_of(plan_ref[1, slot]), :] = found[slot // blocks, rows, :]

    for piece in range(half):
        parts[piece][...] = spread[piece]
    crossed_part[...] = spread[half:]


def join_kernel(*refs):
    for i in range(refs[-1].shape[0]):
        refs[-1][i] = refs[i][...]


def merge_kernel(*refs):
    count = (len(refs) - 3) // 2
    parts, others_ref, gains_ref, before_ref = refs[:count], *refs[count:count + 3]
    outs, joined_ref, gains_out_ref = refs[count + 3:-2], *refs[-2:]
    for i in range(count):
        both = (parts[i][...].astype(F32) + others_ref[i + 1].astype(F32)).astype(BF16)
        if i < count - 1:
            outs[i][...] = both
        else:
            joined_ref[joined_ref.shape[0] - 1] = both
    for head in range(joined_ref.shape[0] - 1):
        joined_ref[head] = before_ref[head]
    gains_out_ref[...] = gains_ref[...]


def query_kernel(blocks, inv_root, kv_heads, depth_ref, t0, t1, t2, t3, gain_ref, q_ref, *refs):
    dq_refs, (k_part_refs, (out_ref, gains_ref)) = refs[:kv_heads], (refs[kv_heads:-2], refs[-2:])
    tokens = q_ref.shape[0]
    head_dim = gain_ref.shape[1]
    group = dq_refs[0].shape[1] // tokens
    cos, sin = own_tables(depth_ref, (t0, t1, t2, t3), blocks)
    gain = gain_ref[...]
    part = jnp.zeros((8, head_dim), F32)
    for head in range(group * len(dq_refs)):
        cols = pl.ds(head * head_dim, head_dim)
        rows = q_ref[:, cols].astype(F32)
        recip = inverse_rms(rows)
        normed = rows * recip
        dq = jnp.transpose(dq_refs[head // group][:, pl.ds(head % group * tokens, tokens)])
        scaled_grad = turned_back(dq, cos, sin) * inv_root
        term = scaled_grad * normed
        part = part + jnp.sum(term.reshape(tokens // 8, 8, head_dim), 0)
        inner = jnp.mean(term * gain, -1, keepdims=True)
        out_ref[:, cols] = (recip * (scaled_grad * gain - normed * inner)).astype(BF16)
    k_part = sum(ref[...] for ref in k_part_refs)
    gains = jnp.concatenate([jnp.sum(part, 0, keepdims=True), jnp.sum(k_part, 0, keepdims=True)], 0)
    gains_ref[...] = jnp.broadcast_to(gains[None], gains_ref.shape)


def summed_terms(refs, places):
    total = 0.0
    for ref, place in zip(refs, places):
        total = total + (ref[...] if place is None else ref[place]).astype(F32)
    return total


def early_kernel(places, gains_ref, *refs):
    terms, (sum_ref, gains_out_ref) = refs[:-2], refs[-2:]
    sum_ref[...] = summed_terms(terms, places)
    gains_out_ref[...] = gains_ref[...]


def key_kernel(blocks, places, depth_ref, t0, t1, t2, t3, gain_ref, k_ref, gains_ref, *refs):
    terms, (dk_out_ref, dv_out_ref, total_ref) = refs[:-3], refs[-3:]
    total_ref[...] = jnp.sum(gains_ref[...], 0)
    head_dim = gain_ref.shape[1]
    cos, sin = own_tables(depth_ref, (t0, t1, t2, t3), blocks)
    gain = gain_ref[...]
    for head, mine in enumerate(places):
        cols = pl.ds(head * head_dim, head_dim)
        rows = k_ref[:, cols].astype(F32)
        recip = inverse_rms(rows)
        normed = rows * recip
        both = summed_terms(terms[:len(mine)], mine)
        terms = terms[len(mine):]
        grad = turned_back(both[:, 0:head_dim], cos, sin) * gain
        inner = jnp.mean(grad * normed, -1, keepdims=True)
        dk_out_ref[:, cols] = (recip * (grad - normed * inner)).astype(BF16)
        dv_out_ref[:, cols] = both[:, head_dim:].astype(BF16)


class Tree:
    def __init__(self, size, cycle):
        self.size, self.cycle = size, cycle

    def order(self, index):
        return (index - 1) % self.size

    def send(self, value, target, wanted):
        pairs = []
        for tree in range(self.cycle // self.size):
            for index in range(self.size):
                if wanted(index):
                    ends = [(tree * self.size + 1 + self.order(i)) % self.cycle for i in (index, target(index))]
                    pairs.append(tuple(ends))
        return lax.ppermute(value, "ctx", pairs)

    def after(self, *pair):
        return self.order(pair[1] % self.size) > self.order(pair[0] % self.size)

    def along(self, own):
        pieces = []
        for step in range(2, self.size, 2):
            there = lambda i: (i + step) % self.size
            pieces.append(self.send(own, there, lambda i: self.after(i, there(i)) or self.after(i, there(i) ^ 1)))
        return pieces

    def across(self, value, steps, back=False):
        if back:
            return self.send(value, lambda i: i ^ 1, lambda i: any(self.after((i ^ 1) - step, i) for step in steps))
        return self.send(value, lambda i: i ^ 1, lambda i: any(self.after(i - step, i ^ 1) for step in steps))

    def home(self, value, step):
        there = lambda i: (i - step) % self.size
        return self.send(value, there, lambda i: self.after(there(i), i) or self.after(there(i), i ^ 1))


def on_device(q_raw, k_raw, values, saved_out, out_grad, q_gain, k_gain, ancestors):
    tokens = q_raw.shape[0]
    head_dim = q_gain.shape[0]
    kv_heads = k_raw.shape[1] // head_dim
    heads = q_raw.shape[1] // head_dim
    group = heads // kv_heads
    blocks = ancestors.shape[0]
    tree_blocks = ancestors.shape[1]
    block_len = tokens // blocks
    tree_dev = tree_blocks // blocks
    cycle = lax.axis_size("ctx")
    inv_root = 1.0 / math.sqrt(head_dim)
    tree = Tree(tree_dev, cycle)
    place = (lax.axis_index("ctx") - 1 + cycle) % cycle % tree_dev
    place = place.reshape(1).astype(jnp.int32)

    depth = jnp.sum((ancestors >= 0).astype(jnp.int32), 1) - 1
    total_blocks = blocks * cycle
    in_tree = jnp.where(
        ancestors >= 0, (ancestors - blocks + total_blocks) % total_blocks % tree_blocks, -1
    )
    tables = [
        jnp.asarray(table)
        for starts in (range(0, tree_blocks * block_len, block_len), range(block_len))
        for table in rope_rows(starts, head_dim)
    ]
    q_gain_row, k_gain_row = q_gain.reshape(1, head_dim), k_gain.reshape(1, head_dim)

    steps = range(2, tree_dev, 2)
    own = []
    for h in range(kv_heads):
        cols = slice(h * head_dim, (h + 1) * head_dim)
        own.append(jnp.concatenate([k_raw[:, cols], values[:, cols]], 1))

    params = pltpu.CompilerParams(vmem_limit_bytes=VMEM_LIMIT)
    smem = pl.BlockSpec(memory_space=pltpu.SMEM)
    vmem = pl.BlockSpec(memory_space=pltpu.VMEM)
    sds = jax.ShapeDtypeStruct
    slow = pl.CostEstimate(flops=4 * 10**9, bytes_accessed=16 * 1024 * 1024, transcendentals=0)
    quick = pl.CostEstimate(flops=1024, bytes_accessed=1024, transcendentals=0)

    plan = pl.pallas_call(
        lambda *refs: plan_kernel(blocks, tree_dev, *refs),
        out_shape=sds((5, tree_blocks), jnp.int32),
        in_specs=[smem, smem],
        out_specs=smem,
        cost_estimate=slow,
        name="plan",
    )(place, in_tree)

    def join(arrays, *after):
        count = len(arrays)
        return pl.pallas_call(
            join_kernel,
            out_shape=sds((count, tokens, 2 * head_dim), BF16),
            in_specs=[vmem] * count + [pl.BlockSpec(memory_space=pl.ANY)] * len(after),
            out_specs=vmem,
            compiler_params=params,
            cost_estimate=quick,
            name="join",
        )(*arrays, *after)

    rows = group * tokens
    queries = pl.pallas_call(
        lambda *refs: prep_kernel(blocks, block_len, kv_heads, *refs),
        out_shape=tuple(
            [
                sds((head_dim, rows), BF16),
                sds((rows, head_dim), BF16),
                sds((head_dim, rows), BF16),
                sds((rows, head_dim), BF16),
                sds((1, rows), F32),
            ]
            * kv_heads
        ),
        in_specs=[smem] + [vmem] * 8,
        out_specs=tuple([vmem] * (5 * kv_heads)),
        compiler_params=params,
        cost_estimate=quick,
        name="prep",
    )(depth, *tables, q_gain_row, q_raw, out_grad, saved_out)

    pieces = []
    for h in range(kv_heads):
        straight = tree.along(own[h])
        if h == 0:
            cross = [tree.across(own[h], [0])]
            crossed = tree.across(join(straight, cross[0], queries[4], queries[-1]), steps)
        else:
            cross = []
            crossed = tree.across(join([own[h], *straight]), [0, *steps])
        pieces.append([own[h], *straight, *cross, crossed])

    half = tree_dev // 2

    def attend(h):
        return pl.pallas_call(
            lambda *refs: main_kernel(blocks, block_len, tree_dev, inv_root, len(pieces[h]), *refs),
            out_shape=(
                sds((head_dim, rows), F32),
                sds((8, head_dim), F32),
                *[sds((tokens, 2 * head_dim), BF16)] * half,
                sds((half, tokens, 2 * head_dim), BF16),
            ),
            in_specs=[smem] + [vmem] * (10 + len(pieces[h])),
            out_specs=tuple([vmem] * (3 + half)),
            scratch_shapes=[
                pltpu.VMEM((tree_dev, tokens, 2 * head_dim), BF16),
                pltpu.VMEM((tree_dev + 1, tokens, head_dim), BF16),
                pltpu.VMEM((tree_dev + 1, head_dim, tokens), BF16),
                pltpu.VMEM((tree_dev + 1, tokens, head_dim), BF16),
                pltpu.VMEM((tree_dev + 1, 8 * ((blocks + 7) // 8), tokens), F32),
                pltpu.VMEM((tree_dev + 1, tokens, head_dim), F32),
                pltpu.VMEM((tree_dev + 1, tokens, head_dim), F32),
                pltpu.VMEM((tree_dev, group, tokens, tokens), F32),
                pltpu.VMEM((group, 8, tokens), F32),
                pltpu.VMEM((tokens, rows), BF16),
                pltpu.VMEM((tokens, rows), BF16),
                pltpu.VMEM((tree_dev, tokens, 2 * head_dim), BF16),
                pltpu.VMEM((tree_dev, tokens, 2 * head_dim), BF16),
            ],
            compiler_params=params,
            cost_estimate=pl.CostEstimate(
                flops=10 * group * tokens * tree_dev * tokens * head_dim,
                bytes_accessed=8 * 1024 * 1024,
                transcendentals=group * tokens * tree_dev * tokens,
            ),
            name="attend",
        )(plan, k_gain_row, *tables, *pieces[h], *queries[5 * h:5 * h + 5])

    dq, attended, k_gain_parts = [], [], []
    for h in range(kv_heads):
        dq_here, k_gain_part, *parts, crossed_part = attend(h)
        dq.append(dq_here)
        k_gain_parts.append(k_gain_part)
        attended.append((parts, crossed_part))

    everyone = cycle * lax.axis_size("heads")
    dq_raw, gains = pl.pallas_call(
        lambda *refs: query_kernel(blocks, inv_root, kv_heads, *refs),
        out_shape=(sds((tokens, heads * head_dim), BF16), sds((everyone, 2, head_dim), F32)),
        in_specs=[smem] + [vmem] * (6 + 2 * kv_heads),
        out_specs=(vmem, vmem),
        compiler_params=params,
        name="query_back",
    )(depth, *tables, q_gain_row, q_raw, *dq, *k_gain_parts)

    terms, farthest = [], []
    for h, (parts, crossed_part) in enumerate(attended):
        others = tree.across(crossed_part, [0, *steps], back=True)
        if h < kv_heads - 1:
            merged = [
                (parts[i + 1].astype(F32) + others[i + 1].astype(F32)).astype(BF16) for i in range(len(steps))
            ]
            farthest.append(merged.pop())
        else:
            *merged, joined, gains = pl.pallas_call(
                merge_kernel,
                out_shape=(
                    *[sds((tokens, 2 * head_dim), BF16)] * (len(steps) - 1),
                    sds((kv_heads, tokens, 2 * head_dim), BF16),
                    sds(gains.shape, F32),
                ),
                in_specs=[vmem] * (len(steps) + 3),
                out_specs=tuple([vmem] * (len(steps) + 1)),
                compiler_params=params,
                name="merge",
            )(*parts[1:], others, gains, jnp.stack(farthest))
            joined = tree.home(joined, steps[-1])
        mine = [(parts[0], None), (others, 0)]
        terms.append(mine + [(tree.home(both, step), None) for both, step in zip(merged, steps)])
    for h in range(kv_heads):
        if h < kv_heads - 1:
            arrays, places = zip(*terms[h])
            early, gains = pl.pallas_call(
                lambda *refs: early_kernel(places, *refs),
                out_shape=(sds((tokens, 2 * head_dim), F32), sds(gains.shape, F32)),
                in_specs=[vmem] * (1 + len(arrays)),
                out_specs=(vmem, vmem),
                compiler_params=params,
                cost_estimate=slow,
                name="early",
            )(gains, *arrays)
            terms[h] = [(early, None)]
        terms[h].append((joined, h))
    gains = lax.all_to_all(gains, ("ctx", "heads"), 0, 0)

    arrays = [array for mine in terms for array, _ in mine]
    places = [[place for _, place in mine] for mine in terms]
    dk_raw, dv, total = pl.pallas_call(
        lambda *refs: key_kernel(blocks, places, *refs),
        out_shape=(sds(k_raw.shape, BF16), sds(k_raw.shape, BF16), sds(gains.shape[1:], F32)),
        in_specs=[smem] + [vmem] * (7 + len(arrays)),
        out_specs=(vmem, vmem, vmem),
        compiler_params=params,
        name="key_back",
    )(depth, *tables, k_gain_row, k_raw, gains, *arrays)
    return (dq_raw, dk_raw, dv, total[0], total[1])


def solution(mesh):
    split = P("ctx", "heads")
    return jax.shard_map(
        on_device,
        mesh=mesh,
        in_specs=(split, split, split, split, split, P(), P(), P("ctx", None)),
        out_specs=(split, split, split, P(), P()),
        check_vma=False,
    )
```

```python
import math

import jax
import jax.numpy as jnp
import numpy as np
from jax import lax
from jax.experimental import pallas as pl
from jax.experimental.pallas import tpu as pltpu
from jax.sharding import PartitionSpec as P

ROPE_BASE = 1000000.0
EPS = 1e-06
HIDDEN = -100000.0
VMEM_LIMIT = 16 * 1024 * 1024
ATTEND_VMEM_LIMIT = 34 * 1024 * 1024
F32 = jnp.float32
BF16 = jnp.bfloat16


def rope_rows(starts, head_dim):
    half = head_dim // 2
    frequency = np.exp(
        np.arange(half, dtype=np.float32) * np.float32(-2.0 * math.log(ROPE_BASE) / head_dim)
    ).astype(np.float32)
    angles = np.asarray(starts, np.float32)[:, None] * frequency[None, :]
    cos = np.cos(angles.astype(np.float64)).astype(np.float32)
    sin = np.sin(angles.astype(np.float64)).astype(np.float32)
    return np.concatenate([cos, cos], 1), np.concatenate([-sin, sin], 1)


def block_tables(depth, tables):
    start_cos, start_sin, offset_cos, offset_sin = tables
    cos, sin = start_cos[pl.ds(depth, 1), :], start_sin[pl.ds(depth, 1), :]
    both_cos = cos * offset_cos[...] - sin * offset_sin[...]
    both_sin = sin * offset_cos[...] + cos * offset_sin[...]
    return both_cos, both_sin


def turned(rows, cos, sin):
    return rows * cos + pltpu.roll(rows, rows.shape[-1] // 2, 1) * sin


def turned_back(rows, cos, sin):
    return rows * cos - pltpu.roll(rows, rows.shape[-1] // 2, 1) * sin


def inverse_rms(rows):
    return lax.rsqrt(jnp.mean(rows * rows, -1, keepdims=True) + EPS)


def own_tables(depth_ref, tables, blocks):
    parts = [block_tables(depth_ref[a], tables) for a in range(blocks)]
    return jnp.concatenate([p[0] for p in parts], 0), jnp.concatenate([p[1] for p in parts], 0)


def dot_nn(lhs, rhs):
    return lax.dot_general(lhs, rhs, (((1,), (0,)), ((), ())), preferred_element_type=F32)


def plan_kernel(blocks, tree_dev, place_ref, anc_ref, plan_ref):
    slots = tree_dev * blocks
    place = place_ref[0]
    here = jnp.where(place + 1 == tree_dev, 0, place + 1)
    for row in range(4):
        for i in range(slots):
            plan_ref[row, i] = 0
    count = jnp.int32(blocks)
    steps = [jnp.int32(0)] * blocks
    for b in range(slots):
        bits = jnp.int32(0)
        depth = jnp.int32(0)
        for a in range(blocks):
            hit = anc_ref[a, jnp.minimum(steps[a], slots - 1)] == b
            bits = bits | jnp.where(hit, 1 << a, 0)
            depth = jnp.where(hit, steps[a], depth)
            steps[a] = steps[a] + jnp.where(hit, 1, 0)
        own = place == b // blocks
        slot = jnp.where(own, b % blocks, jnp.minimum(count, slots - 1))
        there = (b // blocks + 1) % tree_dev
        odd = jnp.bitwise_and(here + there, 1)
        gap = jnp.bitwise_xor(here, odd) - there
        gap = jnp.where(gap < 0, gap + tree_dev, gap)
        plan_ref[0, slot] = odd * (tree_dev // 2) + lax.shift_right_logical(gap, 1)
        plan_ref[1, slot] = b % blocks
        plan_ref[2, slot] = depth
        plan_ref[3, slot] = bits
        count = count + jnp.where(own | (bits == 0), 0, 1)
    for i in range(slots):
        plan_ref[4, i] = count


def prep_kernel(blocks, block_len, kv_heads, depth_ref, t0, t1, t2, t3, gain_ref, q_ref, grad_ref, out_ref, *outs):
    tokens = q_ref.shape[0]
    head_dim = gain_ref.shape[1]
    cos, sin = own_tables(depth_ref, (t0, t1, t2, t3), blocks)
    gain = gain_ref[...]
    group = q_ref.shape[1] // head_dim // kv_heads
    for head in range(group * kv_heads):
        g = head % group
        q_t_ref, q_rot_ref, grad_t_ref, grad_heads_ref, delta_ref = outs[5 * (head // group):][:5]
        cols = pl.ds(head * head_dim, head_dim)
        here = pl.ds(g * tokens, tokens)
        rows = q_ref[:, cols].astype(F32)
        rotated = turned(rows * inverse_rms(rows) * gain, cos, sin)
        q_rot_ref[here, :] = rotated.astype(BF16)
        q_t_ref[:, here] = jnp.transpose(rotated).astype(BF16)
        grad = grad_ref[:, cols]
        grad_heads_ref[here, :] = grad
        grad_rows = jnp.transpose(grad.astype(F32))
        grad_t_ref[:, here] = grad_rows.astype(BF16)
        product = grad_rows * jnp.transpose(out_ref[:, cols].astype(F32))
        delta_ref[:, here] = jnp.sum(product, 0, keepdims=True)


def main_kernel(blocks, block_len, tree_dev, inv_root, n_in, *refs):
    plan_ref, gain_ref = refs[:2]
    tables = refs[2:6]
    half = tree_dev // 2
    pieces, crossed_ref = refs[6:5 + n_in], refs[5 + n_in]
    q_t_ref, q_ref, grad_t_ref, grad_ref, delta_ref = refs[6 + n_in:11 + n_in]
    dq_ref, gain_part_ref = refs[11 + n_in:13 + n_in]
    parts = refs[13 + n_in:13 + n_in + half]
    crossed_part, raw, keys, keys_t, vals, shown, with_cos, with_sin, expo, mass, w_all, ds_all, found, spread = refs[
        13 + n_in + half:]
    head_dim = gain_ref.shape[1]
    tokens = raw.shape[1]
    group = q_ref.shape[0] // tokens
    count = plan_ref[4, 0]
    chunks = (count + blocks - 1) // blocks
    gain = gain_ref[...]
    for i, piece in enumerate(pieces):
        raw[i] = piece[...]
    raw[len(pieces):] = crossed_ref[...]
    query_block = lax.broadcasted_iota(jnp.int32, (1, tokens), 1) // block_len

    def rows_of(start):
        return pl.ds(pl.multiple_of(start * block_len, block_len), block_len)

    def load_chunk(c):
        for j in range(blocks):
            slot = jnp.minimum(c * blocks + j, tree_dev * blocks - 1)
            piece = plan_ref[0, slot]
            rows = rows_of(plan_ref[1, slot])
            cos, sin = block_tables(plan_ref[2, slot], tables)
            unit = raw[piece, rows, 0:head_dim].astype(F32)
            unit = unit * inverse_rms(unit)
            here = pl.ds(j * block_len, block_len)
            with_cos[c, here, :] = unit * cos
            with_sin[c, here, :] = pltpu.roll(unit * sin, head_dim // 2, 1)
            keys[c, here, :] = turned(unit * gain, cos, sin).astype(BF16)
            bits = jnp.where(c * blocks + j < count, plan_ref[3, slot], 0)
            row = jnp.zeros((1, tokens), F32)
            for a in range(blocks):
                seen = lax.rem(lax.shift_right_logical(bits, a), 2)
                row = jnp.where((query_block == a) & (seen == 0), HIDDEN, row)
            shown[c, j:j + 1, :] = row
            vals[c, here, :] = raw[piece, rows, head_dim:]
        keys_t[c] = jnp.transpose(keys[c].astype(F32)).astype(BF16)

    def exps(c, g, scores):
        parts = []
        for j in range(blocks):
            here = slice(j * block_len, (j + 1) * block_len)
            parts.append(jnp.exp(scores[here] * inv_root + shown[c, j:j + 1, :]))
        return jnp.concatenate(parts, 0)

    def summed(e):
        return jnp.sum(e.reshape(tokens // 8, 8, tokens), 0)

    key_row = lax.broadcasted_iota(jnp.int32, (tokens, tokens), 0)
    query_col = lax.broadcasted_iota(jnp.int32, (tokens, tokens), 1)

    def cols_of(g):
        return pl.ds(g * tokens, tokens)

    def masses(c, first):
        for g in range(group):
            scores = dot_nn(keys[c], q_t_ref[:, cols_of(g)])
            e = exps(c, g, scores)
            if first:
                e = jnp.where(key_row <= query_col, e, 0.0)
            expo[c, g] = e
            mass[g] = summed(e) if first else mass[g] + summed(e)

    load_chunk(0)
    masses(0, True)
    load_chunk(1)

    @pl.loop(1, chunks)
    def _(c):
        masses(c, False)
        load_chunk(c + 1)

    for g in range(group):
        total = jnp.sum(mass[g], 0, keepdims=True)
        mass[g] = jnp.broadcast_to(1.0 / total, (8, tokens))
    dq_ref[...] = jnp.zeros(dq_ref.shape, F32)
    gain_part_ref[...] = jnp.zeros(gain_part_ref.shape, F32)
    spread[...] = jnp.zeros(spread.shape, BF16)

    @pl.loop(0, chunks)
    def _(c):
        for g in range(group):
            cols = cols_of(g)
            grad_prob = dot_nn(vals[c], grad_t_ref[:, cols])
            weights = expo[c, g] * mass[g, 0:1, :]
            ds_all[:, cols] = (weights * (grad_prob - delta_ref[:, cols])).astype(BF16)
            w_all[:, cols] = weights.astype(BF16)
        dv = dot_nn(w_all[...], grad_ref[...])
        dk = dot_nn(ds_all[...], q_ref[...])
        dq_ref[...] = dq_ref[...] + dot_nn(keys_t[c], ds_all[...])
        dk = dk * inv_root
        found[c, :, 0:head_dim] = dk.astype(BF16)
        found[c, :, head_dim:] = dv.astype(BF16)
        front = jnp.sum((dk * with_cos[c]).reshape(tokens // 8, 8, head_dim), 0)
        back = jnp.sum((dk * with_sin[c]).reshape(tokens // 8, 8, head_dim), 0)
        gain_part_ref[...] = gain_part_ref[...] + front - pltpu.roll(back, head_dim // 2, 1)

    @pl.loop(0, count)
    def _(slot):
        rows = rows_of(lax.rem(slot, blocks))
        spread[plan_ref[0, slot], rows_of(plan_ref[1, slot]), :] = found[slot // blocks, rows, :]

    for piece in range(half):
        parts[piece][...] = spread[piece]
    crossed_part[...] = spread[half:]


def join_kernel(*refs):
    for i in range(refs[-1].shape[0]):
        refs[-1][i] = refs[i][...]


def merge_kernel(*refs):
    count = (len(refs) - 3) // 2
    parts, others_ref, gains_ref, before_ref = refs[:count], *refs[count:count + 3]
    outs, joined_ref, gains_out_ref = refs[count + 3:-2], *refs[-2:]
    for i in range(count):
        both = (parts[i][...].astype(F32) + others_ref[i + 1].astype(F32)).astype(BF16)
        if i < count - 1:
            outs[i][...] = both
        else:
            joined_ref[joined_ref.shape[0] - 1] = both
    for head in range(joined_ref.shape[0] - 1):
        joined_ref[head] = before_ref[head]
    gains_out_ref[...] = gains_ref[...]


def query_kernel(blocks, inv_root, kv_heads, depth_ref, t0, t1, t2, t3, gain_ref, q_ref, *refs):
    dq_refs, (k_part_refs, (out_ref, gains_ref)) = refs[:kv_heads], (refs[kv_heads:-2], refs[-2:])
    tokens = q_ref.shape[0]
    head_dim = gain_ref.shape[1]
    group = dq_refs[0].shape[1] // tokens
    cos, sin = own_tables(depth_ref, (t0, t1, t2, t3), blocks)
    gain = gain_ref[...]
    part = jnp.zeros((8, head_dim), F32)
    for head in range(group * len(dq_refs)):
        cols = pl.ds(head * head_dim, head_dim)
        rows = q_ref[:, cols].astype(F32)
        recip = inverse_rms(rows)
        normed = rows * recip
        dq = jnp.transpose(dq_refs[head // group][:, pl.ds(head % group * tokens, tokens)])
        scaled_grad = turned_back(dq, cos, sin) * inv_root
        term = scaled_grad * normed
        part = part + jnp.sum(term.reshape(tokens // 8, 8, head_dim), 0)
        inner = jnp.mean(term * gain, -1, keepdims=True)
        out_ref[:, cols] = (recip * (scaled_grad * gain - normed * inner)).astype(BF16)
    k_part = sum(ref[...] for ref in k_part_refs)
    gains = jnp.concatenate([jnp.sum(part, 0, keepdims=True), jnp.sum(k_part, 0, keepdims=True)], 0)
    gains_ref[...] = jnp.broadcast_to(gains[None], gains_ref.shape)


def summed_terms(refs, places):
    total = 0.0
    for ref, place in zip(refs, places):
        total = total + (ref[...] if place is None else ref[place]).astype(F32)
    return total


def early_kernel(places, gains_ref, *refs):
    terms, (sum_ref, gains_out_ref) = refs[:-2], refs[-2:]
    sum_ref[...] = summed_terms(terms, places)
    gains_out_ref[...] = gains_ref[...]


def key_kernel(blocks, places, depth_ref, t0, t1, t2, t3, gain_ref, k_ref, gains_ref, *refs):
    terms, (dk_out_ref, dv_out_ref, total_ref) = refs[:-3], refs[-3:]
    total_ref[...] = jnp.sum(gains_ref[...], 0)
    head_dim = gain_ref.shape[1]
    cos, sin = own_tables(depth_ref, (t0, t1, t2, t3), blocks)
    gain = gain_ref[...]
    for head, mine in enumerate(places):
        cols = pl.ds(head * head_dim, head_dim)
        rows = k_ref[:, cols].astype(F32)
        recip = inverse_rms(rows)
        normed = rows * recip
        both = summed_terms(terms[:len(mine)], mine)
        terms = terms[len(mine):]
        grad = turned_back(both[:, 0:head_dim], cos, sin) * gain
        inner = jnp.mean(grad * normed, -1, keepdims=True)
        dk_out_ref[:, cols] = (recip * (grad - normed * inner)).astype(BF16)
        dv_out_ref[:, cols] = both[:, head_dim:].astype(BF16)


class Tree:
    def __init__(self, size, cycle):
        self.size, self.cycle = size, cycle

    def order(self, index):
        return (index - 1) % self.size

    def send(self, value, target, wanted):
        pairs = []
        for tree in range(self.cycle // self.size):
            for index in range(self.size):
                if wanted(index):
                    ends = [(tree * self.size + 1 + self.order(i)) % self.cycle for i in (index, target(index))]
                    pairs.append(tuple(ends))
        return lax.ppermute(value, "ctx", pairs)

    def after(self, *pair):
        return self.order(pair[1] % self.size) > self.order(pair[0] % self.size)

    def along(self, own):
        pieces = []
        for step in range(2, self.size, 2):
            there = lambda i: (i + step) % self.size
            pieces.append(self.send(own, there, lambda i: self.after(i, there(i)) or self.after(i, there(i) ^ 1)))
        return pieces

    def across(self, value, steps, back=False):
        if back:
            return self.send(value, lambda i: i ^ 1, lambda i: any(self.after((i ^ 1) - step, i) for step in steps))
        return self.send(value, lambda i: i ^ 1, lambda i: any(self.after(i - step, i ^ 1) for step in steps))

    def home(self, value, step):
        there = lambda i: (i - step) % self.size
        return self.send(value, there, lambda i: self.after(there(i), i) or self.after(there(i), i ^ 1))


def on_device(q_raw, k_raw, values, saved_out, out_grad, q_gain, k_gain, ancestors):
    tokens = q_raw.shape[0]
    head_dim = q_gain.shape[0]
    kv_heads = k_raw.shape[1] // head_dim
    heads = q_raw.shape[1] // head_dim
    group = heads // kv_heads
    blocks = ancestors.shape[0]
    tree_blocks = ancestors.shape[1]
    block_len = tokens // blocks
    tree_dev = tree_blocks // blocks
    cycle = lax.axis_size("ctx")
    inv_root = 1.0 / math.sqrt(head_dim)
    tree = Tree(tree_dev, cycle)
    place = (lax.axis_index("ctx") - 1 + cycle) % cycle % tree_dev
    place = place.reshape(1).astype(jnp.int32)

    depth = jnp.sum((ancestors >= 0).astype(jnp.int32), 1) - 1
    total_blocks = blocks * cycle
    in_tree = jnp.where(
        ancestors >= 0, (ancestors - blocks + total_blocks) % total_blocks % tree_blocks, -1
    )
    tables = [
        jnp.asarray(table)
        for starts in (range(0, tree_blocks * block_len, block_len), range(block_len))
        for table in rope_rows(starts, head_dim)
    ]
    q_gain_row, k_gain_row = q_gain.reshape(1, head_dim), k_gain.reshape(1, head_dim)

    steps = range(2, tree_dev, 2)
    own = []
    for h in range(kv_heads):
        cols = slice(h * head_dim, (h + 1) * head_dim)
        own.append(jnp.concatenate([k_raw[:, cols], values[:, cols]], 1))

    params = pltpu.CompilerParams(vmem_limit_bytes=VMEM_LIMIT)
    smem = pl.BlockSpec(memory_space=pltpu.SMEM)
    vmem = pl.BlockSpec(memory_space=pltpu.VMEM)
    sds = jax.ShapeDtypeStruct
    slow = pl.CostEstimate(flops=4 * 10**9, bytes_accessed=16 * 1024 * 1024, transcendentals=0)
    quick = pl.CostEstimate(flops=1024, bytes_accessed=1024, transcendentals=0)

    plan = pl.pallas_call(
        lambda *refs: plan_kernel(blocks, tree_dev, *refs),
        out_shape=sds((5, tree_blocks), jnp.int32),
        in_specs=[smem, smem],
        out_specs=smem,
        cost_estimate=quick,
        name="plan",
    )(place, in_tree)

    def join(arrays, *after):
        count = len(arrays)
        return pl.pallas_call(
            join_kernel,
            out_shape=sds((count, tokens, 2 * head_dim), BF16),
            in_specs=[vmem] * count + [pl.BlockSpec(memory_space=pl.ANY)] * len(after),
            out_specs=vmem,
            compiler_params=params,
            cost_estimate=quick,
            name="join",
        )(*arrays, *after)

    rows = group * tokens
    queries = pl.pallas_call(
        lambda *refs: prep_kernel(blocks, block_len, kv_heads, *refs),
        out_shape=tuple(
            [
                sds((head_dim, rows), BF16),
                sds((rows, head_dim), BF16),
                sds((head_dim, rows), BF16),
                sds((rows, head_dim), BF16),
                sds((1, rows), F32),
            ]
            * kv_heads
        ),
        in_specs=[smem] + [vmem] * 8,
        out_specs=tuple([vmem] * (5 * kv_heads)),
        compiler_params=params,
        cost_estimate=slow,
        name="prep",
    )(depth, *tables, q_gain_row, q_raw, out_grad, saved_out)

    pieces = []
    for h in range(kv_heads):
        straight = tree.along(own[h])
        if h == 0:
            cross = [tree.across(own[h], [0])]
            crossed = tree.across(join(straight, cross[0], plan), steps)
        else:
            cross = []
            crossed = tree.across(join([own[h], *straight], queries[4], queries[-1]), [0, *steps])
        pieces.append([own[h], *straight, *cross, crossed])

    half = tree_dev // 2

    def attend(h):
        return pl.pallas_call(
            lambda *refs: main_kernel(blocks, block_len, tree_dev, inv_root, len(pieces[h]), *refs),
            out_shape=(
                sds((head_dim, rows), F32),
                sds((8, head_dim), F32),
                *[sds((tokens, 2 * head_dim), BF16)] * half,
                sds((half, tokens, 2 * head_dim), BF16),
            ),
            in_specs=[smem] + [vmem] * (10 + len(pieces[h])),
            out_specs=tuple([vmem] * (3 + half)),
            scratch_shapes=[
                pltpu.VMEM((tree_dev, tokens, 2 * head_dim), BF16),
                pltpu.VMEM((tree_dev + 1, tokens, head_dim), BF16),
                pltpu.VMEM((tree_dev + 1, head_dim, tokens), BF16),
                pltpu.VMEM((tree_dev + 1, tokens, head_dim), BF16),
                pltpu.VMEM((tree_dev + 1, 8 * ((blocks + 7) // 8), tokens), F32),
                pltpu.VMEM((tree_dev + 1, tokens, head_dim), F32),
                pltpu.VMEM((tree_dev + 1, tokens, head_dim), F32),
                pltpu.VMEM((tree_dev, group, tokens, tokens), F32),
                pltpu.VMEM((group, 8, tokens), F32),
                pltpu.VMEM((tokens, rows), BF16),
                pltpu.VMEM((tokens, rows), BF16),
                pltpu.VMEM((tree_dev, tokens, 2 * head_dim), BF16),
                pltpu.VMEM((tree_dev, tokens, 2 * head_dim), BF16),
            ],
            compiler_params=pltpu.CompilerParams(vmem_limit_bytes=ATTEND_VMEM_LIMIT),
            cost_estimate=pl.CostEstimate(
                flops=10 * group * tokens * tree_dev * tokens * head_dim,
                bytes_accessed=8 * 1024 * 1024,
                transcendentals=group * tokens * tree_dev * tokens,
            ),
            name="attend",
        )(plan, k_gain_row, *tables, *pieces[h], *queries[5 * h:5 * h + 5])

    dq, attended, k_gain_parts = [], [], []
    for h in range(kv_heads):
        dq_here, k_gain_part, *parts, crossed_part = attend(h)
        dq.append(dq_here)
        k_gain_parts.append(k_gain_part)
        attended.append((parts, crossed_part))

    everyone = cycle * lax.axis_size("heads")
    dq_raw, gains = pl.pallas_call(
        lambda *refs: query_kernel(blocks, inv_root, kv_heads, *refs),
        out_shape=(sds((tokens, heads * head_dim), BF16), sds((everyone, 2, head_dim), F32)),
        in_specs=[smem] + [vmem] * (6 + 2 * kv_heads),
        out_specs=(vmem, vmem),
        compiler_params=params,
        name="query_back",
    )(depth, *tables, q_gain_row, q_raw, *dq, *k_gain_parts)

    terms, farthest = [], []
    for h, (parts, crossed_part) in enumerate(attended):
        others = tree.across(crossed_part, [0, *steps], back=True)
        if h < kv_heads - 1:
            merged = [
                (parts[i + 1].astype(F32) + others[i + 1].astype(F32)).astype(BF16) for i in range(len(steps))
            ]
            farthest.append(merged.pop())
        else:
            *merged, joined, gains = pl.pallas_call(
                merge_kernel,
                out_shape=(
                    *[sds((tokens, 2 * head_dim), BF16)] * (len(steps) - 1),
                    sds((kv_heads, tokens, 2 * head_dim), BF16),
                    sds(gains.shape, F32),
                ),
                in_specs=[vmem] * (len(steps) + 3),
                out_specs=tuple([vmem] * (len(steps) + 1)),
                compiler_params=params,
                name="merge",
            )(*parts[1:], others, gains, jnp.stack(farthest))
            joined = tree.home(joined, steps[-1])
        mine = [(parts[0], None), (others, 0)]
        terms.append(mine + [(tree.home(both, step), None) for both, step in zip(merged, steps)])
    for h in range(kv_heads):
        if h < kv_heads - 1:
            arrays, places = zip(*terms[h])
            early, gains = pl.pallas_call(
                lambda *refs: early_kernel(places, *refs),
                out_shape=(sds((tokens, 2 * head_dim), F32), sds(gains.shape, F32)),
                in_specs=[vmem] * (1 + len(arrays)),
                out_specs=(vmem, vmem),
                compiler_params=params,
                cost_estimate=slow,
                name="early",
            )(gains, *arrays)
            terms[h] = [(early, None)]
        terms[h].append((joined, h))
    gains = lax.all_to_all(gains, ("ctx", "heads"), 0, 0)

    arrays = [array for mine in terms for array, _ in mine]
    places = [[place for _, place in mine] for mine in terms]
    dk_raw, dv, total = pl.pallas_call(
        lambda *refs: key_kernel(blocks, places, *refs),
        out_shape=(sds(k_raw.shape, BF16), sds(k_raw.shape, BF16), sds(gains.shape[1:], F32)),
        in_specs=[smem] + [vmem] * (7 + len(arrays)),
        out_specs=(vmem, vmem, vmem),
        compiler_params=params,
        name="key_back",
    )(depth, *tables, k_gain_row, k_raw, gains, *arrays)
    return (dq_raw, dk_raw, dv, total[0], total[1])


def solution(mesh):
    split = P("ctx", "heads")
    return jax.shard_map(
        on_device,
        mesh=mesh,
        in_specs=(split, split, split, split, split, P(), P(), P("ctx", None)),
        out_specs=(split, split, split, P(), P()),
        check_vma=False,
    )
```

```python
import math

import jax
import jax.numpy as jnp
import numpy as np
from jax import lax
from jax.experimental import pallas as pl
from jax.experimental.pallas import tpu as pltpu
from jax.sharding import PartitionSpec as P

ROPE_BASE = 1000000.0
EPS = 1e-06
HIDDEN = -100000.0
VMEM_LIMIT = 16 * 1024 * 1024
ATTEND_VMEM_LIMIT = 34 * 1024 * 1024
F32 = jnp.float32
BF16 = jnp.bfloat16


def rope_rows(starts, head_dim):
    half = head_dim // 2
    frequency = np.exp(
        np.arange(half, dtype=np.float32) * np.float32(-2.0 * math.log(ROPE_BASE) / head_dim)
    ).astype(np.float32)
    angles = np.asarray(starts, np.float32)[:, None] * frequency[None, :]
    cos = np.cos(angles.astype(np.float64)).astype(np.float32)
    sin = np.sin(angles.astype(np.float64)).astype(np.float32)
    return np.concatenate([cos, cos], 1), np.concatenate([-sin, sin], 1)


def block_tables(depth, tables):
    start_cos, start_sin, offset_cos, offset_sin = tables
    cos, sin = start_cos[pl.ds(depth, 1), :], start_sin[pl.ds(depth, 1), :]
    both_cos = cos * offset_cos[...] - sin * offset_sin[...]
    both_sin = sin * offset_cos[...] + cos * offset_sin[...]
    return both_cos, both_sin


def turned(rows, cos, sin):
    return rows * cos + pltpu.roll(rows, rows.shape[-1] // 2, 1) * sin


def turned_back(rows, cos, sin):
    return rows * cos - pltpu.roll(rows, rows.shape[-1] // 2, 1) * sin


def inverse_rms(rows):
    return lax.rsqrt(jnp.mean(rows * rows, -1, keepdims=True) + EPS)


def own_tables(depth_ref, tables, blocks):
    parts = [block_tables(depth_ref[a], tables) for a in range(blocks)]
    return jnp.concatenate([p[0] for p in parts], 0), jnp.concatenate([p[1] for p in parts], 0)


def dot_nn(lhs, rhs):
    return lax.dot_general(lhs, rhs, (((1,), (0,)), ((), ())), preferred_element_type=F32)


def plan_kernel(blocks, tree_dev, place_ref, anc_ref, plan_ref):
    slots = tree_dev * blocks
    place = place_ref[0]
    here = jnp.where(place + 1 == tree_dev, 0, place + 1)
    for row in range(4):
        for i in range(slots):
            plan_ref[row, i] = 0
    count = jnp.int32(blocks)
    steps = [jnp.int32(0)] * blocks
    for b in range(slots):
        bits = jnp.int32(0)
        depth = jnp.int32(0)
        for a in range(blocks):
            hit = anc_ref[a, jnp.minimum(steps[a], slots - 1)] == b
            bits = bits | jnp.where(hit, 1 << a, 0)
            depth = jnp.where(hit, steps[a], depth)
            steps[a] = steps[a] + jnp.where(hit, 1, 0)
        own = place == b // blocks
        slot = jnp.where(own, b % blocks, jnp.minimum(count, slots - 1))
        there = (b // blocks + 1) % tree_dev
        odd = jnp.bitwise_and(here + there, 1)
        gap = jnp.bitwise_xor(here, odd) - there
        gap = jnp.where(gap < 0, gap + tree_dev, gap)
        plan_ref[0, slot] = odd * (tree_dev // 2) + lax.shift_right_logical(gap, 1)
        plan_ref[1, slot] = b % blocks
        plan_ref[2, slot] = depth
        plan_ref[3, slot] = bits
        count = count + jnp.where(own | (bits == 0), 0, 1)
    for i in range(slots):
        plan_ref[4, i] = count


def prep_kernel(blocks, block_len, kv_heads, depth_ref, t0, t1, t2, t3, gain_ref, q_ref, grad_ref, out_ref, *outs):
    tokens = q_ref.shape[0]
    head_dim = gain_ref.shape[1]
    cos, sin = own_tables(depth_ref, (t0, t1, t2, t3), blocks)
    gain = gain_ref[...]
    group = q_ref.shape[1] // head_dim // kv_heads
    for head in range(group * kv_heads):
        g = head % group
        q_t_ref, q_rot_ref, grad_t_ref, grad_heads_ref, delta_ref = outs[5 * (head // group):][:5]
        cols = pl.ds(head * head_dim, head_dim)
        here = pl.ds(g * tokens, tokens)
        rows = q_ref[:, cols].astype(F32)
        rotated = turned(rows * inverse_rms(rows) * gain, cos, sin)
        q_rot_ref[here, :] = rotated.astype(BF16)
        q_t_ref[:, here] = jnp.transpose(rotated).astype(BF16)
        grad = grad_ref[:, cols]
        grad_heads_ref[here, :] = grad
        grad_rows = jnp.transpose(grad.astype(F32))
        grad_t_ref[:, here] = grad_rows.astype(BF16)
        product = grad_rows * jnp.transpose(out_ref[:, cols].astype(F32))
        delta_ref[:, here] = jnp.sum(product, 0, keepdims=True)


def main_kernel(blocks, block_len, tree_dev, inv_root, n_in, *refs):
    plan_ref, gain_ref = refs[:2]
    tables = refs[2:6]
    half = tree_dev // 2
    pieces, crossed_ref = refs[6:5 + n_in], refs[5 + n_in]
    q_t_ref, q_ref, grad_t_ref, grad_ref, delta_ref = refs[6 + n_in:11 + n_in]
    dq_ref, gain_part_ref = refs[11 + n_in:13 + n_in]
    parts = refs[13 + n_in:13 + n_in + half]
    crossed_part, raw, keys, keys_t, vals, shown, with_cos, with_sin, expo, mass, w_even, ds_even, w_odd, ds_odd, found, spread = refs[
        13 + n_in + half:]
    head_dim = gain_ref.shape[1]
    tokens = raw.shape[1]
    group = q_ref.shape[0] // tokens
    count = plan_ref[4, 0]
    chunks = (count + blocks - 1) // blocks
    gain = gain_ref[...]
    for i, piece in enumerate(pieces):
        raw[i] = piece[...]
    raw[len(pieces):] = crossed_ref[...]
    query_block = lax.broadcasted_iota(jnp.int32, (1, tokens), 1) // block_len

    def rows_of(start):
        return pl.ds(pl.multiple_of(start * block_len, block_len), block_len)

    def load_chunk(c):
        for j in range(blocks):
            slot = jnp.minimum(c * blocks + j, tree_dev * blocks - 1)
            piece = plan_ref[0, slot]
            rows = rows_of(plan_ref[1, slot])
            cos, sin = block_tables(plan_ref[2, slot], tables)
            unit = raw[piece, rows, 0:head_dim].astype(F32)
            unit = unit * inverse_rms(unit)
            here = pl.ds(j * block_len, block_len)
            with_cos[c, here, :] = unit * cos
            with_sin[c, here, :] = pltpu.roll(unit * sin, head_dim // 2, 1)
            keys[c, here, :] = turned(unit * gain, cos, sin).astype(BF16)
            bits = jnp.where(c * blocks + j < count, plan_ref[3, slot], 0)
            row = jnp.zeros((1, tokens), F32)
            for a in range(blocks):
                seen = lax.rem(lax.shift_right_logical(bits, a), 2)
                row = jnp.where((query_block == a) & (seen == 0), HIDDEN, row)
            shown[c, j:j + 1, :] = row
            vals[c, here, :] = raw[piece, rows, head_dim:]
        keys_t[c] = jnp.transpose(keys[c].astype(F32)).astype(BF16)

    def exps(c, g, scores):
        parts = []
        for j in range(blocks):
            here = slice(j * block_len, (j + 1) * block_len)
            parts.append(jnp.exp(scores[here] * inv_root + shown[c, j:j + 1, :]))
        return jnp.concatenate(parts, 0)

    def summed(e):
        return jnp.sum(e.reshape(tokens // 8, 8, tokens), 0)

    key_row = lax.broadcasted_iota(jnp.int32, (tokens, tokens), 0)
    query_col = lax.broadcasted_iota(jnp.int32, (tokens, tokens), 1)

    def cols_of(g):
        return pl.ds(g * tokens, tokens)

    def masses(c, first):
        for g in range(group):
            scores = dot_nn(keys[c], q_t_ref[:, cols_of(g)])
            e = exps(c, g, scores)
            if first:
                e = jnp.where(key_row <= query_col, e, 0.0)
            expo[c, g] = e
            mass[g] = summed(e) if first else mass[g] + summed(e)

    load_chunk(0)
    masses(0, True)
    load_chunk(1)

    @pl.loop(1, chunks)
    def _(c):
        masses(c, False)
        load_chunk(c + 1)

    for g in range(group):
        total = jnp.sum(mass[g], 0, keepdims=True)
        mass[g] = jnp.broadcast_to(1.0 / total, (8, tokens))
    dq_ref[...] = jnp.zeros(dq_ref.shape, F32)
    gain_part_ref[...] = jnp.zeros(gain_part_ref.shape, F32)
    spread[...] = jnp.zeros(spread.shape, BF16)

    def weigh(c, heads, w_all, ds_all):
        for g in heads:
            cols = cols_of(g)
            grad_prob = dot_nn(vals[c], grad_t_ref[:, cols])
            weights = expo[c, g] * mass[g, 0:1, :]
            ds_all[:, cols] = (weights * (grad_prob - delta_ref[:, cols])).astype(BF16)
            w_all[:, cols] = weights.astype(BF16)

    def value_products(c, w_all):
        found[c, :, head_dim:] = dot_nn(w_all[...], grad_ref[...]).astype(BF16)

    def key_products(c, ds_all):
        dk = dot_nn(ds_all[...], q_ref[...]) * inv_root
        found[c, :, 0:head_dim] = dk.astype(BF16)
        front = jnp.sum((dk * with_cos[c]).reshape(tokens // 8, 8, head_dim), 0)
        back = jnp.sum((dk * with_sin[c]).reshape(tokens // 8, 8, head_dim), 0)
        gain_part_ref[...] = gain_part_ref[...] + front - pltpu.roll(back, head_dim // 2, 1)

    def query_products(c, ds_all):
        dq_ref[...] = dq_ref[...] + dot_nn(keys_t[c], ds_all[...])

    thirds = [range(group * i // 3, group * (i + 1) // 3) for i in range(3)]
    buffers = ((w_even, ds_even), (w_odd, ds_odd))

    def step(c, now, later):
        ahead = jnp.minimum(c + 1, chunks - 1)
        value_products(c, now[0])
        weigh(ahead, thirds[0], *later)
        key_products(c, now[1])
        weigh(ahead, thirds[1], *later)
        query_products(c, now[1])
        weigh(ahead, thirds[2], *later)

    weigh(0, range(group), *buffers[0])

    @pl.loop(0, chunks // 2)
    def _(pair):
        step(2 * pair, buffers[0], buffers[1])
        step(2 * pair + 1, buffers[1], buffers[0])

    @pl.when(lax.rem(chunks, 2) == 1)
    def _():
        value_products(chunks - 1, w_even)
        key_products(chunks - 1, ds_even)
        query_products(chunks - 1, ds_even)

    @pl.loop(0, count)
    def _(slot):
        rows = rows_of(lax.rem(slot, blocks))
        spread[plan_ref[0, slot], rows_of(plan_ref[1, slot]), :] = found[slot // blocks, rows, :]

    for piece in range(half):
        parts[piece][...] = spread[piece]
    crossed_part[...] = spread[half:]


def join_kernel(*refs):
    for i in range(refs[-1].shape[0]):
        refs[-1][i] = refs[i][...]


def merge_kernel(*refs):
    count = (len(refs) - 3) // 2
    parts, others_ref, gains_ref, before_ref = refs[:count], *refs[count:count + 3]
    outs, joined_ref, gains_out_ref = refs[count + 3:-2], *refs[-2:]
    for i in range(count):
        both = (parts[i][...].astype(F32) + others_ref[i + 1].astype(F32)).astype(BF16)
        if i < count - 1:
            outs[i][...] = both
        else:
            joined_ref[joined_ref.shape[0] - 1] = both
    for head in range(joined_ref.shape[0] - 1):
        joined_ref[head] = before_ref[head]
    gains_out_ref[...] = gains_ref[...]


def query_kernel(blocks, inv_root, kv_heads, depth_ref, t0, t1, t2, t3, gain_ref, q_ref, *refs):
    dq_refs, (k_part_refs, (out_ref, gains_ref)) = refs[:kv_heads], (refs[kv_heads:-2], refs[-2:])
    tokens = q_ref.shape[0]
    head_dim = gain_ref.shape[1]
    group = dq_refs[0].shape[1] // tokens
    cos, sin = own_tables(depth_ref, (t0, t1, t2, t3), blocks)
    gain = gain_ref[...]
    part = jnp.zeros((8, head_dim), F32)
    for head in range(group * len(dq_refs)):
        cols = pl.ds(head * head_dim, head_dim)
        rows = q_ref[:, cols].astype(F32)
        recip = inverse_rms(rows)
        normed = rows * recip
        dq = jnp.transpose(dq_refs[head // group][:, pl.ds(head % group * tokens, tokens)])
        scaled_grad = turned_back(dq, cos, sin) * inv_root
        term = scaled_grad * normed
        part = part + jnp.sum(term.reshape(tokens // 8, 8, head_dim), 0)
        inner = jnp.mean(term * gain, -1, keepdims=True)
        out_ref[:, cols] = (recip * (scaled_grad * gain - normed * inner)).astype(BF16)
    k_part = sum(ref[...] for ref in k_part_refs)
    gains = jnp.concatenate([jnp.sum(part, 0, keepdims=True), jnp.sum(k_part, 0, keepdims=True)], 0)
    gains_ref[...] = jnp.broadcast_to(gains[None], gains_ref.shape)


def summed_terms(refs, places):
    total = 0.0
    for ref, place in zip(refs, places):
        total = total + (ref[...] if place is None else ref[place]).astype(F32)
    return total


def early_kernel(places, gains_ref, *refs):
    terms, (sum_ref, gains_out_ref) = refs[:-2], refs[-2:]
    sum_ref[...] = summed_terms(terms, places)
    gains_out_ref[...] = gains_ref[...]


def key_kernel(blocks, places, depth_ref, t0, t1, t2, t3, gain_ref, k_ref, gains_ref, *refs):
    terms, (dk_out_ref, dv_out_ref, total_ref) = refs[:-3], refs[-3:]
    total_ref[...] = jnp.sum(gains_ref[...], 0)
    head_dim = gain_ref.shape[1]
    cos, sin = own_tables(depth_ref, (t0, t1, t2, t3), blocks)
    gain = gain_ref[...]
    for head, mine in enumerate(places):
        cols = pl.ds(head * head_dim, head_dim)
        rows = k_ref[:, cols].astype(F32)
        recip = inverse_rms(rows)
        normed = rows * recip
        both = summed_terms(terms[:len(mine)], mine)
        terms = terms[len(mine):]
        grad = turned_back(both[:, 0:head_dim], cos, sin) * gain
        inner = jnp.mean(grad * normed, -1, keepdims=True)
        dk_out_ref[:, cols] = (recip * (grad - normed * inner)).astype(BF16)
        dv_out_ref[:, cols] = both[:, head_dim:].astype(BF16)


class Tree:
    def __init__(self, size, cycle):
        self.size, self.cycle = size, cycle

    def order(self, index):
        return (index - 1) % self.size

    def send(self, value, target, wanted):
        pairs = []
        for tree in range(self.cycle // self.size):
            for index in range(self.size):
                if wanted(index):
                    ends = [(tree * self.size + 1 + self.order(i)) % self.cycle for i in (index, target(index))]
                    pairs.append(tuple(ends))
        return lax.ppermute(value, "ctx", pairs)

    def after(self, *pair):
        return self.order(pair[1] % self.size) > self.order(pair[0] % self.size)

    def along(self, own):
        pieces = []
        for step in range(2, self.size, 2):
            there = lambda i: (i + step) % self.size
            pieces.append(self.send(own, there, lambda i: self.after(i, there(i)) or self.after(i, there(i) ^ 1)))
        return pieces

    def across(self, value, steps, back=False):
        if back:
            return self.send(value, lambda i: i ^ 1, lambda i: any(self.after((i ^ 1) - step, i) for step in steps))
        return self.send(value, lambda i: i ^ 1, lambda i: any(self.after(i - step, i ^ 1) for step in steps))

    def home(self, value, step):
        there = lambda i: (i - step) % self.size
        return self.send(value, there, lambda i: self.after(there(i), i) or self.after(there(i), i ^ 1))


def on_device(q_raw, k_raw, values, saved_out, out_grad, q_gain, k_gain, ancestors):
    tokens = q_raw.shape[0]
    head_dim = q_gain.shape[0]
    kv_heads = k_raw.shape[1] // head_dim
    heads = q_raw.shape[1] // head_dim
    group = heads // kv_heads
    blocks = ancestors.shape[0]
    tree_blocks = ancestors.shape[1]
    block_len = tokens // blocks
    tree_dev = tree_blocks // blocks
    cycle = lax.axis_size("ctx")
    inv_root = 1.0 / math.sqrt(head_dim)
    tree = Tree(tree_dev, cycle)
    place = (lax.axis_index("ctx") - 1 + cycle) % cycle % tree_dev
    place = place.reshape(1).astype(jnp.int32)

    depth = jnp.sum((ancestors >= 0).astype(jnp.int32), 1) - 1
    total_blocks = blocks * cycle
    in_tree = jnp.where(
        ancestors >= 0, (ancestors - blocks + total_blocks) % total_blocks % tree_blocks, -1
    )
    tables = [
        jnp.asarray(table)
        for starts in (range(0, tree_blocks * block_len, block_len), range(block_len))
        for table in rope_rows(starts, head_dim)
    ]
    q_gain_row, k_gain_row = q_gain.reshape(1, head_dim), k_gain.reshape(1, head_dim)

    steps = range(2, tree_dev, 2)
    own = []
    for h in range(kv_heads):
        cols = slice(h * head_dim, (h + 1) * head_dim)
        own.append(jnp.concatenate([k_raw[:, cols], values[:, cols]], 1))

    params = pltpu.CompilerParams(vmem_limit_bytes=VMEM_LIMIT)
    smem = pl.BlockSpec(memory_space=pltpu.SMEM)
    vmem = pl.BlockSpec(memory_space=pltpu.VMEM)
    sds = jax.ShapeDtypeStruct
    slow = pl.CostEstimate(flops=4 * 10**9, bytes_accessed=16 * 1024 * 1024, transcendentals=0)
    quick = pl.CostEstimate(flops=1024, bytes_accessed=1024, transcendentals=0)

    plan = pl.pallas_call(
        lambda *refs: plan_kernel(blocks, tree_dev, *refs),
        out_shape=sds((5, tree_blocks), jnp.int32),
        in_specs=[smem, smem],
        out_specs=smem,
        cost_estimate=quick,
        name="plan",
    )(place, in_tree)

    def join(arrays, *after):
        count = len(arrays)
        return pl.pallas_call(
            join_kernel,
            out_shape=sds((count, tokens, 2 * head_dim), BF16),
            in_specs=[vmem] * count + [pl.BlockSpec(memory_space=pl.ANY)] * len(after),
            out_specs=vmem,
            compiler_params=params,
            cost_estimate=quick,
            name="join",
        )(*arrays, *after)

    rows = group * tokens
    queries = pl.pallas_call(
        lambda *refs: prep_kernel(blocks, block_len, kv_heads, *refs),
        out_shape=tuple(
            [
                sds((head_dim, rows), BF16),
                sds((rows, head_dim), BF16),
                sds((head_dim, rows), BF16),
                sds((rows, head_dim), BF16),
                sds((1, rows), F32),
            ]
            * kv_heads
        ),
        in_specs=[smem] + [vmem] * 8,
        out_specs=tuple([vmem] * (5 * kv_heads)),
        compiler_params=params,
        cost_estimate=slow,
        name="prep",
    )(depth, *tables, q_gain_row, q_raw, out_grad, saved_out)

    pieces = []
    for h in range(kv_heads):
        straight = tree.along(own[h])
        if h == 0:
            cross = [tree.across(own[h], [0])]
            crossed = tree.across(join(straight, cross[0], plan), steps)
        else:
            cross = []
            crossed = tree.across(join([own[h], *straight], queries[4], queries[-1]), [0, *steps])
        pieces.append([own[h], *straight, *cross, crossed])

    half = tree_dev // 2

    def attend(h):
        return pl.pallas_call(
            lambda *refs: main_kernel(blocks, block_len, tree_dev, inv_root, len(pieces[h]), *refs),
            out_shape=(
                sds((head_dim, rows), F32),
                sds((8, head_dim), F32),
                *[sds((tokens, 2 * head_dim), BF16)] * half,
                sds((half, tokens, 2 * head_dim), BF16),
            ),
            in_specs=[smem] + [vmem] * (10 + len(pieces[h])),
            out_specs=tuple([vmem] * (3 + half)),
            scratch_shapes=[
                pltpu.VMEM((tree_dev, tokens, 2 * head_dim), BF16),
                pltpu.VMEM((tree_dev + 1, tokens, head_dim), BF16),
                pltpu.VMEM((tree_dev + 1, head_dim, tokens), BF16),
                pltpu.VMEM((tree_dev + 1, tokens, head_dim), BF16),
                pltpu.VMEM((tree_dev + 1, 8 * ((blocks + 7) // 8), tokens), F32),
                pltpu.VMEM((tree_dev + 1, tokens, head_dim), F32),
                pltpu.VMEM((tree_dev + 1, tokens, head_dim), F32),
                pltpu.VMEM((tree_dev, group, tokens, tokens), F32),
                pltpu.VMEM((group, 8, tokens), F32),
                *[pltpu.VMEM((tokens, rows), BF16)] * 4,
                pltpu.VMEM((tree_dev, tokens, 2 * head_dim), BF16),
                pltpu.VMEM((tree_dev, tokens, 2 * head_dim), BF16),
            ],
            compiler_params=pltpu.CompilerParams(vmem_limit_bytes=ATTEND_VMEM_LIMIT),
            cost_estimate=pl.CostEstimate(
                flops=10 * group * tokens * tree_dev * tokens * head_dim,
                bytes_accessed=8 * 1024 * 1024,
                transcendentals=group * tokens * tree_dev * tokens,
            ),
            name="attend",
        )(plan, k_gain_row, *tables, *pieces[h], *queries[5 * h:5 * h + 5])

    dq, attended, k_gain_parts = [], [], []
    for h in range(kv_heads):
        dq_here, k_gain_part, *parts, crossed_part = attend(h)
        dq.append(dq_here)
        k_gain_parts.append(k_gain_part)
        attended.append((parts, crossed_part))

    everyone = cycle * lax.axis_size("heads")
    dq_raw, gains = pl.pallas_call(
        lambda *refs: query_kernel(blocks, inv_root, kv_heads, *refs),
        out_shape=(sds((tokens, heads * head_dim), BF16), sds((everyone, 2, head_dim), F32)),
        in_specs=[smem] + [vmem] * (6 + 2 * kv_heads),
        out_specs=(vmem, vmem),
        compiler_params=params,
        name="query_back",
    )(depth, *tables, q_gain_row, q_raw, *dq, *k_gain_parts)

    terms, farthest = [], []
    for h, (parts, crossed_part) in enumerate(attended):
        others = tree.across(crossed_part, [0, *steps], back=True)
        if h < kv_heads - 1:
            merged = [
                (parts[i + 1].astype(F32) + others[i + 1].astype(F32)).astype(BF16) for i in range(len(steps))
            ]
            farthest.append(merged.pop())
        else:
            *merged, joined, gains = pl.pallas_call(
                merge_kernel,
                out_shape=(
                    *[sds((tokens, 2 * head_dim), BF16)] * (len(steps) - 1),
                    sds((kv_heads, tokens, 2 * head_dim), BF16),
                    sds(gains.shape, F32),
                ),
                in_specs=[vmem] * (len(steps) + 3),
                out_specs=tuple([vmem] * (len(steps) + 1)),
                compiler_params=params,
                name="merge",
            )(*parts[1:], others, gains, jnp.stack(farthest))
            joined = tree.home(joined, steps[-1])
        mine = [(parts[0], None), (others, 0)]
        terms.append(mine + [(tree.home(both, step), None) for both, step in zip(merged, steps)])
    for h in range(kv_heads):
        if h < kv_heads - 1:
            arrays, places = zip(*terms[h])
            early, gains = pl.pallas_call(
                lambda *refs: early_kernel(places, *refs),
                out_shape=(sds((tokens, 2 * head_dim), F32), sds(gains.shape, F32)),
                in_specs=[vmem] * (1 + len(arrays)),
                out_specs=(vmem, vmem),
                compiler_params=params,
                cost_estimate=slow,
                name="early",
            )(gains, *arrays)
            terms[h] = [(early, None)]
        terms[h].append((joined, h))
    gains = lax.all_to_all(gains, ("ctx", "heads"), 0, 0)

    arrays = [array for mine in terms for array, _ in mine]
    places = [[place for _, place in mine] for mine in terms]
    dk_raw, dv, total = pl.pallas_call(
        lambda *refs: key_kernel(blocks, places, *refs),
        out_shape=(sds(k_raw.shape, BF16), sds(k_raw.shape, BF16), sds(gains.shape[1:], F32)),
        in_specs=[smem] + [vmem] * (7 + len(arrays)),
        out_specs=(vmem, vmem, vmem),
        compiler_params=params,
        name="key_back",
    )(depth, *tables, k_gain_row, k_raw, gains, *arrays)
    return (dq_raw, dk_raw, dv, total[0], total[1])


def solution(mesh):
    split = P("ctx", "heads")
    return jax.shard_map(
        on_device,
        mesh=mesh,
        in_specs=(split, split, split, split, split, P(), P(), P("ctx", None)),
        out_specs=(split, split, split, P(), P()),
        check_vma=False,
    )
```

```python
import math

import jax
import jax.numpy as jnp
import numpy as np
from jax import lax
from jax.experimental import pallas as pl
from jax.experimental.pallas import tpu as pltpu
from jax.sharding import PartitionSpec as P

ROPE_BASE = 1000000.0
EPS = 1e-06
HIDDEN = -100000.0
VMEM_LIMIT = 16 * 1024 * 1024
ATTEND_VMEM_LIMIT = 34 * 1024 * 1024
F32 = jnp.float32
BF16 = jnp.bfloat16


def rope_rows(starts, head_dim):
    half = head_dim // 2
    frequency = np.exp(
        np.arange(half, dtype=np.float32) * np.float32(-2.0 * math.log(ROPE_BASE) / head_dim)
    ).astype(np.float32)
    angles = np.asarray(starts, np.float32)[:, None] * frequency[None, :]
    cos = np.cos(angles.astype(np.float64)).astype(np.float32)
    sin = np.sin(angles.astype(np.float64)).astype(np.float32)
    return np.concatenate([cos, cos], 1), np.concatenate([-sin, sin], 1)


def block_tables(depth, tables):
    start_cos, start_sin, offset_cos, offset_sin = tables
    cos, sin = start_cos[pl.ds(depth, 1), :], start_sin[pl.ds(depth, 1), :]
    both_cos = cos * offset_cos[...] - sin * offset_sin[...]
    both_sin = sin * offset_cos[...] + cos * offset_sin[...]
    return both_cos, both_sin


def turned(rows, cos, sin):
    return rows * cos + pltpu.roll(rows, rows.shape[-1] // 2, 1) * sin


def turned_back(rows, cos, sin):
    return rows * cos - pltpu.roll(rows, rows.shape[-1] // 2, 1) * sin


def inverse_rms(rows):
    return lax.rsqrt(jnp.mean(rows * rows, -1, keepdims=True) + EPS)


def own_tables(depth_ref, tables, blocks):
    parts = [block_tables(depth_ref[a], tables) for a in range(blocks)]
    return jnp.concatenate([p[0] for p in parts], 0), jnp.concatenate([p[1] for p in parts], 0)


def dot_nn(lhs, rhs):
    return lax.dot_general(lhs, rhs, (((1,), (0,)), ((), ())), preferred_element_type=F32)


def plan_kernel(blocks, tree_dev, place_ref, anc_ref, plan_ref):
    slots = tree_dev * blocks
    place = place_ref[0]
    here = jnp.where(place + 1 == tree_dev, 0, place + 1)
    for row in range(4):
        for i in range(slots):
            plan_ref[row, i] = 0
    count = jnp.int32(blocks)
    steps = [jnp.int32(0)] * blocks
    for b in range(slots):
        bits = jnp.int32(0)
        depth = jnp.int32(0)
        for a in range(blocks):
            hit = anc_ref[a, jnp.minimum(steps[a], slots - 1)] == b
            bits = bits | jnp.where(hit, 1 << a, 0)
            depth = jnp.where(hit, steps[a], depth)
            steps[a] = steps[a] + jnp.where(hit, 1, 0)
        own = place == b // blocks
        slot = jnp.where(own, b % blocks, jnp.minimum(count, slots - 1))
        there = (b // blocks + 1) % tree_dev
        odd = jnp.bitwise_and(here + there, 1)
        gap = jnp.bitwise_xor(here, odd) - there
        gap = jnp.where(gap < 0, gap + tree_dev, gap)
        plan_ref[0, slot] = odd * (tree_dev // 2) + lax.shift_right_logical(gap, 1)
        plan_ref[1, slot] = b % blocks
        plan_ref[2, slot] = depth
        plan_ref[3, slot] = bits
        count = count + jnp.where(own | (bits == 0), 0, 1)
    for i in range(slots):
        plan_ref[4, i] = count


def prep_kernel(blocks, block_len, kv_heads, depth_ref, t0, t1, t2, t3, gain_ref, q_ref, grad_ref, out_ref, *outs):
    tokens = q_ref.shape[0]
    head_dim = gain_ref.shape[1]
    cos, sin = own_tables(depth_ref, (t0, t1, t2, t3), blocks)
    gain = gain_ref[...]
    group = q_ref.shape[1] // head_dim // kv_heads
    for head in range(group * kv_heads):
        g = head % group
        q_t_ref, q_rot_ref, grad_t_ref, grad_heads_ref, delta_ref = outs[5 * (head // group):][:5]
        cols = pl.ds(head * head_dim, head_dim)
        here = pl.ds(g * tokens, tokens)
        rows = q_ref[:, cols].astype(F32)
        rotated = turned(rows * inverse_rms(rows) * gain, cos, sin)
        q_rot_ref[here, :] = rotated.astype(BF16)
        q_t_ref[:, here] = jnp.transpose(rotated).astype(BF16)
        grad = grad_ref[:, cols]
        grad_heads_ref[here, :] = grad
        grad_rows = jnp.transpose(grad.astype(F32))
        grad_t_ref[:, here] = grad_rows.astype(BF16)
        product = grad_rows * jnp.transpose(out_ref[:, cols].astype(F32))
        delta_ref[:, here] = jnp.sum(product, 0, keepdims=True)


def main_kernel(blocks, block_len, tree_dev, inv_root, n_in, last, *refs):
    plan_ref, gain_ref = refs[:2]
    tables = refs[2:6]
    half = tree_dev // 2
    pieces, crossed_ref = refs[6:5 + n_in], refs[5 + n_in]
    q_t_ref, q_ref, grad_t_ref, grad_ref, delta_ref = refs[6 + n_in:11 + n_in]
    dq_ref, gain_part_ref = refs[11 + n_in:13 + n_in]
    parts = refs[13 + n_in:13 + n_in + half + last]
    crossed_part, raw, keys, keys_t, vals, shown, with_cos, with_sin, expo, mass, w_even, ds_even, w_odd, ds_odd, found, spread = refs[
        13 + n_in + half + last:]
    head_dim = gain_ref.shape[1]
    tokens = raw.shape[1]
    group = q_ref.shape[0] // tokens
    count = plan_ref[4, 0]
    chunks = (count + blocks - 1) // blocks
    gain = gain_ref[...]
    for i, piece in enumerate(pieces):
        raw[i] = piece[...]
    raw[len(pieces):] = crossed_ref[...]
    query_block = lax.broadcasted_iota(jnp.int32, (1, tokens), 1) // block_len

    def rows_of(start):
        return pl.ds(pl.multiple_of(start * block_len, block_len), block_len)

    def load_chunk(c):
        for j in range(blocks):
            slot = jnp.minimum(c * blocks + j, tree_dev * blocks - 1)
            piece = plan_ref[0, slot]
            rows = rows_of(plan_ref[1, slot])
            cos, sin = block_tables(plan_ref[2, slot], tables)
            unit = raw[piece, rows, 0:head_dim].astype(F32)
            unit = unit * inverse_rms(unit)
            here = pl.ds(j * block_len, block_len)
            with_cos[c, here, :] = unit * cos
            with_sin[c, here, :] = pltpu.roll(unit * sin, head_dim // 2, 1)
            keys[c, here, :] = turned(unit * gain, cos, sin).astype(BF16)
            bits = jnp.where(c * blocks + j < count, plan_ref[3, slot], 0)
            row = jnp.zeros((1, tokens), F32)
            for a in range(blocks):
                seen = lax.rem(lax.shift_right_logical(bits, a), 2)
                row = jnp.where((query_block == a) & (seen == 0), HIDDEN, row)
            shown[c, j:j + 1, :] = row
            vals[c, here, :] = raw[piece, rows, head_dim:]
        keys_t[c] = jnp.transpose(keys[c].astype(F32)).astype(BF16)

    def exps(c, g, scores):
        parts = []
        for j in range(blocks):
            here = slice(j * block_len, (j + 1) * block_len)
            parts.append(jnp.exp(scores[here] * inv_root + shown[c, j:j + 1, :]))
        return jnp.concatenate(parts, 0)

    def summed(e):
        return jnp.sum(e.reshape(tokens // 8, 8, tokens), 0)

    key_row = lax.broadcasted_iota(jnp.int32, (tokens, tokens), 0)
    query_col = lax.broadcasted_iota(jnp.int32, (tokens, tokens), 1)

    def cols_of(g):
        return pl.ds(g * tokens, tokens)

    def masses(c, first):
        for g in range(group):
            scores = dot_nn(keys[c], q_t_ref[:, cols_of(g)])
            e = exps(c, g, scores)
            if first:
                e = jnp.where(key_row <= query_col, e, 0.0)
            expo[c, g] = e
            mass[g] = summed(e) if first else mass[g] + summed(e)

    load_chunk(0)
    masses(0, True)
    load_chunk(1)

    @pl.loop(1, chunks)
    def _(c):
        masses(c, False)
        load_chunk(c + 1)

    for g in range(group):
        total = jnp.sum(mass[g], 0, keepdims=True)
        mass[g] = jnp.broadcast_to(1.0 / total, (8, tokens))
    dq_ref[...] = jnp.zeros(dq_ref.shape, F32)
    gain_part_ref[...] = jnp.zeros(gain_part_ref.shape, F32)
    spread[...] = jnp.zeros(spread.shape, BF16)

    def weigh(c, heads, w_all, ds_all):
        for g in heads:
            cols = cols_of(g)
            grad_prob = dot_nn(vals[c], grad_t_ref[:, cols])
            weights = expo[c, g] * mass[g, 0:1, :]
            ds_all[:, cols] = (weights * (grad_prob - delta_ref[:, cols])).astype(BF16)
            w_all[:, cols] = weights.astype(BF16)

    def value_products(c, w_all):
        found[c, :, head_dim:] = dot_nn(w_all[...], grad_ref[...]).astype(BF16)

    def key_products(c, ds_all):
        dk = dot_nn(ds_all[...], q_ref[...]) * inv_root
        found[c, :, 0:head_dim] = dk.astype(BF16)
        front = jnp.sum((dk * with_cos[c]).reshape(tokens // 8, 8, head_dim), 0)
        back = jnp.sum((dk * with_sin[c]).reshape(tokens // 8, 8, head_dim), 0)
        gain_part_ref[...] = gain_part_ref[...] + front - pltpu.roll(back, head_dim // 2, 1)

    def query_products(c, ds_all):
        dq_ref[...] = dq_ref[...] + dot_nn(keys_t[c], ds_all[...])

    thirds = [range(group * i // 3, group * (i + 1) // 3) for i in range(3)]
    buffers = ((w_even, ds_even), (w_odd, ds_odd))

    def products(c, now):
        value_products(c, now[0])
        key_products(c, now[1])
        query_products(c, now[1])

    def step(c, now, later):
        value_products(c, now[0])
        weigh(c + 1, thirds[0], *later)
        key_products(c, now[1])
        weigh(c + 1, thirds[1], *later)
        query_products(c, now[1])
        weigh(c + 1, thirds[2], *later)

    weigh(0, range(group), *buffers[0])

    @pl.loop(0, (chunks - 1) // 2)
    def _(pair):
        step(2 * pair, buffers[0], buffers[1])
        step(2 * pair + 1, buffers[1], buffers[0])

    odd_count = lax.rem(chunks, 2) == 1

    @pl.when(odd_count)
    def _():
        products(chunks - 1, buffers[0])

    @pl.when(jnp.logical_not(odd_count))
    def _():
        step(chunks - 2, buffers[0], buffers[1])
        products(chunks - 1, buffers[1])

    @pl.loop(0, count)
    def _(slot):
        rows = rows_of(lax.rem(slot, blocks))
        spread[plan_ref[0, slot], rows_of(plan_ref[1, slot]), :] = found[slot // blocks, rows, :]

    for piece in range(half + last):
        parts[piece][...] = spread[piece]
    crossed_part[...] = spread[half + last:]


def join_kernel(*refs):
    for i in range(refs[-1].shape[0]):
        refs[-1][i] = refs[i][...]


def merge_kernel(*refs):
    count = (len(refs) - 5) // 2
    parts, (near_ref, others_ref, gains_ref, before_ref) = refs[:count], refs[count:count + 4]
    outs, (near_out_ref, joined_ref, gains_out_ref) = refs[count + 4:-3], refs[-3:]
    for i in range(count):
        both = (parts[i][...].astype(F32) + others_ref[i].astype(F32)).astype(BF16)
        if i < count - 1:
            outs[i][...] = both
        else:
            joined_ref[joined_ref.shape[0] - 1] = both
    for head in range(joined_ref.shape[0] - 1):
        joined_ref[head] = before_ref[head]
    near_out_ref[...] = near_ref[...]
    gains_out_ref[...] = gains_ref[...]


def query_kernel(blocks, inv_root, kv_heads, depth_ref, t0, t1, t2, t3, gain_ref, q_ref, *refs):
    dq_refs, (k_part_refs, (out_ref, gains_ref)) = refs[:kv_heads], (refs[kv_heads:-2], refs[-2:])
    tokens = q_ref.shape[0]
    head_dim = gain_ref.shape[1]
    group = dq_refs[0].shape[1] // tokens
    cos, sin = own_tables(depth_ref, (t0, t1, t2, t3), blocks)
    gain = gain_ref[...]
    part = jnp.zeros((8, head_dim), F32)
    for head in range(group * len(dq_refs)):
        cols = pl.ds(head * head_dim, head_dim)
        rows = q_ref[:, cols].astype(F32)
        recip = inverse_rms(rows)
        normed = rows * recip
        dq = jnp.transpose(dq_refs[head // group][:, pl.ds(head % group * tokens, tokens)])
        scaled_grad = turned_back(dq, cos, sin) * inv_root
        term = scaled_grad * normed
        part = part + jnp.sum(term.reshape(tokens // 8, 8, head_dim), 0)
        inner = jnp.mean(term * gain, -1, keepdims=True)
        out_ref[:, cols] = (recip * (scaled_grad * gain - normed * inner)).astype(BF16)
    k_part = sum(ref[...] for ref in k_part_refs)
    gains = jnp.concatenate([jnp.sum(part, 0, keepdims=True), jnp.sum(k_part, 0, keepdims=True)], 0)
    gains_ref[...] = jnp.broadcast_to(gains[None], gains_ref.shape)


def summed_terms(refs, places):
    total = 0.0
    for ref, place in zip(refs, places):
        total = total + (ref[...] if place is None else ref[place]).astype(F32)
    return total


def early_kernel(places, gains_ref, *refs):
    terms, (sum_ref, gains_out_ref) = refs[:-2], refs[-2:]
    sum_ref[...] = summed_terms(terms, places)
    gains_out_ref[...] = gains_ref[...]


def key_kernel(blocks, places, depth_ref, t0, t1, t2, t3, gain_ref, k_ref, gains_ref, *refs):
    terms, (dk_out_ref, dv_out_ref, total_ref) = refs[:-3], refs[-3:]
    total_ref[...] = jnp.sum(gains_ref[...], 0)
    head_dim = gain_ref.shape[1]
    cos, sin = own_tables(depth_ref, (t0, t1, t2, t3), blocks)
    gain = gain_ref[...]
    for head, mine in enumerate(places):
        cols = pl.ds(head * head_dim, head_dim)
        rows = k_ref[:, cols].astype(F32)
        recip = inverse_rms(rows)
        normed = rows * recip
        both = summed_terms(terms[:len(mine)], mine)
        terms = terms[len(mine):]
        grad = turned_back(both[:, 0:head_dim], cos, sin) * gain
        inner = jnp.mean(grad * normed, -1, keepdims=True)
        dk_out_ref[:, cols] = (recip * (grad - normed * inner)).astype(BF16)
        dv_out_ref[:, cols] = both[:, head_dim:].astype(BF16)


class Tree:
    def __init__(self, size, cycle):
        self.size, self.cycle = size, cycle

    def order(self, index):
        return (index - 1) % self.size

    def send(self, value, target, wanted):
        pairs = []
        for tree in range(self.cycle // self.size):
            for index in range(self.size):
                if wanted(index):
                    ends = [(tree * self.size + 1 + self.order(i)) % self.cycle for i in (index, target(index))]
                    pairs.append(tuple(ends))
        return lax.ppermute(value, "ctx", pairs)

    def after(self, *pair):
        return self.order(pair[1] % self.size) > self.order(pair[0] % self.size)

    def along(self, own):
        pieces = []
        for step in range(2, self.size, 2):
            there = lambda i: (i + step) % self.size
            pieces.append(self.send(own, there, lambda i: self.after(i, there(i)) or self.after(i, there(i) ^ 1)))
        return pieces

    def across(self, value, steps, back=False):
        if back:
            return self.send(value, lambda i: i ^ 1, lambda i: any(self.after((i ^ 1) - step, i) for step in steps))
        return self.send(value, lambda i: i ^ 1, lambda i: any(self.after(i - step, i ^ 1) for step in steps))

    def home(self, value, step):
        there = lambda i: (i - step) % self.size
        return self.send(value, there, lambda i: self.after(there(i), i) or self.after(there(i), i ^ 1))


def on_device(q_raw, k_raw, values, saved_out, out_grad, q_gain, k_gain, ancestors):
    tokens = q_raw.shape[0]
    head_dim = q_gain.shape[0]
    kv_heads = k_raw.shape[1] // head_dim
    heads = q_raw.shape[1] // head_dim
    group = heads // kv_heads
    blocks = ancestors.shape[0]
    tree_blocks = ancestors.shape[1]
    block_len = tokens // blocks
    tree_dev = tree_blocks // blocks
    cycle = lax.axis_size("ctx")
    inv_root = 1.0 / math.sqrt(head_dim)
    tree = Tree(tree_dev, cycle)
    place = (lax.axis_index("ctx") - 1 + cycle) % cycle % tree_dev
    place = place.reshape(1).astype(jnp.int32)

    depth = jnp.sum((ancestors >= 0).astype(jnp.int32), 1) - 1
    total_blocks = blocks * cycle
    in_tree = jnp.where(
        ancestors >= 0, (ancestors - blocks + total_blocks) % total_blocks % tree_blocks, -1
    )
    tables = [
        jnp.asarray(table)
        for starts in (range(0, tree_blocks * block_len, block_len), range(block_len))
        for table in rope_rows(starts, head_dim)
    ]
    q_gain_row, k_gain_row = q_gain.reshape(1, head_dim), k_gain.reshape(1, head_dim)

    steps = range(2, tree_dev, 2)
    own = []
    for h in range(kv_heads):
        cols = slice(h * head_dim, (h + 1) * head_dim)
        own.append(jnp.concatenate([k_raw[:, cols], values[:, cols]], 1))

    params = pltpu.CompilerParams(vmem_limit_bytes=VMEM_LIMIT)
    smem = pl.BlockSpec(memory_space=pltpu.SMEM)
    vmem = pl.BlockSpec(memory_space=pltpu.VMEM)
    sds = jax.ShapeDtypeStruct
    slow = pl.CostEstimate(flops=4 * 10**9, bytes_accessed=16 * 1024 * 1024, transcendentals=0)
    quick = pl.CostEstimate(flops=1024, bytes_accessed=1024, transcendentals=0)

    plan = pl.pallas_call(
        lambda *refs: plan_kernel(blocks, tree_dev, *refs),
        out_shape=sds((5, tree_blocks), jnp.int32),
        in_specs=[smem, smem],
        out_specs=smem,
        cost_estimate=quick,
        name="plan",
    )(place, in_tree)

    def join(arrays, *after):
        count = len(arrays)
        return pl.pallas_call(
            join_kernel,
            out_shape=sds((count, tokens, 2 * head_dim), BF16),
            in_specs=[vmem] * count + [pl.BlockSpec(memory_space=pl.ANY)] * len(after),
            out_specs=vmem,
            compiler_params=params,
            cost_estimate=quick,
            name="join",
        )(*arrays, *after)

    rows = group * tokens
    queries = pl.pallas_call(
        lambda *refs: prep_kernel(blocks, block_len, kv_heads, *refs),
        out_shape=tuple(
            [
                sds((head_dim, rows), BF16),
                sds((rows, head_dim), BF16),
                sds((head_dim, rows), BF16),
                sds((rows, head_dim), BF16),
                sds((1, rows), F32),
            ]
            * kv_heads
        ),
        in_specs=[smem] + [vmem] * 8,
        out_specs=tuple([vmem] * (5 * kv_heads)),
        compiler_params=params,
        cost_estimate=slow,
        name="prep",
    )(depth, *tables, q_gain_row, q_raw, out_grad, saved_out)

    pieces = []
    for h in range(kv_heads):
        straight = tree.along(own[h])
        if h == 0:
            cross = [tree.across(own[h], [0])]
            crossed = tree.across(join(straight, cross[0], plan), steps)
        else:
            cross = []
            crossed = tree.across(join([own[h], *straight], queries[4], queries[-1]), [0, *steps])
        pieces.append([own[h], *straight, *cross, crossed])

    half = tree_dev // 2

    def attend(h):
        last = h == kv_heads - 1
        return pl.pallas_call(
            lambda *refs: main_kernel(blocks, block_len, tree_dev, inv_root, len(pieces[h]), last, *refs),
            out_shape=(
                sds((head_dim, rows), F32),
                sds((8, head_dim), F32),
                *[sds((tokens, 2 * head_dim), BF16)] * (half + last),
                sds((half - last, tokens, 2 * head_dim), BF16),
            ),
            in_specs=[smem] + [vmem] * (10 + len(pieces[h])),
            out_specs=tuple([vmem] * (3 + half + last)),
            scratch_shapes=[
                pltpu.VMEM((tree_dev, tokens, 2 * head_dim), BF16),
                pltpu.VMEM((tree_dev + 1, tokens, head_dim), BF16),
                pltpu.VMEM((tree_dev + 1, head_dim, tokens), BF16),
                pltpu.VMEM((tree_dev + 1, tokens, head_dim), BF16),
                pltpu.VMEM((tree_dev + 1, 8 * ((blocks + 7) // 8), tokens), F32),
                pltpu.VMEM((tree_dev + 1, tokens, head_dim), F32),
                pltpu.VMEM((tree_dev + 1, tokens, head_dim), F32),
                pltpu.VMEM((tree_dev, group, tokens, tokens), F32),
                pltpu.VMEM((group, 8, tokens), F32),
                *[pltpu.VMEM((tokens, rows), BF16)] * 4,
                pltpu.VMEM((tree_dev, tokens, 2 * head_dim), BF16),
                pltpu.VMEM((tree_dev, tokens, 2 * head_dim), BF16),
            ],
            compiler_params=pltpu.CompilerParams(vmem_limit_bytes=ATTEND_VMEM_LIMIT),
            cost_estimate=pl.CostEstimate(
                flops=10 * group * tokens * tree_dev * tokens * head_dim,
                bytes_accessed=8 * 1024 * 1024,
                transcendentals=group * tokens * tree_dev * tokens,
            ),
            name="attend",
        )(plan, k_gain_row, *tables, *pieces[h], *queries[5 * h:5 * h + 5])

    dq, attended, k_gain_parts = [], [], []
    for h in range(kv_heads):
        dq_here, k_gain_part, *parts, crossed_part = attend(h)
        dq.append(dq_here)
        k_gain_parts.append(k_gain_part)
        attended.append((parts, crossed_part))

    everyone = cycle * lax.axis_size("heads")
    dq_raw, gains = pl.pallas_call(
        lambda *refs: query_kernel(blocks, inv_root, kv_heads, *refs),
        out_shape=(sds((tokens, heads * head_dim), BF16), sds((everyone, 2, head_dim), F32)),
        in_specs=[smem] + [vmem] * (6 + 2 * kv_heads),
        out_specs=(vmem, vmem),
        compiler_params=params,
        name="query_back",
    )(depth, *tables, q_gain_row, q_raw, *dq, *k_gain_parts)

    terms, farthest = [], []
    for h, (parts, crossed_part) in enumerate(attended):
        if h < kv_heads - 1:
            others = tree.across(crossed_part, [0, *steps], back=True)
            merged = [
                (parts[i + 1].astype(F32) + others[i + 1].astype(F32)).astype(BF16) for i in range(len(steps))
            ]
            farthest.append(merged.pop())
        else:
            others = tree.across(crossed_part, steps, back=True)
            *merged, near, joined, gains = pl.pallas_call(
                merge_kernel,
                out_shape=(
                    *[sds((tokens, 2 * head_dim), BF16)] * len(steps),
                    sds((kv_heads, tokens, 2 * head_dim), BF16),
                    sds(gains.shape, F32),
                ),
                in_specs=[vmem] * (len(steps) + 4),
                out_specs=tuple([vmem] * (len(steps) + 2)),
                compiler_params=params,
                name="merge",
            )(*parts[1:], others, gains, jnp.stack(farthest))
            joined = tree.home(joined, steps[-1])
            others = tree.across(near[None], [0], back=True)
        mine = [(parts[0], None), (others, 0)]
        terms.append(mine + [(tree.home(both, step), None) for both, step in zip(merged, steps)])
    for h in range(kv_heads):
        if h < kv_heads - 1:
            arrays, places = zip(*terms[h])
            early, gains = pl.pallas_call(
                lambda *refs: early_kernel(places, *refs),
                out_shape=(sds((tokens, 2 * head_dim), F32), sds(gains.shape, F32)),
                in_specs=[vmem] * (1 + len(arrays)),
                out_specs=(vmem, vmem),
                compiler_params=params,
                cost_estimate=slow,
                name="early",
            )(gains, *arrays)
            terms[h] = [(early, None)]
        terms[h].append((joined, h))
    gains = lax.all_to_all(gains, ("ctx", "heads"), 0, 0)

    arrays = [array for mine in terms for array, _ in mine]
    places = [[place for _, place in mine] for mine in terms]
    dk_raw, dv, total = pl.pallas_call(
        lambda *refs: key_kernel(blocks, places, *refs),
        out_shape=(sds(k_raw.shape, BF16), sds(k_raw.shape, BF16), sds(gains.shape[1:], F32)),
        in_specs=[smem] + [vmem] * (7 + len(arrays)),
        out_specs=(vmem, vmem, vmem),
        compiler_params=params,
        name="key_back",
    )(depth, *tables, k_gain_row, k_raw, gains, *arrays)
    return (dq_raw, dk_raw, dv, total[0], total[1])


def solution(mesh):
    split = P("ctx", "heads")
    return jax.shard_map(
        on_device,
        mesh=mesh,
        in_specs=(split, split, split, split, split, P(), P(), P("ctx", None)),
        out_specs=(split, split, split, P(), P()),
        check_vma=False,
    )
```

```python
import math

import jax
import jax.numpy as jnp
import numpy as np
from jax import lax
from jax.experimental import pallas as pl
from jax.experimental.pallas import tpu as pltpu
from jax.sharding import PartitionSpec as P

ROPE_BASE = 1000000.0
EPS = 1e-06
HIDDEN = -100000.0
VMEM_LIMIT = 16 * 1024 * 1024
ATTEND_VMEM_LIMIT = 34 * 1024 * 1024
F32 = jnp.float32
BF16 = jnp.bfloat16


def rope_rows(starts, head_dim):
    half = head_dim // 2
    frequency = np.exp(
        np.arange(half, dtype=np.float32) * np.float32(-2.0 * math.log(ROPE_BASE) / head_dim)
    ).astype(np.float32)
    angles = np.asarray(starts, np.float32)[:, None] * frequency[None, :]
    cos = np.cos(angles.astype(np.float64)).astype(np.float32)
    sin = np.sin(angles.astype(np.float64)).astype(np.float32)
    return np.concatenate([cos, cos], 1), np.concatenate([-sin, sin], 1)


def block_tables(depth, tables):
    start_cos, start_sin, offset_cos, offset_sin = tables
    cos, sin = start_cos[pl.ds(depth, 1), :], start_sin[pl.ds(depth, 1), :]
    both_cos = cos * offset_cos[...] - sin * offset_sin[...]
    both_sin = sin * offset_cos[...] + cos * offset_sin[...]
    return both_cos, both_sin


def turned(rows, cos, sin):
    return rows * cos + pltpu.roll(rows, rows.shape[-1] // 2, 1) * sin


def turned_back(rows, cos, sin):
    return rows * cos - pltpu.roll(rows, rows.shape[-1] // 2, 1) * sin


def inverse_rms(rows):
    return lax.rsqrt(jnp.mean(rows * rows, -1, keepdims=True) + EPS)


def own_tables(depth_ref, tables, blocks):
    parts = [block_tables(depth_ref[a], tables) for a in range(blocks)]
    return jnp.concatenate([p[0] for p in parts], 0), jnp.concatenate([p[1] for p in parts], 0)


def dot_nn(lhs, rhs):
    return lax.dot_general(lhs, rhs, (((1,), (0,)), ((), ())), preferred_element_type=F32)


def plan_kernel(blocks, tree_dev, place_ref, anc_ref, plan_ref):
    slots = tree_dev * blocks
    place = place_ref[0]
    here = jnp.where(place + 1 == tree_dev, 0, place + 1)
    for row in range(4):
        for i in range(slots):
            plan_ref[row, i] = 0
    count = jnp.int32(blocks)
    steps = [jnp.int32(0)] * blocks
    for b in range(slots):
        bits = jnp.int32(0)
        depth = jnp.int32(0)
        for a in range(blocks):
            hit = anc_ref[a, jnp.minimum(steps[a], slots - 1)] == b
            bits = bits | jnp.where(hit, 1 << a, 0)
            depth = jnp.where(hit, steps[a], depth)
            steps[a] = steps[a] + jnp.where(hit, 1, 0)
        own = place == b // blocks
        slot = jnp.where(own, b % blocks, jnp.minimum(count, slots - 1))
        there = (b // blocks + 1) % tree_dev
        odd = jnp.bitwise_and(here + there, 1)
        gap = jnp.bitwise_xor(here, odd) - there
        gap = jnp.where(gap < 0, gap + tree_dev, gap)
        plan_ref[0, slot] = odd * (tree_dev // 2) + lax.shift_right_logical(gap, 1)
        plan_ref[1, slot] = b % blocks
        plan_ref[2, slot] = depth
        plan_ref[3, slot] = bits
        count = count + jnp.where(own | (bits == 0), 0, 1)
    for i in range(slots):
        plan_ref[4, i] = count


def prep_kernel(blocks, block_len, kv_heads, depth_ref, t0, t1, t2, t3, gain_ref, q_ref, grad_ref, out_ref, *outs):
    tokens = q_ref.shape[0]
    head_dim = gain_ref.shape[1]
    cos, sin = own_tables(depth_ref, (t0, t1, t2, t3), blocks)
    gain = gain_ref[...]
    group = q_ref.shape[1] // head_dim // kv_heads
    for head in range(group * kv_heads):
        g = head % group
        q_t_ref, q_rot_ref, grad_t_ref, grad_heads_ref, delta_ref = outs[5 * (head // group):][:5]
        cols = pl.ds(head * head_dim, head_dim)
        here = pl.ds(g * tokens, tokens)
        rows = q_ref[:, cols].astype(F32)
        rotated = turned(rows * inverse_rms(rows) * gain, cos, sin)
        q_rot_ref[here, :] = rotated.astype(BF16)
        q_t_ref[:, here] = jnp.transpose(rotated).astype(BF16)
        grad = grad_ref[:, cols]
        grad_heads_ref[here, :] = grad
        grad_rows = jnp.transpose(grad.astype(F32))
        grad_t_ref[:, here] = grad_rows.astype(BF16)
        product = grad_rows * jnp.transpose(out_ref[:, cols].astype(F32))
        delta_ref[:, here] = jnp.sum(product, 0, keepdims=True)


def main_kernel(blocks, block_len, tree_dev, inv_root, n_in, last, *refs):
    plan_ref, gain_ref = refs[:2]
    tables = refs[2:6]
    half = tree_dev // 2
    pieces, crossed_ref = refs[6:5 + n_in], refs[5 + n_in]
    q_t_ref, q_ref, grad_t_ref, grad_ref, delta_ref = refs[6 + n_in:11 + n_in]
    dq_ref, gain_part_ref = refs[11 + n_in:13 + n_in]
    parts = refs[13 + n_in:13 + n_in + half + last]
    crossed_part, raw, keys, keys_t, vals, shown, with_cos, with_sin, expo, mass, w_even, ds_even, w_odd, ds_odd, found, spread = refs[
        13 + n_in + half + last:]
    head_dim = gain_ref.shape[1]
    tokens = raw.shape[1]
    group = q_ref.shape[0] // tokens
    count = plan_ref[4, 0]
    chunks = (count + blocks - 1) // blocks
    gain = gain_ref[...]
    for i, piece in enumerate(pieces):
        raw[i] = piece[...]
    raw[len(pieces):] = crossed_ref[...]
    query_block = lax.broadcasted_iota(jnp.int32, (1, tokens), 1) // block_len

    def rows_of(start):
        return pl.ds(pl.multiple_of(start * block_len, block_len), block_len)

    def load_chunk(c):
        for j in range(blocks):
            slot = jnp.minimum(c * blocks + j, tree_dev * blocks - 1)
            piece = plan_ref[0, slot]
            rows = rows_of(plan_ref[1, slot])
            cos, sin = block_tables(plan_ref[2, slot], tables)
            unit = raw[piece, rows, 0:head_dim].astype(F32)
            unit = unit * inverse_rms(unit)
            here = pl.ds(j * block_len, block_len)
            with_cos[c, here, :] = unit * cos
            with_sin[c, here, :] = pltpu.roll(unit * sin, head_dim // 2, 1)
            keys[c, here, :] = turned(unit * gain, cos, sin).astype(BF16)
            bits = jnp.where(c * blocks + j < count, plan_ref[3, slot], 0)
            row = jnp.zeros((1, tokens), F32)
            for a in range(blocks):
                seen = lax.rem(lax.shift_right_logical(bits, a), 2)
                row = jnp.where((query_block == a) & (seen == 0), HIDDEN, row)
            shown[c, j:j + 1, :] = row
            vals[c, here, :] = raw[piece, rows, head_dim:]
        keys_t[c] = jnp.transpose(keys[c].astype(F32)).astype(BF16)

    def exps(c, g, scores):
        parts = []
        for j in range(blocks):
            here = slice(j * block_len, (j + 1) * block_len)
            parts.append(jnp.exp(scores[here] * inv_root + shown[c, j:j + 1, :]))
        return jnp.concatenate(parts, 0)

    def summed(e):
        return jnp.sum(e.reshape(tokens // 8, 8, tokens), 0)

    key_row = lax.broadcasted_iota(jnp.int32, (tokens, tokens), 0)
    query_col = lax.broadcasted_iota(jnp.int32, (tokens, tokens), 1)

    def cols_of(g):
        return pl.ds(g * tokens, tokens)

    def masses(c, first):
        for g in range(group):
            scores = dot_nn(keys[c], q_t_ref[:, cols_of(g)])
            e = exps(c, g, scores)
            if first:
                e = jnp.where(key_row <= query_col, e, 0.0)
            expo[c, g] = e
            mass[g] = summed(e) if first else mass[g] + summed(e)

    load_chunk(0)
    masses(0, True)
    load_chunk(1)

    @pl.loop(1, chunks)
    def _(c):
        masses(c, False)
        load_chunk(c + 1)

    for g in range(group):
        total = jnp.sum(mass[g], 0, keepdims=True)
        mass[g] = jnp.broadcast_to(1.0 / total, (8, tokens))
    dq_ref[...] = jnp.zeros(dq_ref.shape, F32)
    gain_part_ref[...] = jnp.zeros(gain_part_ref.shape, F32)
    spread[...] = jnp.zeros(spread.shape, BF16)

    def weigh(c, heads, w_all, ds_all):
        for g in heads:
            cols = cols_of(g)
            grad_prob = dot_nn(vals[c], grad_t_ref[:, cols])
            weights = expo[c, g] * mass[g, 0:1, :]
            ds_all[:, cols] = (weights * (grad_prob - delta_ref[:, cols])).astype(BF16)
            w_all[:, cols] = weights.astype(BF16)

    def value_products(c, w_all):
        found[c, :, head_dim:] = dot_nn(w_all[...], grad_ref[...]).astype(BF16)

    def key_products(c, ds_all):
        dk = dot_nn(ds_all[...], q_ref[...]) * inv_root
        found[c, :, 0:head_dim] = dk.astype(BF16)
        front = jnp.sum((dk * with_cos[c]).reshape(tokens // 8, 8, head_dim), 0)
        back = jnp.sum((dk * with_sin[c]).reshape(tokens // 8, 8, head_dim), 0)
        gain_part_ref[...] = gain_part_ref[...] + front - pltpu.roll(back, head_dim // 2, 1)

    def query_products(c, ds_all):
        dq_ref[...] = dq_ref[...] + dot_nn(keys_t[c], ds_all[...])

    thirds = [range(group * i // 3, group * (i + 1) // 3) for i in range(3)]
    buffers = ((w_even, ds_even), (w_odd, ds_odd))

    def products(c, now):
        value_products(c, now[0])
        key_products(c, now[1])
        query_products(c, now[1])

    def step(c, now, later):
        value_products(c, now[0])
        weigh(c + 1, thirds[0], *later)
        key_products(c, now[1])
        weigh(c + 1, thirds[1], *later)
        query_products(c, now[1])
        weigh(c + 1, thirds[2], *later)

    weigh(0, range(group), *buffers[0])

    @pl.loop(0, (chunks - 1) // 2)
    def _(pair):
        step(2 * pair, buffers[0], buffers[1])
        step(2 * pair + 1, buffers[1], buffers[0])

    odd_count = lax.rem(chunks, 2) == 1

    @pl.when(odd_count)
    def _():
        products(chunks - 1, buffers[0])

    @pl.when(jnp.logical_not(odd_count))
    def _():
        step(chunks - 2, buffers[0], buffers[1])
        products(chunks - 1, buffers[1])

    @pl.loop(0, count)
    def _(slot):
        rows = rows_of(lax.rem(slot, blocks))
        spread[plan_ref[0, slot], rows_of(plan_ref[1, slot]), :] = found[slot // blocks, rows, :]

    for piece in range(half + last):
        parts[piece][...] = spread[piece]
    crossed_part[...] = spread[half + last:]


def join_kernel(*refs):
    for i in range(refs[-1].shape[0]):
        refs[-1][i] = refs[i][...]


def merge_kernel(*refs):
    count = (len(refs) - 5) // 2
    parts, (near_ref, others_ref, gains_ref, before_ref) = refs[:count], refs[count:count + 4]
    outs, (near_out_ref, joined_ref, gains_out_ref) = refs[count + 4:-3], refs[-3:]
    for i in range(count):
        both = (parts[i][...].astype(F32) + others_ref[i].astype(F32)).astype(BF16)
        if i < count - 1:
            outs[i][...] = both
        else:
            joined_ref[joined_ref.shape[0] - 1] = both
    for head in range(joined_ref.shape[0] - 1):
        joined_ref[head] = before_ref[head]
    near_out_ref[...] = near_ref[...]
    gains_out_ref[...] = gains_ref[...]


def query_kernel(blocks, inv_root, kv_heads, depth_ref, t0, t1, t2, t3, gain_ref, q_ref, *refs):
    dq_refs, (k_part_refs, (out_ref, gains_ref)) = refs[:kv_heads], (refs[kv_heads:-2], refs[-2:])
    tokens = q_ref.shape[0]
    head_dim = gain_ref.shape[1]
    group = dq_refs[0].shape[1] // tokens
    cos, sin = own_tables(depth_ref, (t0, t1, t2, t3), blocks)
    gain = gain_ref[...]
    part = jnp.zeros((8, head_dim), F32)
    for head in range(group * len(dq_refs)):
        cols = pl.ds(head * head_dim, head_dim)
        rows = q_ref[:, cols].astype(F32)
        recip = inverse_rms(rows)
        normed = rows * recip
        dq = jnp.transpose(dq_refs[head // group][:, pl.ds(head % group * tokens, tokens)])
        scaled_grad = turned_back(dq, cos, sin) * inv_root
        term = scaled_grad * normed
        part = part + jnp.sum(term.reshape(tokens // 8, 8, head_dim), 0)
        inner = jnp.mean(term * gain, -1, keepdims=True)
        out_ref[:, cols] = (recip * (scaled_grad * gain - normed * inner)).astype(BF16)
    k_part = sum(ref[...] for ref in k_part_refs)
    gains = jnp.concatenate([jnp.sum(part, 0, keepdims=True), jnp.sum(k_part, 0, keepdims=True)], 0)
    gains_ref[...] = jnp.broadcast_to(gains[None], gains_ref.shape)


def summed_terms(refs, places):
    total = 0.0
    for ref, place in zip(refs, places):
        total = total + (ref[...] if place is None else ref[place]).astype(F32)
    return total


def early_kernel(places, gains_ref, *refs):
    terms, (sum_ref, gains_out_ref) = refs[:-2], refs[-2:]
    sum_ref[...] = summed_terms(terms, places)
    gains_out_ref[...] = jnp.broadcast_to(jnp.sum(gains_ref[...], 0, keepdims=True), gains_out_ref.shape)


def key_kernel(blocks, places, depth_ref, t0, t1, t2, t3, gain_ref, k_ref, gains_ref, *refs):
    terms, (dk_out_ref, dv_out_ref, total_ref) = refs[:-3], refs[-3:]
    total_ref[...] = jnp.sum(gains_ref[...], 0)
    head_dim = gain_ref.shape[1]
    cos, sin = own_tables(depth_ref, (t0, t1, t2, t3), blocks)
    gain = gain_ref[...]
    for head, mine in enumerate(places):
        cols = pl.ds(head * head_dim, head_dim)
        rows = k_ref[:, cols].astype(F32)
        recip = inverse_rms(rows)
        normed = rows * recip
        both = summed_terms(terms[:len(mine)], mine)
        terms = terms[len(mine):]
        grad = turned_back(both[:, 0:head_dim], cos, sin) * gain
        inner = jnp.mean(grad * normed, -1, keepdims=True)
        dk_out_ref[:, cols] = (recip * (grad - normed * inner)).astype(BF16)
        dv_out_ref[:, cols] = both[:, head_dim:].astype(BF16)


class Tree:
    def __init__(self, size, cycle):
        self.size, self.cycle = size, cycle

    def order(self, index):
        return (index - 1) % self.size

    def send(self, value, target, wanted):
        pairs = []
        for tree in range(self.cycle // self.size):
            for index in range(self.size):
                if wanted(index):
                    ends = [(tree * self.size + 1 + self.order(i)) % self.cycle for i in (index, target(index))]
                    pairs.append(tuple(ends))
        return lax.ppermute(value, "ctx", pairs)

    def after(self, *pair):
        return self.order(pair[1] % self.size) > self.order(pair[0] % self.size)

    def along(self, own):
        pieces = []
        for step in range(2, self.size, 2):
            there = lambda i: (i + step) % self.size
            pieces.append(self.send(own, there, lambda i: self.after(i, there(i)) or self.after(i, there(i) ^ 1)))
        return pieces

    def across(self, value, steps, back=False):
        if back:
            return self.send(value, lambda i: i ^ 1, lambda i: any(self.after((i ^ 1) - step, i) for step in steps))
        return self.send(value, lambda i: i ^ 1, lambda i: any(self.after(i - step, i ^ 1) for step in steps))

    def home(self, value, step):
        there = lambda i: (i - step) % self.size
        return self.send(value, there, lambda i: self.after(there(i), i) or self.after(there(i), i ^ 1))


def on_device(q_raw, k_raw, values, saved_out, out_grad, q_gain, k_gain, ancestors):
    tokens = q_raw.shape[0]
    head_dim = q_gain.shape[0]
    kv_heads = k_raw.shape[1] // head_dim
    heads = q_raw.shape[1] // head_dim
    group = heads // kv_heads
    blocks = ancestors.shape[0]
    tree_blocks = ancestors.shape[1]
    block_len = tokens // blocks
    tree_dev = tree_blocks // blocks
    cycle = lax.axis_size("ctx")
    inv_root = 1.0 / math.sqrt(head_dim)
    tree = Tree(tree_dev, cycle)
    place = (lax.axis_index("ctx") - 1 + cycle) % cycle % tree_dev
    place = place.reshape(1).astype(jnp.int32)

    depth = jnp.sum((ancestors >= 0).astype(jnp.int32), 1) - 1
    total_blocks = blocks * cycle
    in_tree = jnp.where(
        ancestors >= 0, (ancestors - blocks + total_blocks) % total_blocks % tree_blocks, -1
    )
    tables = [
        jnp.asarray(table)
        for starts in (range(0, tree_blocks * block_len, block_len), range(block_len))
        for table in rope_rows(starts, head_dim)
    ]
    q_gain_row, k_gain_row = q_gain.reshape(1, head_dim), k_gain.reshape(1, head_dim)

    steps = range(2, tree_dev, 2)
    own = []
    for h in range(kv_heads):
        cols = slice(h * head_dim, (h + 1) * head_dim)
        own.append(jnp.concatenate([k_raw[:, cols], values[:, cols]], 1))

    params = pltpu.CompilerParams(vmem_limit_bytes=VMEM_LIMIT)
    smem = pl.BlockSpec(memory_space=pltpu.SMEM)
    vmem = pl.BlockSpec(memory_space=pltpu.VMEM)
    sds = jax.ShapeDtypeStruct
    slow = pl.CostEstimate(flops=4 * 10**9, bytes_accessed=16 * 1024 * 1024, transcendentals=0)
    quick = pl.CostEstimate(flops=1024, bytes_accessed=1024, transcendentals=0)

    plan = pl.pallas_call(
        lambda *refs: plan_kernel(blocks, tree_dev, *refs),
        out_shape=sds((5, tree_blocks), jnp.int32),
        in_specs=[smem, smem],
        out_specs=smem,
        cost_estimate=quick,
        name="plan",
    )(place, in_tree)

    def join(arrays, *after):
        count = len(arrays)
        return pl.pallas_call(
            join_kernel,
            out_shape=sds((count, tokens, 2 * head_dim), BF16),
            in_specs=[vmem] * count + [pl.BlockSpec(memory_space=pl.ANY)] * len(after),
            out_specs=vmem,
            compiler_params=params,
            cost_estimate=quick,
            name="join",
        )(*arrays, *after)

    rows = group * tokens
    queries = pl.pallas_call(
        lambda *refs: prep_kernel(blocks, block_len, kv_heads, *refs),
        out_shape=tuple(
            [
                sds((head_dim, rows), BF16),
                sds((rows, head_dim), BF16),
                sds((head_dim, rows), BF16),
                sds((rows, head_dim), BF16),
                sds((1, rows), F32),
            ]
            * kv_heads
        ),
        in_specs=[smem] + [vmem] * 8,
        out_specs=tuple([vmem] * (5 * kv_heads)),
        compiler_params=params,
        cost_estimate=slow,
        name="prep",
    )(depth, *tables, q_gain_row, q_raw, out_grad, saved_out)

    pieces = []
    for h in range(kv_heads):
        straight = tree.along(own[h])
        if h == 0:
            cross = [tree.across(own[h], [0])]
            crossed = tree.across(join(straight, cross[0], plan), steps)
        else:
            cross = []
            crossed = tree.across(join([own[h], *straight], queries[4], queries[-1]), [0, *steps])
        pieces.append([own[h], *straight, *cross, crossed])

    half = tree_dev // 2

    def attend(h):
        last = h == kv_heads - 1
        return pl.pallas_call(
            lambda *refs: main_kernel(blocks, block_len, tree_dev, inv_root, len(pieces[h]), last, *refs),
            out_shape=(
                sds((head_dim, rows), F32),
                sds((8, head_dim), F32),
                *[sds((tokens, 2 * head_dim), BF16)] * (half + last),
                sds((half - last, tokens, 2 * head_dim), BF16),
            ),
            in_specs=[smem] + [vmem] * (10 + len(pieces[h])),
            out_specs=tuple([vmem] * (3 + half + last)),
            scratch_shapes=[
                pltpu.VMEM((tree_dev, tokens, 2 * head_dim), BF16),
                pltpu.VMEM((tree_dev + 1, tokens, head_dim), BF16),
                pltpu.VMEM((tree_dev + 1, head_dim, tokens), BF16),
                pltpu.VMEM((tree_dev + 1, tokens, head_dim), BF16),
                pltpu.VMEM((tree_dev + 1, 8 * ((blocks + 7) // 8), tokens), F32),
                pltpu.VMEM((tree_dev + 1, tokens, head_dim), F32),
                pltpu.VMEM((tree_dev + 1, tokens, head_dim), F32),
                pltpu.VMEM((tree_dev, group, tokens, tokens), F32),
                pltpu.VMEM((group, 8, tokens), F32),
                *[pltpu.VMEM((tokens, rows), BF16)] * 4,
                pltpu.VMEM((tree_dev, tokens, 2 * head_dim), BF16),
                pltpu.VMEM((tree_dev, tokens, 2 * head_dim), BF16),
            ],
            compiler_params=pltpu.CompilerParams(vmem_limit_bytes=ATTEND_VMEM_LIMIT),
            cost_estimate=pl.CostEstimate(
                flops=10 * group * tokens * tree_dev * tokens * head_dim,
                bytes_accessed=8 * 1024 * 1024,
                transcendentals=group * tokens * tree_dev * tokens,
            ),
            name="attend",
        )(plan, k_gain_row, *tables, *pieces[h], *queries[5 * h:5 * h + 5])

    dq, attended, k_gain_parts = [], [], []
    for h in range(kv_heads):
        dq_here, k_gain_part, *parts, crossed_part = attend(h)
        dq.append(dq_here)
        k_gain_parts.append(k_gain_part)
        attended.append((parts, crossed_part))

    sharers = lax.axis_size("heads")
    dq_raw, gains = pl.pallas_call(
        lambda *refs: query_kernel(blocks, inv_root, kv_heads, *refs),
        out_shape=(sds((tokens, heads * head_dim), BF16), sds((sharers, 2, head_dim), F32)),
        in_specs=[smem] + [vmem] * (6 + 2 * kv_heads),
        out_specs=(vmem, vmem),
        compiler_params=params,
        name="query_back",
    )(depth, *tables, q_gain_row, q_raw, *dq, *k_gain_parts)

    terms, farthest = [], []
    for h, (parts, crossed_part) in enumerate(attended):
        if h < kv_heads - 1:
            others = tree.across(crossed_part, [0, *steps], back=True)
            merged = [
                (parts[i + 1].astype(F32) + others[i + 1].astype(F32)).astype(BF16) for i in range(len(steps))
            ]
            farthest.append(merged.pop())
        else:
            others = tree.across(crossed_part, steps, back=True)
            *merged, near, joined, gains = pl.pallas_call(
                merge_kernel,
                out_shape=(
                    *[sds((tokens, 2 * head_dim), BF16)] * len(steps),
                    sds((kv_heads, tokens, 2 * head_dim), BF16),
                    sds(gains.shape, F32),
                ),
                in_specs=[vmem] * (len(steps) + 4),
                out_specs=tuple([vmem] * (len(steps) + 2)),
                compiler_params=params,
                name="merge",
            )(*parts[1:], others, gains, jnp.stack(farthest))
            joined = tree.home(joined, steps[-1])
            others = tree.across(near[None], [0], back=True)
        mine = [(parts[0], None), (others, 0)]
        terms.append(mine + [(tree.home(both, step), None) for both, step in zip(merged, steps)])
    gains = lax.all_to_all(gains, "heads", 0, 0)
    for h in range(kv_heads):
        if h < kv_heads - 1:
            arrays, places = zip(*terms[h])
            early, gains = pl.pallas_call(
                lambda *refs: early_kernel(places, *refs),
                out_shape=(sds((tokens, 2 * head_dim), F32), sds((cycle, 2, head_dim), F32)),
                in_specs=[vmem] * (1 + len(arrays)),
                out_specs=(vmem, vmem),
                compiler_params=params,
                cost_estimate=slow,
                name="early",
            )(gains, *arrays)
            terms[h] = [(early, None)]
        terms[h].append((joined, h))
    gains = lax.all_to_all(gains, "ctx", 0, 0)

    arrays = [array for mine in terms for array, _ in mine]
    places = [[place for _, place in mine] for mine in terms]
    dk_raw, dv, total = pl.pallas_call(
        lambda *refs: key_kernel(blocks, places, *refs),
        out_shape=(sds(k_raw.shape, BF16), sds(k_raw.shape, BF16), sds(gains.shape[1:], F32)),
        in_specs=[smem] + [vmem] * (7 + len(arrays)),
        out_specs=(vmem, vmem, vmem),
        compiler_params=params,
        name="key_back",
    )(depth, *tables, k_gain_row, k_raw, gains, *arrays)
    return (dq_raw, dk_raw, dv, total[0], total[1])


def solution(mesh):
    split = P("ctx", "heads")
    return jax.shard_map(
        on_device,
        mesh=mesh,
        in_specs=(split, split, split, split, split, P(), P(), P("ctx", None)),
        out_specs=(split, split, split, P(), P()),
        check_vma=False,
    )
```

```python
import math

import jax
import jax.numpy as jnp
import numpy as np
from jax import lax
from jax.experimental import pallas as pl
from jax.experimental.pallas import tpu as pltpu
from jax.sharding import PartitionSpec as P

ROPE_BASE = 1000000.0
EPS = 1e-06
HIDDEN = -100000.0
VMEM_LIMIT = 16 * 1024 * 1024
ATTEND_VMEM_LIMIT = 34 * 1024 * 1024
F32 = jnp.float32
BF16 = jnp.bfloat16


def rope_rows(starts, head_dim):
    half = head_dim // 2
    frequency = np.exp(
        np.arange(half, dtype=np.float32) * np.float32(-2.0 * math.log(ROPE_BASE) / head_dim)
    ).astype(np.float32)
    angles = np.asarray(starts, np.float32)[:, None] * frequency[None, :]
    cos = np.cos(angles.astype(np.float64)).astype(np.float32)
    sin = np.sin(angles.astype(np.float64)).astype(np.float32)
    return np.concatenate([cos, cos], 1), np.concatenate([-sin, sin], 1)


def block_tables(depth, tables):
    start_cos, start_sin, offset_cos, offset_sin = tables
    cos, sin = start_cos[pl.ds(depth, 1), :], start_sin[pl.ds(depth, 1), :]
    both_cos = cos * offset_cos[...] - sin * offset_sin[...]
    both_sin = sin * offset_cos[...] + cos * offset_sin[...]
    return both_cos, both_sin


def turned(rows, cos, sin):
    return rows * cos + pltpu.roll(rows, rows.shape[-1] // 2, 1) * sin


def turned_back(rows, cos, sin):
    return rows * cos - pltpu.roll(rows, rows.shape[-1] // 2, 1) * sin


def inverse_rms(rows):
    return lax.rsqrt(jnp.mean(rows * rows, -1, keepdims=True) + EPS)


def own_tables(depth_ref, tables, blocks):
    parts = [block_tables(depth_ref[a], tables) for a in range(blocks)]
    return jnp.concatenate([p[0] for p in parts], 0), jnp.concatenate([p[1] for p in parts], 0)


def dot_nn(lhs, rhs):
    return lax.dot_general(lhs, rhs, (((1,), (0,)), ((), ())), preferred_element_type=F32)


def plan_kernel(blocks, tree_dev, place_ref, anc_ref, plan_ref):
    slots = tree_dev * blocks
    place = place_ref[0]
    here = jnp.where(place + 1 == tree_dev, 0, place + 1)
    for row in range(4):
        for i in range(slots):
            plan_ref[row, i] = 0
    count = jnp.int32(blocks)
    steps = [jnp.int32(0)] * blocks
    for b in range(slots):
        bits = jnp.int32(0)
        depth = jnp.int32(0)
        for a in range(blocks):
            hit = anc_ref[a, jnp.minimum(steps[a], slots - 1)] == b
            bits = bits | jnp.where(hit, 1 << a, 0)
            depth = jnp.where(hit, steps[a], depth)
            steps[a] = steps[a] + jnp.where(hit, 1, 0)
        own = place == b // blocks
        slot = jnp.where(own, b % blocks, jnp.minimum(count, slots - 1))
        there = (b // blocks + 1) % tree_dev
        odd = jnp.bitwise_and(here + there, 1)
        gap = jnp.bitwise_xor(here, odd) - there
        gap = jnp.where(gap < 0, gap + tree_dev, gap)
        plan_ref[0, slot] = odd * (tree_dev // 2) + lax.shift_right_logical(gap, 1)
        plan_ref[1, slot] = b % blocks
        plan_ref[2, slot] = depth
        plan_ref[3, slot] = bits
        count = count + jnp.where(own | (bits == 0), 0, 1)
    for i in range(slots):
        plan_ref[4, i] = count


def prep_kernel(blocks, block_len, kv_heads, depth_ref, t0, t1, t2, t3, gain_ref, q_ref, grad_ref, out_ref, *outs):
    tokens = q_ref.shape[0]
    head_dim = gain_ref.shape[1]
    cos, sin = own_tables(depth_ref, (t0, t1, t2, t3), blocks)
    gain = gain_ref[...]
    group = q_ref.shape[1] // head_dim // kv_heads
    for head in range(group * kv_heads):
        g = head % group
        q_t_ref, q_rot_ref, grad_t_ref, grad_heads_ref, delta_ref = outs[5 * (head // group):][:5]
        cols = pl.ds(head * head_dim, head_dim)
        here = pl.ds(g * tokens, tokens)
        rows = q_ref[:, cols].astype(F32)
        rotated = turned(rows * inverse_rms(rows) * gain, cos, sin)
        q_rot_ref[here, :] = rotated.astype(BF16)
        q_t_ref[:, here] = jnp.transpose(rotated).astype(BF16)
        grad = grad_ref[:, cols]
        grad_heads_ref[here, :] = grad
        grad_rows = jnp.transpose(grad.astype(F32))
        grad_t_ref[:, here] = grad_rows.astype(BF16)
        product = grad_rows * jnp.transpose(out_ref[:, cols].astype(F32))
        delta_ref[:, here] = jnp.sum(product, 0, keepdims=True)


def main_kernel(blocks, block_len, tree_dev, inv_root, n_in, *refs):
    plan_ref, gain_ref = refs[:2]
    tables = refs[2:6]
    half = tree_dev // 2
    pieces, crossed_ref = refs[6:5 + n_in], refs[5 + n_in]
    q_t_ref, q_ref, grad_t_ref, grad_ref, delta_ref = refs[6 + n_in:11 + n_in]
    dq_ref, gain_part_ref = refs[11 + n_in:13 + n_in]
    parts = refs[13 + n_in:13 + n_in + half]
    crossed_part, raw, keys, keys_t, vals, shown, with_cos, with_sin, expo, mass, w_even, ds_even, w_odd, ds_odd, found, spread = refs[
        13 + n_in + half:]
    head_dim = gain_ref.shape[1]
    tokens = raw.shape[1]
    group = q_ref.shape[0] // tokens
    count = plan_ref[4, 0]
    chunks = (count + blocks - 1) // blocks
    gain = gain_ref[...]
    for i, piece in enumerate(pieces):
        raw[i] = piece[...]
    raw[len(pieces):] = crossed_ref[...]
    query_block = lax.broadcasted_iota(jnp.int32, (1, tokens), 1) // block_len

    def rows_of(start):
        return pl.ds(pl.multiple_of(start * block_len, block_len), block_len)

    def load_chunk(c):
        for j in range(blocks):
            slot = jnp.minimum(c * blocks + j, tree_dev * blocks - 1)
            piece = plan_ref[0, slot]
            rows = rows_of(plan_ref[1, slot])
            cos, sin = block_tables(plan_ref[2, slot], tables)
            unit = raw[piece, rows, 0:head_dim].astype(F32)
            unit = unit * inverse_rms(unit)
            here = pl.ds(j * block_len, block_len)
            with_cos[c, here, :] = unit * cos
            with_sin[c, here, :] = pltpu.roll(unit * sin, head_dim // 2, 1)
            keys[c, here, :] = turned(unit * gain, cos, sin).astype(BF16)
            bits = jnp.where(c * blocks + j < count, plan_ref[3, slot], 0)
            row = jnp.zeros((1, tokens), F32)
            for a in range(blocks):
                seen = lax.rem(lax.shift_right_logical(bits, a), 2)
                row = jnp.where((query_block == a) & (seen == 0), HIDDEN, row)
            shown[c, j:j + 1, :] = row
            vals[c, here, :] = raw[piece, rows, head_dim:]
        keys_t[c] = jnp.transpose(keys[c].astype(F32)).astype(BF16)

    def exps(c, g, scores):
        parts = []
        for j in range(blocks):
            here = slice(j * block_len, (j + 1) * block_len)
            parts.append(jnp.exp(scores[here] * inv_root + shown[c, j:j + 1, :]))
        return jnp.concatenate(parts, 0)

    def summed(e):
        return jnp.sum(e.reshape(tokens // 8, 8, tokens), 0)

    key_row = lax.broadcasted_iota(jnp.int32, (tokens, tokens), 0)
    query_col = lax.broadcasted_iota(jnp.int32, (tokens, tokens), 1)

    def cols_of(g):
        return pl.ds(g * tokens, tokens)

    def masses(c, first):
        for g in range(group):
            scores = dot_nn(keys[c], q_t_ref[:, cols_of(g)])
            e = exps(c, g, scores)
            if first:
                e = jnp.where(key_row <= query_col, e, 0.0)
            expo[c, g] = e
            mass[g] = summed(e) if first else mass[g] + summed(e)

    load_chunk(0)
    masses(0, True)
    load_chunk(1)

    @pl.loop(1, chunks)
    def _(c):
        masses(c, False)
        load_chunk(c + 1)

    for g in range(group):
        total = jnp.sum(mass[g], 0, keepdims=True)
        mass[g] = jnp.broadcast_to(1.0 / total, (8, tokens))
    dq_ref[...] = jnp.zeros(dq_ref.shape, F32)
    gain_part_ref[...] = jnp.zeros(gain_part_ref.shape, F32)
    spread[...] = jnp.zeros(spread.shape, BF16)

    def weigh(c, heads, w_all, ds_all):
        for g in heads:
            cols = cols_of(g)
            grad_prob = dot_nn(vals[c], grad_t_ref[:, cols])
            weights = expo[c, g] * mass[g, 0:1, :]
            ds_all[:, cols] = (weights * (grad_prob - delta_ref[:, cols])).astype(BF16)
            w_all[:, cols] = weights.astype(BF16)

    def value_products(c, w_all):
        found[c, :, head_dim:] = dot_nn(w_all[...], grad_ref[...]).astype(BF16)

    def key_products(c, ds_all):
        dk = dot_nn(ds_all[...], q_ref[...]) * inv_root
        found[c, :, 0:head_dim] = dk.astype(BF16)
        front = jnp.sum((dk * with_cos[c]).reshape(tokens // 8, 8, head_dim), 0)
        back = jnp.sum((dk * with_sin[c]).reshape(tokens // 8, 8, head_dim), 0)
        gain_part_ref[...] = gain_part_ref[...] + front - pltpu.roll(back, head_dim // 2, 1)

    def query_products(c, ds_all):
        dq_ref[...] = dq_ref[...] + dot_nn(keys_t[c], ds_all[...])

    thirds = [range(group * i // 3, group * (i + 1) // 3) for i in range(3)]
    buffers = ((w_even, ds_even), (w_odd, ds_odd))

    def products(c, now):
        value_products(c, now[0])
        key_products(c, now[1])
        query_products(c, now[1])

    def step(c, now, later):
        value_products(c, now[0])
        weigh(c + 1, thirds[0], *later)
        key_products(c, now[1])
        weigh(c + 1, thirds[1], *later)
        query_products(c, now[1])
        weigh(c + 1, thirds[2], *later)

    weigh(0, range(group), *buffers[0])

    @pl.loop(0, (chunks - 1) // 2)
    def _(pair):
        step(2 * pair, buffers[0], buffers[1])
        step(2 * pair + 1, buffers[1], buffers[0])

    odd_count = lax.rem(chunks, 2) == 1

    @pl.when(odd_count)
    def _():
        products(chunks - 1, buffers[0])

    @pl.when(jnp.logical_not(odd_count))
    def _():
        step(chunks - 2, buffers[0], buffers[1])
        products(chunks - 1, buffers[1])

    @pl.loop(0, count)
    def _(slot):
        rows = rows_of(lax.rem(slot, blocks))
        spread[plan_ref[0, slot], rows_of(plan_ref[1, slot]), :] = found[slot // blocks, rows, :]

    for piece in range(half):
        parts[piece][...] = spread[piece]
    crossed_part[...] = spread[half:]


def join_kernel(*refs):
    for i in range(refs[-1].shape[0]):
        refs[-1][i] = refs[i][...]


def merge_kernel(*refs):
    count = (len(refs) - 3) // 2
    parts, others_ref, gains_ref, before_ref = refs[:count], *refs[count:count + 3]
    outs, joined_ref, gains_out_ref = refs[count + 3:-2], *refs[-2:]
    for i in range(count):
        both = (parts[i][...].astype(F32) + others_ref[i + 1].astype(F32)).astype(BF16)
        if i < count - 1:
            outs[i][...] = both
        else:
            joined_ref[joined_ref.shape[0] - 1] = both
    for head in range(joined_ref.shape[0] - 1):
        joined_ref[head] = before_ref[head]
    gains_out_ref[...] = gains_ref[...]


def query_kernel(blocks, inv_root, kv_heads, depth_ref, t0, t1, t2, t3, gain_ref, q_ref, *refs):
    dq_refs, (k_part_refs, (out_ref, gains_ref)) = refs[:kv_heads], (refs[kv_heads:-2], refs[-2:])
    tokens = q_ref.shape[0]
    head_dim = gain_ref.shape[1]
    group = dq_refs[0].shape[1] // tokens
    cos, sin = own_tables(depth_ref, (t0, t1, t2, t3), blocks)
    gain = gain_ref[...]
    part = jnp.zeros((8, head_dim), F32)
    for head in range(group * len(dq_refs)):
        cols = pl.ds(head * head_dim, head_dim)
        rows = q_ref[:, cols].astype(F32)
        recip = inverse_rms(rows)
        normed = rows * recip
        dq = jnp.transpose(dq_refs[head // group][:, pl.ds(head % group * tokens, tokens)])
        scaled_grad = turned_back(dq, cos, sin) * inv_root
        term = scaled_grad * normed
        part = part + jnp.sum(term.reshape(tokens // 8, 8, head_dim), 0)
        inner = jnp.mean(term * gain, -1, keepdims=True)
        out_ref[:, cols] = (recip * (scaled_grad * gain - normed * inner)).astype(BF16)
    k_part = sum(ref[...] for ref in k_part_refs)
    gains = jnp.concatenate([jnp.sum(part, 0, keepdims=True), jnp.sum(k_part, 0, keepdims=True)], 0)
    gains_ref[...] = jnp.broadcast_to(gains[None], gains_ref.shape)


def summed_terms(refs, places):
    total = 0.0
    for ref, place in zip(refs, places):
        total = total + (ref[...] if place is None else ref[place]).astype(F32)
    return total


def early_kernel(places, gains_ref, *refs):
    terms, (sum_ref, gains_out_ref) = refs[:-2], refs[-2:]
    sum_ref[...] = summed_terms(terms, places)
    gains_out_ref[...] = gains_ref[...]


def key_kernel(blocks, places, depth_ref, t0, t1, t2, t3, gain_ref, k_ref, gains_ref, *refs):
    terms, (dk_out_ref, dv_out_ref, total_ref) = refs[:-3], refs[-3:]
    total_ref[...] = jnp.sum(gains_ref[...], 0)
    head_dim = gain_ref.shape[1]
    cos, sin = own_tables(depth_ref, (t0, t1, t2, t3), blocks)
    gain = gain_ref[...]
    for head, mine in enumerate(places):
        cols = pl.ds(head * head_dim, head_dim)
        rows = k_ref[:, cols].astype(F32)
        recip = inverse_rms(rows)
        normed = rows * recip
        both = summed_terms(terms[:len(mine)], mine)
        terms = terms[len(mine):]
        grad = turned_back(both[:, 0:head_dim], cos, sin) * gain
        inner = jnp.mean(grad * normed, -1, keepdims=True)
        dk_out_ref[:, cols] = (recip * (grad - normed * inner)).astype(BF16)
        dv_out_ref[:, cols] = both[:, head_dim:].astype(BF16)


class Tree:
    def __init__(self, size, cycle):
        self.size, self.cycle = size, cycle

    def order(self, index):
        return (index - 1) % self.size

    def send(self, value, target, wanted):
        pairs = []
        for tree in range(self.cycle // self.size):
            for index in range(self.size):
                if wanted(index):
                    ends = [(tree * self.size + 1 + self.order(i)) % self.cycle for i in (index, target(index))]
                    pairs.append(tuple(ends))
        return lax.ppermute(value, "ctx", pairs)

    def after(self, *pair):
        return self.order(pair[1] % self.size) > self.order(pair[0] % self.size)

    def along(self, own):
        pieces = []
        for step in range(2, self.size, 2):
            there = lambda i: (i + step) % self.size
            pieces.append(self.send(own, there, lambda i: self.after(i, there(i)) or self.after(i, there(i) ^ 1)))
        return pieces

    def across(self, value, steps, back=False):
        if back:
            return self.send(value, lambda i: i ^ 1, lambda i: any(self.after((i ^ 1) - step, i) for step in steps))
        return self.send(value, lambda i: i ^ 1, lambda i: any(self.after(i - step, i ^ 1) for step in steps))

    def home(self, value, step):
        there = lambda i: (i - step) % self.size
        return self.send(value, there, lambda i: self.after(there(i), i) or self.after(there(i), i ^ 1))


def on_device(q_raw, k_raw, values, saved_out, out_grad, q_gain, k_gain, ancestors):
    tokens = q_raw.shape[0]
    head_dim = q_gain.shape[0]
    kv_heads = k_raw.shape[1] // head_dim
    heads = q_raw.shape[1] // head_dim
    group = heads // kv_heads
    blocks = ancestors.shape[0]
    tree_blocks = ancestors.shape[1]
    block_len = tokens // blocks
    tree_dev = tree_blocks // blocks
    cycle = lax.axis_size("ctx")
    inv_root = 1.0 / math.sqrt(head_dim)
    tree = Tree(tree_dev, cycle)
    place = (lax.axis_index("ctx") - 1 + cycle) % cycle % tree_dev
    place = place.reshape(1).astype(jnp.int32)

    depth = jnp.sum((ancestors >= 0).astype(jnp.int32), 1) - 1
    total_blocks = blocks * cycle
    in_tree = jnp.where(
        ancestors >= 0, (ancestors - blocks + total_blocks) % total_blocks % tree_blocks, -1
    )
    tables = [
        jnp.asarray(table)
        for starts in (range(0, tree_blocks * block_len, block_len), range(block_len))
        for table in rope_rows(starts, head_dim)
    ]
    q_gain_row, k_gain_row = q_gain.reshape(1, head_dim), k_gain.reshape(1, head_dim)

    steps = range(2, tree_dev, 2)
    own = []
    for h in range(kv_heads):
        cols = slice(h * head_dim, (h + 1) * head_dim)
        own.append(jnp.concatenate([k_raw[:, cols], values[:, cols]], 1))

    params = pltpu.CompilerParams(vmem_limit_bytes=VMEM_LIMIT)
    smem = pl.BlockSpec(memory_space=pltpu.SMEM)
    vmem = pl.BlockSpec(memory_space=pltpu.VMEM)
    sds = jax.ShapeDtypeStruct
    slow = pl.CostEstimate(flops=4 * 10**9, bytes_accessed=16 * 1024 * 1024, transcendentals=0)
    quick = pl.CostEstimate(flops=1024, bytes_accessed=1024, transcendentals=0)

    plan = pl.pallas_call(
        lambda *refs: plan_kernel(blocks, tree_dev, *refs),
        out_shape=sds((5, tree_blocks), jnp.int32),
        in_specs=[smem, smem],
        out_specs=smem,
        cost_estimate=quick,
        name="plan",
    )(place, in_tree)

    def join(arrays, *after):
        count = len(arrays)
        return pl.pallas_call(
            join_kernel,
            out_shape=sds((count, tokens, 2 * head_dim), BF16),
            in_specs=[vmem] * count + [pl.BlockSpec(memory_space=pl.ANY)] * len(after),
            out_specs=vmem,
            compiler_params=params,
            cost_estimate=quick,
            name="join",
        )(*arrays, *after)

    rows = group * tokens
    queries = pl.pallas_call(
        lambda *refs: prep_kernel(blocks, block_len, kv_heads, *refs),
        out_shape=tuple(
            [
                sds((head_dim, rows), BF16),
                sds((rows, head_dim), BF16),
                sds((head_dim, rows), BF16),
                sds((rows, head_dim), BF16),
                sds((1, rows), F32),
            ]
            * kv_heads
        ),
        in_specs=[smem] + [vmem] * 8,
        out_specs=tuple([vmem] * (5 * kv_heads)),
        compiler_params=params,
        cost_estimate=slow,
        name="prep",
    )(depth, *tables, q_gain_row, q_raw, out_grad, saved_out)

    pieces = []
    for h in range(kv_heads):
        straight = tree.along(own[h])
        if h == 0:
            cross = [tree.across(own[h], [0])]
            crossed = tree.across(join(straight, cross[0], plan), steps)
        else:
            cross = []
            crossed = tree.across(join([own[h], *straight], queries[4], queries[-1]), [0, *steps])
        pieces.append([own[h], *straight, *cross, crossed])

    half = tree_dev // 2

    def attend(h):
        return pl.pallas_call(
            lambda *refs: main_kernel(blocks, block_len, tree_dev, inv_root, len(pieces[h]), *refs),
            out_shape=(
                sds((head_dim, rows), F32),
                sds((8, head_dim), F32),
                *[sds((tokens, 2 * head_dim), BF16)] * half,
                sds((half, tokens, 2 * head_dim), BF16),
            ),
            in_specs=[smem] + [vmem] * (10 + len(pieces[h])),
            out_specs=tuple([vmem] * (3 + half)),
            scratch_shapes=[
                pltpu.VMEM((tree_dev, tokens, 2 * head_dim), BF16),
                pltpu.VMEM((tree_dev + 1, tokens, head_dim), BF16),
                pltpu.VMEM((tree_dev + 1, head_dim, tokens), BF16),
                pltpu.VMEM((tree_dev + 1, tokens, head_dim), BF16),
                pltpu.VMEM((tree_dev + 1, 8 * ((blocks + 7) // 8), tokens), F32),
                pltpu.VMEM((tree_dev + 1, tokens, head_dim), F32),
                pltpu.VMEM((tree_dev + 1, tokens, head_dim), F32),
                pltpu.VMEM((tree_dev, group, tokens, tokens), F32),
                pltpu.VMEM((group, 8, tokens), F32),
                *[pltpu.VMEM((tokens, rows), BF16)] * 4,
                pltpu.VMEM((tree_dev, tokens, 2 * head_dim), BF16),
                pltpu.VMEM((tree_dev, tokens, 2 * head_dim), BF16),
            ],
            compiler_params=pltpu.CompilerParams(vmem_limit_bytes=ATTEND_VMEM_LIMIT),
            cost_estimate=pl.CostEstimate(
                flops=10 * group * tokens * tree_dev * tokens * head_dim,
                bytes_accessed=8 * 1024 * 1024,
                transcendentals=group * tokens * tree_dev * tokens,
            ),
            name="attend",
        )(plan, k_gain_row, *tables, *pieces[h], *queries[5 * h:5 * h + 5])

    dq, attended, k_gain_parts = [], [], []
    for h in range(kv_heads):
        dq_here, k_gain_part, *parts, crossed_part = attend(h)
        dq.append(dq_here)
        k_gain_parts.append(k_gain_part)
        attended.append((parts, crossed_part))

    everyone = cycle * lax.axis_size("heads")
    dq_raw, gains = pl.pallas_call(
        lambda *refs: query_kernel(blocks, inv_root, kv_heads, *refs),
        out_shape=(sds((tokens, heads * head_dim), BF16), sds((everyone, 2, head_dim), F32)),
        in_specs=[smem] + [vmem] * (6 + 2 * kv_heads),
        out_specs=(vmem, vmem),
        compiler_params=params,
        name="query_back",
    )(depth, *tables, q_gain_row, q_raw, *dq, *k_gain_parts)

    terms, farthest = [], []
    for h, (parts, crossed_part) in enumerate(attended):
        others = tree.across(crossed_part, [0, *steps], back=True)
        if h < kv_heads - 1:
            merged = [
                (parts[i + 1].astype(F32) + others[i + 1].astype(F32)).astype(BF16) for i in range(len(steps))
            ]
            farthest.append(merged.pop())
        else:
            *merged, joined, gains = pl.pallas_call(
                merge_kernel,
                out_shape=(
                    *[sds((tokens, 2 * head_dim), BF16)] * (len(steps) - 1),
                    sds((kv_heads, tokens, 2 * head_dim), BF16),
                    sds(gains.shape, F32),
                ),
                in_specs=[vmem] * (len(steps) + 3),
                out_specs=tuple([vmem] * (len(steps) + 1)),
                compiler_params=params,
                name="merge",
            )(*parts[1:], others, gains, jnp.stack(farthest))
            joined = tree.home(joined, steps[-1])
        mine = [(parts[0], None), (others, 0)]
        terms.append(mine + [(tree.home(both, step), None) for both, step in zip(merged, steps)])
    for h in range(kv_heads):
        if h < kv_heads - 1:
            arrays, places = zip(*terms[h])
            early, gains = pl.pallas_call(
                lambda *refs: early_kernel(places, *refs),
                out_shape=(sds((tokens, 2 * head_dim), F32), sds(gains.shape, F32)),
                in_specs=[vmem] * (1 + len(arrays)),
                out_specs=(vmem, vmem),
                compiler_params=params,
                cost_estimate=slow,
                name="early",
            )(gains, *arrays)
            terms[h] = [(early, None)]
        terms[h].append((joined, h))
    gains = lax.all_to_all(gains, ("ctx", "heads"), 0, 0)

    arrays = [array for mine in terms for array, _ in mine]
    places = [[place for _, place in mine] for mine in terms]
    dk_raw, dv, total = pl.pallas_call(
        lambda *refs: key_kernel(blocks, places, *refs),
        out_shape=(sds(k_raw.shape, BF16), sds(k_raw.shape, BF16), sds(gains.shape[1:], F32)),
        in_specs=[smem] + [vmem] * (7 + len(arrays)),
        out_specs=(vmem, vmem, vmem),
        compiler_params=params,
        name="key_back",
    )(depth, *tables, k_gain_row, k_raw, gains, *arrays)
    return (dq_raw, dk_raw, dv, total[0], total[1])


def solution(mesh):
    split = P("ctx", "heads")
    return jax.shard_map(
        on_device,
        mesh=mesh,
        in_specs=(split, split, split, split, split, P(), P(), P("ctx", None)),
        out_specs=(split, split, split, P(), P()),
        check_vma=False,
    )
```

```python
import math

import jax
import jax.numpy as jnp
import numpy as np
from jax import lax
from jax.experimental import pallas as pl
from jax.experimental.pallas import tpu as pltpu
from jax.sharding import PartitionSpec as P

ROPE_BASE = 1000000.0
EPS = 1e-06
HIDDEN = -100000.0
VMEM_LIMIT = 16 * 1024 * 1024
ATTEND_VMEM_LIMIT = 34 * 1024 * 1024
F32 = jnp.float32
BF16 = jnp.bfloat16


def rope_rows(starts, head_dim):
    half = head_dim // 2
    frequency = np.exp(
        np.arange(half, dtype=np.float32) * np.float32(-2.0 * math.log(ROPE_BASE) / head_dim)
    ).astype(np.float32)
    angles = np.asarray(starts, np.float32)[:, None] * frequency[None, :]
    cos = np.cos(angles.astype(np.float64)).astype(np.float32)
    sin = np.sin(angles.astype(np.float64)).astype(np.float32)
    return np.concatenate([cos, cos], 1), np.concatenate([-sin, sin], 1)


def block_tables(depth, tables):
    start_cos, start_sin, offset_cos, offset_sin = tables
    cos, sin = start_cos[pl.ds(depth, 1), :], start_sin[pl.ds(depth, 1), :]
    both_cos = cos * offset_cos[...] - sin * offset_sin[...]
    both_sin = sin * offset_cos[...] + cos * offset_sin[...]
    return both_cos, both_sin


def turned(rows, cos, sin):
    return rows * cos + pltpu.roll(rows, rows.shape[-1] // 2, 1) * sin


def turned_back(rows, cos, sin):
    return rows * cos - pltpu.roll(rows, rows.shape[-1] // 2, 1) * sin


def inverse_rms(rows):
    return lax.rsqrt(jnp.mean(rows * rows, -1, keepdims=True) + EPS)


def own_tables(depth_ref, tables, blocks):
    parts = [block_tables(depth_ref[a], tables) for a in range(blocks)]
    return jnp.concatenate([p[0] for p in parts], 0), jnp.concatenate([p[1] for p in parts], 0)


def dot_nn(lhs, rhs):
    return lax.dot_general(lhs, rhs, (((1,), (0,)), ((), ())), preferred_element_type=F32)


def plan_kernel(blocks, tree_dev, place_ref, anc_ref, plan_ref):
    slots = tree_dev * blocks
    place = place_ref[0]
    here = jnp.where(place + 1 == tree_dev, 0, place + 1)
    for row in range(4):
        for i in range(slots):
            plan_ref[row, i] = 0
    count = jnp.int32(blocks)
    steps = [jnp.int32(0)] * blocks
    for b in range(slots):
        bits = jnp.int32(0)
        depth = jnp.int32(0)
        for a in range(blocks):
            hit = anc_ref[a, jnp.minimum(steps[a], slots - 1)] == b
            bits = bits | jnp.where(hit, 1 << a, 0)
            depth = jnp.where(hit, steps[a], depth)
            steps[a] = steps[a] + jnp.where(hit, 1, 0)
        own = place == b // blocks
        slot = jnp.where(own, b % blocks, jnp.minimum(count, slots - 1))
        there = (b // blocks + 1) % tree_dev
        odd = jnp.bitwise_and(here + there, 1)
        gap = jnp.bitwise_xor(here, odd) - there
        gap = jnp.where(gap < 0, gap + tree_dev, gap)
        plan_ref[0, slot] = odd * (tree_dev // 2) + lax.shift_right_logical(gap, 1)
        plan_ref[1, slot] = b % blocks
        plan_ref[2, slot] = depth
        plan_ref[3, slot] = bits
        count = count + jnp.where(own | (bits == 0), 0, 1)
    for i in range(slots):
        plan_ref[4, i] = count


def prep_kernel(blocks, block_len, kv_heads, depth_ref, t0, t1, t2, t3, gain_ref, q_ref, grad_ref, out_ref, *outs):
    tokens = q_ref.shape[0]
    head_dim = gain_ref.shape[1]
    cos, sin = own_tables(depth_ref, (t0, t1, t2, t3), blocks)
    gain = gain_ref[...]
    group = q_ref.shape[1] // head_dim // kv_heads
    for head in range(group * kv_heads):
        g = head % group
        q_t_ref, q_rot_ref, grad_t_ref, grad_heads_ref, delta_ref = outs[5 * (head // group):][:5]
        cols = pl.ds(head * head_dim, head_dim)
        here = pl.ds(g * tokens, tokens)
        rows = q_ref[:, cols].astype(F32)
        rotated = turned(rows * inverse_rms(rows) * gain, cos, sin)
        q_rot_ref[here, :] = rotated.astype(BF16)
        q_t_ref[:, here] = jnp.transpose(rotated).astype(BF16)
        grad = grad_ref[:, cols]
        grad_heads_ref[here, :] = grad
        grad_rows = jnp.transpose(grad.astype(F32))
        grad_t_ref[:, here] = grad_rows.astype(BF16)
        product = grad_rows * jnp.transpose(out_ref[:, cols].astype(F32))
        delta_ref[:, here] = jnp.sum(product, 0, keepdims=True)


def main_kernel(blocks, block_len, tree_dev, inv_root, n_in, *refs):
    plan_ref, gain_ref = refs[:2]
    tables = refs[2:6]
    half = tree_dev // 2
    pieces, crossed_ref = refs[6:5 + n_in], refs[5 + n_in]
    q_t_ref, q_ref, grad_t_ref, grad_ref, delta_ref = refs[6 + n_in:11 + n_in]
    dq_ref, gain_part_ref = refs[11 + n_in:13 + n_in]
    parts = refs[13 + n_in:13 + n_in + half]
    crossed_part, raw, keys, keys_t, vals, shown, with_cos, with_sin, expo, mass, w_even, ds_even, w_odd, ds_odd, found, spread = refs[
        13 + n_in + half:]
    head_dim = gain_ref.shape[1]
    tokens = raw.shape[1]
    group = q_ref.shape[0] // tokens
    count = plan_ref[4, 0]
    chunks = (count + blocks - 1) // blocks
    gain = gain_ref[...]
    for i, piece in enumerate(pieces):
        raw[i] = piece[...]
    raw[len(pieces):] = crossed_ref[...]
    query_block = lax.broadcasted_iota(jnp.int32, (1, tokens), 1) // block_len

    def rows_of(start):
        return pl.ds(pl.multiple_of(start * block_len, block_len), block_len)

    def load_chunk(c):
        for j in range(blocks):
            slot = jnp.minimum(c * blocks + j, tree_dev * blocks - 1)
            piece = plan_ref[0, slot]
            rows = rows_of(plan_ref[1, slot])
            cos, sin = block_tables(plan_ref[2, slot], tables)
            unit = raw[piece, rows, 0:head_dim].astype(F32)
            unit = unit * inverse_rms(unit)
            here = pl.ds(j * block_len, block_len)
            with_cos[c, here, :] = unit * cos
            with_sin[c, here, :] = pltpu.roll(unit * sin, head_dim // 2, 1)
            keys[c, here, :] = turned(unit * gain, cos, sin).astype(BF16)
            bits = jnp.where(c * blocks + j < count, plan_ref[3, slot], 0)
            row = jnp.zeros((1, tokens), F32)
            for a in range(blocks):
                seen = lax.rem(lax.shift_right_logical(bits, a), 2)
                row = jnp.where((query_block == a) & (seen == 0), HIDDEN, row)
            shown[c, j:j + 1, :] = row
            vals[c, here, :] = raw[piece, rows, head_dim:]
        keys_t[c] = jnp.transpose(keys[c].astype(F32)).astype(BF16)

    def exps(c, g, scores):
        parts = []
        for j in range(blocks):
            here = slice(j * block_len, (j + 1) * block_len)
            parts.append(jnp.exp(scores[here] * inv_root + shown[c, j:j + 1, :]))
        return jnp.concatenate(parts, 0)

    def summed(e):
        return jnp.sum(e.reshape(tokens // 8, 8, tokens), 0)

    key_row = lax.broadcasted_iota(jnp.int32, (tokens, tokens), 0)
    query_col = lax.broadcasted_iota(jnp.int32, (tokens, tokens), 1)

    def cols_of(g):
        return pl.ds(g * tokens, tokens)

    def masses(c, first):
        for g in range(group):
            scores = dot_nn(keys[c], q_t_ref[:, cols_of(g)])
            e = exps(c, g, scores)
            if first:
                e = jnp.where(key_row <= query_col, e, 0.0)
            expo[c, g] = e
            mass[g] = summed(e) if first else mass[g] + summed(e)

    load_chunk(0)
    masses(0, True)
    load_chunk(1)

    @pl.loop(1, chunks)
    def _(c):
        masses(c, False)
        load_chunk(c + 1)

    for g in range(group):
        total = jnp.sum(mass[g], 0, keepdims=True)
        mass[g] = jnp.broadcast_to(1.0 / total, (8, tokens))
    dq_ref[...] = jnp.zeros(dq_ref.shape, F32)
    gain_part_ref[...] = jnp.zeros(gain_part_ref.shape, F32)
    spread[...] = jnp.zeros(spread.shape, BF16)

    def weigh(c, heads, w_all, ds_all):
        for g in heads:
            cols = cols_of(g)
            grad_prob = dot_nn(vals[c], grad_t_ref[:, cols])
            weights = expo[c, g] * mass[g, 0:1, :]
            ds_all[:, cols] = (weights * (grad_prob - delta_ref[:, cols])).astype(BF16)
            w_all[:, cols] = weights.astype(BF16)

    def value_products(c, w_all):
        found[c, :, head_dim:] = dot_nn(w_all[...], grad_ref[...]).astype(BF16)

    def key_products(c, ds_all):
        dk = dot_nn(ds_all[...], q_ref[...]) * inv_root
        found[c, :, 0:head_dim] = dk.astype(BF16)
        front = jnp.sum((dk * with_cos[c]).reshape(tokens // 8, 8, head_dim), 0)
        back = jnp.sum((dk * with_sin[c]).reshape(tokens // 8, 8, head_dim), 0)
        gain_part_ref[...] = gain_part_ref[...] + front - pltpu.roll(back, head_dim // 2, 1)

    def query_products(c, ds_all):
        dq_ref[...] = dq_ref[...] + dot_nn(keys_t[c], ds_all[...])

    thirds = [range(group * i // 3, group * (i + 1) // 3) for i in range(3)]
    buffers = ((w_even, ds_even), (w_odd, ds_odd))

    def step(c, now, later):
        ahead = jnp.minimum(c + 1, chunks - 1)
        value_products(c, now[0])
        weigh(ahead, thirds[0], *later)
        key_products(c, now[1])
        weigh(ahead, thirds[1], *later)
        query_products(c, now[1])
        weigh(ahead, thirds[2], *later)

    weigh(0, range(group), *buffers[0])

    @pl.loop(0, chunks // 2)
    def _(pair):
        step(2 * pair, buffers[0], buffers[1])
        step(2 * pair + 1, buffers[1], buffers[0])

    @pl.when(lax.rem(chunks, 2) == 1)
    def _():
        value_products(chunks - 1, w_even)
        key_products(chunks - 1, ds_even)
        query_products(chunks - 1, ds_even)

    @pl.loop(0, count)
    def _(slot):
        rows = rows_of(lax.rem(slot, blocks))
        spread[plan_ref[0, slot], rows_of(plan_ref[1, slot]), :] = found[slot // blocks, rows, :]

    for piece in range(half):
        parts[piece][...] = spread[piece]
    crossed_part[...] = spread[half:]


def join_kernel(*refs):
    for i in range(refs[-1].shape[0]):
        refs[-1][i] = refs[i][...]


def merge_kernel(*refs):
    count = (len(refs) - 3) // 2
    parts, others_ref, gains_ref, before_ref = refs[:count], *refs[count:count + 3]
    outs, joined_ref, gains_out_ref = refs[count + 3:-2], *refs[-2:]
    for i in range(count):
        both = (parts[i][...].astype(F32) + others_ref[i + 1].astype(F32)).astype(BF16)
        if i < count - 1:
            outs[i][...] = both
        else:
            joined_ref[joined_ref.shape[0] - 1] = both
    for head in range(joined_ref.shape[0] - 1):
        joined_ref[head] = before_ref[head]
    gains_out_ref[...] = gains_ref[...]


def query_kernel(blocks, inv_root, kv_heads, depth_ref, t0, t1, t2, t3, gain_ref, q_ref, *refs):
    dq_refs, (k_part_refs, (out_ref, gains_ref)) = refs[:kv_heads], (refs[kv_heads:-2], refs[-2:])
    tokens = q_ref.shape[0]
    head_dim = gain_ref.shape[1]
    group = dq_refs[0].shape[1] // tokens
    cos, sin = own_tables(depth_ref, (t0, t1, t2, t3), blocks)
    gain = gain_ref[...]
    part = jnp.zeros((8, head_dim), F32)
    for head in range(group * len(dq_refs)):
        cols = pl.ds(head * head_dim, head_dim)
        rows = q_ref[:, cols].astype(F32)
        recip = inverse_rms(rows)
        normed = rows * recip
        dq = jnp.transpose(dq_refs[head // group][:, pl.ds(head % group * tokens, tokens)])
        scaled_grad = turned_back(dq, cos, sin) * inv_root
        term = scaled_grad * normed
        part = part + jnp.sum(term.reshape(tokens // 8, 8, head_dim), 0)
        inner = jnp.mean(term * gain, -1, keepdims=True)
        out_ref[:, cols] = (recip * (scaled_grad * gain - normed * inner)).astype(BF16)
    k_part = sum(ref[...] for ref in k_part_refs)
    gains = jnp.concatenate([jnp.sum(part, 0, keepdims=True), jnp.sum(k_part, 0, keepdims=True)], 0)
    gains_ref[...] = jnp.broadcast_to(gains[None], gains_ref.shape)


def summed_terms(refs, places):
    total = 0.0
    for ref, place in zip(refs, places):
        total = total + (ref[...] if place is None else ref[place]).astype(F32)
    return total


def early_kernel(places, gains_ref, *refs):
    terms, (sum_ref, gains_out_ref) = refs[:-2], refs[-2:]
    sum_ref[...] = summed_terms(terms, places)
    gains_out_ref[...] = gains_ref[...]


def key_kernel(blocks, places, depth_ref, t0, t1, t2, t3, gain_ref, k_ref, gains_ref, *refs):
    terms, (dk_out_ref, dv_out_ref, q_total_ref, k_total_ref) = refs[:-4], refs[-4:]
    total = jnp.sum(gains_ref[...], 0)
    q_total_ref[...] = total[0:1]
    k_total_ref[...] = total[1:2]
    head_dim = gain_ref.shape[1]
    cos, sin = own_tables(depth_ref, (t0, t1, t2, t3), blocks)
    gain = gain_ref[...]
    for head, mine in enumerate(places):
        cols = pl.ds(head * head_dim, head_dim)
        rows = k_ref[:, cols].astype(F32)
        recip = inverse_rms(rows)
        normed = rows * recip
        both = summed_terms(terms[:len(mine)], mine)
        terms = terms[len(mine):]
        grad = turned_back(both[:, 0:head_dim], cos, sin) * gain
        inner = jnp.mean(grad * normed, -1, keepdims=True)
        dk_out_ref[:, cols] = (recip * (grad - normed * inner)).astype(BF16)
        dv_out_ref[:, cols] = both[:, head_dim:].astype(BF16)


class Tree:
    def __init__(self, size, cycle):
        self.size, self.cycle = size, cycle

    def order(self, index):
        return (index - 1) % self.size

    def send(self, value, target, wanted):
        pairs = []
        for tree in range(self.cycle // self.size):
            for index in range(self.size):
                if wanted(index):
                    ends = [(tree * self.size + 1 + self.order(i)) % self.cycle for i in (index, target(index))]
                    pairs.append(tuple(ends))
        return lax.ppermute(value, "ctx", pairs)

    def after(self, *pair):
        return self.order(pair[1] % self.size) > self.order(pair[0] % self.size)

    def along(self, own):
        pieces = []
        for step in range(2, self.size, 2):
            there = lambda i: (i + step) % self.size
            pieces.append(self.send(own, there, lambda i: self.after(i, there(i)) or self.after(i, there(i) ^ 1)))
        return pieces

    def across(self, value, steps, back=False):
        if back:
            return self.send(value, lambda i: i ^ 1, lambda i: any(self.after((i ^ 1) - step, i) for step in steps))
        return self.send(value, lambda i: i ^ 1, lambda i: any(self.after(i - step, i ^ 1) for step in steps))

    def home(self, value, step):
        there = lambda i: (i - step) % self.size
        return self.send(value, there, lambda i: self.after(there(i), i) or self.after(there(i), i ^ 1))


def on_device(q_raw, k_raw, values, saved_out, out_grad, q_gain, k_gain, ancestors):
    tokens = q_raw.shape[0]
    head_dim = q_gain.shape[0]
    kv_heads = k_raw.shape[1] // head_dim
    heads = q_raw.shape[1] // head_dim
    group = heads // kv_heads
    blocks = ancestors.shape[0]
    tree_blocks = ancestors.shape[1]
    block_len = tokens // blocks
    tree_dev = tree_blocks // blocks
    cycle = lax.axis_size("ctx")
    inv_root = 1.0 / math.sqrt(head_dim)
    tree = Tree(tree_dev, cycle)
    place = (lax.axis_index("ctx") - 1 + cycle) % cycle % tree_dev
    place = place.reshape(1).astype(jnp.int32)

    depth = jnp.sum((ancestors >= 0).astype(jnp.int32), 1) - 1
    total_blocks = blocks * cycle
    in_tree = jnp.where(
        ancestors >= 0, (ancestors - blocks + total_blocks) % total_blocks % tree_blocks, -1
    )
    tables = [
        jnp.asarray(table)
        for starts in (range(0, tree_blocks * block_len, block_len), range(block_len))
        for table in rope_rows(starts, head_dim)
    ]
    q_gain_row, k_gain_row = q_gain.reshape(1, head_dim), k_gain.reshape(1, head_dim)

    steps = range(2, tree_dev, 2)
    own = []
    for h in range(kv_heads):
        cols = slice(h * head_dim, (h + 1) * head_dim)
        own.append(jnp.concatenate([k_raw[:, cols], values[:, cols]], 1))

    params = pltpu.CompilerParams(vmem_limit_bytes=VMEM_LIMIT)
    smem = pl.BlockSpec(memory_space=pltpu.SMEM)
    vmem = pl.BlockSpec(memory_space=pltpu.VMEM)
    sds = jax.ShapeDtypeStruct
    slow = pl.CostEstimate(flops=4 * 10**9, bytes_accessed=16 * 1024 * 1024, transcendentals=0)
    quick = pl.CostEstimate(flops=1024, bytes_accessed=1024, transcendentals=0)

    plan = pl.pallas_call(
        lambda *refs: plan_kernel(blocks, tree_dev, *refs),
        out_shape=sds((5, tree_blocks), jnp.int32),
        in_specs=[smem, smem],
        out_specs=smem,
        cost_estimate=quick,
        name="plan",
    )(place, in_tree)

    def join(arrays, *after):
        count = len(arrays)
        return pl.pallas_call(
            join_kernel,
            out_shape=sds((count, tokens, 2 * head_dim), BF16),
            in_specs=[vmem] * count + [pl.BlockSpec(memory_space=pl.ANY)] * len(after),
            out_specs=vmem,
            compiler_params=params,
            cost_estimate=quick,
            name="join",
        )(*arrays, *after)

    rows = group * tokens
    queries = pl.pallas_call(
        lambda *refs: prep_kernel(blocks, block_len, kv_heads, *refs),
        out_shape=tuple(
            [
                sds((head_dim, rows), BF16),
                sds((rows, head_dim), BF16),
                sds((head_dim, rows), BF16),
                sds((rows, head_dim), BF16),
                sds((1, rows), F32),
            ]
            * kv_heads
        ),
        in_specs=[smem] + [vmem] * 8,
        out_specs=tuple([vmem] * (5 * kv_heads)),
        compiler_params=params,
        cost_estimate=slow,
        name="prep",
    )(depth, *tables, q_gain_row, q_raw, out_grad, saved_out)

    pieces = []
    for h in range(kv_heads):
        straight = tree.along(own[h])
        if h == 0:
            cross = [tree.across(own[h], [0])]
            crossed = tree.across(join(straight, cross[0], plan), steps)
        else:
            cross = []
            crossed = tree.across(join([own[h], *straight], queries[4], queries[-1]), [0, *steps])
        pieces.append([own[h], *straight, *cross, crossed])

    half = tree_dev // 2

    def attend(h):
        return pl.pallas_call(
            lambda *refs: main_kernel(blocks, block_len, tree_dev, inv_root, len(pieces[h]), *refs),
            out_shape=(
                sds((head_dim, rows), F32),
                sds((8, head_dim), F32),
                *[sds((tokens, 2 * head_dim), BF16)] * half,
                sds((half, tokens, 2 * head_dim), BF16),
            ),
            in_specs=[smem] + [vmem] * (10 + len(pieces[h])),
            out_specs=tuple([vmem] * (3 + half)),
            scratch_shapes=[
                pltpu.VMEM((tree_dev, tokens, 2 * head_dim), BF16),
                pltpu.VMEM((tree_dev + 1, tokens, head_dim), BF16),
                pltpu.VMEM((tree_dev + 1, head_dim, tokens), BF16),
                pltpu.VMEM((tree_dev + 1, tokens, head_dim), BF16),
                pltpu.VMEM((tree_dev + 1, 8 * ((blocks + 7) // 8), tokens), F32),
                pltpu.VMEM((tree_dev + 1, tokens, head_dim), F32),
                pltpu.VMEM((tree_dev + 1, tokens, head_dim), F32),
                pltpu.VMEM((tree_dev, group, tokens, tokens), F32),
                pltpu.VMEM((group, 8, tokens), F32),
                *[pltpu.VMEM((tokens, rows), BF16)] * 4,
                pltpu.VMEM((tree_dev, tokens, 2 * head_dim), BF16),
                pltpu.VMEM((tree_dev, tokens, 2 * head_dim), BF16),
            ],
            compiler_params=pltpu.CompilerParams(vmem_limit_bytes=ATTEND_VMEM_LIMIT),
            cost_estimate=pl.CostEstimate(
                flops=10 * group * tokens * tree_dev * tokens * head_dim,
                bytes_accessed=8 * 1024 * 1024,
                transcendentals=group * tokens * tree_dev * tokens,
            ),
            name="attend",
        )(plan, k_gain_row, *tables, *pieces[h], *queries[5 * h:5 * h + 5])

    dq, attended, k_gain_parts = [], [], []
    for h in range(kv_heads):
        dq_here, k_gain_part, *parts, crossed_part = attend(h)
        dq.append(dq_here)
        k_gain_parts.append(k_gain_part)
        attended.append((parts, crossed_part))

    everyone = cycle * lax.axis_size("heads")
    dq_raw, gains = pl.pallas_call(
        lambda *refs: query_kernel(blocks, inv_root, kv_heads, *refs),
        out_shape=(sds((tokens, heads * head_dim), BF16), sds((everyone, 2, head_dim), F32)),
        in_specs=[smem] + [vmem] * (6 + 2 * kv_heads),
        out_specs=(vmem, vmem),
        compiler_params=params,
        name="query_back",
    )(depth, *tables, q_gain_row, q_raw, *dq, *k_gain_parts)

    terms, farthest = [], []
    for h, (parts, crossed_part) in enumerate(attended):
        others = tree.across(crossed_part, [0, *steps], back=True)
        if h < kv_heads - 1:
            merged = [
                (parts[i + 1].astype(F32) + others[i + 1].astype(F32)).astype(BF16) for i in range(len(steps))
            ]
            farthest.append(merged.pop())
        else:
            *merged, joined, gains = pl.pallas_call(
                merge_kernel,
                out_shape=(
                    *[sds((tokens, 2 * head_dim), BF16)] * (len(steps) - 1),
                    sds((kv_heads, tokens, 2 * head_dim), BF16),
                    sds(gains.shape, F32),
                ),
                in_specs=[vmem] * (len(steps) + 3),
                out_specs=tuple([vmem] * (len(steps) + 1)),
                compiler_params=params,
                name="merge",
            )(*parts[1:], others, gains, jnp.stack(farthest))
            joined = tree.home(joined, steps[-1])
        mine = [(parts[0], None), (others, 0)]
        terms.append(mine + [(tree.home(both, step), None) for both, step in zip(merged, steps)])
    for h in range(kv_heads):
        if h < kv_heads - 1:
            arrays, places = zip(*terms[h])
            early, gains = pl.pallas_call(
                lambda *refs: early_kernel(places, *refs),
                out_shape=(sds((tokens, 2 * head_dim), F32), sds(gains.shape, F32)),
                in_specs=[vmem] * (1 + len(arrays)),
                out_specs=(vmem, vmem),
                compiler_params=params,
                cost_estimate=slow,
                name="early",
            )(gains, *arrays)
            terms[h] = [(early, None)]
        terms[h].append((joined, h))
    gains = lax.all_to_all(gains, ("ctx", "heads"), 0, 0)

    arrays = [array for mine in terms for array, _ in mine]
    places = [[place for _, place in mine] for mine in terms]
    dk_raw, dv, q_total, k_total = pl.pallas_call(
        lambda *refs: key_kernel(blocks, places, *refs),
        out_shape=(sds(k_raw.shape, BF16), sds(k_raw.shape, BF16), *[sds((1, head_dim), F32)] * 2),
        in_specs=[smem] + [vmem] * (7 + len(arrays)),
        out_specs=(vmem, vmem, vmem, vmem),
        compiler_params=params,
        name="key_back",
    )(depth, *tables, k_gain_row, k_raw, gains, *arrays)
    return (dq_raw, dk_raw, dv, q_total.reshape(head_dim), k_total.reshape(head_dim))


def solution(mesh):
    split = P("ctx", "heads")
    return jax.shard_map(
        on_device,
        mesh=mesh,
        in_specs=(split, split, split, split, split, P(), P(), P("ctx", None)),
        out_specs=(split, split, split, P(), P()),
        check_vma=False,
    )
```
